32 devices in a mesh: dp: 4 (over y, x), expert: 8 (over z, core).
Axes of the slice: x: 2, y: 2, z: 4, core: 2. Of those that a mesh axis runs over, the one named last changes fastest.
Arguments:
- tokens: bfloat16 [10240, 1024], P(('dp', 'expert')), may hold values from -6 to 6
- attn_gain: bfloat16 [1024], P('dp'), may hold values from 0.5 to 1.5
- w_query: bfloat16 [1024, 1024], P('dp'), may hold values from -0.1875 to 0.1875
- w_keyval: bfloat16 [1024, 1024], P('dp'), may hold values from -0.1875 to 0.1875
- w_output: bfloat16 [1024, 1024], P('dp'), may hold values from -1.5 to 1.5
- moe_gain: bfloat16 [1024], P('dp'), may hold values from 0.5 to 1.5
- w_router: bfloat16 [1024, 32], P('dp'), may hold values from -0.09375 to 0.09375
- expert_in: bfloat16 [32, 1024, 1024], P('expert'), may hold values from -0.1875 to 0.1875
- expert_out: bfloat16 [32, 512, 1024], P('expert'), may hold values from -0.75 to 0.75
- cotangent: bfloat16 [10240, 1024], P(('dp', 'expert')), may hold values from -6 to 6
- routes: int32 [10240, 8], P(('dp', 'expert')), may hold values from 0 to 31, all different within a row; in each aligned block of 320 rows (0 to 319, 320 to 639, ...) at most 120 rows name the same one
- parents: int32 [32, 13], P(('dp', 'expert')), may hold values from 0 to 4, as said below
Outputs:
- block_out: bfloat16 [10240, 1024], P(('dp', 'expert'))
- input_grad: float32 [10240, 1024], P(('dp', 'expert'))
- grad_attn_gain: float32 [1024], P('dp')
- grad_w_query: float32 [1024, 1024], P('dp')
- grad_w_keyval: float32 [1024, 1024], P('dp')
- grad_w_output: float32 [1024, 1024], P('dp')
- grad_moe_gain: float32 [1024], P('dp')
- grad_w_router: float32 [1024, 32], P('dp')
- grad_expert_in: float32 [32, 1024, 1024], P('expert', 'dp')
- grad_expert_out: float32 [32, 512, 1024], P('expert', 'dp')
The draws below stay inside these ranges and needn't reach their ends.
Inputs may be any that keep to these rules, and one draw needn't show every extreme that they name: `routes`: each row names 8 different experts. In each aligned block of 320 rows (the rows of one tree) no expert is named by more than 120 rows, and in some block one expert is named by exactly 120 rows. `parents`: in each tree, segments 0 to 4 have parent 0, and segments 5 to 12 name each of 1, 2, 3, 4 as parent exactly twice.
All inputs are finite; a program needn't handle non-finite values.
Results may differ from the reference program's by a relative error of at most 0.02.
Values may be sent and summed in bfloat16 or wider, within the bound.
A program may use at most 256 MiB of HBM per device.

```python
import math
import jax
import jax.numpy as jnp
import numpy as np
from jax import lax

D = 1024
H = 16
KV = 8
HD = 64
FF = 512
EXPERTS = 32
TOPK = 8
TOK_DEV = 320
CAP = 120
TREES = 32
TOKENS = 10240


def draw_parents(key, part):
    key = jax.random.fold_in(key, 7)
    pattern = jnp.array([0, 0, 1, 1, 2, 2, 3, 3], jnp.int32)
    tree_keys = jax.random.split(key, TREES)
    leaf_parents = jax.vmap(lambda tree_key: jax.random.permutation(tree_key, pattern))(tree_keys) + 1
    heads = jnp.zeros((TREES, 5), jnp.int32)
    return jnp.concatenate([heads, leaf_parents.astype(jnp.int32)], axis=1)


def block_scale(own_key, shape, cuts, smallest, largest):
    factor_of, own = 1.0, jax.random.fold_in(own_key, 6)
    for axis_at, blocks in cuts:
        steps = jnp.exp(jax.random.uniform(jax.random.fold_in(own, axis_at), (blocks,), jnp.float32, smallest / len(cuts), largest / len(cuts)))
        factor_of = factor_of * jnp.repeat(steps, shape[axis_at] // blocks).reshape([-1 if axis == axis_at else 1 for axis in range(len(shape))])
    return factor_of


def deal_out(own_key, own, number, rows, count, top, most, lean):
    ranking = jax.random.permutation(own_key, count)
    crowded, common = shares(count, rows * top, most, lean, True), shares(count, rows * top, most, lean, False)
    places = jnp.arange(count)

    def named(tallies, offset_by):
        used = int((tallies > 0).sum())
        fixed = max(1, used // 4)
        moved = fixed + (places - fixed + offset_by * (used - fixed)) % max(1, count - fixed)
        return jnp.zeros((count,), jnp.int32).at[ranking[jnp.where(places < fixed, places, moved)]].set(jnp.asarray(tallies, jnp.int32))

    tallies = jnp.where(number % 4 == 0, named(crowded, number // 4), named(common, number - number // 4 - 1))
    mixed = jax.random.permutation(jax.random.fold_in(own, 3), count)
    giver, taker = mixed[0:count // 2 * 2:2], mixed[1:count // 2 * 2:2]
    margin = jnp.minimum(tallies[giver] - 1, most - tallies[taker]) // 2
    margin = jnp.where((giver == ranking[0]) | (taker == ranking[0]) | (tallies[taker] == 0), 0, jnp.maximum(margin, 0))
    moved = jax.random.randint(jax.random.fold_in(own, 4), (count // 2,), 0, 1 << 20) % (margin + 1)
    tallies = tallies.at[giver].add(-moved).at[taker].add(moved)
    items = jnp.searchsorted(jnp.cumsum(tallies), jnp.arange(rows * top), side="right").astype(jnp.int32)
    grid = items.reshape(top, rows).T
    grid = grid[jax.random.permutation(jax.random.fold_in(own, 1), rows)]
    offset_by = jax.random.randint(jax.random.fold_in(own, 2), (rows, 1), 0, top)
    return jnp.take_along_axis(grid, (jnp.arange(top)[None, :] + offset_by) % top, axis=1)


def shares(count, total, most, slope, full):
    loads = [(1 << 20) // math.isqrt(standing ** slope) + 1 for standing in range(1, count + 1)]
    largest = most if full else min(most, max(-(-total // count), total * loads[0] // sum(loads)))
    least = 1 if total - largest >= count - 1 else 0
    given, rest = [largest] + [least] * (count - 1), total - largest - least * (count - 1)
    while rest > 0:
        candidates = [i for i in range(1, count) if given[i] < largest] or [i for i in range(1, count) if given[i] < most]
        whole, left = sum([loads[i] for i in candidates]), rest
        for i in candidates:
            extra = min(most - given[i], max(1, left * loads[i] // whole), rest)
            given[i] = given[i] + extra
            rest = rest - extra
    return np.array(given)


def normal_values(own_key, extent, width, limit, cuts=(), kind=jnp.bfloat16):
    values = jax.random.normal(own_key, extent, jnp.float32) * width
    if len(cuts) > 0:
        values = block_scale(own_key, extent, cuts, -0.22, 0.18) * values
    return jnp.clip(values, min=-limit, max=limit).astype(kind)


def setup_inputs(seed: int = 0) -> dict:
    splits = jax.random.split(jax.random.key(seed), 13)
    tokens = normal_values(splits[0], (TOKENS, D), 1.0, 6.0, ((0, 32),))
    attn_gain = jnp.clip(1.0 + 0.1 * jax.random.normal(splits[1], (D,), jnp.float32), 0.5, 1.5).astype(jnp.bfloat16)
    w_query = normal_values(splits[2], (D, H * HD), D ** -0.5, 0.1875, ((0, 4),))
    w_keyval = normal_values(splits[3], (D, 2 * KV * HD), D ** -0.5, 0.1875, ((0, 4),))
    w_output = normal_values(splits[4], (H * HD, D), (max(H * HD // 64, 4)) ** -0.5, 1.5, ((0, 4),))
    moe_gain = jnp.clip(1.0 + 0.1 * jax.random.normal(splits[5], (D,), jnp.float32), 0.5, 1.5).astype(jnp.bfloat16)
    w_router = normal_values(splits[6], (D, EXPERTS), (4 * D) ** -0.5, 0.09375, ((0, 4),))
    expert_in = normal_values(splits[7], (EXPERTS, D, 2 * FF), D ** -0.5, 0.1875, ((0, 8),))
    expert_out = normal_values(splits[8], (EXPERTS, FF, D), (FF // 8) ** -0.5, 0.75, ((0, 8),))
    cotangent = normal_values(splits[9], (TOKENS, D), 1.0, 6.0, ((0, 32),))
    routes_keys = jax.random.split(jax.random.fold_in(splits[10], 1), TOKENS // TOK_DEV)
    routes_turns = jax.random.permutation(jax.random.fold_in(splits[10], 3), TOKENS // TOK_DEV)
    routes = jax.vmap(lambda own, number: deal_out(jax.random.fold_in(splits[10], 2), own, number, TOK_DEV, EXPERTS, TOPK, CAP, 1))(routes_keys, routes_turns).reshape((TOKENS, TOPK))
    parents = draw_parents(jax.random.fold_in(splits[12], 71), 0)
    return {"tokens": tokens, "attn_gain": attn_gain, "w_query": w_query, "w_keyval": w_keyval, "w_output": w_output, "moe_gain": moe_gain, "w_router": w_router, "expert_in": expert_in, "expert_out": expert_out, "cotangent": cotangent, "routes": routes, "parents": parents}


EPSILON = 1e-06
HIGHEST = lax.Precision.HIGHEST

@jax.custom_vjp
def low(v):
    return lax.optimization_barrier(v.astype(jnp.bfloat16)).astype(jnp.float32)

@jax.custom_vjp
def low_back(v):
    return v

def low_keep(v):
    return (low(v), None)

def low_pass(kept, grad):
    return (grad,)

def back_keep(v):
    return (v, None)

def back_low(kept, grad):
    return (low(grad),)
low.defvjp(low_keep, low_pass)
low_back.defvjp(back_keep, back_low)

def tree_layout(tree_rows):
    unit_rows = tree_rows // 20
    row_index = jnp.arange(tree_rows, dtype=jnp.int32)
    segment = jnp.where(row_index < 8 * unit_rows, 0, jnp.where(row_index < 12 * unit_rows, 1 + (row_index - 8 * unit_rows) // unit_rows, 5 + (row_index - 12 * unit_rows) // unit_rows)).astype(jnp.int32)
    depth_start = jnp.where(segment == 0, 0, jnp.where(segment < 5, 8 * unit_rows, 9 * unit_rows))
    seg_start = jnp.where(segment == 0, 0, jnp.where(segment < 5, 8 * unit_rows + (segment - 1) * unit_rows, 12 * unit_rows + (segment - 5) * unit_rows))
    position = (depth_start + row_index - seg_start).astype(jnp.int32)
    return (segment, position)

def path_allowed(parent_row, segment):
    segment_ids = jnp.arange(parent_row.shape[0], dtype=jnp.int32)
    grandparent = parent_row[parent_row]
    on_path = ((segment_ids[None, :] == segment_ids[:, None]) | (segment_ids[None, :] == parent_row[:, None]) | (segment_ids[None, :] == grandparent[:, None])).astype(jnp.float32)
    seg_hot = (segment[:, None] == segment_ids[None, :]).astype(jnp.float32)
    reach = jnp.dot(jnp.dot(seg_hot, on_path, precision=HIGHEST), seg_hot.T, precision=HIGHEST)
    row_index = jnp.arange(segment.shape[0], dtype=jnp.int32)
    return (reach > 0.5) & (row_index[None, :] <= row_index[:, None])

def rope_tables(position):
    frequency = 10000.0 ** (-jnp.arange(0, HD, 2, dtype=jnp.float32) / HD)
    angles = position.astype(jnp.float32)[:, None] * frequency[None, :]
    return (jnp.concatenate([jnp.cos(angles)] * 2, -1), jnp.concatenate([jnp.sin(angles)] * 2, -1))

def rotary(field, cosine, sine_table):
    half_width = field.shape[-1] // 2
    turned = jnp.concatenate([-field[..., half_width:], field[..., :half_width]], axis=-1)
    return field * cosine + turned * sine_table

def rms_norm(field, gain_vector):
    return field * lax.rsqrt(lax.optimization_barrier(jnp.mean(field * field, axis=-1, keepdims=True)) + EPSILON) * gain_vector

def swish_act(field):
    return field / (1.0 + jnp.exp(-field))

def slot_tables(route_rows, capacity):
    flat_routes = route_rows.reshape(-1)
    row_total = flat_routes.shape[0]
    expert_ids = jnp.arange(EXPERTS, dtype=jnp.int32)
    route_hot = (flat_routes[:, None] == expert_ids[None, :]).astype(jnp.int32)
    before = jnp.cumsum(route_hot, axis=0) - route_hot
    slot_rank = lax.optimization_barrier(jnp.sum(before * route_hot, axis=1))
    slot_index = (flat_routes * capacity + slot_rank).astype(jnp.int32)
    source = jnp.full((EXPERTS * capacity,), row_total, jnp.int32).at[slot_index].set(jnp.arange(row_total, dtype=jnp.int32))
    return (slot_index, source)

def tree_forward(weights, inputs, route_rows, parent_row):
    gain_first, query_full, keyval_full, output_full, gain_second, router_full, gate_up_w, down_w = weights
    tree_rows = inputs.shape[0]
    groups = H // KV
    segment, position = tree_layout(tree_rows)
    allowed = path_allowed(parent_row, segment)
    cosine, sine_table = rope_tables(position)
    hidden = low(rms_norm(inputs, gain_first))
    query_pre = low_back(jnp.dot(hidden, query_full, precision=HIGHEST))
    keyval_pre = low_back(jnp.dot(hidden, keyval_full, precision=HIGHEST))
    queries = low(rotary(query_pre.reshape(tree_rows, KV, groups, HD), cosine[:, None, None, :], sine_table[:, None, None, :]))
    key_heads = low(rotary(keyval_pre[:, :KV * HD].reshape(tree_rows, KV, HD), cosine[:, None, :], sine_table[:, None, :]))
    values = low(keyval_pre[:, KV * HD:].reshape(tree_rows, KV, HD))
    scores = low_back(jnp.einsum('tkgd,skd->kgts', queries, key_heads, precision=HIGHEST) * HD ** (-0.5))
    scores = jnp.where(allowed, scores, -1e+30)
    row_max = lax.optimization_barrier(jnp.max(scores, axis=-1, keepdims=True))
    exp_scores = jnp.exp(scores - row_max)
    attn_probs = low(exp_scores / lax.optimization_barrier(jnp.sum(exp_scores, axis=-1, keepdims=True)))
    attended = jnp.einsum('kgts,skd->tkgd', attn_probs, values, precision=HIGHEST).reshape(tree_rows, H * HD)
    attended = low(low_back(attended))
    middle = inputs + low_back(jnp.dot(attended, output_full, precision=HIGHEST))
    hidden2 = low(rms_norm(middle, gain_second))
    logits = low_back(jnp.dot(hidden2, router_full, precision=HIGHEST))
    picked = jnp.take_along_axis(logits, route_rows, axis=1)
    picked_max = lax.optimization_barrier(jnp.max(picked, axis=1, keepdims=True))
    picked_exp = jnp.exp(picked - picked_max)
    gate_weights = picked_exp / lax.optimization_barrier(jnp.sum(picked_exp, axis=1, keepdims=True))
    capacity = CAP
    slot_index, source = slot_tables(route_rows, capacity)
    row_copies = low_back(jnp.repeat(hidden2, TOPK, axis=0))
    padded = jnp.concatenate([row_copies, jnp.zeros((1, D), jnp.float32)], axis=0)
    sent_rows = padded[source].reshape(EXPERTS, capacity, D)
    gate_up = low_back(jnp.einsum('ecd,edf->ecf', sent_rows, gate_up_w, precision=HIGHEST))
    activated = low(swish_act(gate_up[..., :FF]) * gate_up[..., FF:])
    expert_made = low(low_back(jnp.einsum('ecf,efd->ecd', activated, down_w, precision=HIGHEST)))
    back_rows = expert_made.reshape(EXPERTS * capacity, D)[slot_index].reshape(tree_rows, TOPK, D)
    return middle + lax.optimization_barrier(jnp.sum(gate_weights[:, :, None] * back_rows, axis=1))

def reference(tokens, attn_gain, w_query, w_keyval, w_output, moe_gain, w_router, expert_in, expert_out, cotangent, routes, parents):
    weights = tuple((weight_item.astype(jnp.float32) for weight_item in (attn_gain, w_query, w_keyval, w_output, moe_gain, w_router, expert_in, expert_out)))
    inputs = tokens.astype(jnp.float32).reshape(TREES, TOK_DEV, D)
    route_trees = routes.reshape(TREES, TOK_DEV, TOPK)
    checked = jax.checkpoint(tree_forward)

    def forward(weight_set, input_set):

        def scan_step(carry_value, tree_item):
            return (carry_value, checked(weight_set, tree_item[0], tree_item[1], tree_item[2]))
        _, outputs = lax.scan(scan_step, jnp.zeros((), jnp.float32), (input_set, route_trees, parents))
        return outputs
    result, pullback = jax.vjp(forward, weights, inputs)
    grad_weights, grad_inputs = pullback(cotangent.astype(jnp.float32).reshape(TREES, TOK_DEV, D))
    return (result.reshape(TOKENS, D).astype(jnp.bfloat16), grad_inputs.reshape(TOKENS, D), grad_weights[0], grad_weights[1], grad_weights[2], grad_weights[3], grad_weights[4], grad_weights[5], grad_weights[6], grad_weights[7])
```

```python
import jax
import jax.numpy as jnp
from jax import lax
from jax.sharding import PartitionSpec as P

H = 16
KV = 8
HD = 64
EXPERTS = 32
TOPK = 8
CAP = 120


EPSILON = 1e-06


def tree_layout(tree_rows):
    unit_rows = tree_rows // 20
    row_index = jnp.arange(tree_rows, dtype=jnp.int32)
    segment = jnp.where(
        row_index < 8 * unit_rows,
        0,
        jnp.where(
            row_index < 12 * unit_rows,
            1 + (row_index - 8 * unit_rows) // unit_rows,
            5 + (row_index - 12 * unit_rows) // unit_rows,
        ),
    )
    depth_start = jnp.where(segment == 0, 0, jnp.where(segment < 5, 8 * unit_rows, 9 * unit_rows))
    seg_start = jnp.where(
        segment == 0,
        0,
        jnp.where(
            segment < 5,
            8 * unit_rows + (segment - 1) * unit_rows,
            12 * unit_rows + (segment - 5) * unit_rows,
        ),
    )
    position = depth_start + row_index - seg_start
    return (segment, position)


def path_allowed(parent_row, segment):
    segment_ids = jnp.arange(parent_row.shape[0], dtype=jnp.int32)
    grandparent = parent_row[parent_row]
    on_path = (
        (segment_ids[None, :] == segment_ids[:, None])
        | (segment_ids[None, :] == parent_row[:, None])
        | (segment_ids[None, :] == grandparent[:, None])
    ).astype(jnp.float32)
    seg_hot = (segment[:, None] == segment_ids[None, :]).astype(jnp.float32)
    reach = jnp.dot(
        jnp.dot(seg_hot, on_path, precision=lax.Precision.HIGHEST),
        seg_hot.T,
        precision=lax.Precision.HIGHEST,
    )
    row_index = jnp.arange(segment.shape[0], dtype=jnp.int32)
    return (reach > 0.5) & (row_index[None, :] <= row_index[:, None])


def rope_tables(position):
    frequency = 10000.0 ** (-jnp.arange(0, HD, 2, dtype=jnp.float32) / HD)
    angles = position.astype(jnp.float32)[:, None] * frequency[None, :]
    return (jnp.concatenate([jnp.cos(angles)] * 2, -1), jnp.concatenate([jnp.sin(angles)] * 2, -1))


def turn_half(field):
    half_width = field.shape[-1] // 2
    return jnp.concatenate([-field[..., half_width:], field[..., :half_width]], axis=-1)


def rotary(field, cosine, sine_table):
    return field * cosine + turn_half(field) * sine_table


def unrotate(grad_field, cosine, sine_table):
    return grad_field * cosine - turn_half(grad_field * sine_table)


def rms_norm(field, gain_vector):
    return (
        field * lax.rsqrt(jnp.mean(field * field, axis=-1, keepdims=True) + EPSILON) * gain_vector
    )


def gated_unit(gate_up):
    width_ff = gate_up.shape[-1] // 2
    gate_part = gate_up[..., :width_ff]
    return gate_part / (1.0 + jnp.exp(-gate_part)) * gate_up[..., width_ff:]


def shards(
    tokens,
    attn_gain,
    w_query,
    w_keyval,
    w_output,
    moe_gain,
    w_router,
    expert_in,
    expert_out,
    cotangent,
    routes,
    parents,
):
    tree_rows = tokens.shape[0]
    width = tokens.shape[1]
    capacity = CAP
    groups = H // KV
    kv_width = KV * HD
    score_scale = HD ** (-0.5)
    gathered = (
        lax.all_gather(attn_gain, "dp", axis=0, tiled=True),
        lax.all_gather(w_query, "dp", axis=0, tiled=True),
        lax.all_gather(w_keyval, "dp", axis=0, tiled=True),
        lax.all_gather(w_output, "dp", axis=0, tiled=True),
        lax.all_gather(moe_gain, "dp", axis=0, tiled=True),
        lax.all_gather(w_router, "dp", axis=0, tiled=True),
    )
    gain_first, query_full, keyval_full, output_full, gain_second, router_full = gathered
    inputs = tokens.astype(jnp.float32)
    segment, position = tree_layout(tree_rows)
    allowed = path_allowed(parents[0], segment)
    cosine, sine_table = rope_tables(position)
    cos_four, sin_four = (cosine[:, None, None, :], sine_table[:, None, None, :])
    cos_three, sin_three = (cosine[:, None, :], sine_table[:, None, :])
    normed, first_back = jax.vjp(rms_norm, inputs, gain_first.astype(jnp.float32))
    hidden = normed.astype(jnp.bfloat16)
    query_pre = jnp.dot(hidden, query_full, preferred_element_type=jnp.float32)
    keyval_pre = jnp.dot(hidden, keyval_full, preferred_element_type=jnp.float32)
    queries = rotary(query_pre.reshape(tree_rows, KV, groups, HD), cos_four, sin_four).astype(
        jnp.bfloat16
    )
    key_heads = rotary(
        keyval_pre[:, :kv_width].reshape(tree_rows, KV, HD), cos_three, sin_three
    ).astype(jnp.bfloat16)
    values = keyval_pre[:, kv_width:].reshape(tree_rows, KV, HD).astype(jnp.bfloat16)

    def score_block():
        raw_scores = (
            jnp.einsum("tkgd,skd->kgts", queries, key_heads, preferred_element_type=jnp.float32)
            * score_scale
        )
        return jnp.where(allowed, raw_scores, -1e30)

    scores = score_block()
    row_max = jnp.max(scores, axis=-1, keepdims=True)
    exp_scores = jnp.exp(scores - row_max)
    row_total = jnp.sum(exp_scores, axis=-1, keepdims=True)
    log_total = row_max + jnp.log(row_total)
    attn_low = (exp_scores / row_total).astype(jnp.bfloat16)
    attended = jnp.einsum("kgts,skd->tkgd", attn_low, values, preferred_element_type=jnp.float32)
    attended = attended.reshape(tree_rows, H * HD).astype(jnp.bfloat16)
    middle = inputs + jnp.dot(attended, output_full, preferred_element_type=jnp.float32)
    normed2, second_back = jax.vjp(rms_norm, middle, gain_second.astype(jnp.float32))
    hidden2 = normed2.astype(jnp.bfloat16)
    logits = jnp.dot(hidden2, router_full, preferred_element_type=jnp.float32)
    expert_ids = jnp.arange(EXPERTS, dtype=jnp.int32)
    route_hot = (routes[:, :, None] == expert_ids[None, None, :]).astype(jnp.float32)
    picked = jnp.sum(route_hot * logits[:, None, :], axis=2)
    picked_exp = jnp.exp(picked - jnp.max(picked, axis=1, keepdims=True))
    gate_weights = picked_exp / jnp.sum(picked_exp, axis=1, keepdims=True)
    trees = lax.axis_size("expert")
    here = lax.axis_index("expert")
    local = expert_in.shape[0]
    first = here * local
    routes_all = lax.all_gather(routes, "expert", axis=0, tiled=False)
    grad_y = lax.all_gather(cotangent, "expert", axis=0, tiled=False)
    hidden_all = lax.all_gather(hidden2, "expert", axis=0, tiled=False)
    own_ids = first + jnp.arange(local, dtype=jnp.int32)
    hot_all = routes_all[:, :, :, None] == expert_ids[None, None, None, :]
    chosen_all = jnp.any(hot_all, axis=2)
    chosen = jnp.any(routes_all[:, :, :, None] == own_ids[None, None, None, :], axis=2)
    lower = jnp.tril(jnp.ones((tree_rows, tree_rows), jnp.bfloat16), -1)
    rank = jnp.einsum(
        "tu,jue->jet", lower, chosen.astype(jnp.bfloat16), preferred_element_type=jnp.float32
    ).astype(jnp.int32)
    slots = jnp.arange(capacity, dtype=jnp.int32)
    chosen_t = chosen.transpose(0, 2, 1)
    place = (rank[:, :, None, :] == slots[None, None, :, None]) & chosen_t[:, :, None, :]
    place = place.astype(jnp.bfloat16)
    logits_all = jnp.einsum(
        "jtd,de->jte", hidden_all, router_full, preferred_element_type=jnp.float32
    )
    masked = jnp.where(chosen_all, logits_all, -1e30)
    weight = jnp.exp(masked - jnp.max(masked, axis=-1, keepdims=True))
    weight = weight / jnp.sum(weight, axis=-1, keepdims=True)
    gates_own = lax.dynamic_slice_in_dim(weight, first, local, axis=2)
    gate_slot = jnp.einsum(
        "jest,jte->ejs", place.astype(jnp.float32), gates_own, precision=lax.Precision.HIGHEST
    )[..., None]
    sent = jnp.einsum("jest,jtd->ejsd", place, hidden_all, preferred_element_type=jnp.float32)
    sent = sent.astype(jnp.bfloat16)
    grad_rows = jnp.einsum("jest,jtd->ejsd", place, grad_y, preferred_element_type=jnp.float32)
    grad_rows = grad_rows.astype(jnp.bfloat16)
    gate_up = jnp.einsum("ejsd,edf->ejsf", sent, expert_in, preferred_element_type=jnp.float32)
    activated, glu_back = jax.vjp(gated_unit, gate_up)
    act_low = activated.astype(jnp.bfloat16).astype(jnp.float32)
    act_scaled = (act_low * gate_slot).astype(jnp.bfloat16)
    made = jnp.einsum(
        "ejsf,efd->ejsd", act_scaled, expert_out, preferred_element_type=jnp.float32
    ).astype(jnp.bfloat16)
    out_part = jnp.einsum("jest,ejsd->jtd", place, made, preferred_element_type=jnp.float32)
    out_sum = lax.psum_scatter(
        out_part.astype(jnp.bfloat16), "expert", scatter_dimension=0, tiled=False
    ).astype(jnp.float32)
    result = middle + out_sum
    block_out = result.astype(jnp.bfloat16)
    grad_result = cotangent.astype(jnp.float32)
    grad_act = jnp.einsum(
        "ejsd,efd->ejsf", grad_rows, expert_out, preferred_element_type=jnp.float32
    )
    gate_dot = jnp.sum(act_low * grad_act, axis=-1)
    gates_back = jnp.einsum(
        "jest,ejs->jte", place.astype(jnp.float32), gate_dot, precision=lax.Precision.HIGHEST
    )
    grad_out_w = jnp.einsum(
        "ejsf,ejsd->efd", act_scaled, grad_rows, preferred_element_type=jnp.float32
    )
    grad_gate_up = glu_back(grad_act * gate_slot)[0].astype(jnp.bfloat16)
    grad_sent = jnp.einsum(
        "ejsf,edf->ejsd", grad_gate_up, expert_in, preferred_element_type=jnp.float32
    ).astype(jnp.bfloat16)
    grad_in_w = jnp.einsum(
        "ejsd,ejsf->edf", sent, grad_gate_up, preferred_element_type=jnp.float32
    )
    hid_part = jnp.einsum("jest,ejsd->jtd", place, grad_sent, preferred_element_type=jnp.float32)
    gates_mine = lax.all_to_all(gates_back, "expert", split_axis=0, concat_axis=2, tiled=True)[0]
    hid_sum = lax.psum_scatter(
        hid_part.astype(jnp.bfloat16), "expert", scatter_dimension=0, tiled=False
    ).astype(jnp.float32)
    gate_dense = jnp.sum(route_hot * gate_weights[:, :, None], axis=1)
    grad_logits = (
        gate_dense
        * (gates_mine - jnp.sum(gate_dense * gates_mine, axis=1, keepdims=True))
    ).astype(jnp.bfloat16)
    grad_router = jnp.einsum("td,te->de", hidden2, grad_logits, preferred_element_type=jnp.float32)
    grad_hidden2 = hid_sum + jnp.einsum(
        "te,de->td", grad_logits, router_full, preferred_element_type=jnp.float32
    )
    expert_in_share, expert_out_share = (
        lax.psum_scatter(
            grad_in_w.astype(jnp.bfloat16), "dp", scatter_dimension=1, tiled=True
        ).astype(jnp.float32),
        lax.psum_scatter(
            grad_out_w.astype(jnp.bfloat16), "dp", scatter_dimension=1, tiled=True
        ).astype(jnp.float32),
    )
    grad_mid_norm, grad_gain_second = second_back(grad_hidden2)
    grad_middle = grad_result + grad_mid_norm
    grad_branch = grad_middle.astype(jnp.bfloat16)
    grad_w_out = jnp.einsum("ti,td->id", attended, grad_branch, preferred_element_type=jnp.float32)
    grad_attended = jnp.einsum(
        "td,id->ti", grad_branch, output_full, preferred_element_type=jnp.float32
    )
    grad_attended = grad_attended.astype(jnp.bfloat16).reshape(tree_rows, KV, groups, HD)
    attn_probs = jnp.exp(score_block() - log_total)
    probs_low = attn_probs.astype(jnp.bfloat16)
    grad_values = jnp.einsum(
        "kgts,tkgd->skd", probs_low, grad_attended, preferred_element_type=jnp.float32
    )
    grad_probs = jnp.einsum(
        "tkgd,skd->kgts", grad_attended, values, preferred_element_type=jnp.float32
    )
    grad_scores = (
        attn_probs * (grad_probs - jnp.sum(attn_probs * grad_probs, axis=-1, keepdims=True))
    ).astype(jnp.bfloat16)
    grad_query_rot = (
        jnp.einsum("kgts,skd->tkgd", grad_scores, key_heads, preferred_element_type=jnp.float32)
        * score_scale
    )
    grad_keys_rot = (
        jnp.einsum("kgts,tkgd->skd", grad_scores, queries, preferred_element_type=jnp.float32)
        * score_scale
    )
    grad_query_pre = (
        unrotate(grad_query_rot, cos_four, sin_four).reshape(tree_rows, H * HD).astype(jnp.bfloat16)
    )
    grad_keyval_pre = jnp.concatenate(
        [
            unrotate(grad_keys_rot, cos_three, sin_three).reshape(tree_rows, kv_width),
            grad_values.reshape(tree_rows, kv_width),
        ],
        axis=1,
    ).astype(jnp.bfloat16)
    grad_w_q = jnp.einsum("td,ti->di", hidden, grad_query_pre, preferred_element_type=jnp.float32)
    grad_w_kv = jnp.einsum("td,ti->di", hidden, grad_keyval_pre, preferred_element_type=jnp.float32)
    grad_hidden = jnp.einsum(
        "ti,di->td", grad_query_pre, query_full, preferred_element_type=jnp.float32
    ) + jnp.einsum("ti,di->td", grad_keyval_pre, keyval_full, preferred_element_type=jnp.float32)
    grad_in_norm, grad_gain_first = first_back(grad_hidden)
    input_grad = grad_middle + grad_in_norm
    pieces = (
        lax.psum_scatter(
            grad_gain_first.astype(jnp.bfloat16), "dp", scatter_dimension=0, tiled=True
        ).astype(jnp.float32),
        lax.psum_scatter(
            grad_w_q.astype(jnp.bfloat16), "dp", scatter_dimension=0, tiled=True
        ).astype(jnp.float32),
        lax.psum_scatter(
            grad_w_kv.astype(jnp.bfloat16), "dp", scatter_dimension=0, tiled=True
        ).astype(jnp.float32),
        lax.psum_scatter(
            grad_w_out.astype(jnp.bfloat16), "dp", scatter_dimension=0, tiled=True
        ).astype(jnp.float32),
        lax.psum_scatter(
            grad_gain_second.astype(jnp.bfloat16), "dp", scatter_dimension=0, tiled=True
        ).astype(jnp.float32),
        lax.psum_scatter(
            grad_router.astype(jnp.bfloat16), "dp", scatter_dimension=0, tiled=True
        ).astype(jnp.float32),
    )
    shares = (
        lax.psum(pieces[0].astype(jnp.bfloat16), "expert").astype(jnp.float32),
        lax.psum(pieces[1].astype(jnp.bfloat16), "expert").astype(jnp.float32),
        lax.psum(pieces[2].astype(jnp.bfloat16), "expert").astype(jnp.float32),
        lax.psum(pieces[3].astype(jnp.bfloat16), "expert").astype(jnp.float32),
        lax.psum(pieces[4].astype(jnp.bfloat16), "expert").astype(jnp.float32),
        lax.psum(pieces[5].astype(jnp.bfloat16), "expert").astype(jnp.float32),
    )
    return (
        block_out,
        input_grad,
        shares[0],
        shares[1],
        shares[2],
        shares[3],
        shares[4],
        shares[5],
        expert_in_share,
        expert_out_share,
    )


def solution(mesh):
    in_specs = (
        P(("dp", "expert"), None),
        P("dp"),
        P("dp", None),
        P("dp", None),
        P("dp", None),
        P("dp"),
        P("dp", None),
        P("expert", None, None),
        P("expert", None, None),
        P(("dp", "expert"), None),
        P(("dp", "expert"), None),
        P(("dp", "expert"), None),
    )
    out_specs = (
        P(("dp", "expert"), None),
        P(("dp", "expert"), None),
        P("dp"),
        P("dp", None),
        P("dp", None),
        P("dp", None),
        P("dp"),
        P("dp", None),
        P("expert", "dp", None),
        P("expert", "dp", None),
    )
    return jax.shard_map(shards, mesh=mesh, in_specs=in_specs, out_specs=out_specs, check_vma=False)
```

```python
import functools

import jax
import jax.numpy as jnp
from jax import lax
from jax.experimental import pallas as pl
from jax.experimental.pallas import tpu as pltpu
from jax.sharding import PartitionSpec as P

H = 16
KV = 8
HD = 64
EXPERTS = 32
TOPK = 8
CAP = 120


EPSILON = 1e-06


MESH = pl.DeviceIdType.MESH
MIB = 1024 * 1024
VMEM = pltpu.VMEM
ANY = pl.ANY


def remote(src, dst, send_sem, recv_sem, **where):
    return pltpu.make_async_remote_copy(
        src_ref=src, dst_ref=dst, send_sem=send_sem, recv_sem=recv_sem,
        device_id=where, device_id_type=MESH,
    )


def greet(partners):
    barrier = pltpu.get_barrier_semaphore()
    for condition, where in partners:
        def signal(where=where):
            pl.semaphore_signal(barrier, inc=1, device_id=where, device_id_type=MESH)
        if condition is None:
            signal()
        else:
            pl.when(condition)(signal)
    count = sum(1 if c is None else c.astype(jnp.int32) for c, _ in partners)
    pl.semaphore_wait(barrier, count)


def add_rows(out, *terms, step=16):
    rows = out.shape[0]

    def body(i, carry):
        at = pl.ds(pl.multiple_of(i * step, step), step)
        total = terms[0][at, :].astype(jnp.float32)
        for term in terms[1:]:
            total = total + term[at, :].astype(jnp.float32)
        out[at, :] = total.astype(out.dtype)
        return carry

    lax.fori_loop(0, rows // step, body, 0)


def bit_orders(n):
    bits = [1 << j for j in range(n.bit_length() - 1)]
    return [bits[p:] + bits[:p] for p in range(len(bits))] or [[]]


def weights_body(n_dp, *refs):
    arrays = 4
    ins, outs = refs[:arrays], refs[arrays : 2 * arrays]
    send_sem, recv_sem, pair_send, pair_recv, own_sem = refs[2 * arrays :]
    me, mine = lax.axis_index("dp"), lax.axis_index("expert")
    core = lax.rem(mine, 2)
    pair = mine + 1 - 2 * core
    orders = bit_orders(n_dp)
    greet([(None, {"dp": me ^ bit}) for bit in orders[0]] + [(None, {"expert": pair})])
    shard = ins[0].shape[0]
    half = shard // 2
    sends, pairs, owns = [], [], []
    cuts = min(2, len(orders), half // 16)
    size = half // cuts

    def pieces(a):
        return cuts

    def rows(start, side, p):
        return pl.ds(pl.multiple_of(start + side * half + p * size, 16), size)

    def push(a, p, r, bit):
        to = me ^ bit
        there = outs[a].at[rows((me ^ r) * shard, core, p)]
        src = ins[a].at[rows(0, core, p)] if r == 0 else there
        copy = remote(src, there, send_sem.at[a, p, r, bit.bit_length() - 1], recv_sem.at[a, p, r ^ bit], dp=to)
        copy.start()
        sends.append(copy)

    for a in range(arrays):
        for p in range(pieces(a)):
            for bit in orders[p]:
                push(a, p, 0, bit)
    for a in range(arrays):
        copy = pltpu.make_async_copy(
            ins[a], outs[a].at[pl.ds(pl.multiple_of(me * shard, 16), shard)], own_sem.at[a])
        copy.start()
        owns.append(copy)
    def reach(order):
        blocks = [0]
        steps = []
        for j, bit in enumerate(order):
            new = [r | bit for r in blocks]
            steps.append((j, new))
            blocks = blocks + new
        return steps

    for j in range(len(orders[0])):
        for a in range(arrays):
            for p in range(pieces(a)):
                order = orders[p]
                for r in reach(order)[j][1]:
                    here = outs[a].at[rows((me ^ r) * shard, core, p)]
                    remote(here, here, send_sem.at[a, p, r, 0], recv_sem.at[a, p, r], dp=me).wait_recv()
                    for bit in order[j + 1 :]:
                        push(a, p, r, bit)
                    copy = remote(here, here, pair_send.at[a, p, r], pair_recv.at[a, p, r], expert=pair)
                    copy.start()
                    pairs.append((copy, a, p, r))
    for copy in owns:
        copy.wait()
    for copy in sends:
        copy.wait_send()
    for copy, a, p, r in pairs:
        copy.wait_send()
        here = outs[a].at[rows((me ^ r) * shard, 1 - core, p)]
        remote(here, here, pair_send.at[a, p, r], pair_recv.at[a, p, r], expert=pair).wait_recv()


def gather_weights(n_dp, arrays, collective_id):
    orders = bit_orders(n_dp)
    count, pieces = len(arrays), min(2, len(orders))
    out_shape = [jax.ShapeDtypeStruct((n_dp * a.shape[0], a.shape[1]), a.dtype) for a in arrays]
    return pl.pallas_call(
        functools.partial(weights_body, n_dp),
        out_shape=out_shape,
        in_specs=[pl.BlockSpec(memory_space=VMEM)] * count,
        out_specs=[pl.BlockSpec(memory_space=ANY)] * count,
        scratch_shapes=[
            pltpu.SemaphoreType.DMA((count, pieces, n_dp, max(1, n_dp.bit_length() - 1))),
            pltpu.SemaphoreType.DMA((count, pieces, n_dp)),
            pltpu.SemaphoreType.DMA((count, pieces, n_dp)),
            pltpu.SemaphoreType.DMA((count, pieces, n_dp)),
            pltpu.SemaphoreType.DMA((count,)),
        ],
        compiler_params=pltpu.CompilerParams(collective_id=collective_id, has_side_effects=True),
        name="gather_weights",
    )(*arrays)


class Ring:
    def __init__(self, n_exp):
        self.mine = lax.axis_index("expert")
        self.core = lax.rem(self.mine, 2)
        self.z = lax.div(self.mine, 2)
        self.depth = n_exp // 2
        self.far = self.depth // 2
        self.pair = self.mine + 1 - 2 * self.core
        self.right, self.left = self.dev(1), self.dev(-1)

    def dev(self, d):
        return lax.rem(self.z + d + self.depth, self.depth) * 2 + self.core

    def partners(self):
        return [(None, {"expert": e}) for e in (self.pair, self.right, self.left)]


class RingGather:
    def __init__(self, ring, own, out, sems):
        self.ring, self.own, self.out = ring, own, out
        self.send, self.recv, self.pair_send, self.pair_recv = sems
        self.half = own.shape[0] // 2
        self.copies, self.pairs = [], []

    @staticmethod
    def scratch(n_exp):
        far, depth = n_exp // 4, n_exp // 2
        sem = pltpu.SemaphoreType.DMA
        return [sem((2, far + 1, 2)), sem((2, far + 1, 2)), sem((depth, 2)), sem((depth, 2))]

    def rows(self, h):
        return pl.ds(h * self.half, self.half)

    def goes(self, side, s, h):
        far = self.ring.far
        return s < far or (s == far and h == side)

    def block(self, d, h):
        return self.out.at[self.ring.dev(d), self.rows(h)]

    def push(self, side, s, h):
        d = -s if side == 0 else s
        src = self.own.at[self.rows(h)] if s == 0 else self.block(d, h)
        to = self.ring.right if side == 0 else self.ring.left
        copy = remote(src, self.block(d, h), self.send.at[side, s, h], self.recv.at[side, s + 1, h], expert=to)
        copy.start()
        self.copies.append(copy)

    def across(self, d, h):
        src = self.own.at[self.rows(h)] if d == 0 else self.block(d, h)
        slot = d % self.ring.depth
        copy = remote(src, self.block(d, h), self.pair_send.at[slot, h], self.pair_recv.at[slot, h], expert=self.ring.pair)
        copy.start()
        self.pairs.append((copy, d, h))

    def start(self):
        for side, h in ((0, 0), (1, 1), (0, 1), (1, 0)):
            if self.goes(side, 1, h):
                self.push(side, 0, h)
        self.across(0, 0)
        self.across(0, 1)

    def events(self):
        return [
            (side, s, h)
            for s in range(1, self.ring.far + 1)
            for side, h in ((0, 0), (1, 1), (0, 1), (1, 0))
            if self.goes(side, s, h)
        ]

    def handle(self, event):
        side, s, h = event
        d = -s if side == 0 else s
        here = self.block(d, h)
        remote(here, here, self.send.at[side, s, h], self.recv.at[side, s, h], expert=self.ring.mine).wait_recv()
        if self.goes(side, s + 1, h):
            self.push(side, s, h)
        self.across(d, h)

    def wait_pair(self, d, h):
        slot = d % self.ring.depth
        here = self.out.at[self.ring.pair - self.ring.mine + self.ring.dev(d), self.rows(h)]
        remote(here, here, self.pair_send.at[slot, h], self.pair_recv.at[slot, h], expert=self.ring.mine).wait_recv()

    def finish_pairs(self):
        for _, d, h in self.pairs:
            self.wait_pair(d, h)

    def finish_sends(self):
        for copy in self.copies:
            copy.wait_send()
        for copy, _, _ in self.pairs:
            copy.wait_send()


class RingScatter:
    def __init__(self, ring, part, bufs, sems):
        self.ring, self.part = ring, part
        self.pair_buf, self.held, self.got = bufs
        self.pair_send, self.pair_recv, self.send, self.recv = sems
        self.half = self.held.shape[1] // 2
        self.copies = []

    @staticmethod
    def scratch(n_exp, block, dtype):
        far, depth = n_exp // 4, n_exp // 2
        sem = pltpu.SemaphoreType.DMA
        bufs = [pltpu.VMEM((depth,) + block, dtype), pltpu.VMEM((depth,) + block, dtype),
                pltpu.VMEM((2, far) + block, dtype)]
        return bufs, [sem((depth,)), sem((depth,)), sem((2, far + 1, 2)), sem((2, far + 1, 2))]

    def rows(self, h):
        return pl.ds(h * self.half, self.half)

    def order(self):
        far, depth = self.ring.far, self.ring.depth
        order = [far]
        for s in range(far - 1, 0, -1):
            order += [s, depth - s]
        return order + [0]

    def comes(self, side, d, h):
        far = self.ring.far
        return d + 1 < far or (d + 1 == far and h == side)

    def across(self, d):
        ring = self.ring
        return remote(self.part(ring.dev(d) + 1 - 2 * ring.core), self.pair_buf.at[d],
                      self.pair_send.at[d], self.pair_recv.at[d], expert=ring.pair)

    def start_pair(self, d):
        self.across(d).start()

    def wait_pair(self, d):
        self.across(d).wait_recv()

    def wait_got(self, side, d, h):
        here = self.got.at[side, d, self.rows(h)]
        remote(here, here, self.send.at[side, d, h], self.recv.at[side, d, h], expert=self.ring.mine).wait_recv()

    def push(self, side, d, h):
        ring = self.ring
        slot = d if side == 0 else ring.depth - d
        rows = self.rows(h)
        terms = [self.part(ring.dev(slot)).at[rows], self.pair_buf.at[slot, rows]]
        if self.comes(side, d, h):
            self.wait_got(side, d, h)
            terms.append(self.got.at[side, d, rows])
        add_rows(self.held.at[slot, rows], *terms)
        copy = remote(self.held.at[slot, rows], self.got.at[side, d - 1, rows], self.send.at[side, d, h],
                      self.recv.at[side, d - 1, h], expert=ring.right if side == 0 else ring.left)
        copy.start()
        self.copies.append(copy)

    def first(self):
        far = self.ring.far
        self.wait_pair(far)
        self.push(0, far, 0)
        self.push(1, far, 1)

    def rest(self):
        ring, far = self.ring, self.ring.far
        for d in range(far - 1, 0, -1):
            self.wait_pair(d)
            self.push(0, d, 1)
            self.wait_pair(ring.depth - d)
            self.push(1, d, 0)
            self.push(0, d, 0)
            self.push(1, d, 1)

    def last(self, out, *more):
        self.wait_pair(0)
        for h in range(2):
            rows = self.rows(h)
            terms = [self.part(self.ring.mine).at[rows], self.pair_buf.at[0, rows]] + [m.at[rows] for m in more]
            for side in range(2):
                if self.comes(side, 0, h):
                    self.wait_got(side, 0, h)
                    terms.append(self.got.at[side, 0, rows])
            add_rows(out.at[rows], *terms)

    def finish_sends(self):
        for copy in self.copies:
            copy.wait_send()
        for d in range(self.ring.depth):
            self.across(d).wait_send()


def ring_gather_body(n_exp, x_ref, out_ref, own_sem, *sems):
    ring = Ring(n_exp)
    greet(ring.partners())
    own = pltpu.make_async_copy(x_ref, out_ref.at[ring.mine], own_sem)
    own.start()
    gather = RingGather(ring, x_ref, out_ref, sems)
    gather.start()
    for event in gather.events():
        gather.handle(event)
    own.wait()
    gather.finish_pairs()
    gather.finish_sends()


def ring_gather(n_exp, x, collective_id):
    return pl.pallas_call(
        functools.partial(ring_gather_body, n_exp),
        out_shape=jax.ShapeDtypeStruct((n_exp,) + x.shape, x.dtype),
        in_specs=[pl.BlockSpec(memory_space=VMEM)],
        out_specs=pl.BlockSpec(memory_space=ANY),
        scratch_shapes=[pltpu.SemaphoreType.DMA] + RingGather.scratch(n_exp),
        compiler_params=pltpu.CompilerParams(collective_id=collective_id, has_side_effects=True),
        name="ring_gather",
    )(x)


def ring_scatter_body(n_exp, more, part, *refs):
    extra, (out, *rest) = refs[:more], refs[more:]
    ring = Ring(n_exp)
    greet(ring.partners())
    scatter = RingScatter(ring, lambda e: part.at[e], rest[:3], rest[3:])
    for d in scatter.order():
        scatter.start_pair(d)
    scatter.first()
    scatter.rest()
    scatter.last(out, *extra)
    scatter.finish_sends()


def ring_scatter(n_exp, part, more, out_type, collective_id):
    block = part.shape[1:]
    bufs, sems = RingScatter.scratch(n_exp, block, part.dtype)
    return pl.pallas_call(
        functools.partial(ring_scatter_body, n_exp, len(more)),
        out_shape=jax.ShapeDtypeStruct(block, out_type),
        in_specs=[pl.BlockSpec(memory_space=VMEM)] * (1 + len(more)),
        out_specs=pl.BlockSpec(memory_space=VMEM),
        scratch_shapes=bufs + sems,
        compiler_params=pltpu.CompilerParams(
            collective_id=collective_id, has_side_effects=True, vmem_limit_bytes=48 * MIB),
        name="ring_scatter",
    )(part, *more)


def grads_body(n_dp, n_exp, chunks, g_ref, out_ref, pair_buf, total, dp_buf, prefix, suffix, go_r, go_l, final, other,
               pair_send, pair_recv, dp_send, dp_recv, send_r, send_l, recv_r, recv_l, last_send, last_recv):
    me, mine = lax.axis_index("dp"), lax.axis_index("expert")
    core = lax.rem(mine, 2)
    z = lax.div(mine, 2)
    depth = n_exp // 2
    pair = mine + 1 - 2 * core
    has_left, has_right = z > 0, z < depth - 1
    orders = bit_orders(n_dp)
    rows = g_ref.shape[0] // n_dp
    half = rows // 2
    width = g_ref.shape[1] // chunks
    greet([(None, {"expert": pair})] + [(None, {"dp": me ^ bit}) for bit in orders[0]]
          + [(has_left, {"expert": mine - 2}), (has_right, {"expert": mine + 2})])

    def columns(i):
        return pl.ds(pl.multiple_of(i * width, 128), width)

    def block_of(d, side, i):
        return g_ref.at[pl.ds(pl.multiple_of(d * rows + side * half, 16), half), columns(i)]

    def across(i, d):
        return remote(block_of(d, 1 - core, i), pair_buf.at[i, d], pair_send.at[i, d], pair_recv.at[i, d], expert=pair)

    for i in range(chunks):
        for d in range(n_dp):
            across(i, d).start()

    def moved(i, j):
        order = orders[i % len(orders)]
        blocks = [0]
        for bit in order[j + 1 :]:
            blocks = blocks + [r | bit for r in blocks]
        return order[j], [r | order[j] for r in blocks]

    def dp_copy(i, j, r, bit):
        return remote(total.at[i, r], dp_buf.at[i, r ^ bit, j], dp_send.at[i, r], dp_recv.at[i, r ^ bit, j], dp=me ^ bit)

    stages = len(orders[0])
    for i in range(chunks):
        for r in range(n_dp - 1, -1, -1):
            d = me ^ r
            across(i, d).wait_recv()
            add_rows(total.at[i, r], block_of(d, core, i), pair_buf.at[i, d])
        if stages:
            bit, blocks = moved(i, 0)
            for r in blocks:
                dp_copy(i, 0, r, bit).start()
    for j in range(stages):
        for i in range(chunks):
            bit, blocks = moved(i, j)
            for r in blocks:
                kept = r ^ bit
                dp_copy(i, j, r, bit).wait_recv()
                add_rows(total.at[i, kept], total.at[i, kept], dp_buf.at[i, kept, j])
            if j + 1 < stages:
                bit, blocks = moved(i, j + 1)
                for r in blocks:
                    dp_copy(i, j + 1, r, bit).start()

    def right(i):
        return remote(go_r.at[i], prefix.at[i], send_r.at[i], recv_r.at[i], expert=mine + 2)

    def left(i):
        return remote(go_l.at[i], suffix.at[i], send_l.at[i], recv_l.at[i], expert=mine - 2)

    def line(t, carry):
        i = t - z

        @pl.when(jnp.logical_and(i >= 0, i < chunks))
        def _():
            @pl.when(has_left)
            def _():
                remote(go_r.at[i], prefix.at[i], send_r.at[i], recv_r.at[i], expert=mine).wait_recv()

            @pl.when(jnp.logical_and(has_left, has_right))
            def _():
                add_rows(go_r.at[i], total.at[i, 0], prefix.at[i])

            @pl.when(jnp.logical_not(has_left))
            def _():
                add_rows(go_r.at[i], total.at[i, 0])

            pl.when(has_right)(lambda: right(i).start())

        k = t - (depth - 1 - z)

        @pl.when(jnp.logical_and(k >= 0, k < chunks))
        def _():
            @pl.when(has_right)
            def _():
                remote(go_l.at[k], suffix.at[k], send_l.at[k], recv_l.at[k], expert=mine).wait_recv()

            @pl.when(jnp.logical_and(has_left, has_right))
            def _():
                add_rows(go_l.at[k], total.at[k, 0], suffix.at[k])

            @pl.when(jnp.logical_not(has_right))
            def _():
                add_rows(go_l.at[k], total.at[k, 0])

            pl.when(has_left)(lambda: left(k).start())

        return carry

    lax.fori_loop(0, chunks + depth - 1, line, 0)

    def last(i):
        return remote(final.at[i], other.at[i], last_send.at[i], last_recv.at[i], expert=pair)

    for i in range(chunks):
        @pl.when(jnp.logical_and(has_left, has_right))
        def _():
            add_rows(final.at[i], total.at[i, 0], prefix.at[i], suffix.at[i])

        @pl.when(jnp.logical_not(has_left))
        def _():
            add_rows(final.at[i], total.at[i, 0], suffix.at[i])

        @pl.when(jnp.logical_not(has_right))
        def _():
            add_rows(final.at[i], total.at[i, 0], prefix.at[i])

        last(i).start()

    def place(side, i):
        return out_ref.at[pl.ds(pl.multiple_of(side * half, 16), half), columns(i)]

    for i in range(chunks):
        add_rows(place(core, i), final.at[i])
    for i in range(chunks):
        last(i).wait_recv()
        add_rows(place(1 - core, i), other.at[i])
        last(i).wait_send()
        pl.when(has_right)(lambda: right(i).wait_send())
        pl.when(has_left)(lambda: left(i).wait_send())
        for d in range(n_dp):
            across(i, d).wait_send()
        for j in range(stages):
            bit, blocks = moved(i, j)
            for r in blocks:
                dp_copy(i, j, r, bit).wait_send()


def reduce_grads(n_dp, n_exp, grads, chunks, collective_id):
    rows = grads.shape[0] // n_dp
    half, width = rows // 2, grads.shape[1] // chunks
    stages = max(1, n_dp.bit_length() - 1)
    sem = pltpu.SemaphoreType.DMA
    one = pltpu.VMEM((chunks, half, width), grads.dtype)
    return pl.pallas_call(
        functools.partial(grads_body, n_dp, n_exp, chunks),
        out_shape=jax.ShapeDtypeStruct((rows, grads.shape[1]), jnp.float32),
        in_specs=[pl.BlockSpec(memory_space=VMEM)],
        out_specs=pl.BlockSpec(memory_space=VMEM),
        scratch_shapes=[
            pltpu.VMEM((chunks, n_dp, half, width), grads.dtype),
            pltpu.VMEM((chunks, n_dp, half, width), grads.dtype),
            pltpu.VMEM((chunks, n_dp, stages, half, width), grads.dtype),
            one, one, one, one, one, one,
            sem((chunks, n_dp)), sem((chunks, n_dp)), sem((chunks, n_dp)), sem((chunks, n_dp, stages)),
            sem((chunks,)), sem((chunks,)), sem((chunks,)), sem((chunks,)), sem((chunks,)), sem((chunks,)),
        ],
        compiler_params=pltpu.CompilerParams(
            collective_id=collective_id, has_side_effects=True, vmem_limit_bytes=56 * MIB),
        name="reduce_grads",
    )(grads)


def tree_layout(tree_rows):
    unit_rows = tree_rows // 20
    row_index = jnp.arange(tree_rows, dtype=jnp.int32)
    segment = jnp.where(
        row_index < 8 * unit_rows,
        0,
        jnp.where(
            row_index < 12 * unit_rows,
            1 + (row_index - 8 * unit_rows) // unit_rows,
            5 + (row_index - 12 * unit_rows) // unit_rows,
        ),
    )
    depth_start = jnp.where(segment == 0, 0, jnp.where(segment < 5, 8 * unit_rows, 9 * unit_rows))
    seg_start = jnp.where(
        segment == 0,
        0,
        jnp.where(
            segment < 5,
            8 * unit_rows + (segment - 1) * unit_rows,
            12 * unit_rows + (segment - 5) * unit_rows,
        ),
    )
    position = depth_start + row_index - seg_start
    return (segment, position)


def path_allowed(parent_row, segment):
    segment_ids = jnp.arange(parent_row.shape[0], dtype=jnp.int32)
    grandparent = parent_row[parent_row]
    on_path = (
        (segment_ids[None, :] == segment_ids[:, None])
        | (segment_ids[None, :] == parent_row[:, None])
        | (segment_ids[None, :] == grandparent[:, None])
    ).astype(jnp.float32)
    seg_hot = (segment[:, None] == segment_ids[None, :]).astype(jnp.float32)
    reach = jnp.dot(
        jnp.dot(seg_hot, on_path, precision=lax.Precision.HIGHEST),
        seg_hot.T,
        precision=lax.Precision.HIGHEST,
    )
    row_index = jnp.arange(segment.shape[0], dtype=jnp.int32)
    return (reach > 0.5) & (row_index[None, :] <= row_index[:, None])


def rope_tables(position):
    frequency = 10000.0 ** (-jnp.arange(0, HD, 2, dtype=jnp.float32) / HD)
    angles = position.astype(jnp.float32)[:, None] * frequency[None, :]
    return (jnp.concatenate([jnp.cos(angles)] * 2, -1), jnp.concatenate([jnp.sin(angles)] * 2, -1))


def turn_half(field):
    half_width = field.shape[-1] // 2
    return jnp.concatenate([-field[..., half_width:], field[..., :half_width]], axis=-1)


def rotary(field, cosine, sine_table):
    return field * cosine + turn_half(field) * sine_table


def unrotate(grad_field, cosine, sine_table):
    return grad_field * cosine - turn_half(grad_field * sine_table)


def rms_norm(field, gain_vector):
    return (
        field * lax.rsqrt(jnp.mean(field * field, axis=-1, keepdims=True) + EPSILON) * gain_vector
    )


def gated_unit(gate_up):
    width_ff = gate_up.shape[-1] // 2
    gate_part = gate_up[..., :width_ff]
    return gate_part / (1.0 + jnp.exp(-gate_part)) * gate_up[..., width_ff:]


def shards(
    tokens,
    attn_gain,
    w_query,
    w_keyval,
    w_output,
    moe_gain,
    w_router,
    expert_in,
    expert_out,
    cotangent,
    routes,
    parents,
):
    tree_rows = tokens.shape[0]
    width = tokens.shape[1]
    capacity = CAP
    groups = H // KV
    kv_width = KV * HD
    score_scale = HD ** (-0.5)
    n_dp, n_exp = lax.axis_size("dp"), lax.axis_size("expert")
    rows = w_query.shape[0]
    small = jnp.concatenate(
        [w_router, attn_gain[:, None], moe_gain[:, None], jnp.zeros((rows, 128 - EXPERTS - 2), w_router.dtype)], axis=1
    )
    query_full, keyval_full, output_full, small_full = gather_weights(
        n_dp, (w_query, w_keyval, w_output, small), 1
    )
    router_full = small_full[:, :EXPERTS]
    gain_first, gain_second = small_full[:, EXPERTS], small_full[:, EXPERTS + 1]
    inputs = tokens.astype(jnp.float32)
    segment, position = tree_layout(tree_rows)
    allowed = path_allowed(parents[0], segment)
    cosine, sine_table = rope_tables(position)
    cos_four, sin_four = (cosine[:, None, None, :], sine_table[:, None, None, :])
    cos_three, sin_three = (cosine[:, None, :], sine_table[:, None, :])
    normed, first_back = jax.vjp(rms_norm, inputs, gain_first.astype(jnp.float32))
    hidden = normed.astype(jnp.bfloat16)
    query_pre = jnp.dot(hidden, query_full, preferred_element_type=jnp.float32)
    keyval_pre = jnp.dot(hidden, keyval_full, preferred_element_type=jnp.float32)
    queries = rotary(query_pre.reshape(tree_rows, KV, groups, HD), cos_four, sin_four).astype(
        jnp.bfloat16
    )
    key_heads = rotary(
        keyval_pre[:, :kv_width].reshape(tree_rows, KV, HD), cos_three, sin_three
    ).astype(jnp.bfloat16)
    values = keyval_pre[:, kv_width:].reshape(tree_rows, KV, HD).astype(jnp.bfloat16)

    def score_block():
        raw_scores = (
            jnp.einsum("tkgd,skd->kgts", queries, key_heads, preferred_element_type=jnp.float32)
            * score_scale
        )
        return jnp.where(allowed, raw_scores, -1e30)

    scores = score_block()
    row_max = jnp.max(scores, axis=-1, keepdims=True)
    exp_scores = jnp.exp(scores - row_max)
    row_total = jnp.sum(exp_scores, axis=-1, keepdims=True)
    log_total = row_max + jnp.log(row_total)
    attn_low = (exp_scores / row_total).astype(jnp.bfloat16)
    attended = jnp.einsum("kgts,skd->tkgd", attn_low, values, preferred_element_type=jnp.float32)
    attended = attended.reshape(tree_rows, H * HD).astype(jnp.bfloat16)
    middle = inputs + jnp.dot(attended, output_full, preferred_element_type=jnp.float32)
    normed2, second_back = jax.vjp(rms_norm, middle, gain_second.astype(jnp.float32))
    hidden2 = normed2.astype(jnp.bfloat16)
    logits = jnp.dot(hidden2, router_full, preferred_element_type=jnp.float32)
    expert_ids = jnp.arange(EXPERTS, dtype=jnp.int32)
    route_hot = (routes[:, :, None] == expert_ids[None, None, :]).astype(jnp.float32)
    picked = jnp.sum(route_hot * logits[:, None, :], axis=2)
    picked_exp = jnp.exp(picked - jnp.max(picked, axis=1, keepdims=True))
    gate_weights = picked_exp / jnp.sum(picked_exp, axis=1, keepdims=True)
    trees = lax.axis_size("expert")
    here = lax.axis_index("expert")
    local = expert_in.shape[0]
    first = here * local
    routes_all = lax.all_gather(routes, "expert", axis=0, tiled=False)
    grad_y = lax.all_gather(cotangent, "expert", axis=0, tiled=False)
    hidden_all = ring_gather(n_exp, hidden2, 2)
    own_ids = first + jnp.arange(local, dtype=jnp.int32)
    hot_all = routes_all[:, :, :, None] == expert_ids[None, None, None, :]
    chosen_all = jnp.any(hot_all, axis=2)
    chosen = jnp.any(routes_all[:, :, :, None] == own_ids[None, None, None, :], axis=2)
    lower = jnp.tril(jnp.ones((tree_rows, tree_rows), jnp.bfloat16), -1)
    rank = jnp.einsum(
        "tu,jue->jet", lower, chosen.astype(jnp.bfloat16), preferred_element_type=jnp.float32
    ).astype(jnp.int32)
    slots = jnp.arange(capacity, dtype=jnp.int32)
    chosen_t = chosen.transpose(0, 2, 1)
    place = (rank[:, :, None, :] == slots[None, None, :, None]) & chosen_t[:, :, None, :]
    place = place.astype(jnp.bfloat16)
    logits_all = jnp.einsum(
        "jtd,de->jte", hidden_all, router_full, preferred_element_type=jnp.float32
    )
    masked = jnp.where(chosen_all, logits_all, -1e30)
    weight = jnp.exp(masked - jnp.max(masked, axis=-1, keepdims=True))
    weight = weight / jnp.sum(weight, axis=-1, keepdims=True)
    gates_own = lax.dynamic_slice_in_dim(weight, first, local, axis=2)
    gate_slot = jnp.einsum(
        "jest,jte->ejs", place.astype(jnp.float32), gates_own, precision=lax.Precision.HIGHEST
    )[..., None]
    sent = jnp.einsum("jest,jtd->ejsd", place, hidden_all, preferred_element_type=jnp.float32)
    sent = sent.astype(jnp.bfloat16)
    grad_rows = jnp.einsum("jest,jtd->ejsd", place, grad_y, preferred_element_type=jnp.float32)
    grad_rows = grad_rows.astype(jnp.bfloat16)
    gate_up = jnp.einsum("ejsd,edf->ejsf", sent, expert_in, preferred_element_type=jnp.float32)
    activated, glu_back = jax.vjp(gated_unit, gate_up)
    act_low = activated.astype(jnp.bfloat16).astype(jnp.float32)
    act_scaled = (act_low * gate_slot).astype(jnp.bfloat16)
    made = jnp.einsum(
        "ejsf,efd->ejsd", act_scaled, expert_out, preferred_element_type=jnp.float32
    ).astype(jnp.bfloat16)
    out_part = jnp.einsum("jest,ejsd->jtd", place, made, preferred_element_type=jnp.float32)
    block_out = ring_scatter(n_exp, out_part.astype(jnp.bfloat16), (middle,), jnp.bfloat16, 3)
    grad_result = cotangent.astype(jnp.float32)
    grad_act = jnp.einsum(
        "ejsd,efd->ejsf", grad_rows, expert_out, preferred_element_type=jnp.float32
    )
    gate_dot = jnp.sum(act_low * grad_act, axis=-1)
    gates_back = jnp.einsum(
        "jest,ejs->jte", place.astype(jnp.float32), gate_dot, precision=lax.Precision.HIGHEST
    )
    grad_out_w = jnp.einsum(
        "ejsf,ejsd->efd", act_scaled, grad_rows, preferred_element_type=jnp.float32
    )
    grad_gate_up = glu_back(grad_act * gate_slot)[0].astype(jnp.bfloat16)
    grad_sent = jnp.einsum(
        "ejsf,edf->ejsd", grad_gate_up, expert_in, preferred_element_type=jnp.float32
    ).astype(jnp.bfloat16)
    grad_in_w = jnp.einsum(
        "ejsd,ejsf->edf", sent, grad_gate_up, preferred_element_type=jnp.float32
    )
    hid_part = jnp.einsum("jest,ejsd->jtd", place, grad_sent, preferred_element_type=jnp.float32)
    gates_mine = lax.all_to_all(gates_back, "expert", split_axis=0, concat_axis=2, tiled=True)[0]
    hid_sum = ring_scatter(n_exp, hid_part.astype(jnp.bfloat16), (), jnp.float32, 4)
    gate_dense = jnp.sum(route_hot * gate_weights[:, :, None], axis=1)
    grad_logits = (
        gate_dense
        * (gates_mine - jnp.sum(gate_dense * gates_mine, axis=1, keepdims=True))
    ).astype(jnp.bfloat16)
    grad_router = jnp.einsum("td,te->de", hidden2, grad_logits, preferred_element_type=jnp.float32)
    grad_hidden2 = hid_sum + jnp.einsum(
        "te,de->td", grad_logits, router_full, preferred_element_type=jnp.float32
    )
    expert_in_share, expert_out_share = (
        lax.psum_scatter(
            grad_in_w.astype(jnp.bfloat16), "dp", scatter_dimension=1, tiled=True
        ).astype(jnp.float32),
        lax.psum_scatter(
            grad_out_w.astype(jnp.bfloat16), "dp", scatter_dimension=1, tiled=True
        ).astype(jnp.float32),
    )
    grad_mid_norm, grad_gain_second = second_back(grad_hidden2)
    grad_middle = grad_result + grad_mid_norm
    grad_branch = grad_middle.astype(jnp.bfloat16)
    grad_w_out = jnp.einsum("ti,td->id", attended, grad_branch, preferred_element_type=jnp.float32)
    grad_attended = jnp.einsum(
        "td,id->ti", grad_branch, output_full, preferred_element_type=jnp.float32
    )
    grad_attended = grad_attended.astype(jnp.bfloat16).reshape(tree_rows, KV, groups, HD)
    attn_probs = jnp.exp(score_block() - log_total)
    probs_low = attn_probs.astype(jnp.bfloat16)
    grad_values = jnp.einsum(
        "kgts,tkgd->skd", probs_low, grad_attended, preferred_element_type=jnp.float32
    )
    grad_probs = jnp.einsum(
        "tkgd,skd->kgts", grad_attended, values, preferred_element_type=jnp.float32
    )
    grad_scores = (
        attn_probs * (grad_probs - jnp.sum(attn_probs * grad_probs, axis=-1, keepdims=True))
    ).astype(jnp.bfloat16)
    grad_query_rot = (
        jnp.einsum("kgts,skd->tkgd", grad_scores, key_heads, preferred_element_type=jnp.float32)
        * score_scale
    )
    grad_keys_rot = (
        jnp.einsum("kgts,tkgd->skd", grad_scores, queries, preferred_element_type=jnp.float32)
        * score_scale
    )
    grad_query_pre = (
        unrotate(grad_query_rot, cos_four, sin_four).reshape(tree_rows, H * HD).astype(jnp.bfloat16)
    )
    grad_keyval_pre = jnp.concatenate(
        [
            unrotate(grad_keys_rot, cos_three, sin_three).reshape(tree_rows, kv_width),
            grad_values.reshape(tree_rows, kv_width),
        ],
        axis=1,
    ).astype(jnp.bfloat16)
    grad_w_q = jnp.einsum("td,ti->di", hidden, grad_query_pre, preferred_element_type=jnp.float32)
    grad_w_kv = jnp.einsum("td,ti->di", hidden, grad_keyval_pre, preferred_element_type=jnp.float32)
    grad_hidden = jnp.einsum(
        "ti,di->td", grad_query_pre, query_full, preferred_element_type=jnp.float32
    ) + jnp.einsum("ti,di->td", grad_keyval_pre, keyval_full, preferred_element_type=jnp.float32)
    grad_in_norm, grad_gain_first = first_back(grad_hidden)
    input_grad = grad_middle + grad_in_norm
    low = jnp.bfloat16
    share = reduce_grads(
        n_dp,
        n_exp,
        jnp.concatenate(
            [
                grad_w_q.astype(low),
                grad_w_kv.astype(low),
                grad_w_out.astype(low),
                grad_router.astype(low),
                grad_gain_first.astype(low)[:, None],
                grad_gain_second.astype(low)[:, None],
                jnp.zeros((width, 128 - EXPERTS - 2), low),
            ],
            axis=1,
        ),
        5,
        5,
    )
    at = 3 * width
    shares = (
        share[:, at + EXPERTS],
        share[:, :width],
        share[:, width : 2 * width],
        share[:, 2 * width : at],
        share[:, at + EXPERTS + 1],
        share[:, at : at + EXPERTS],
    )
    return (
        block_out,
        input_grad,
        shares[0],
        shares[1],
        shares[2],
        shares[3],
        shares[4],
        shares[5],
        expert_in_share,
        expert_out_share,
    )


def solution(mesh):
    in_specs = (
        P(("dp", "expert"), None),
        P("dp"),
        P("dp", None),
        P("dp", None),
        P("dp", None),
        P("dp"),
        P("dp", None),
        P("expert", None, None),
        P("expert", None, None),
        P(("dp", "expert"), None),
        P(("dp", "expert"), None),
        P(("dp", "expert"), None),
    )
    out_specs = (
        P(("dp", "expert"), None),
        P(("dp", "expert"), None),
        P("dp"),
        P("dp", None),
        P("dp", None),
        P("dp", None),
        P("dp"),
        P("dp", None),
        P("expert", "dp", None),
        P("expert", "dp", None),
    )
    return jax.shard_map(shards, mesh=mesh, in_specs=in_specs, out_specs=out_specs, check_vma=False)
```

```python
import functools

import jax
import jax.numpy as jnp
from jax import lax
from jax.experimental import pallas as pl
from jax.experimental.pallas import tpu as pltpu
from jax.sharding import PartitionSpec as P

H = 16
KV = 8
HD = 64
EXPERTS = 32
TOPK = 8
CAP = 120


EPSILON = 1e-06


MESH = pl.DeviceIdType.MESH
MIB = 1024 * 1024
VMEM = pltpu.VMEM
ANY = pl.ANY


def remote(src, dst, send_sem, recv_sem, **where):
    return pltpu.make_async_remote_copy(
        src_ref=src, dst_ref=dst, send_sem=send_sem, recv_sem=recv_sem,
        device_id=where, device_id_type=MESH,
    )


def greet(partners):
    barrier = pltpu.get_barrier_semaphore()
    for condition, where in partners:
        def signal(where=where):
            pl.semaphore_signal(barrier, inc=1, device_id=where, device_id_type=MESH)
        if condition is None:
            signal()
        else:
            pl.when(condition)(signal)
    count = sum(1 if c is None else c.astype(jnp.int32) for c, _ in partners)
    pl.semaphore_wait(barrier, count)


def add_rows(out, *terms, step=16):
    rows = out.shape[0]

    def body(i, carry):
        at = pl.ds(pl.multiple_of(i * step, step), step)
        total = terms[0][at, :].astype(jnp.float32)
        for term in terms[1:]:
            total = total + term[at, :].astype(jnp.float32)
        out[at, :] = total.astype(out.dtype)
        return carry

    lax.fori_loop(0, rows // step, body, 0)


def bit_orders(n):
    bits = [1 << j for j in range(n.bit_length() - 1)]
    return [bits[p:] + bits[:p] for p in range(len(bits))] or [[]]


def weights_body(n_dp, *refs):
    arrays = 4
    ins, outs = refs[:arrays], refs[arrays : 2 * arrays]
    send_sem, recv_sem, pair_send, pair_recv, own_sem = refs[2 * arrays :]
    me, mine = lax.axis_index("dp"), lax.axis_index("expert")
    core = lax.rem(mine, 2)
    pair = mine + 1 - 2 * core
    orders = bit_orders(n_dp)
    greet([(None, {"dp": me ^ bit}) for bit in orders[0]] + [(None, {"expert": pair})])
    shard = ins[0].shape[0]
    half = shard // 2
    sends, pairs, owns = [], [], []
    cuts = min(2, len(orders), half // 16)
    size = half // cuts

    def pieces(a):
        return cuts

    def rows(start, side, p):
        return pl.ds(pl.multiple_of(start + side * half + p * size, 16), size)

    def push(a, p, r, bit):
        to = me ^ bit
        there = outs[a].at[rows((me ^ r) * shard, core, p)]
        src = ins[a].at[rows(0, core, p)] if r == 0 else there
        copy = remote(src, there, send_sem.at[a, p, r, bit.bit_length() - 1], recv_sem.at[a, p, r ^ bit], dp=to)
        copy.start()
        sends.append(copy)

    for a in range(arrays):
        for p in range(pieces(a)):
            for bit in orders[p]:
                push(a, p, 0, bit)
    for a in range(arrays):
        copy = pltpu.make_async_copy(
            ins[a], outs[a].at[pl.ds(pl.multiple_of(me * shard, 16), shard)], own_sem.at[a])
        copy.start()
        owns.append(copy)
    def reach(order):
        blocks = [0]
        steps = []
        for j, bit in enumerate(order):
            new = [r | bit for r in blocks]
            steps.append((j, new))
            blocks = blocks + new
        return steps

    for j in range(len(orders[0])):
        for a in range(arrays):
            for p in range(pieces(a)):
                order = orders[p]
                for r in reach(order)[j][1]:
                    here = outs[a].at[rows((me ^ r) * shard, core, p)]
                    remote(here, here, send_sem.at[a, p, r, 0], recv_sem.at[a, p, r], dp=me).wait_recv()
                    for bit in order[j + 1 :]:
                        push(a, p, r, bit)
                    copy = remote(here, here, pair_send.at[a, p, r], pair_recv.at[a, p, r], expert=pair)
                    copy.start()
                    pairs.append((copy, a, p, r))
    for copy in owns:
        copy.wait()
    for copy in sends:
        copy.wait_send()
    for copy, a, p, r in pairs:
        copy.wait_send()
        here = outs[a].at[rows((me ^ r) * shard, 1 - core, p)]
        remote(here, here, pair_send.at[a, p, r], pair_recv.at[a, p, r], expert=pair).wait_recv()


def gather_weights(n_dp, arrays, collective_id):
    orders = bit_orders(n_dp)
    count, pieces = len(arrays), min(2, len(orders))
    out_shape = [jax.ShapeDtypeStruct((n_dp * a.shape[0], a.shape[1]), a.dtype) for a in arrays]
    return pl.pallas_call(
        functools.partial(weights_body, n_dp),
        out_shape=out_shape,
        in_specs=[pl.BlockSpec(memory_space=VMEM)] * count,
        out_specs=[pl.BlockSpec(memory_space=ANY)] * count,
        scratch_shapes=[
            pltpu.SemaphoreType.DMA((count, pieces, n_dp, max(1, n_dp.bit_length() - 1))),
            pltpu.SemaphoreType.DMA((count, pieces, n_dp)),
            pltpu.SemaphoreType.DMA((count, pieces, n_dp)),
            pltpu.SemaphoreType.DMA((count, pieces, n_dp)),
            pltpu.SemaphoreType.DMA((count,)),
        ],
        compiler_params=pltpu.CompilerParams(collective_id=collective_id, has_side_effects=True),
        name="gather_weights",
    )(*arrays)


class Ring:
    def __init__(self, n_exp):
        self.mine = lax.axis_index("expert")
        self.core = lax.rem(self.mine, 2)
        self.z = lax.div(self.mine, 2)
        self.depth = n_exp // 2
        self.far = self.depth // 2
        self.pair = self.mine + 1 - 2 * self.core
        self.right, self.left = self.dev(1), self.dev(-1)

    def dev(self, d):
        return lax.rem(self.z + d + self.depth, self.depth) * 2 + self.core

    def partners(self):
        return [(None, {"expert": e}) for e in (self.pair, self.right, self.left)]


class RingGather:
    def __init__(self, ring, own, out, sems):
        self.ring, self.own, self.out = ring, own, out
        self.send, self.recv, self.pair_send, self.pair_recv = sems
        self.half = own.shape[0] // 2

    @staticmethod
    def scratch(n_exp):
        far, depth = n_exp // 4, n_exp // 2
        sem = pltpu.SemaphoreType.DMA
        return [sem((2, far + 1, 2)), sem((2, far + 1, 2)), sem((depth, 2)), sem((depth, 2))]

    def rows(self, h):
        return pl.ds(h * self.half, self.half)

    def goes(self, side, s, h):
        far = self.ring.far
        return s < far or (s == far and h == side)

    def block(self, d, h):
        return self.out.at[self.ring.dev(d), self.rows(h)]

    def hop(self, side, s, h):
        d = -s if side == 0 else s
        src = self.own.at[self.rows(h)] if s == 0 else self.block(d, h)
        to = self.ring.right if side == 0 else self.ring.left
        return remote(src, self.block(d, h), self.send.at[side, s, h], self.recv.at[side, s + 1, h], expert=to)

    def across(self, d, h):
        src = self.own.at[self.rows(h)] if d == 0 else self.block(d, h)
        slot = d % self.ring.depth
        return remote(src, self.block(d, h), self.pair_send.at[slot, h], self.pair_recv.at[slot, h], expert=self.ring.pair)

    ORDER = ((0, 0), (1, 1), (0, 1), (1, 0))

    def start(self):
        for side, h in self.ORDER:
            if self.goes(side, 1, h):
                self.hop(side, 0, h).start()
        self.across(0, 0).start()
        self.across(0, 1).start()

    def events(self):
        return [(side, s, h) for s in range(1, self.ring.far + 1) for side, h in self.ORDER if self.goes(side, s, h)]

    def handle(self, event):
        side, s, h = event
        d = -s if side == 0 else s
        here = self.block(d, h)
        remote(here, here, self.send.at[side, s, h], self.recv.at[side, s, h], expert=self.ring.mine).wait_recv()
        if self.goes(side, s + 1, h):
            self.hop(side, s, h).start()
        self.across(d, h).start()

    def wait_pair(self, d, h):
        slot = d % self.ring.depth
        here = self.out.at[self.ring.pair - self.ring.mine + self.ring.dev(d), self.rows(h)]
        remote(here, here, self.pair_send.at[slot, h], self.pair_recv.at[slot, h], expert=self.ring.mine).wait_recv()

    def finish_own(self):
        for side, h in self.ORDER:
            if self.goes(side, 1, h):
                self.hop(side, 0, h).wait_send()
        self.across(0, 0).wait_send()
        self.across(0, 1).wait_send()

    def finish_event(self, event):
        side, s, h = event
        if self.goes(side, s + 1, h):
            self.hop(side, s, h).wait_send()
        self.across(-s if side == 0 else s, h).wait_send()


class RingScatter:
    def __init__(self, ring, part, bufs, sems):
        self.ring, self.part = ring, part
        self.pair_buf, self.held, self.got = bufs
        self.pair_send, self.pair_recv, self.send, self.recv = sems
        self.half = self.held(0).shape[0] // 2

    @staticmethod
    def scratch(n_exp, block, dtype):
        far, depth = n_exp // 4, n_exp // 2
        sem = pltpu.SemaphoreType.DMA
        bufs = [pltpu.VMEM((depth,) + block, dtype), pltpu.VMEM((depth,) + block, dtype),
                pltpu.VMEM((2, far) + block, dtype)]
        return bufs, [sem((depth,)), sem((depth,)), sem((2, far + 1, 2)), sem((2, far + 1, 2))]

    def rows(self, h):
        return pl.ds(h * self.half, self.half)

    def order(self):
        far, depth = self.ring.far, self.ring.depth
        order = [far]
        for s in range(far - 1, 0, -1):
            order += [s, depth - s]
        return order + [0]

    def comes(self, side, d, h):
        far = self.ring.far
        return d + 1 < far or (d + 1 == far and h == side)

    def across(self, d):
        ring = self.ring
        return remote(self.part(ring.dev(d) + 1 - 2 * ring.core), self.pair_buf(d),
                      self.pair_send.at[d], self.pair_recv.at[d], expert=ring.pair)

    def start_pair(self, d):
        self.across(d).start()

    def wait_pair(self, d):
        self.across(d).wait_recv()

    def wait_got(self, side, d, h):
        here = self.got(side, d).at[self.rows(h)]
        remote(here, here, self.send.at[side, d, h], self.recv.at[side, d, h], expert=self.ring.mine).wait_recv()

    def hop(self, side, d, h):
        slot = d if side == 0 else self.ring.depth - d
        rows = self.rows(h)
        return remote(self.held(slot).at[rows], self.got(side, d - 1).at[rows], self.send.at[side, d, h],
                      self.recv.at[side, d - 1, h], expert=self.ring.right if side == 0 else self.ring.left)

    def push(self, side, d, h):
        ring = self.ring
        slot = d if side == 0 else ring.depth - d
        rows = self.rows(h)
        terms = [self.part(ring.dev(slot)).at[rows], self.pair_buf(slot).at[rows]]
        if self.comes(side, d, h):
            self.wait_got(side, d, h)
            terms.append(self.got(side, d).at[rows])
        add_rows(self.held(slot).at[rows], *terms)
        self.hop(side, d, h).start()

    def first(self):
        far = self.ring.far
        self.wait_pair(far)
        self.push(0, far, 0)
        self.push(1, far, 1)

    def early(self):
        for d in range(self.ring.far - 1, 0, -1):
            self.wait_pair(d)
            self.push(0, d, 1)
            self.wait_pair(self.ring.depth - d)
            self.push(1, d, 0)

    def late(self):
        for d in range(self.ring.far - 1, 0, -1):
            self.push(0, d, 0)
            self.push(1, d, 1)

    def last(self, out, *more):
        self.wait_pair(0)
        for h in range(2):
            rows = self.rows(h)
            terms = [self.part(self.ring.mine).at[rows], self.pair_buf(0).at[rows]] + [m.at[rows] for m in more]
            for side in range(2):
                if self.comes(side, 0, h):
                    self.wait_got(side, 0, h)
                    terms.append(self.got(side, 0).at[rows])
            add_rows(out.at[rows], *terms)

    def finish_sends(self):
        far = self.ring.far
        for side in range(2):
            for d in range(1, far + 1):
                for h in range(2):
                    if d < far or h == side:
                        self.hop(side, d, h).wait_send()
        for d in range(self.ring.depth):
            self.across(d).wait_send()


def views(bufs):
    pair_buf, held, got = bufs
    return (lambda d: pair_buf.at[d], lambda d: held.at[d], lambda side, d: got.at[side, d])


def grads_body(n_dp, n_exp, chunks, g_ref, out_ref, pair_buf, total, dp_buf, prefix, suffix, go_r, go_l, final, other,
               pair_send, pair_recv, dp_send, dp_recv, send_r, send_l, recv_r, recv_l, last_send, last_recv):
    me, mine = lax.axis_index("dp"), lax.axis_index("expert")
    core = lax.rem(mine, 2)
    z = lax.div(mine, 2)
    depth = n_exp // 2
    pair = mine + 1 - 2 * core
    has_left, has_right = z > 0, z < depth - 1
    orders = bit_orders(n_dp)
    rows = g_ref.shape[0] // n_dp
    half = rows // 2
    width = g_ref.shape[1] // chunks
    greet([(None, {"expert": pair})] + [(None, {"dp": me ^ bit}) for bit in orders[0]]
          + [(has_left, {"expert": mine - 2}), (has_right, {"expert": mine + 2})])

    def columns(i):
        return pl.ds(pl.multiple_of(i * width, 128), width)

    def block_of(d, side, i):
        return g_ref.at[pl.ds(pl.multiple_of(d * rows + side * half, 16), half), columns(i)]

    def across(i, d):
        return remote(block_of(d, 1 - core, i), pair_buf.at[i, d], pair_send.at[i, d], pair_recv.at[i, d], expert=pair)

    for i in range(chunks):
        for d in range(n_dp):
            across(i, d).start()

    def moved(i, j):
        order = orders[i % len(orders)]
        blocks = [0]
        for bit in order[j + 1 :]:
            blocks = blocks + [r | bit for r in blocks]
        return order[j], [r | order[j] for r in blocks]

    def dp_copy(i, j, r, bit):
        return remote(total.at[i, r], dp_buf.at[i, r ^ bit, j], dp_send.at[i, r], dp_recv.at[i, r ^ bit, j], dp=me ^ bit)

    stages = len(orders[0])
    for i in range(chunks):
        for r in range(n_dp - 1, -1, -1):
            d = me ^ r
            across(i, d).wait_recv()
            add_rows(total.at[i, r], block_of(d, core, i), pair_buf.at[i, d])
        if stages:
            bit, blocks = moved(i, 0)
            for r in blocks:
                dp_copy(i, 0, r, bit).start()
    for j in range(stages):
        for i in range(chunks):
            bit, blocks = moved(i, j)
            for r in blocks:
                kept = r ^ bit
                dp_copy(i, j, r, bit).wait_recv()
                add_rows(total.at[i, kept], total.at[i, kept], dp_buf.at[i, kept, j])
            if j + 1 < stages:
                bit, blocks = moved(i, j + 1)
                for r in blocks:
                    dp_copy(i, j + 1, r, bit).start()

    def right(i):
        return remote(go_r.at[i], prefix.at[i], send_r.at[i], recv_r.at[i], expert=mine + 2)

    def left(i):
        return remote(go_l.at[i], suffix.at[i], send_l.at[i], recv_l.at[i], expert=mine - 2)

    def line(t, carry):
        i = t - z

        @pl.when(jnp.logical_and(i >= 0, i < chunks))
        def _():
            @pl.when(has_left)
            def _():
                remote(go_r.at[i], prefix.at[i], send_r.at[i], recv_r.at[i], expert=mine).wait_recv()

            @pl.when(jnp.logical_and(has_left, has_right))
            def _():
                add_rows(go_r.at[i], total.at[i, 0], prefix.at[i])

            @pl.when(jnp.logical_not(has_left))
            def _():
                add_rows(go_r.at[i], total.at[i, 0])

            pl.when(has_right)(lambda: right(i).start())

        k = t - (depth - 1 - z)

        @pl.when(jnp.logical_and(k >= 0, k < chunks))
        def _():
            @pl.when(has_right)
            def _():
                remote(go_l.at[k], suffix.at[k], send_l.at[k], recv_l.at[k], expert=mine).wait_recv()

            @pl.when(jnp.logical_and(has_left, has_right))
            def _():
                add_rows(go_l.at[k], total.at[k, 0], suffix.at[k])

            @pl.when(jnp.logical_not(has_right))
            def _():
                add_rows(go_l.at[k], total.at[k, 0])

            pl.when(has_left)(lambda: left(k).start())

        return carry

    lax.fori_loop(0, chunks + depth - 1, line, 0)

    def last(i):
        return remote(final.at[i], other.at[i], last_send.at[i], last_recv.at[i], expert=pair)

    for i in range(chunks):
        @pl.when(jnp.logical_and(has_left, has_right))
        def _():
            add_rows(final.at[i], total.at[i, 0], prefix.at[i], suffix.at[i])

        @pl.when(jnp.logical_not(has_left))
        def _():
            add_rows(final.at[i], total.at[i, 0], suffix.at[i])

        @pl.when(jnp.logical_not(has_right))
        def _():
            add_rows(final.at[i], total.at[i, 0], prefix.at[i])

        last(i).start()

    def place(side, i):
        return out_ref.at[pl.ds(pl.multiple_of(side * half, 16), half), columns(i)]

    for i in range(chunks):
        add_rows(place(core, i), final.at[i])
    for i in range(chunks):
        last(i).wait_recv()
        add_rows(place(1 - core, i), other.at[i])
        last(i).wait_send()
        pl.when(has_right)(lambda: right(i).wait_send())
        pl.when(has_left)(lambda: left(i).wait_send())
        for d in range(n_dp):
            across(i, d).wait_send()
        for j in range(stages):
            bit, blocks = moved(i, j)
            for r in blocks:
                dp_copy(i, j, r, bit).wait_send()


def reduce_grads(n_dp, n_exp, grads, chunks, collective_id):
    rows = grads.shape[0] // n_dp
    half, width = rows // 2, grads.shape[1] // chunks
    stages = max(1, n_dp.bit_length() - 1)
    sem = pltpu.SemaphoreType.DMA
    one = pltpu.VMEM((chunks, half, width), grads.dtype)
    return pl.pallas_call(
        functools.partial(grads_body, n_dp, n_exp, chunks),
        out_shape=jax.ShapeDtypeStruct((rows, grads.shape[1]), jnp.float32),
        in_specs=[pl.BlockSpec(memory_space=VMEM)],
        out_specs=pl.BlockSpec(memory_space=VMEM),
        scratch_shapes=[
            pltpu.VMEM((chunks, n_dp, half, width), grads.dtype),
            pltpu.VMEM((chunks, n_dp, half, width), grads.dtype),
            pltpu.VMEM((chunks, n_dp, stages, half, width), grads.dtype),
            one, one, one, one, one, one,
            sem((chunks, n_dp)), sem((chunks, n_dp)), sem((chunks, n_dp)), sem((chunks, n_dp, stages)),
            sem((chunks,)), sem((chunks,)), sem((chunks,)), sem((chunks,)), sem((chunks,)), sem((chunks,)),
        ],
        compiler_params=pltpu.CompilerParams(
            collective_id=collective_id, has_side_effects=True, vmem_limit_bytes=56 * MIB),
        name="reduce_grads",
    )(grads)


SLOTS = 128
F32, LOW = jnp.float32, jnp.bfloat16


def dot(a, b, over_a=1, over_b=0):
    return lax.dot_general(a, b, (((over_a,), (over_b,)), ((), ())), preferred_element_type=F32)


def experts_body(n_dp, n_exp, hid_ref, gy_hbm, routes_t, routes_c, wr_t, w_in_hbm, w_out_hbm, middle,
                 block_out, hid_sum, gates_out, grads_hbm,
                 x_all, w_in, w_out, sent, grows, gu, tmp, acts, stage, slots, gates, dots,
                 pair_buf, held, got, *sems):
    w_sem, gy_sem, stage_sem, own_sem, ready, gate_send, gate_recv = sems[:7]
    gather_sems, out_sems, hid_sems = sems[7:11], sems[11:15], sems[15:19]
    local, _, width = sent.shape
    tree, hidden_units = hid_ref.shape[0], w_out.shape[1]
    rows_e = local * SLOTS
    ring = Ring(n_exp)
    mine, core, depth = ring.mine, ring.core, ring.depth
    first = mine * local
    peers = [lax.rem(mine + k, n_exp) for k in range(1, n_exp)]
    greet([(None, {"expert": e}) for e in peers])

    weights = [pltpu.make_async_copy(w_in_hbm, w_in, w_sem.at[0]), pltpu.make_async_copy(w_out_hbm, w_out, w_sem.at[1])]
    gather = RingGather(ring, hid_ref, x_all, gather_sems)
    gather.start()
    for copy in weights:
        copy.start()
    own = pltpu.make_async_copy(hid_ref, x_all.at[mine], own_sem)
    own.start()

    def gy_buf(j):
        return stage.at[pl.ds(pl.multiple_of(lax.rem(j, 2) * tree, 16), tree)]

    def gy_copy(j):
        return pltpu.make_async_copy(gy_hbm.at[j], gy_buf(j), gy_sem.at[lax.rem(j, 2)])

    gy_copy(0).start()

    below = (lax.broadcasted_iota(jnp.int32, (tree, tree), 0) < lax.broadcasted_iota(jnp.int32, (tree, tree), 1)).astype(LOW)
    sub16 = lax.broadcasted_iota(jnp.int32, (16, tree), 0)

    def find_slots(j, carry):
        names = routes_t[j]
        chosen = jnp.zeros((16, tree), F32)
        for k in range(names.shape[0]):
            chosen = jnp.maximum(chosen, jnp.where(names[k : k + 1, :] == first + sub16, 1.0, 0.0))
        chosen = jnp.where(sub16 < local, chosen, 0.0)
        rank = dot(chosen.astype(LOW), below)
        slots[j] = jnp.where(chosen > 0.5, rank, -1.0)[:8]
        return carry

    lax.fori_loop(0, n_exp, find_slots, 0)

    slot_ids = lax.broadcasted_iota(jnp.int32, (SLOTS, tree), 0).astype(F32)

    def places(j):
        return jnp.concatenate(
            [jnp.where(slot_ids == slots[j, i : i + 1, :], 1.0, 0.0).astype(LOW) for i in range(local)], axis=0)

    def places_t(j):
        names = routes_c[j]
        lane = lax.broadcasted_iota(jnp.int32, (tree, 128), 1)
        chosen = jnp.zeros((tree, 128), F32)
        for k in range(names.shape[1]):
            chosen = jnp.maximum(chosen, jnp.where(names[:, k : k + 1] == first + lane, 1.0, 0.0))
        chosen = jnp.where(lane < local, chosen, 0.0)
        above = (lax.broadcasted_iota(jnp.int32, (tree, tree), 1) < lax.broadcasted_iota(jnp.int32, (tree, tree), 0)).astype(LOW)
        slot = jnp.where(chosen > 0.5, dot(above, chosen.astype(LOW)), -1.0)
        lanes = lane.astype(F32)
        return jnp.concatenate(
            [jnp.where(lanes == slot[:, i : i + 1], 1.0, 0.0).astype(LOW) for i in range(local)], axis=1)

    def find_gates(j):
        names = routes_t[j]
        experts = lax.broadcasted_iota(jnp.int32, (EXPERTS, tree), 0)
        chosen = jnp.zeros((EXPERTS, tree), F32)
        for k in range(names.shape[0]):
            chosen = jnp.maximum(chosen, jnp.where(names[k : k + 1, :] == experts, 1.0, 0.0))
        logits = jnp.where(chosen > 0.5, dot(wr_t[...], x_all[j], 1, 1), -1e30)
        powers = jnp.exp(logits - jnp.max(logits, axis=0, keepdims=True))
        share = powers / jnp.sum(powers, axis=0, keepdims=True)
        sub = lax.broadcasted_iota(jnp.int32, (8, tree), 0)
        own_gates = jnp.zeros((8, tree), F32)
        for i in range(local):
            row = jnp.sum(jnp.where(experts == first + i, share, 0.0), axis=0, keepdims=True)
            own_gates = jnp.where(sub == i, row, own_gates)
        gates[j] = own_gates

    halves = width // 512

    def dispatch(j, src, dest):
        place = places(j)

        def body(n, carry):
            cols = pl.ds(pl.multiple_of(n * 512, 512), 512)
            picked = dot(place, src[:, cols]).astype(LOW)
            for i in range(local):
                dest[i, pl.ds(pl.multiple_of(j * SLOTS, SLOTS), SLOTS), cols] = picked[i * SLOTS : (i + 1) * SLOTS]
            return carry

        lax.fori_loop(0, halves, body, 0)

    def slot_gate(j, e):
        return jnp.sum(jnp.where(slot_ids == slots[j, pl.ds(e, 1), :], gates[j, pl.ds(e, 1), :], 0.0), axis=1, keepdims=True)

    def forward(chip):
        pair_rows = pl.ds(pl.multiple_of(chip * 2 * SLOTS, 2 * SLOTS), 2 * SLOTS)

        def one_tree(q, carry):
            j = 2 * chip + q
            find_gates(j)
            dispatch(j, x_all.at[j], sent)
            return carry

        lax.fori_loop(0, 2, one_tree, 0)

        def one_expert(e, carry):
            both = dot(sent[e, pair_rows, :], w_in[e])
            gu[e, pair_rows, :] = both.astype(LOW)
            a, b = both[:, :hidden_units], both[:, hidden_units:]
            act = (a / (1.0 + jnp.exp(-a)) * b).astype(LOW).astype(F32)
            gate = jnp.concatenate([slot_gate(2 * chip, e), slot_gate(2 * chip + 1, e)], axis=0)
            made = dot((act * gate).astype(LOW), w_out[e]).astype(LOW)
            for q in range(2):
                tmp[pl.ds(pl.multiple_of(q * rows_e + e * SLOTS, SLOTS), SLOTS), :] = made[q * SLOTS : (q + 1) * SLOTS]
            return carry

        lax.fori_loop(0, local, one_expert, 0)

    def combine_out(chip):
        def one_tree(q, carry):
            j = 2 * chip + q
            rows = pl.ds(pl.multiple_of(q * rows_e, rows_e), rows_e)
            x_all[j] = dot(places_t(j), tmp[rows, :]).astype(LOW)
            return carry

        lax.fori_loop(0, 2, one_tree, 0)

    def grad_rows(j, carry):
        pl.when(j + 1 < n_exp)(lambda: gy_copy(j + 1).start())
        gy_copy(j).wait()
        dispatch(j, gy_buf(j), grows)
        return carry

    events = gather.events()
    out = RingScatter(ring, lambda e: x_all.at[e], views((pair_buf, held, got)), out_sems)

    def chip_at(d):
        return lax.rem(ring.z + d, depth)

    def group(g, carry):
        d = jnp.where(g == 0, 0, jnp.where(g == 1, depth - 1, jnp.where(g == 2, 1, 2)))
        chip = chip_at(d)

        @pl.when(g == 0)
        def _():
            own.wait()
            gather.wait_pair(0, 0)
            gather.wait_pair(0, 1)
            for copy in weights:
                copy.wait()

        @pl.when(g == 1)
        def _():
            for event in events[:4]:
                gather.handle(event)
            gather.wait_pair(-1, 0)
            gather.wait_pair(-1, 1)

        @pl.when(g == 2)
        def _():
            gather.wait_pair(1, 0)
            gather.wait_pair(1, 1)

        @pl.when(g == 3)
        def _():
            for event in events[4:]:
                gather.handle(event)
            gather.wait_pair(2, 0)
            gather.wait_pair(2, 1)

        forward(chip)

        @pl.when(g == 0)
        def _():
            gather.finish_own()
            lax.fori_loop(0, n_exp, grad_rows, 0)

        for at, d in ((1, -1), (2, 1), (3, 2)):
            @pl.when(g == at)
            def _():
                for event in events:
                    if event[1] == abs(d) and (abs(d) == 2 or (event[0] == 0) == (d < 0)):
                        gather.finish_event(event)

        combine_out(chip)
        pl.when(g == 0)(lambda: out.start_pair(0))
        pl.when(g == 1)(lambda: out.start_pair(depth - 1))
        pl.when(g == 2)(lambda: out.start_pair(1))
        pl.when(g == 3)(lambda: out.start_pair(2))
        return carry

    lax.fori_loop(0, depth, group, 0)
    out.first()
    out.early()

    def stage_copy(e):
        return pltpu.make_async_copy(stage, grads_hbm.at[e], stage_sem)

    block = 4 * SLOTS
    sub8 = lax.broadcasted_iota(jnp.int32, (8, tree), 0)

    def backward(e, carry):
        def one_block(m, inner):
            rows = pl.ds(pl.multiple_of(m * block, block), block)
            grad_act = dot(grows[e, rows, :], w_out[e], 1, 1)
            a = gu[e, rows, pl.ds(0, hidden_units)].astype(F32)
            b = gu[e, rows, pl.ds(hidden_units, hidden_units)].astype(F32)
            sg = 1.0 / (1.0 + jnp.exp(-a))
            sw = a * sg
            act = (sw * b).astype(LOW).astype(F32)
            gate = jnp.concatenate([slot_gate(4 * m + q, e) for q in range(4)], axis=0)
            told = jnp.sum(act * grad_act, axis=1, keepdims=True)
            acts[rows, :] = (act * gate).astype(LOW)
            grad_act = grad_act * gate
            tmp[rows, pl.ds(0, hidden_units)] = (grad_act * b * sg * (1.0 + a * (1.0 - sg))).astype(LOW)
            tmp[rows, pl.ds(hidden_units, hidden_units)] = (grad_act * sw).astype(LOW)
            for q in range(4):
                j = 4 * m + q
                row = jnp.sum(
                    jnp.where(slot_ids == slots[j, pl.ds(e, 1), :], told[q * SLOTS : (q + 1) * SLOTS], 0.0),
                    axis=0, keepdims=True)
                dots[j] = jnp.where(sub8 == e, row, dots[j])
            return inner

        lax.fori_loop(0, n_exp // 4, one_block, 0)
        pl.when(e > 0)(lambda: stage_copy(e - 1).wait())
        in_rows, out_rows = width // n_dp, hidden_units // n_dp
        grad_out = dot(acts[...], grows[e], 0, 0).astype(LOW)
        for d in range(n_dp):
            stage[pl.ds(d * (in_rows + out_rows) + in_rows, out_rows), :] = grad_out[d * out_rows : (d + 1) * out_rows]

        def in_half(h, inner):
            grad_in = dot(sent[e, :, pl.ds(pl.multiple_of(h * 512, 512), 512)], tmp[...], 0, 0).astype(LOW)
            per = 512 // in_rows
            for k in range(per):
                at = pl.multiple_of((h * per + k) * (in_rows + out_rows), 16)
                stage[pl.ds(at, in_rows), :] = grad_in[k * in_rows : (k + 1) * in_rows]
            return inner

        lax.fori_loop(0, halves, in_half, 0)
        stage_copy(e).start()

        def back_half(m, inner):
            rows = pl.ds(pl.multiple_of(m * 512, 512), 512)
            sent[e, rows, :] = dot(tmp[rows, :], w_in[e], 1, 1).astype(LOW)
            return inner

        lax.fori_loop(0, n_exp * SLOTS // 512, back_half, 0)
        pl.when(e == local // 2 - 1)(out.late)
        return carry

    dots[...] = jnp.zeros(dots.shape, F32)
    lax.fori_loop(0, local, backward, 0)
    for partner in (ring.pair, ring.right, ring.left):
        pl.semaphore_signal(ready, inc=1, device_id={"expert": partner}, device_id_type=MESH)

    gate_copies = []
    for k, e in enumerate(peers):
        copy = remote(dots.at[e], gates_out.at[mine], gate_send.at[k], gate_recv.at[k], expert=e)
        copy.start()
        gate_copies.append(copy)
    gates_out[mine] = dots[mine]
    out.last(block_out, middle)

    def part(j):
        return grows.at[lax.div(j, 2), pl.ds(pl.multiple_of(lax.rem(j, 2) * tree, 16), tree)]

    def spare(b):
        return gu.at[b // 3, pl.ds((b % 3) * tree, tree)]

    hid = RingScatter(ring, part, (spare, lambda d: spare(depth + d), lambda side, d: spare(2 * depth + 2 * side + d)), hid_sems)

    def combine_hid(g, carry):
        d = jnp.where(g == 0, 2, jnp.where(g == 1, 1, jnp.where(g == 2, depth - 1, 0)))
        chip = chip_at(d)

        def one_tree(q, inner):
            j = 2 * chip + q
            rows = pl.ds(pl.multiple_of(j * SLOTS, SLOTS), SLOTS)
            made = jnp.concatenate([sent[i, rows, :] for i in range(local)], axis=0)
            part(j)[...] = dot(places_t(j), made).astype(LOW)
            return inner

        lax.fori_loop(0, 2, one_tree, 0)

        @pl.when(g == 0)
        def _():
            pl.semaphore_wait(ready, 3)
            hid.start_pair(2)

        pl.when(g == 1)(lambda: hid.start_pair(1))
        pl.when(g == 2)(lambda: hid.start_pair(depth - 1))
        pl.when(g == 3)(lambda: hid.start_pair(0))
        pl.when(g == 1)(hid.first)
        return carry

    lax.fori_loop(0, depth, combine_hid, 0)
    hid.early()
    hid.late()
    hid.last(hid_sum)

    for k, copy in enumerate(gate_copies):
        copy.wait_send()
        source = lax.rem(mine + n_exp - 1 - k, n_exp)
        remote(dots.at[mine], gates_out.at[source], gate_send.at[k], gate_recv.at[k], expert=mine).wait_recv()
    stage_copy(local - 1).wait()
    out.finish_sends()
    hid.finish_sends()


def experts(n_dp, n_exp, hidden2, grad_y, routes_all, router, expert_in, expert_out, middle, collective_id):
    local, width, both = expert_in.shape
    units = expert_out.shape[1]
    tree = hidden2.shape[0]
    rows = n_exp * SLOTS
    sem = pltpu.SemaphoreType.DMA
    bufs, out_sems = RingScatter.scratch(n_exp, (tree, width), LOW)
    _, hid_sems = RingScatter.scratch(n_exp, (tree, width), LOW)
    shape = jax.ShapeDtypeStruct
    return pl.pallas_call(
        functools.partial(experts_body, n_dp, n_exp),
        out_shape=[
            shape((tree, width), LOW),
            shape((tree, width), F32),
            shape((n_exp, 8, tree), F32),
            shape((local, width + units, width), LOW),
        ],
        in_specs=[pl.BlockSpec(memory_space=s) for s in (VMEM, ANY, VMEM, VMEM, VMEM, ANY, ANY, VMEM)],
        out_specs=[pl.BlockSpec(memory_space=s) for s in (VMEM, VMEM, VMEM, ANY)],
        scratch_shapes=[
            pltpu.VMEM((n_exp, tree, width), LOW),
            pltpu.VMEM((local, width, both), LOW),
            pltpu.VMEM((local, units, width), LOW),
            pltpu.VMEM((local, rows, width), LOW),
            pltpu.VMEM((local, rows, width), LOW),
            pltpu.VMEM((local, rows, both), LOW),
            pltpu.VMEM((max(rows, 2 * local * SLOTS), width), LOW),
            pltpu.VMEM((rows, units), LOW),
            pltpu.VMEM((width + units, width), LOW),
            pltpu.VMEM((n_exp, 8, tree), F32),
            pltpu.VMEM((n_exp, 8, tree), F32),
            pltpu.VMEM((n_exp, 8, tree), F32),
            *bufs,
            sem((2,)), sem((2,)), sem, sem, pltpu.SemaphoreType.REGULAR, sem((n_exp - 1,)), sem((n_exp - 1,)),
            *RingGather.scratch(n_exp), *out_sems, *hid_sems,
        ],
        compiler_params=pltpu.CompilerParams(
            collective_id=collective_id, has_side_effects=True, vmem_limit_bytes=63 * MIB),
        name="experts",
    )(hidden2, grad_y, routes_all.transpose(0, 2, 1), routes_all, router.T, expert_in, expert_out, middle)


def tree_layout(tree_rows):
    unit_rows = tree_rows // 20
    row_index = jnp.arange(tree_rows, dtype=jnp.int32)
    segment = jnp.where(
        row_index < 8 * unit_rows,
        0,
        jnp.where(
            row_index < 12 * unit_rows,
            1 + (row_index - 8 * unit_rows) // unit_rows,
            5 + (row_index - 12 * unit_rows) // unit_rows,
        ),
    )
    depth_start = jnp.where(segment == 0, 0, jnp.where(segment < 5, 8 * unit_rows, 9 * unit_rows))
    seg_start = jnp.where(
        segment == 0,
        0,
        jnp.where(
            segment < 5,
            8 * unit_rows + (segment - 1) * unit_rows,
            12 * unit_rows + (segment - 5) * unit_rows,
        ),
    )
    position = depth_start + row_index - seg_start
    return (segment, position)


def path_allowed(parent_row, segment):
    segment_ids = jnp.arange(parent_row.shape[0], dtype=jnp.int32)
    grandparent = parent_row[parent_row]
    on_path = (
        (segment_ids[None, :] == segment_ids[:, None])
        | (segment_ids[None, :] == parent_row[:, None])
        | (segment_ids[None, :] == grandparent[:, None])
    ).astype(jnp.float32)
    seg_hot = (segment[:, None] == segment_ids[None, :]).astype(jnp.float32)
    reach = jnp.dot(
        jnp.dot(seg_hot, on_path, precision=lax.Precision.HIGHEST),
        seg_hot.T,
        precision=lax.Precision.HIGHEST,
    )
    row_index = jnp.arange(segment.shape[0], dtype=jnp.int32)
    return (reach > 0.5) & (row_index[None, :] <= row_index[:, None])


def rope_tables(position):
    frequency = 10000.0 ** (-jnp.arange(0, HD, 2, dtype=jnp.float32) / HD)
    angles = position.astype(jnp.float32)[:, None] * frequency[None, :]
    return (jnp.concatenate([jnp.cos(angles)] * 2, -1), jnp.concatenate([jnp.sin(angles)] * 2, -1))


def turn_half(field):
    half_width = field.shape[-1] // 2
    return jnp.concatenate([-field[..., half_width:], field[..., :half_width]], axis=-1)


def rotary(field, cosine, sine_table):
    return field * cosine + turn_half(field) * sine_table


def unrotate(grad_field, cosine, sine_table):
    return grad_field * cosine - turn_half(grad_field * sine_table)


def rms_norm(field, gain_vector):
    return (
        field * lax.rsqrt(jnp.mean(field * field, axis=-1, keepdims=True) + EPSILON) * gain_vector
    )


def gated_unit(gate_up):
    width_ff = gate_up.shape[-1] // 2
    gate_part = gate_up[..., :width_ff]
    return gate_part / (1.0 + jnp.exp(-gate_part)) * gate_up[..., width_ff:]


def experts_plain(
    n_dp, n_exp, hidden2, grad_y, routes_all, router_full, expert_in, expert_out, middle, collective_id
):
    tree_rows, width = hidden2.shape
    capacity = CAP
    expert_ids = jnp.arange(EXPERTS, dtype=jnp.int32)
    here = lax.axis_index("expert")
    local = expert_in.shape[0]
    first = here * local
    hidden_all = lax.all_gather(hidden2, "expert", axis=0, tiled=False)
    own_ids = first + jnp.arange(local, dtype=jnp.int32)
    hot_all = routes_all[:, :, :, None] == expert_ids[None, None, None, :]
    chosen_all = jnp.any(hot_all, axis=2)
    chosen = jnp.any(routes_all[:, :, :, None] == own_ids[None, None, None, :], axis=2)
    lower = jnp.tril(jnp.ones((tree_rows, tree_rows), jnp.bfloat16), -1)
    rank = jnp.einsum(
        "tu,jue->jet", lower, chosen.astype(jnp.bfloat16), preferred_element_type=jnp.float32
    ).astype(jnp.int32)
    slots = jnp.arange(capacity, dtype=jnp.int32)
    chosen_t = chosen.transpose(0, 2, 1)
    place = (rank[:, :, None, :] == slots[None, None, :, None]) & chosen_t[:, :, None, :]
    place = place.astype(jnp.bfloat16)
    logits_all = jnp.einsum(
        "jtd,de->jte", hidden_all, router_full, preferred_element_type=jnp.float32
    )
    masked = jnp.where(chosen_all, logits_all, -1e30)
    weight = jnp.exp(masked - jnp.max(masked, axis=-1, keepdims=True))
    weight = weight / jnp.sum(weight, axis=-1, keepdims=True)
    gates_own = lax.dynamic_slice_in_dim(weight, first, local, axis=2)
    gate_slot = jnp.einsum(
        "jest,jte->ejs", place.astype(jnp.float32), gates_own, precision=lax.Precision.HIGHEST
    )[..., None]
    sent = jnp.einsum("jest,jtd->ejsd", place, hidden_all, preferred_element_type=jnp.float32)
    sent = sent.astype(jnp.bfloat16)
    grad_rows = jnp.einsum("jest,jtd->ejsd", place, grad_y, preferred_element_type=jnp.float32)
    grad_rows = grad_rows.astype(jnp.bfloat16)
    gate_up = jnp.einsum("ejsd,edf->ejsf", sent, expert_in, preferred_element_type=jnp.float32)
    activated, glu_back = jax.vjp(gated_unit, gate_up)
    act_low = activated.astype(jnp.bfloat16).astype(jnp.float32)
    act_scaled = (act_low * gate_slot).astype(jnp.bfloat16)
    made = jnp.einsum(
        "ejsf,efd->ejsd", act_scaled, expert_out, preferred_element_type=jnp.float32
    ).astype(jnp.bfloat16)
    out_part = jnp.einsum("jest,ejsd->jtd", place, made, preferred_element_type=jnp.float32)
    out_sum = lax.psum_scatter(
        out_part.astype(jnp.bfloat16), "expert", scatter_dimension=0, tiled=False
    ).astype(jnp.float32)
    result = middle + out_sum
    block_out = result.astype(jnp.bfloat16)
    grad_act = jnp.einsum(
        "ejsd,efd->ejsf", grad_rows, expert_out, preferred_element_type=jnp.float32
    )
    gate_dot = jnp.sum(act_low * grad_act, axis=-1)
    gates_back = jnp.einsum(
        "jest,ejs->jte", place.astype(jnp.float32), gate_dot, precision=lax.Precision.HIGHEST
    )
    grad_out_w = jnp.einsum(
        "ejsf,ejsd->efd", act_scaled, grad_rows, preferred_element_type=jnp.float32
    )
    grad_gate_up = glu_back(grad_act * gate_slot)[0].astype(jnp.bfloat16)
    grad_sent = jnp.einsum(
        "ejsf,edf->ejsd", grad_gate_up, expert_in, preferred_element_type=jnp.float32
    ).astype(jnp.bfloat16)
    grad_in_w = jnp.einsum(
        "ejsd,ejsf->edf", sent, grad_gate_up, preferred_element_type=jnp.float32
    )
    hid_part = jnp.einsum("jest,ejsd->jtd", place, grad_sent, preferred_element_type=jnp.float32)
    gates_mine = lax.all_to_all(gates_back, "expert", split_axis=0, concat_axis=2, tiled=True)[0]
    hid_sum = lax.psum_scatter(
        hid_part.astype(jnp.bfloat16), "expert", scatter_dimension=0, tiled=False
    ).astype(jnp.float32)
    local, units = expert_in.shape[0], expert_out.shape[1]
    low = jnp.bfloat16
    grads = jnp.concatenate(
        [
            grad_in_w.astype(low).reshape(local, n_dp, width // n_dp, width),
            grad_out_w.astype(low).reshape(local, n_dp, units // n_dp, width),
        ],
        axis=2,
    ).reshape(local, width + units, width)
    return block_out, hid_sum, gates_mine.T.reshape(n_exp, local, tree_rows), grads


def shards(
    tokens,
    attn_gain,
    w_query,
    w_keyval,
    w_output,
    moe_gain,
    w_router,
    expert_in,
    expert_out,
    cotangent,
    routes,
    parents,
):
    tree_rows = tokens.shape[0]
    width = tokens.shape[1]
    capacity = CAP
    groups = H // KV
    kv_width = KV * HD
    score_scale = HD ** (-0.5)
    n_dp, n_exp = lax.axis_size("dp"), lax.axis_size("expert")
    grad_y = lax.all_gather(cotangent, "expert", axis=0, tiled=False)
    routes_all = lax.all_gather(routes, "expert", axis=0, tiled=False)
    rows = w_query.shape[0]
    small = jnp.concatenate(
        [w_router, attn_gain[:, None], moe_gain[:, None], jnp.zeros((rows, 128 - EXPERTS - 2), w_router.dtype)], axis=1
    )
    query_full, keyval_full, output_full, small_full = gather_weights(
        n_dp, (w_query, w_keyval, w_output, small), 1
    )
    router_full = small_full[:, :EXPERTS]
    gain_first, gain_second = small_full[:, EXPERTS], small_full[:, EXPERTS + 1]
    inputs = tokens.astype(jnp.float32)
    segment, position = tree_layout(tree_rows)
    allowed = path_allowed(parents[0], segment)
    cosine, sine_table = rope_tables(position)
    cos_four, sin_four = (cosine[:, None, None, :], sine_table[:, None, None, :])
    cos_three, sin_three = (cosine[:, None, :], sine_table[:, None, :])
    normed, first_back = jax.vjp(rms_norm, inputs, gain_first.astype(jnp.float32))
    hidden = normed.astype(jnp.bfloat16)
    query_pre = jnp.dot(hidden, query_full, preferred_element_type=jnp.float32)
    keyval_pre = jnp.dot(hidden, keyval_full, preferred_element_type=jnp.float32)
    queries = rotary(query_pre.reshape(tree_rows, KV, groups, HD), cos_four, sin_four).astype(
        jnp.bfloat16
    )
    key_heads = rotary(
        keyval_pre[:, :kv_width].reshape(tree_rows, KV, HD), cos_three, sin_three
    ).astype(jnp.bfloat16)
    values = keyval_pre[:, kv_width:].reshape(tree_rows, KV, HD).astype(jnp.bfloat16)

    def score_block():
        raw_scores = (
            jnp.einsum("tkgd,skd->kgts", queries, key_heads, preferred_element_type=jnp.float32)
            * score_scale
        )
        return jnp.where(allowed, raw_scores, -1e30)

    scores = score_block()
    row_max = jnp.max(scores, axis=-1, keepdims=True)
    exp_scores = jnp.exp(scores - row_max)
    row_total = jnp.sum(exp_scores, axis=-1, keepdims=True)
    log_total = row_max + jnp.log(row_total)
    attn_low = (exp_scores / row_total).astype(jnp.bfloat16)
    attended = jnp.einsum("kgts,skd->tkgd", attn_low, values, preferred_element_type=jnp.float32)
    attended = attended.reshape(tree_rows, H * HD).astype(jnp.bfloat16)
    middle = inputs + jnp.dot(attended, output_full, preferred_element_type=jnp.float32)
    normed2, second_back = jax.vjp(rms_norm, middle, gain_second.astype(jnp.float32))
    hidden2 = normed2.astype(jnp.bfloat16)
    logits = jnp.dot(hidden2, router_full, preferred_element_type=jnp.float32)
    expert_ids = jnp.arange(EXPERTS, dtype=jnp.int32)
    route_hot = (routes[:, :, None] == expert_ids[None, None, :]).astype(jnp.float32)
    picked = jnp.sum(route_hot * logits[:, None, :], axis=2)
    picked_exp = jnp.exp(picked - jnp.max(picked, axis=1, keepdims=True))
    gate_weights = picked_exp / jnp.sum(picked_exp, axis=1, keepdims=True)
    run_experts = experts if n_exp == 8 else experts_plain
    block_out, hid_sum, gates_mine, grads_low = run_experts(
        n_dp, n_exp, hidden2, grad_y, routes_all, router_full, expert_in, expert_out, middle, 2
    )
    gates_mine = gates_mine[:, : expert_in.shape[0]].reshape(EXPERTS, tree_rows).T
    grad_result = cotangent.astype(jnp.float32)
    gate_dense = jnp.sum(route_hot * gate_weights[:, :, None], axis=1)
    grad_logits = (
        gate_dense
        * (gates_mine - jnp.sum(gate_dense * gates_mine, axis=1, keepdims=True))
    ).astype(jnp.bfloat16)
    grad_router = jnp.einsum("td,te->de", hidden2, grad_logits, preferred_element_type=jnp.float32)
    grad_hidden2 = hid_sum + jnp.einsum(
        "te,de->td", grad_logits, router_full, preferred_element_type=jnp.float32
    )
    expert_share = lax.psum_scatter(grads_low, "dp", scatter_dimension=1, tiled=True)
    expert_in_share = expert_share[:, : width // n_dp].astype(jnp.float32)
    expert_out_share = expert_share[:, width // n_dp :].astype(jnp.float32)
    grad_mid_norm, grad_gain_second = second_back(grad_hidden2)
    grad_middle = grad_result + grad_mid_norm
    grad_branch = grad_middle.astype(jnp.bfloat16)
    grad_w_out = jnp.einsum("ti,td->id", attended, grad_branch, preferred_element_type=jnp.float32)
    grad_attended = jnp.einsum(
        "td,id->ti", grad_branch, output_full, preferred_element_type=jnp.float32
    )
    grad_attended = grad_attended.astype(jnp.bfloat16).reshape(tree_rows, KV, groups, HD)
    attn_probs = jnp.exp(score_block() - log_total)
    probs_low = attn_probs.astype(jnp.bfloat16)
    grad_values = jnp.einsum(
        "kgts,tkgd->skd", probs_low, grad_attended, preferred_element_type=jnp.float32
    )
    grad_probs = jnp.einsum(
        "tkgd,skd->kgts", grad_attended, values, preferred_element_type=jnp.float32
    )
    grad_scores = (
        attn_probs * (grad_probs - jnp.sum(attn_probs * grad_probs, axis=-1, keepdims=True))
    ).astype(jnp.bfloat16)
    grad_query_rot = (
        jnp.einsum("kgts,skd->tkgd", grad_scores, key_heads, preferred_element_type=jnp.float32)
        * score_scale
    )
    grad_keys_rot = (
        jnp.einsum("kgts,tkgd->skd", grad_scores, queries, preferred_element_type=jnp.float32)
        * score_scale
    )
    grad_query_pre = (
        unrotate(grad_query_rot, cos_four, sin_four).reshape(tree_rows, H * HD).astype(jnp.bfloat16)
    )
    grad_keyval_pre = jnp.concatenate(
        [
            unrotate(grad_keys_rot, cos_three, sin_three).reshape(tree_rows, kv_width),
            grad_values.reshape(tree_rows, kv_width),
        ],
        axis=1,
    ).astype(jnp.bfloat16)
    grad_w_q = jnp.einsum("td,ti->di", hidden, grad_query_pre, preferred_element_type=jnp.float32)
    grad_w_kv = jnp.einsum("td,ti->di", hidden, grad_keyval_pre, preferred_element_type=jnp.float32)
    grad_hidden = jnp.einsum(
        "ti,di->td", grad_query_pre, query_full, preferred_element_type=jnp.float32
    ) + jnp.einsum("ti,di->td", grad_keyval_pre, keyval_full, preferred_element_type=jnp.float32)
    grad_in_norm, grad_gain_first = first_back(grad_hidden)
    input_grad = grad_middle + grad_in_norm
    low = jnp.bfloat16
    share = reduce_grads(
        n_dp,
        n_exp,
        jnp.concatenate(
            [
                grad_w_q.astype(low),
                grad_w_kv.astype(low),
                grad_w_out.astype(low),
                grad_router.astype(low),
                grad_gain_first.astype(low)[:, None],
                grad_gain_second.astype(low)[:, None],
                jnp.zeros((width, 128 - EXPERTS - 2), low),
            ],
            axis=1,
        ),
        5,
        5,
    )
    at = 3 * width
    shares = (
        share[:, at + EXPERTS],
        share[:, :width],
        share[:, width : 2 * width],
        share[:, 2 * width : at],
        share[:, at + EXPERTS + 1],
        share[:, at : at + EXPERTS],
    )
    return (
        block_out,
        input_grad,
        shares[0],
        shares[1],
        shares[2],
        shares[3],
        shares[4],
        shares[5],
        expert_in_share,
        expert_out_share,
    )


def solution(mesh):
    in_specs = (
        P(("dp", "expert"), None),
        P("dp"),
        P("dp", None),
        P("dp", None),
        P("dp", None),
        P("dp"),
        P("dp", None),
        P("expert", None, None),
        P("expert", None, None),
        P(("dp", "expert"), None),
        P(("dp", "expert"), None),
        P(("dp", "expert"), None),
    )
    out_specs = (
        P(("dp", "expert"), None),
        P(("dp", "expert"), None),
        P("dp"),
        P("dp", None),
        P("dp", None),
        P("dp", None),
        P("dp"),
        P("dp", None),
        P("expert", "dp", None),
        P("expert", "dp", None),
    )
    return jax.shard_map(shards, mesh=mesh, in_specs=in_specs, out_specs=out_specs, check_vma=False)
```

```python
import functools

import jax
import jax.numpy as jnp
from jax import lax
from jax.experimental import pallas as pl
from jax.experimental.pallas import tpu as pltpu
from jax.sharding import PartitionSpec as P

H = 16
KV = 8
HD = 64
EXPERTS = 32
TOPK = 8
CAP = 120


EPSILON = 1e-06


MESH = pl.DeviceIdType.MESH
MIB = 1024 * 1024
VMEM = pltpu.VMEM
ANY = pl.ANY


def remote(src, dst, send_sem, recv_sem, **where):
    return pltpu.make_async_remote_copy(
        src_ref=src, dst_ref=dst, send_sem=send_sem, recv_sem=recv_sem,
        device_id=where, device_id_type=MESH,
    )


def greet(partners):
    barrier = pltpu.get_barrier_semaphore()
    for condition, where in partners:
        def signal(where=where):
            pl.semaphore_signal(barrier, inc=1, device_id=where, device_id_type=MESH)
        if condition is None:
            signal()
        else:
            pl.when(condition)(signal)
    count = sum(1 if c is None else c.astype(jnp.int32) for c, _ in partners)
    pl.semaphore_wait(barrier, count)


def add_rows(out, *terms, step=16):
    rows = out.shape[0]

    def body(i, carry):
        at = pl.ds(pl.multiple_of(i * step, step), step)
        total = terms[0][at, :].astype(jnp.float32)
        for term in terms[1:]:
            total = total + term[at, :].astype(jnp.float32)
        out[at, :] = total.astype(out.dtype)
        return carry

    lax.fori_loop(0, rows // step, body, 0)


def bit_orders(n):
    bits = [1 << j for j in range(n.bit_length() - 1)]
    return [bits[p:] + bits[:p] for p in range(len(bits))] or [[]]


def weights_body(n_dp, *refs):
    arrays = 4
    ins, outs = refs[:arrays], refs[arrays : 2 * arrays]
    send_sem, recv_sem, pair_send, pair_recv, own_sem = refs[2 * arrays :]
    me, mine = lax.axis_index("dp"), lax.axis_index("expert")
    core = lax.rem(mine, 2)
    pair = mine + 1 - 2 * core
    orders = bit_orders(n_dp)
    greet([(None, {"dp": me ^ bit}) for bit in orders[0]] + [(None, {"expert": pair})])
    shard = ins[0].shape[0]
    half = shard // 2
    sends, pairs, owns = [], [], []
    cuts = min(2, len(orders), half // 16)
    size = half // cuts

    def pieces(a):
        return cuts

    def rows(start, side, p):
        return pl.ds(pl.multiple_of(start + side * half + p * size, 16), size)

    def push(a, p, r, bit):
        to = me ^ bit
        there = outs[a].at[rows((me ^ r) * shard, core, p)]
        src = ins[a].at[rows(0, core, p)] if r == 0 else there
        copy = remote(src, there, send_sem.at[a, p, r, bit.bit_length() - 1], recv_sem.at[a, p, r ^ bit], dp=to)
        copy.start()
        sends.append(copy)

    for a in range(arrays):
        for p in range(pieces(a)):
            for bit in orders[p]:
                push(a, p, 0, bit)
    for a in range(arrays):
        copy = pltpu.make_async_copy(
            ins[a], outs[a].at[pl.ds(pl.multiple_of(me * shard, 16), shard)], own_sem.at[a])
        copy.start()
        owns.append(copy)
    def reach(order):
        blocks = [0]
        steps = []
        for j, bit in enumerate(order):
            new = [r | bit for r in blocks]
            steps.append((j, new))
            blocks = blocks + new
        return steps

    for j in range(len(orders[0])):
        for a in range(arrays):
            for p in range(pieces(a)):
                order = orders[p]
                for r in reach(order)[j][1]:
                    here = outs[a].at[rows((me ^ r) * shard, core, p)]
                    remote(here, here, send_sem.at[a, p, r, 0], recv_sem.at[a, p, r], dp=me).wait_recv()
                    for bit in order[j + 1 :]:
                        push(a, p, r, bit)
                    copy = remote(here, here, pair_send.at[a, p, r], pair_recv.at[a, p, r], expert=pair)
                    copy.start()
                    pairs.append((copy, a, p, r))
    for copy in owns:
        copy.wait()
    for copy in sends:
        copy.wait_send()
    for copy, a, p, r in pairs:
        copy.wait_send()
        here = outs[a].at[rows((me ^ r) * shard, 1 - core, p)]
        remote(here, here, pair_send.at[a, p, r], pair_recv.at[a, p, r], expert=pair).wait_recv()


def gather_weights(n_dp, arrays, collective_id):
    orders = bit_orders(n_dp)
    count, pieces = len(arrays), min(2, len(orders))
    out_shape = [jax.ShapeDtypeStruct((n_dp * a.shape[0], a.shape[1]), a.dtype) for a in arrays]
    return pl.pallas_call(
        functools.partial(weights_body, n_dp),
        out_shape=out_shape,
        in_specs=[pl.BlockSpec(memory_space=VMEM)] * count,
        out_specs=[pl.BlockSpec(memory_space=ANY)] * count,
        scratch_shapes=[
            pltpu.SemaphoreType.DMA((count, pieces, n_dp, max(1, n_dp.bit_length() - 1))),
            pltpu.SemaphoreType.DMA((count, pieces, n_dp)),
            pltpu.SemaphoreType.DMA((count, pieces, n_dp)),
            pltpu.SemaphoreType.DMA((count, pieces, n_dp)),
            pltpu.SemaphoreType.DMA((count,)),
        ],
        compiler_params=pltpu.CompilerParams(collective_id=collective_id, has_side_effects=True),
        name="gather_weights",
    )(*arrays)


class Ring:
    def __init__(self, n_exp):
        self.mine = lax.axis_index("expert")
        self.core = lax.rem(self.mine, 2)
        self.z = lax.div(self.mine, 2)
        self.depth = n_exp // 2
        self.far = self.depth // 2
        self.pair = self.mine + 1 - 2 * self.core
        self.right, self.left = self.dev(1), self.dev(-1)

    def dev(self, d):
        return lax.rem(self.z + d + self.depth, self.depth) * 2 + self.core

    def partners(self):
        return [(None, {"expert": e}) for e in (self.pair, self.right, self.left)]


class RingGather:
    def __init__(self, ring, own, out, sems):
        self.ring, self.own, self.out = ring, own, out
        self.send, self.recv, self.pair_send, self.pair_recv = sems
        self.half = own.shape[0] // 2

    @staticmethod
    def scratch(n_exp):
        far, depth = n_exp // 4, n_exp // 2
        sem = pltpu.SemaphoreType.DMA
        return [sem((2, far + 1, 2)), sem((2, far + 1, 2)), sem((depth, 2)), sem((depth, 2))]

    def rows(self, h):
        return pl.ds(h * self.half, self.half)

    def goes(self, side, s, h):
        far = self.ring.far
        return s < far or (s == far and h == side)

    def block(self, d, h):
        return self.out.at[self.ring.dev(d), self.rows(h)]

    def hop(self, side, s, h):
        d = -s if side == 0 else s
        src = self.own.at[self.rows(h)] if s == 0 else self.block(d, h)
        to = self.ring.right if side == 0 else self.ring.left
        return remote(src, self.block(d, h), self.send.at[side, s, h], self.recv.at[side, s + 1, h], expert=to)

    def across(self, d, h):
        src = self.own.at[self.rows(h)] if d == 0 else self.block(d, h)
        slot = d % self.ring.depth
        return remote(src, self.block(d, h), self.pair_send.at[slot, h], self.pair_recv.at[slot, h], expert=self.ring.pair)

    ORDER = ((0, 0), (1, 1), (0, 1), (1, 0))

    def start(self):
        for side, h in self.ORDER:
            if self.goes(side, 1, h):
                self.hop(side, 0, h).start()
        self.across(0, 0).start()
        self.across(0, 1).start()

    def events(self):
        return [(side, s, h) for s in range(1, self.ring.far + 1) for side, h in self.ORDER if self.goes(side, s, h)]

    def handle(self, event):
        side, s, h = event
        d = -s if side == 0 else s
        here = self.block(d, h)
        remote(here, here, self.send.at[side, s, h], self.recv.at[side, s, h], expert=self.ring.mine).wait_recv()
        if self.goes(side, s + 1, h):
            self.hop(side, s, h).start()
        self.across(d, h).start()

    def wait_pair(self, d, h):
        slot = d % self.ring.depth
        here = self.out.at[self.ring.pair - self.ring.mine + self.ring.dev(d), self.rows(h)]
        remote(here, here, self.pair_send.at[slot, h], self.pair_recv.at[slot, h], expert=self.ring.mine).wait_recv()

    def finish_own(self):
        for side, h in self.ORDER:
            if self.goes(side, 1, h):
                self.hop(side, 0, h).wait_send()
        self.across(0, 0).wait_send()
        self.across(0, 1).wait_send()

    def finish_event(self, event):
        side, s, h = event
        if self.goes(side, s + 1, h):
            self.hop(side, s, h).wait_send()
        self.across(-s if side == 0 else s, h).wait_send()


class RingScatter:
    def __init__(self, ring, part, bufs, sems):
        self.ring, self.part = ring, part
        self.pair_buf, self.held, self.got = bufs
        self.pair_send, self.pair_recv, self.send, self.recv = sems
        self.half = self.held(0).shape[0] // 2

    @staticmethod
    def scratch(n_exp, block, dtype):
        far, depth = n_exp // 4, n_exp // 2
        sem = pltpu.SemaphoreType.DMA
        bufs = [pltpu.VMEM((depth,) + block, dtype), pltpu.VMEM((depth,) + block, dtype),
                pltpu.VMEM((2, far) + block, dtype)]
        return bufs, [sem((depth,)), sem((depth,)), sem((2, far + 1, 2)), sem((2, far + 1, 2))]

    def rows(self, h):
        return pl.ds(h * self.half, self.half)

    def order(self):
        far, depth = self.ring.far, self.ring.depth
        order = [far]
        for s in range(far - 1, 0, -1):
            order += [s, depth - s]
        return order + [0]

    def comes(self, side, d, h):
        far = self.ring.far
        return d + 1 < far or (d + 1 == far and h == side)

    def across(self, d):
        ring = self.ring
        return remote(self.part(ring.dev(d) + 1 - 2 * ring.core), self.pair_buf(d),
                      self.pair_send.at[d], self.pair_recv.at[d], expert=ring.pair)

    def start_pair(self, d):
        self.across(d).start()

    def wait_pair(self, d):
        self.across(d).wait_recv()

    def wait_got(self, side, d, h):
        here = self.got(side, d).at[self.rows(h)]
        remote(here, here, self.send.at[side, d, h], self.recv.at[side, d, h], expert=self.ring.mine).wait_recv()

    def hop(self, side, d, h):
        slot = d if side == 0 else self.ring.depth - d
        rows = self.rows(h)
        return remote(self.held(slot).at[rows], self.got(side, d - 1).at[rows], self.send.at[side, d, h],
                      self.recv.at[side, d - 1, h], expert=self.ring.right if side == 0 else self.ring.left)

    def push(self, side, d, h):
        ring = self.ring
        slot = d if side == 0 else ring.depth - d
        rows = self.rows(h)
        terms = [self.part(ring.dev(slot)).at[rows], self.pair_buf(slot).at[rows]]
        if self.comes(side, d, h):
            self.wait_got(side, d, h)
            terms.append(self.got(side, d).at[rows])
        add_rows(self.held(slot).at[rows], *terms)
        self.hop(side, d, h).start()

    def first(self):
        far = self.ring.far
        self.wait_pair(far)
        self.push(0, far, 0)
        self.push(1, far, 1)

    def early(self):
        for d in range(self.ring.far - 1, 0, -1):
            self.wait_pair(d)
            self.push(0, d, 1)
            self.wait_pair(self.ring.depth - d)
            self.push(1, d, 0)

    def late(self):
        for d in range(self.ring.far - 1, 0, -1):
            self.push(0, d, 0)
            self.push(1, d, 1)

    def last(self, out, *more):
        self.wait_pair(0)
        for h in range(2):
            rows = self.rows(h)
            terms = [self.part(self.ring.mine).at[rows], self.pair_buf(0).at[rows]] + [m.at[rows] for m in more]
            for side in range(2):
                if self.comes(side, 0, h):
                    self.wait_got(side, 0, h)
                    terms.append(self.got(side, 0).at[rows])
            add_rows(out.at[rows], *terms)

    def finish_sends(self):
        far = self.ring.far
        for side in range(2):
            for d in range(1, far + 1):
                for h in range(2):
                    if d < far or h == side:
                        self.hop(side, d, h).wait_send()
        for d in range(self.ring.depth):
            self.across(d).wait_send()


def views(bufs):
    pair_buf, held, got = bufs
    return (lambda d: pair_buf.at[d], lambda d: held.at[d], lambda side, d: got.at[side, d])


def grads_body(n_dp, n_exp, chunks, g_ref, out_ref, pair_buf, total, dp_buf, prefix, suffix, go_r, go_l, final, other,
               pair_send, pair_recv, dp_send, dp_recv, send_r, send_l, recv_r, recv_l, last_send, last_recv):
    me, mine = lax.axis_index("dp"), lax.axis_index("expert")
    core = lax.rem(mine, 2)
    z = lax.div(mine, 2)
    depth = n_exp // 2
    pair = mine + 1 - 2 * core
    has_left, has_right = z > 0, z < depth - 1
    orders = bit_orders(n_dp)
    rows = g_ref.shape[0] // n_dp
    half = rows // 2
    width = g_ref.shape[1] // chunks
    greet([(None, {"expert": pair})] + [(None, {"dp": me ^ bit}) for bit in orders[0]]
          + [(has_left, {"expert": mine - 2}), (has_right, {"expert": mine + 2})])

    def columns(i):
        return pl.ds(pl.multiple_of(i * width, 128), width)

    def block_of(d, side, i):
        return g_ref.at[pl.ds(pl.multiple_of(d * rows + side * half, 16), half), columns(i)]

    def across(i, d):
        return remote(block_of(d, 1 - core, i), pair_buf.at[i, d], pair_send.at[i, d], pair_recv.at[i, d], expert=pair)

    for i in range(chunks):
        for d in range(n_dp):
            across(i, d).start()

    def moved(i, j):
        order = orders[i % len(orders)]
        blocks = [0]
        for bit in order[j + 1 :]:
            blocks = blocks + [r | bit for r in blocks]
        return order[j], [r | order[j] for r in blocks]

    def dp_copy(i, j, r, bit):
        return remote(total.at[i, r], dp_buf.at[i, r ^ bit, j], dp_send.at[i, r], dp_recv.at[i, r ^ bit, j], dp=me ^ bit)

    stages = len(orders[0])
    for i in range(chunks):
        for r in range(n_dp - 1, -1, -1):
            d = me ^ r
            across(i, d).wait_recv()
            add_rows(total.at[i, r], block_of(d, core, i), pair_buf.at[i, d])
        if stages:
            bit, blocks = moved(i, 0)
            for r in blocks:
                dp_copy(i, 0, r, bit).start()
    for j in range(stages):
        for i in range(chunks):
            bit, blocks = moved(i, j)
            for r in blocks:
                kept = r ^ bit
                dp_copy(i, j, r, bit).wait_recv()
                add_rows(total.at[i, kept], total.at[i, kept], dp_buf.at[i, kept, j])
            if j + 1 < stages:
                bit, blocks = moved(i, j + 1)
                for r in blocks:
                    dp_copy(i, j + 1, r, bit).start()

    def right(i):
        return remote(go_r.at[i], prefix.at[i], send_r.at[i], recv_r.at[i], expert=mine + 2)

    def left(i):
        return remote(go_l.at[i], suffix.at[i], send_l.at[i], recv_l.at[i], expert=mine - 2)

    def line(t, carry):
        i = t - z

        @pl.when(jnp.logical_and(i >= 0, i < chunks))
        def _():
            @pl.when(has_left)
            def _():
                remote(go_r.at[i], prefix.at[i], send_r.at[i], recv_r.at[i], expert=mine).wait_recv()

            @pl.when(jnp.logical_and(has_left, has_right))
            def _():
                add_rows(go_r.at[i], total.at[i, 0], prefix.at[i])

            @pl.when(jnp.logical_not(has_left))
            def _():
                add_rows(go_r.at[i], total.at[i, 0])

            pl.when(has_right)(lambda: right(i).start())

        k = t - (depth - 1 - z)

        @pl.when(jnp.logical_and(k >= 0, k < chunks))
        def _():
            @pl.when(has_right)
            def _():
                remote(go_l.at[k], suffix.at[k], send_l.at[k], recv_l.at[k], expert=mine).wait_recv()

            @pl.when(jnp.logical_and(has_left, has_right))
            def _():
                add_rows(go_l.at[k], total.at[k, 0], suffix.at[k])

            @pl.when(jnp.logical_not(has_right))
            def _():
                add_rows(go_l.at[k], total.at[k, 0])

            pl.when(has_left)(lambda: left(k).start())

        return carry

    lax.fori_loop(0, chunks + depth - 1, line, 0)

    def last(i):
        return remote(final.at[i], other.at[i], last_send.at[i], last_recv.at[i], expert=pair)

    for i in range(chunks):
        @pl.when(jnp.logical_and(has_left, has_right))
        def _():
            add_rows(final.at[i], total.at[i, 0], prefix.at[i], suffix.at[i])

        @pl.when(jnp.logical_not(has_left))
        def _():
            add_rows(final.at[i], total.at[i, 0], suffix.at[i])

        @pl.when(jnp.logical_not(has_right))
        def _():
            add_rows(final.at[i], total.at[i, 0], prefix.at[i])

        last(i).start()

    def place(side, i):
        return out_ref.at[pl.ds(pl.multiple_of(side * half, 16), half), columns(i)]

    for i in range(chunks):
        add_rows(place(core, i), final.at[i])
    for i in range(chunks):
        last(i).wait_recv()
        add_rows(place(1 - core, i), other.at[i])
        last(i).wait_send()
        pl.when(has_right)(lambda: right(i).wait_send())
        pl.when(has_left)(lambda: left(i).wait_send())
        for d in range(n_dp):
            across(i, d).wait_send()
        for j in range(stages):
            bit, blocks = moved(i, j)
            for r in blocks:
                dp_copy(i, j, r, bit).wait_send()


def reduce_grads(n_dp, n_exp, grads, chunks, collective_id):
    rows = grads.shape[0] // n_dp
    half, width = rows // 2, grads.shape[1] // chunks
    stages = max(1, n_dp.bit_length() - 1)
    sem = pltpu.SemaphoreType.DMA
    one = pltpu.VMEM((chunks, half, width), grads.dtype)
    return pl.pallas_call(
        functools.partial(grads_body, n_dp, n_exp, chunks),
        out_shape=jax.ShapeDtypeStruct((rows, grads.shape[1]), jnp.float32),
        in_specs=[pl.BlockSpec(memory_space=VMEM)],
        out_specs=pl.BlockSpec(memory_space=VMEM),
        scratch_shapes=[
            pltpu.VMEM((chunks, n_dp, half, width), grads.dtype),
            pltpu.VMEM((chunks, n_dp, half, width), grads.dtype),
            pltpu.VMEM((chunks, n_dp, stages, half, width), grads.dtype),
            one, one, one, one, one, one,
            sem((chunks, n_dp)), sem((chunks, n_dp)), sem((chunks, n_dp)), sem((chunks, n_dp, stages)),
            sem((chunks,)), sem((chunks,)), sem((chunks,)), sem((chunks,)), sem((chunks,)), sem((chunks,)),
        ],
        compiler_params=pltpu.CompilerParams(
            collective_id=collective_id, has_side_effects=True, vmem_limit_bytes=56 * MIB),
        name="reduce_grads",
    )(grads)


SLOTS = 128
F32, LOW = jnp.float32, jnp.bfloat16


def dot(a, b, over_a=1, over_b=0):
    return lax.dot_general(a, b, (((over_a,), (over_b,)), ((), ())), preferred_element_type=F32)


def experts_body(n_dp, n_exp, hid_ref, gy_hbm, routes_t, routes_c, wr_t, w_in_hbm, w_out_hbm, middle,
                 block_out, hid_sum, gates_out, in_share, out_share,
                 x_all, w_in, w_out, sent, grows, gu, tmp, acts, stage, slots, gates, dots, wide,
                 pair_buf, held, got, *sems):
    w_sem, gy_sem, wide_sem, own_sem, ready, gate_send, gate_recv, dp_ready, dp_send, dp_recv = sems[:10]
    gather_sems, out_sems, hid_sems = sems[10:14], sems[14:18], sems[18:22]
    me = lax.axis_index("dp")
    local, _, width = sent.shape
    tree, hidden_units = hid_ref.shape[0], w_out.shape[1]
    rows_e = local * SLOTS
    ring = Ring(n_exp)
    mine, core, depth = ring.mine, ring.core, ring.depth
    first = mine * local
    peers = [lax.rem(mine + k, n_exp) for k in range(1, n_exp)]
    greet([(None, {"expert": e}) for e in peers] + [(None, {"dp": me ^ bit}) for bit in (1, 2)])

    weights = [pltpu.make_async_copy(w_in_hbm, w_in, w_sem.at[0]), pltpu.make_async_copy(w_out_hbm, w_out, w_sem.at[1])]
    gather = RingGather(ring, hid_ref, x_all, gather_sems)
    gather.start()
    for copy in weights:
        copy.start()
    own = pltpu.make_async_copy(hid_ref, x_all.at[mine], own_sem)
    own.start()

    def gy_buf(j):
        return stage.at[lax.rem(j, 2), pl.ds(0, tree)]

    def gy_copy(j):
        return pltpu.make_async_copy(gy_hbm.at[j], gy_buf(j), gy_sem.at[lax.rem(j, 2)])

    gy_copy(0).start()

    below = (lax.broadcasted_iota(jnp.int32, (tree, tree), 0) < lax.broadcasted_iota(jnp.int32, (tree, tree), 1)).astype(LOW)
    sub16 = lax.broadcasted_iota(jnp.int32, (16, tree), 0)

    def find_slots(j, carry):
        names = routes_t[j]
        chosen = jnp.zeros((16, tree), F32)
        for k in range(names.shape[0]):
            chosen = jnp.maximum(chosen, jnp.where(names[k : k + 1, :] == first + sub16, 1.0, 0.0))
        chosen = jnp.where(sub16 < local, chosen, 0.0)
        rank = dot(chosen.astype(LOW), below)
        slots[j] = jnp.where(chosen > 0.5, rank, -1.0)[:8]
        return carry

    lax.fori_loop(0, n_exp, find_slots, 0)

    slot_ids = lax.broadcasted_iota(jnp.int32, (SLOTS, tree), 0).astype(F32)

    def places(j):
        return jnp.concatenate(
            [jnp.where(slot_ids == slots[j, i : i + 1, :], 1.0, 0.0).astype(LOW) for i in range(local)], axis=0)

    def places_t(j):
        names = routes_c[j]
        lane = lax.broadcasted_iota(jnp.int32, (tree, 128), 1)
        chosen = jnp.zeros((tree, 128), F32)
        for k in range(names.shape[1]):
            chosen = jnp.maximum(chosen, jnp.where(names[:, k : k + 1] == first + lane, 1.0, 0.0))
        chosen = jnp.where(lane < local, chosen, 0.0)
        above = (lax.broadcasted_iota(jnp.int32, (tree, tree), 1) < lax.broadcasted_iota(jnp.int32, (tree, tree), 0)).astype(LOW)
        slot = jnp.where(chosen > 0.5, dot(above, chosen.astype(LOW)), -1.0)
        lanes = lane.astype(F32)
        return jnp.concatenate(
            [jnp.where(lanes == slot[:, i : i + 1], 1.0, 0.0).astype(LOW) for i in range(local)], axis=1)

    def find_gates(j):
        names = routes_t[j]
        experts = lax.broadcasted_iota(jnp.int32, (EXPERTS, tree), 0)
        chosen = jnp.zeros((EXPERTS, tree), F32)
        for k in range(names.shape[0]):
            chosen = jnp.maximum(chosen, jnp.where(names[k : k + 1, :] == experts, 1.0, 0.0))
        logits = jnp.where(chosen > 0.5, dot(wr_t[...], x_all[j], 1, 1), -1e30)
        powers = jnp.exp(logits - jnp.max(logits, axis=0, keepdims=True))
        share = powers / jnp.sum(powers, axis=0, keepdims=True)
        sub = lax.broadcasted_iota(jnp.int32, (8, tree), 0)
        own_gates = jnp.zeros((8, tree), F32)
        for i in range(local):
            row = jnp.sum(jnp.where(experts == first + i, share, 0.0), axis=0, keepdims=True)
            own_gates = jnp.where(sub == i, row, own_gates)
        gates[j] = own_gates

    halves = width // 512

    def dispatch(j, src, dest):
        place = places(j)

        def body(n, carry):
            cols = pl.ds(pl.multiple_of(n * 512, 512), 512)
            picked = dot(place, src[:, cols]).astype(LOW)
            for i in range(local):
                dest[i, pl.ds(pl.multiple_of(j * SLOTS, SLOTS), SLOTS), cols] = picked[i * SLOTS : (i + 1) * SLOTS]
            return carry

        lax.fori_loop(0, halves, body, 0)

    def slot_gate(j, e):
        return jnp.sum(jnp.where(slot_ids == slots[j, pl.ds(e, 1), :], gates[j, pl.ds(e, 1), :], 0.0), axis=1, keepdims=True)

    def forward(chip):
        pair_rows = pl.ds(pl.multiple_of(chip * 2 * SLOTS, 2 * SLOTS), 2 * SLOTS)

        def one_tree(q, carry):
            j = 2 * chip + q
            find_gates(j)
            dispatch(j, x_all.at[j], sent)
            return carry

        lax.fori_loop(0, 2, one_tree, 0)

        def one_expert(e, carry):
            both = dot(sent[e, pair_rows, :], w_in[e])
            gu[e, pair_rows, :] = both.astype(LOW)
            a, b = both[:, :hidden_units], both[:, hidden_units:]
            act = (a / (1.0 + jnp.exp(-a)) * b).astype(LOW).astype(F32)
            gate = jnp.concatenate([slot_gate(2 * chip, e), slot_gate(2 * chip + 1, e)], axis=0)
            made = dot((act * gate).astype(LOW), w_out[e]).astype(LOW)
            for q in range(2):
                tmp[pl.ds(pl.multiple_of(q * rows_e + e * SLOTS, SLOTS), SLOTS), :] = made[q * SLOTS : (q + 1) * SLOTS]
            return carry

        lax.fori_loop(0, local, one_expert, 0)

    def combine_out(chip):
        def one_tree(q, carry):
            j = 2 * chip + q
            rows = pl.ds(pl.multiple_of(q * rows_e, rows_e), rows_e)
            x_all[j] = dot(places_t(j), tmp[rows, :]).astype(LOW)
            return carry

        lax.fori_loop(0, 2, one_tree, 0)

    def grad_rows(j, carry):
        pl.when(j + 1 < n_exp)(lambda: gy_copy(j + 1).start())
        gy_copy(j).wait()
        dispatch(j, gy_buf(j), grows)
        return carry

    events = gather.events()
    out = RingScatter(ring, lambda e: x_all.at[e], views((pair_buf, held, got)), out_sems)

    def chip_at(d):
        return lax.rem(ring.z + d, depth)

    def group(g, carry):
        d = jnp.where(g == 0, 0, jnp.where(g == 1, depth - 1, jnp.where(g == 2, 1, 2)))
        chip = chip_at(d)

        @pl.when(g == 0)
        def _():
            own.wait()
            gather.wait_pair(0, 0)
            gather.wait_pair(0, 1)
            for copy in weights:
                copy.wait()

        @pl.when(g == 1)
        def _():
            for event in events[:4]:
                gather.handle(event)
            gather.wait_pair(-1, 0)
            gather.wait_pair(-1, 1)

        @pl.when(g == 2)
        def _():
            gather.wait_pair(1, 0)
            gather.wait_pair(1, 1)

        @pl.when(g == 3)
        def _():
            for event in events[4:]:
                gather.handle(event)
            gather.wait_pair(2, 0)
            gather.wait_pair(2, 1)

        forward(chip)

        @pl.when(g == 0)
        def _():
            gather.finish_own()
            lax.fori_loop(0, n_exp, grad_rows, 0)

        for at, d in ((1, -1), (2, 1), (3, 2)):
            @pl.when(g == at)
            def _():
                for event in events:
                    if event[1] == abs(d) and (abs(d) == 2 or (event[0] == 0) == (d < 0)):
                        gather.finish_event(event)

        combine_out(chip)
        pl.when(g == 0)(lambda: out.start_pair(0))
        pl.when(g == 1)(lambda: out.start_pair(depth - 1))
        pl.when(g == 2)(lambda: out.start_pair(1))
        pl.when(g == 3)(lambda: out.start_pair(2))
        return carry

    lax.fori_loop(0, depth, group, 0)
    out.first()
    out.early()

    in_rows, out_rows = width // n_dp, hidden_units // n_dp
    cut = (in_rows + out_rows) // 2

    def grad_half(e, r, h):
        at = 2 * r + h
        return gu.at[e, pl.ds(at * cut, cut)] if at < 5 else stage.at[e, pl.ds((at - 5) * cut, cut)]

    def grad_land(e, k):
        return w_in.at[e, pl.ds(k * cut, cut)] if k < 5 else w_out.at[e, pl.ds(0, cut)]

    def grad_hop(e, step, h, which):
        bit = (1, 2)[h] if step == 0 else (2, 1)[h]
        r = bit if which == 0 else 3
        k = 2 * h + which if step == 0 else 4 + h
        return remote(grad_half(e, r, h), grad_land(e, k), dp_send.at[e, k], dp_recv.at[e, k], dp=me ^ bit)

    def grads_start(e):
        pl.semaphore_wait(dp_ready.at[e], 2)
        for which in (1, 0):
            for h in range(2):
                grad_hop(e, 0, h, which).start()

    def grads_turn(e):
        for which in (1, 0):
            for h in range(2):
                grad_hop(e, 0, h, which).wait_recv()
                kept = 0 if which == 0 else (2, 1)[h]
                add_rows(grad_half(e, kept, h), grad_half(e, kept, h), grad_land(e, 2 * h + which))
                if which == 1:
                    grad_hop(e, 1, h, 0).start()

    def wide_copies(e):
        return (
            pltpu.make_async_copy(wide.at[pl.ds(0, in_rows)], in_share.at[e], wide_sem.at[0]),
            pltpu.make_async_copy(wide.at[pl.ds(in_rows, out_rows)], out_share.at[e], wide_sem.at[1]),
        )

    def grads_end(e):
        for h in range(2):
            grad_hop(e, 1, h, 0).wait_recv()
            add_rows(wide.at[pl.ds(h * cut, cut)], grad_half(e, 0, h), grad_land(e, 4 + h))
        for copy in wide_copies(e):
            copy.start()
        for step, h, which in ((0, 0, 0), (0, 0, 1), (0, 1, 0), (0, 1, 1), (1, 0, 0), (1, 1, 0)):
            grad_hop(e, step, h, which).wait_send()
        for copy in wide_copies(e):
            copy.wait()

    block = 4 * SLOTS
    sub8 = lax.broadcasted_iota(jnp.int32, (8, tree), 0)

    def backward(e, carry):
        def one_block(m, inner):
            rows = pl.ds(pl.multiple_of(m * block, block), block)
            grad_act = dot(grows[e, rows, :], w_out[e], 1, 1)
            a = gu[e, rows, pl.ds(0, hidden_units)].astype(F32)
            b = gu[e, rows, pl.ds(hidden_units, hidden_units)].astype(F32)
            sg = 1.0 / (1.0 + jnp.exp(-a))
            sw = a * sg
            act = (sw * b).astype(LOW).astype(F32)
            gate = jnp.concatenate([slot_gate(4 * m + q, e) for q in range(4)], axis=0)
            told = jnp.sum(act * grad_act, axis=1, keepdims=True)
            acts[rows, :] = (act * gate).astype(LOW)
            grad_act = grad_act * gate
            tmp[rows, pl.ds(0, hidden_units)] = (grad_act * b * sg * (1.0 + a * (1.0 - sg))).astype(LOW)
            tmp[rows, pl.ds(hidden_units, hidden_units)] = (grad_act * sw).astype(LOW)
            for q in range(4):
                j = 4 * m + q
                row = jnp.sum(
                    jnp.where(slot_ids == slots[j, pl.ds(e, 1), :], told[q * SLOTS : (q + 1) * SLOTS], 0.0),
                    axis=0, keepdims=True)
                dots[j] = jnp.where(sub8 == e, row, dots[j])
            return inner

        lax.fori_loop(0, n_exp // 4, one_block, 0)
        pl.when(e > 0)(lambda: grads_start(e - 1))
        for r in range(n_dp):
            d = me ^ r
            grad_in = dot(sent[e, :, pl.ds(pl.multiple_of(d * in_rows, in_rows), in_rows)], tmp[...], 0, 0).astype(LOW)
            grad_out = dot(acts[:, pl.ds(pl.multiple_of(d * out_rows, out_rows), out_rows)], grows[e], 0, 0).astype(LOW)
            grad_half(e, r, 0)[...] = grad_in[:cut]
            half = grad_half(e, r, 1)
            half[pl.ds(0, in_rows - cut), :] = grad_in[cut:]
            half[pl.ds(in_rows - cut, out_rows), :] = grad_out

        def back_half(m, inner):
            rows = pl.ds(pl.multiple_of(m * 512, 512), 512)
            sent[e, rows, :] = dot(tmp[rows, :], w_in[e], 1, 1).astype(LOW)
            return inner

        lax.fori_loop(0, n_exp * SLOTS // 512, back_half, 0)
        for bit in (1, 2):
            pl.semaphore_signal(dp_ready.at[e], inc=1, device_id={"dp": me ^ bit}, device_id_type=MESH)
        pl.when(e == local // 2 - 1)(out.late)
        pl.when(e >= 2)(lambda: grads_turn(e - 2))
        return carry

    dots[...] = jnp.zeros(dots.shape, F32)
    middle_copy = pltpu.make_async_copy(middle, wide.at[pl.ds(0, tree)], wide_sem.at[0])
    middle_copy.start()
    lax.fori_loop(0, local, backward, 0)
    grads_start(local - 1)

    gate_copies = []
    for k, e in enumerate(peers):
        copy = remote(dots.at[e], gates_out.at[mine], gate_send.at[k], gate_recv.at[k], expert=e)
        copy.start()
        gate_copies.append(copy)
    gates_out[mine] = dots[mine]
    middle_copy.wait()
    out.last(block_out, wide.at[pl.ds(0, tree)])
    out.finish_sends()
    for partner in (ring.pair, ring.right, ring.left):
        pl.semaphore_signal(ready, inc=1, device_id={"expert": partner}, device_id_type=MESH)
    hid = RingScatter(ring, lambda e: x_all.at[e], views((pair_buf, held, got)), hid_sems)

    def combine_hid(g, carry):
        d = jnp.where(g == 0, 2, jnp.where(g == 1, 1, jnp.where(g == 2, depth - 1, 0)))
        chip = chip_at(d)

        def one_tree(q, inner):
            j = 2 * chip + q
            rows = pl.ds(pl.multiple_of(j * SLOTS, SLOTS), SLOTS)
            made = jnp.concatenate([sent[i, rows, :] for i in range(local)], axis=0)
            x_all[j] = dot(places_t(j), made).astype(LOW)
            return inner

        lax.fori_loop(0, 2, one_tree, 0)

        @pl.when(g == 0)
        def _():
            pl.semaphore_wait(ready, 3)
            hid.start_pair(2)

        pl.when(g == 1)(lambda: hid.start_pair(1))
        pl.when(g == 2)(lambda: hid.start_pair(depth - 1))
        pl.when(g == 3)(lambda: hid.start_pair(0))
        pl.when(g == 1)(hid.first)
        return carry

    lax.fori_loop(0, depth, combine_hid, 0)
    hid.early()
    grads_turn(local - 2)
    grads_end(0)
    hid.late()
    grads_end(1)
    grads_turn(local - 1)
    hid.last(wide.at[pl.ds(0, tree)])
    hid_copy = pltpu.make_async_copy(wide.at[pl.ds(0, tree)], hid_sum, wide_sem.at[0])
    hid_copy.start()
    hid_copy.wait()
    for e in range(2, local):
        grads_end(e)

    for k, copy in enumerate(gate_copies):
        copy.wait_send()
        source = lax.rem(mine + n_exp - 1 - k, n_exp)
        remote(dots.at[mine], gates_out.at[source], gate_send.at[k], gate_recv.at[k], expert=mine).wait_recv()
    hid.finish_sends()


def experts(n_dp, n_exp, hidden2, grad_y, routes_all, router, expert_in, expert_out, middle, collective_id):
    local, width, both = expert_in.shape
    units = expert_out.shape[1]
    tree = hidden2.shape[0]
    rows = n_exp * SLOTS
    sem = pltpu.SemaphoreType.DMA
    bufs, out_sems = RingScatter.scratch(n_exp, (tree, width), LOW)
    _, hid_sems = RingScatter.scratch(n_exp, (tree, width), LOW)
    shape = jax.ShapeDtypeStruct
    return pl.pallas_call(
        functools.partial(experts_body, n_dp, n_exp),
        out_shape=[
            shape((tree, width), LOW),
            shape((tree, width), F32),
            shape((n_exp, 8, tree), F32),
            shape((local, width // n_dp, width), F32),
            shape((local, units // n_dp, width), F32),
        ],
        in_specs=[pl.BlockSpec(memory_space=s) for s in (VMEM, ANY, VMEM, VMEM, VMEM, ANY, ANY, ANY)],
        out_specs=[pl.BlockSpec(memory_space=s) for s in (VMEM, ANY, VMEM, ANY, ANY)],
        scratch_shapes=[
            pltpu.VMEM((n_exp, tree, width), LOW),
            pltpu.VMEM((local, width, both), LOW),
            pltpu.VMEM((local, units, width), LOW),
            pltpu.VMEM((local, rows, width), LOW),
            pltpu.VMEM((local, rows, width), LOW),
            pltpu.VMEM((local, rows, both), LOW),
            pltpu.VMEM((max(rows, 2 * local * SLOTS), width), LOW),
            pltpu.VMEM((rows, units), LOW),
            pltpu.VMEM((local, 3 * (width + units) // (2 * n_dp), width), LOW),
            pltpu.VMEM((n_exp, 8, tree), F32),
            pltpu.VMEM((n_exp, 8, tree), F32),
            pltpu.VMEM((n_exp, 8, tree), F32),
            pltpu.VMEM(((width + units) // n_dp, width), F32),
            *bufs,
            sem((2,)), sem((2,)), sem((2,)), sem, pltpu.SemaphoreType.REGULAR, sem((n_exp - 1,)), sem((n_exp - 1,)),
            pltpu.SemaphoreType.REGULAR((local,)), sem((local, 6)), sem((local, 6)),
            *RingGather.scratch(n_exp), *out_sems, *hid_sems,
        ],
        compiler_params=pltpu.CompilerParams(
            collective_id=collective_id, has_side_effects=True, vmem_limit_bytes=63 * MIB),
        name="experts",
    )(hidden2, grad_y, routes_all.transpose(0, 2, 1), routes_all, router.T, expert_in, expert_out, middle)


def tree_layout(tree_rows):
    unit_rows = tree_rows // 20
    row_index = jnp.arange(tree_rows, dtype=jnp.int32)
    segment = jnp.where(
        row_index < 8 * unit_rows,
        0,
        jnp.where(
            row_index < 12 * unit_rows,
            1 + (row_index - 8 * unit_rows) // unit_rows,
            5 + (row_index - 12 * unit_rows) // unit_rows,
        ),
    )
    depth_start = jnp.where(segment == 0, 0, jnp.where(segment < 5, 8 * unit_rows, 9 * unit_rows))
    seg_start = jnp.where(
        segment == 0,
        0,
        jnp.where(
            segment < 5,
            8 * unit_rows + (segment - 1) * unit_rows,
            12 * unit_rows + (segment - 5) * unit_rows,
        ),
    )
    position = depth_start + row_index - seg_start
    return (segment, position)


def path_allowed(parent_row, segment):
    segment_ids = jnp.arange(parent_row.shape[0], dtype=jnp.int32)
    grandparent = parent_row[parent_row]
    on_path = (
        (segment_ids[None, :] == segment_ids[:, None])
        | (segment_ids[None, :] == parent_row[:, None])
        | (segment_ids[None, :] == grandparent[:, None])
    ).astype(jnp.float32)
    seg_hot = (segment[:, None] == segment_ids[None, :]).astype(jnp.float32)
    reach = jnp.dot(
        jnp.dot(seg_hot, on_path, precision=lax.Precision.HIGHEST),
        seg_hot.T,
        precision=lax.Precision.HIGHEST,
    )
    row_index = jnp.arange(segment.shape[0], dtype=jnp.int32)
    return (reach > 0.5) & (row_index[None, :] <= row_index[:, None])


def rope_tables(position):
    frequency = 10000.0 ** (-jnp.arange(0, HD, 2, dtype=jnp.float32) / HD)
    angles = position.astype(jnp.float32)[:, None] * frequency[None, :]
    return (jnp.concatenate([jnp.cos(angles)] * 2, -1), jnp.concatenate([jnp.sin(angles)] * 2, -1))


def turn_half(field):
    half_width = field.shape[-1] // 2
    return jnp.concatenate([-field[..., half_width:], field[..., :half_width]], axis=-1)


def rotary(field, cosine, sine_table):
    return field * cosine + turn_half(field) * sine_table


def unrotate(grad_field, cosine, sine_table):
    return grad_field * cosine - turn_half(grad_field * sine_table)


def rms_norm(field, gain_vector):
    return (
        field * lax.rsqrt(jnp.mean(field * field, axis=-1, keepdims=True) + EPSILON) * gain_vector
    )


def gated_unit(gate_up):
    width_ff = gate_up.shape[-1] // 2
    gate_part = gate_up[..., :width_ff]
    return gate_part / (1.0 + jnp.exp(-gate_part)) * gate_up[..., width_ff:]


def experts_plain(
    n_dp, n_exp, hidden2, grad_y, routes_all, router_full, expert_in, expert_out, middle, collective_id
):
    tree_rows, width = hidden2.shape
    capacity = CAP
    expert_ids = jnp.arange(EXPERTS, dtype=jnp.int32)
    here = lax.axis_index("expert")
    local = expert_in.shape[0]
    first = here * local
    hidden_all = lax.all_gather(hidden2, "expert", axis=0, tiled=False)
    own_ids = first + jnp.arange(local, dtype=jnp.int32)
    hot_all = routes_all[:, :, :, None] == expert_ids[None, None, None, :]
    chosen_all = jnp.any(hot_all, axis=2)
    chosen = jnp.any(routes_all[:, :, :, None] == own_ids[None, None, None, :], axis=2)
    lower = jnp.tril(jnp.ones((tree_rows, tree_rows), jnp.bfloat16), -1)
    rank = jnp.einsum(
        "tu,jue->jet", lower, chosen.astype(jnp.bfloat16), preferred_element_type=jnp.float32
    ).astype(jnp.int32)
    slots = jnp.arange(capacity, dtype=jnp.int32)
    chosen_t = chosen.transpose(0, 2, 1)
    place = (rank[:, :, None, :] == slots[None, None, :, None]) & chosen_t[:, :, None, :]
    place = place.astype(jnp.bfloat16)
    logits_all = jnp.einsum(
        "jtd,de->jte", hidden_all, router_full, preferred_element_type=jnp.float32
    )
    masked = jnp.where(chosen_all, logits_all, -1e30)
    weight = jnp.exp(masked - jnp.max(masked, axis=-1, keepdims=True))
    weight = weight / jnp.sum(weight, axis=-1, keepdims=True)
    gates_own = lax.dynamic_slice_in_dim(weight, first, local, axis=2)
    gate_slot = jnp.einsum(
        "jest,jte->ejs", place.astype(jnp.float32), gates_own, precision=lax.Precision.HIGHEST
    )[..., None]
    sent = jnp.einsum("jest,jtd->ejsd", place, hidden_all, preferred_element_type=jnp.float32)
    sent = sent.astype(jnp.bfloat16)
    grad_rows = jnp.einsum("jest,jtd->ejsd", place, grad_y, preferred_element_type=jnp.float32)
    grad_rows = grad_rows.astype(jnp.bfloat16)
    gate_up = jnp.einsum("ejsd,edf->ejsf", sent, expert_in, preferred_element_type=jnp.float32)
    activated, glu_back = jax.vjp(gated_unit, gate_up)
    act_low = activated.astype(jnp.bfloat16).astype(jnp.float32)
    act_scaled = (act_low * gate_slot).astype(jnp.bfloat16)
    made = jnp.einsum(
        "ejsf,efd->ejsd", act_scaled, expert_out, preferred_element_type=jnp.float32
    ).astype(jnp.bfloat16)
    out_part = jnp.einsum("jest,ejsd->jtd", place, made, preferred_element_type=jnp.float32)
    out_sum = lax.psum_scatter(
        out_part.astype(jnp.bfloat16), "expert", scatter_dimension=0, tiled=False
    ).astype(jnp.float32)
    result = middle + out_sum
    block_out = result.astype(jnp.bfloat16)
    grad_act = jnp.einsum(
        "ejsd,efd->ejsf", grad_rows, expert_out, preferred_element_type=jnp.float32
    )
    gate_dot = jnp.sum(act_low * grad_act, axis=-1)
    gates_back = jnp.einsum(
        "jest,ejs->jte", place.astype(jnp.float32), gate_dot, precision=lax.Precision.HIGHEST
    )
    grad_out_w = jnp.einsum(
        "ejsf,ejsd->efd", act_scaled, grad_rows, preferred_element_type=jnp.float32
    )
    grad_gate_up = glu_back(grad_act * gate_slot)[0].astype(jnp.bfloat16)
    grad_sent = jnp.einsum(
        "ejsf,edf->ejsd", grad_gate_up, expert_in, preferred_element_type=jnp.float32
    ).astype(jnp.bfloat16)
    grad_in_w = jnp.einsum(
        "ejsd,ejsf->edf", sent, grad_gate_up, preferred_element_type=jnp.float32
    )
    hid_part = jnp.einsum("jest,ejsd->jtd", place, grad_sent, preferred_element_type=jnp.float32)
    gates_mine = lax.all_to_all(gates_back, "expert", split_axis=0, concat_axis=2, tiled=True)[0]
    hid_sum = lax.psum_scatter(
        hid_part.astype(jnp.bfloat16), "expert", scatter_dimension=0, tiled=False
    ).astype(jnp.float32)
    local, units = expert_in.shape[0], expert_out.shape[1]
    low = jnp.bfloat16
    grads = jnp.concatenate(
        [
            grad_in_w.astype(low).reshape(local, n_dp, width // n_dp, width),
            grad_out_w.astype(low).reshape(local, n_dp, units // n_dp, width),
        ],
        axis=2,
    ).reshape(local, width + units, width)
    share = lax.psum_scatter(grads, "dp", scatter_dimension=1, tiled=True).astype(jnp.float32)
    gates_mine = gates_mine.T.reshape(n_exp, local, tree_rows)
    return block_out, hid_sum, gates_mine, share[:, : width // n_dp], share[:, width // n_dp :]


def shards(
    tokens,
    attn_gain,
    w_query,
    w_keyval,
    w_output,
    moe_gain,
    w_router,
    expert_in,
    expert_out,
    cotangent,
    routes,
    parents,
):
    tree_rows = tokens.shape[0]
    width = tokens.shape[1]
    capacity = CAP
    groups = H // KV
    kv_width = KV * HD
    score_scale = HD ** (-0.5)
    n_dp, n_exp = lax.axis_size("dp"), lax.axis_size("expert")
    grad_y = lax.all_gather(cotangent, "expert", axis=0, tiled=False)
    routes_all = lax.all_gather(routes, "expert", axis=0, tiled=False)
    rows = w_query.shape[0]
    small = jnp.concatenate(
        [w_router, attn_gain[:, None], moe_gain[:, None], jnp.zeros((rows, 128 - EXPERTS - 2), w_router.dtype)], axis=1
    )
    query_full, keyval_full, output_full, small_full = gather_weights(
        n_dp, (w_query, w_keyval, w_output, small), 1
    )
    router_full = small_full[:, :EXPERTS]
    gain_first, gain_second = small_full[:, EXPERTS], small_full[:, EXPERTS + 1]
    inputs = tokens.astype(jnp.float32)
    segment, position = tree_layout(tree_rows)
    allowed = path_allowed(parents[0], segment)
    cosine, sine_table = rope_tables(position)
    cos_four, sin_four = (cosine[:, None, None, :], sine_table[:, None, None, :])
    cos_three, sin_three = (cosine[:, None, :], sine_table[:, None, :])
    normed, first_back = jax.vjp(rms_norm, inputs, gain_first.astype(jnp.float32))
    hidden = normed.astype(jnp.bfloat16)
    query_pre = jnp.dot(hidden, query_full, preferred_element_type=jnp.float32)
    keyval_pre = jnp.dot(hidden, keyval_full, preferred_element_type=jnp.float32)
    queries = rotary(query_pre.reshape(tree_rows, KV, groups, HD), cos_four, sin_four).astype(
        jnp.bfloat16
    )
    key_heads = rotary(
        keyval_pre[:, :kv_width].reshape(tree_rows, KV, HD), cos_three, sin_three
    ).astype(jnp.bfloat16)
    values = keyval_pre[:, kv_width:].reshape(tree_rows, KV, HD).astype(jnp.bfloat16)

    def score_block():
        raw_scores = (
            jnp.einsum("tkgd,skd->kgts", queries, key_heads, preferred_element_type=jnp.float32)
            * score_scale
        )
        return jnp.where(allowed, raw_scores, -1e30)

    scores = score_block()
    row_max = jnp.max(scores, axis=-1, keepdims=True)
    exp_scores = jnp.exp(scores - row_max)
    row_total = jnp.sum(exp_scores, axis=-1, keepdims=True)
    log_total = row_max + jnp.log(row_total)
    attn_low = (exp_scores / row_total).astype(jnp.bfloat16)
    attended = jnp.einsum("kgts,skd->tkgd", attn_low, values, preferred_element_type=jnp.float32)
    attended = attended.reshape(tree_rows, H * HD).astype(jnp.bfloat16)
    middle = inputs + jnp.dot(attended, output_full, preferred_element_type=jnp.float32)
    normed2, second_back = jax.vjp(rms_norm, middle, gain_second.astype(jnp.float32))
    hidden2 = normed2.astype(jnp.bfloat16)
    logits = jnp.dot(hidden2, router_full, preferred_element_type=jnp.float32)
    expert_ids = jnp.arange(EXPERTS, dtype=jnp.int32)
    route_hot = (routes[:, :, None] == expert_ids[None, None, :]).astype(jnp.float32)
    picked = jnp.sum(route_hot * logits[:, None, :], axis=2)
    picked_exp = jnp.exp(picked - jnp.max(picked, axis=1, keepdims=True))
    gate_weights = picked_exp / jnp.sum(picked_exp, axis=1, keepdims=True)
    run_experts = experts if (n_dp, n_exp) == (4, 8) else experts_plain
    block_out, hid_sum, gates_mine, expert_in_share, expert_out_share = run_experts(
        n_dp, n_exp, hidden2, grad_y, routes_all, router_full, expert_in, expert_out, middle, 2
    )
    gates_mine = gates_mine[:, : expert_in.shape[0]].reshape(EXPERTS, tree_rows).T
    grad_result = cotangent.astype(jnp.float32)
    gate_dense = jnp.sum(route_hot * gate_weights[:, :, None], axis=1)
    grad_logits = (
        gate_dense
        * (gates_mine - jnp.sum(gate_dense * gates_mine, axis=1, keepdims=True))
    ).astype(jnp.bfloat16)
    grad_router = jnp.einsum("td,te->de", hidden2, grad_logits, preferred_element_type=jnp.float32)
    grad_hidden2 = hid_sum + jnp.einsum(
        "te,de->td", grad_logits, router_full, preferred_element_type=jnp.float32
    )
    grad_mid_norm, grad_gain_second = second_back(grad_hidden2)
    grad_middle = grad_result + grad_mid_norm
    grad_branch = grad_middle.astype(jnp.bfloat16)
    grad_w_out = jnp.einsum("ti,td->id", attended, grad_branch, preferred_element_type=jnp.float32)
    grad_attended = jnp.einsum(
        "td,id->ti", grad_branch, output_full, preferred_element_type=jnp.float32
    )
    grad_attended = grad_attended.astype(jnp.bfloat16).reshape(tree_rows, KV, groups, HD)
    attn_probs = jnp.exp(score_block() - log_total)
    probs_low = attn_probs.astype(jnp.bfloat16)
    grad_values = jnp.einsum(
        "kgts,tkgd->skd", probs_low, grad_attended, preferred_element_type=jnp.float32
    )
    grad_probs = jnp.einsum(
        "tkgd,skd->kgts", grad_attended, values, preferred_element_type=jnp.float32
    )
    grad_scores = (
        attn_probs * (grad_probs - jnp.sum(attn_probs * grad_probs, axis=-1, keepdims=True))
    ).astype(jnp.bfloat16)
    grad_query_rot = (
        jnp.einsum("kgts,skd->tkgd", grad_scores, key_heads, preferred_element_type=jnp.float32)
        * score_scale
    )
    grad_keys_rot = (
        jnp.einsum("kgts,tkgd->skd", grad_scores, queries, preferred_element_type=jnp.float32)
        * score_scale
    )
    grad_query_pre = (
        unrotate(grad_query_rot, cos_four, sin_four).reshape(tree_rows, H * HD).astype(jnp.bfloat16)
    )
    grad_keyval_pre = jnp.concatenate(
        [
            unrotate(grad_keys_rot, cos_three, sin_three).reshape(tree_rows, kv_width),
            grad_values.reshape(tree_rows, kv_width),
        ],
        axis=1,
    ).astype(jnp.bfloat16)
    grad_w_q = jnp.einsum("td,ti->di", hidden, grad_query_pre, preferred_element_type=jnp.float32)
    grad_w_kv = jnp.einsum("td,ti->di", hidden, grad_keyval_pre, preferred_element_type=jnp.float32)
    grad_hidden = jnp.einsum(
        "ti,di->td", grad_query_pre, query_full, preferred_element_type=jnp.float32
    ) + jnp.einsum("ti,di->td", grad_keyval_pre, keyval_full, preferred_element_type=jnp.float32)
    grad_in_norm, grad_gain_first = first_back(grad_hidden)
    input_grad = grad_middle + grad_in_norm
    low = jnp.bfloat16
    share = reduce_grads(
        n_dp,
        n_exp,
        jnp.concatenate(
            [
                grad_w_q.astype(low),
                grad_w_kv.astype(low),
                grad_w_out.astype(low),
                grad_router.astype(low),
                grad_gain_first.astype(low)[:, None],
                grad_gain_second.astype(low)[:, None],
                jnp.zeros((width, 128 - EXPERTS - 2), low),
            ],
            axis=1,
        ),
        5,
        5,
    )
    at = 3 * width
    shares = (
        share[:, at + EXPERTS],
        share[:, :width],
        share[:, width : 2 * width],
        share[:, 2 * width : at],
        share[:, at + EXPERTS + 1],
        share[:, at : at + EXPERTS],
    )
    return (
        block_out,
        input_grad,
        shares[0],
        shares[1],
        shares[2],
        shares[3],
        shares[4],
        shares[5],
        expert_in_share,
        expert_out_share,
    )


def solution(mesh):
    in_specs = (
        P(("dp", "expert"), None),
        P("dp"),
        P("dp", None),
        P("dp", None),
        P("dp", None),
        P("dp"),
        P("dp", None),
        P("expert", None, None),
        P("expert", None, None),
        P(("dp", "expert"), None),
        P(("dp", "expert"), None),
        P(("dp", "expert"), None),
    )
    out_specs = (
        P(("dp", "expert"), None),
        P(("dp", "expert"), None),
        P("dp"),
        P("dp", None),
        P("dp", None),
        P("dp", None),
        P("dp"),
        P("dp", None),
        P("expert", "dp", None),
        P("expert", "dp", None),
    )
    return jax.shard_map(shards, mesh=mesh, in_specs=in_specs, out_specs=out_specs, check_vma=False)
```

```python
import functools

import jax
import jax.numpy as jnp
from jax import lax
from jax.experimental import pallas as pl
from jax.experimental.pallas import tpu as pltpu
from jax.sharding import PartitionSpec as P

H = 16
KV = 8
HD = 64
EXPERTS = 32
TOPK = 8
CAP = 120


EPSILON = 1e-06


MESH = pl.DeviceIdType.MESH
MIB = 1024 * 1024
VMEM = pltpu.VMEM
ANY = pl.ANY


def remote(src, dst, send_sem, recv_sem, **where):
    return pltpu.make_async_remote_copy(
        src_ref=src, dst_ref=dst, send_sem=send_sem, recv_sem=recv_sem,
        device_id=where, device_id_type=MESH,
    )


def greet(partners):
    barrier = pltpu.get_barrier_semaphore()
    for condition, where in partners:
        def signal(where=where):
            pl.semaphore_signal(barrier, inc=1, device_id=where, device_id_type=MESH)
        if condition is None:
            signal()
        else:
            pl.when(condition)(signal)
    count = sum(1 if c is None else c.astype(jnp.int32) for c, _ in partners)
    pl.semaphore_wait(barrier, count)


def add_rows(out, *terms, step=16):
    rows = out.shape[0]

    def body(i, carry):
        at = pl.ds(pl.multiple_of(i * step, step), step)
        total = terms[0][at, :].astype(jnp.float32)
        for term in terms[1:]:
            total = total + term[at, :].astype(jnp.float32)
        out[at, :] = total.astype(out.dtype)
        return carry

    lax.fori_loop(0, rows // step, body, 0)


def bit_orders(n):
    bits = [1 << j for j in range(n.bit_length() - 1)]
    return [bits[p:] + bits[:p] for p in range(len(bits))] or [[]]


class Ring:
    def __init__(self, n_exp):
        self.mine = lax.axis_index("expert")
        self.core = lax.rem(self.mine, 2)
        self.z = lax.div(self.mine, 2)
        self.depth = n_exp // 2
        self.far = self.depth // 2
        self.pair = self.mine + 1 - 2 * self.core
        self.right, self.left = self.dev(1), self.dev(-1)

    def dev(self, d):
        return lax.rem(self.z + d + self.depth, self.depth) * 2 + self.core

    def partners(self):
        return [(None, {"expert": e}) for e in (self.pair, self.right, self.left)]


class RingGather:
    def __init__(self, ring, own, out, sems):
        self.ring, self.own, self.out = ring, own, out
        self.send, self.recv, self.pair_send, self.pair_recv = sems
        self.half = own.shape[0] // 2

    @staticmethod
    def scratch(n_exp):
        far, depth = n_exp // 4, n_exp // 2
        sem = pltpu.SemaphoreType.DMA
        return [sem((2, far + 1, 2)), sem((2, far + 1, 2)), sem((depth, 2)), sem((depth, 2))]

    def rows(self, h):
        return pl.ds(h * self.half, self.half)

    def goes(self, side, s, h):
        far = self.ring.far
        return s < far or (s == far and h == side)

    def block(self, d, h):
        return self.out.at[self.ring.dev(d), self.rows(h)]

    def hop(self, side, s, h):
        d = -s if side == 0 else s
        src = self.own.at[self.rows(h)] if s == 0 else self.block(d, h)
        to = self.ring.right if side == 0 else self.ring.left
        return remote(src, self.block(d, h), self.send.at[side, s, h], self.recv.at[side, s + 1, h], expert=to)

    def across(self, d, h):
        src = self.own.at[self.rows(h)] if d == 0 else self.block(d, h)
        slot = d % self.ring.depth
        return remote(src, self.block(d, h), self.pair_send.at[slot, h], self.pair_recv.at[slot, h], expert=self.ring.pair)

    ORDER = ((0, 0), (1, 1), (0, 1), (1, 0))

    def start(self):
        for side, h in self.ORDER:
            if self.goes(side, 1, h):
                self.hop(side, 0, h).start()
        self.across(0, 0).start()
        self.across(0, 1).start()

    def events(self):
        return [(side, s, h) for s in range(1, self.ring.far + 1) for side, h in self.ORDER if self.goes(side, s, h)]

    def handle(self, event):
        side, s, h = event
        d = -s if side == 0 else s
        here = self.block(d, h)
        remote(here, here, self.send.at[side, s, h], self.recv.at[side, s, h], expert=self.ring.mine).wait_recv()
        if self.goes(side, s + 1, h):
            self.hop(side, s, h).start()
        self.across(d, h).start()

    def wait_pair(self, d, h):
        slot = d % self.ring.depth
        here = self.out.at[self.ring.pair - self.ring.mine + self.ring.dev(d), self.rows(h)]
        remote(here, here, self.pair_send.at[slot, h], self.pair_recv.at[slot, h], expert=self.ring.mine).wait_recv()

    def finish_own(self):
        for side, h in self.ORDER:
            if self.goes(side, 1, h):
                self.hop(side, 0, h).wait_send()
        self.across(0, 0).wait_send()
        self.across(0, 1).wait_send()

    def finish_event(self, event):
        side, s, h = event
        if self.goes(side, s + 1, h):
            self.hop(side, s, h).wait_send()
        self.across(-s if side == 0 else s, h).wait_send()


class RingScatter:
    def __init__(self, ring, part, bufs, sems):
        self.ring, self.part = ring, part
        self.pair_buf, self.held, self.got = bufs
        self.pair_send, self.pair_recv, self.send, self.recv = sems
        self.half = self.held(0).shape[0] // 2

    @staticmethod
    def scratch(n_exp, block, dtype):
        far, depth = n_exp // 4, n_exp // 2
        sem = pltpu.SemaphoreType.DMA
        bufs = [pltpu.VMEM((depth,) + block, dtype), pltpu.VMEM((depth,) + block, dtype),
                pltpu.VMEM((2, far) + block, dtype)]
        return bufs, [sem((depth,)), sem((depth,)), sem((2, far + 1, 2)), sem((2, far + 1, 2))]

    def rows(self, h):
        return pl.ds(h * self.half, self.half)

    def order(self):
        far, depth = self.ring.far, self.ring.depth
        order = [far]
        for s in range(far - 1, 0, -1):
            order += [s, depth - s]
        return order + [0]

    def comes(self, side, d, h):
        far = self.ring.far
        return d + 1 < far or (d + 1 == far and h == side)

    def across(self, d):
        ring = self.ring
        return remote(self.part(ring.dev(d) + 1 - 2 * ring.core), self.pair_buf(d),
                      self.pair_send.at[d], self.pair_recv.at[d], expert=ring.pair)

    def start_pair(self, d):
        self.across(d).start()

    def wait_pair(self, d):
        self.across(d).wait_recv()

    def wait_got(self, side, d, h):
        here = self.got(side, d).at[self.rows(h)]
        remote(here, here, self.send.at[side, d, h], self.recv.at[side, d, h], expert=self.ring.mine).wait_recv()

    def hop(self, side, d, h):
        slot = d if side == 0 else self.ring.depth - d
        rows = self.rows(h)
        return remote(self.held(slot).at[rows], self.got(side, d - 1).at[rows], self.send.at[side, d, h],
                      self.recv.at[side, d - 1, h], expert=self.ring.right if side == 0 else self.ring.left)

    def push(self, side, d, h):
        ring = self.ring
        slot = d if side == 0 else ring.depth - d
        rows = self.rows(h)
        terms = [self.part(ring.dev(slot)).at[rows], self.pair_buf(slot).at[rows]]
        if self.comes(side, d, h):
            self.wait_got(side, d, h)
            terms.append(self.got(side, d).at[rows])
        add_rows(self.held(slot).at[rows], *terms)
        self.hop(side, d, h).start()

    def first(self):
        far = self.ring.far
        self.wait_pair(far)
        self.push(0, far, 0)
        self.push(1, far, 1)

    def early(self):
        for d in range(self.ring.far - 1, 0, -1):
            self.wait_pair(d)
            self.push(0, d, 1)
            self.wait_pair(self.ring.depth - d)
            self.push(1, d, 0)

    def late(self):
        for d in range(self.ring.far - 1, 0, -1):
            self.push(0, d, 0)
            self.push(1, d, 1)

    def last(self, out, *more):
        self.wait_pair(0)
        for h in range(2):
            rows = self.rows(h)
            terms = [self.part(self.ring.mine).at[rows], self.pair_buf(0).at[rows]] + [m.at[rows] for m in more]
            for side in range(2):
                if self.comes(side, 0, h):
                    self.wait_got(side, 0, h)
                    terms.append(self.got(side, 0).at[rows])
            add_rows(out.at[rows], *terms)

    def finish_sends(self):
        far = self.ring.far
        for side in range(2):
            for d in range(1, far + 1):
                for h in range(2):
                    if d < far or h == side:
                        self.hop(side, d, h).wait_send()
        for d in range(self.ring.depth):
            self.across(d).wait_send()


def views(bufs):
    pair_buf, held, got = bufs
    return (lambda d: pair_buf.at[d], lambda d: held.at[d], lambda side, d: got.at[side, d])


SLOTS = 128
F32, LOW = jnp.float32, jnp.bfloat16


def dot(a, b, over_a=1, over_b=0):
    return lax.dot_general(a, b, (((over_a,), (over_b,)), ((), ())), preferred_element_type=F32)


def experts_body(n_dp, n_exp, hid_ref, gy_hbm, routes_t, wr_t, w_in_hbm, w_out_hbm, middle,
                 block_out, hid_sum, gates_out, in_share, out_share,
                 x_all, w_in, w_out, sent, grows, gu, tmp, acts, stage, slots, gates, dots, wide,
                 pair_buf, held, got, *sems):
    w_sem, gy_sem, wide_sem, own_sem, ready, gate_send, gate_recv, dp_ready, dp_send, dp_recv = sems[:10]
    gather_sems, out_sems, hid_sems = sems[10:14], sems[14:18], sems[18:22]
    me = lax.axis_index("dp")
    local, _, width = sent.shape
    tree, hidden_units = hid_ref.shape[0], w_out.shape[1]
    rows_e = local * SLOTS
    ring = Ring(n_exp)
    mine, core, depth = ring.mine, ring.core, ring.depth
    first = mine * local
    peers = [lax.rem(mine + k, n_exp) for k in range(1, n_exp)]
    greet([(None, {"expert": e}) for e in peers] + [(None, {"dp": me ^ bit}) for bit in (1, 2)])

    weights = [pltpu.make_async_copy(w_in_hbm, w_in, w_sem.at[0]), pltpu.make_async_copy(w_out_hbm, w_out, w_sem.at[1])]
    gather = RingGather(ring, hid_ref, x_all, gather_sems)
    gather.start()
    for copy in weights:
        copy.start()
    own = pltpu.make_async_copy(hid_ref, x_all.at[mine], own_sem)
    own.start()

    def gy_buf(j):
        return stage.at[lax.rem(j, 2), pl.ds(0, tree)]

    def gy_copy(j):
        return pltpu.make_async_copy(gy_hbm.at[j], gy_buf(j), gy_sem.at[lax.rem(j, 2)])

    gy_copy(0).start()

    below = (lax.broadcasted_iota(jnp.int32, (tree, tree), 0) < lax.broadcasted_iota(jnp.int32, (tree, tree), 1)).astype(LOW)
    sub16 = lax.broadcasted_iota(jnp.int32, (16, tree), 0)

    def find_slots(j, carry):
        names = routes_t[j]
        chosen = jnp.zeros((16, tree), F32)
        for k in range(names.shape[0]):
            chosen = jnp.maximum(chosen, jnp.where(names[k : k + 1, :] == first + sub16, 1.0, 0.0))
        chosen = jnp.where(sub16 < local, chosen, 0.0)
        rank = dot(chosen.astype(LOW), below)
        slots[j] = jnp.where(chosen > 0.5, rank, -1.0)[:8]
        return carry

    lax.fori_loop(0, n_exp, find_slots, 0)

    slot_ids = lax.broadcasted_iota(jnp.int32, (SLOTS, tree), 0).astype(F32)

    def places(j):
        return jnp.concatenate(
            [jnp.where(slot_ids == slots[j, i : i + 1, :], 1.0, 0.0).astype(LOW) for i in range(local)], axis=0)

    def places_t(j):
        lane = lax.broadcasted_iota(jnp.int32, (tree, 128), 1)
        pick = jnp.where(lax.broadcasted_iota(jnp.int32, (16, 128), 0) == lax.broadcasted_iota(jnp.int32, (16, 128), 1), 1.0, 0.0)
        slot = dot(jnp.concatenate([slots[j], jnp.zeros((8, tree), F32)], axis=0).astype(LOW), pick.astype(LOW), 0, 0)
        lanes = lane.astype(F32)
        return jnp.concatenate(
            [jnp.where(lanes == slot[:, i : i + 1], 1.0, 0.0).astype(LOW) for i in range(local)], axis=1)

    def find_gates(j):
        names = routes_t[j]
        experts = lax.broadcasted_iota(jnp.int32, (EXPERTS, tree), 0)
        chosen = jnp.zeros((EXPERTS, tree), F32)
        for k in range(names.shape[0]):
            chosen = jnp.maximum(chosen, jnp.where(names[k : k + 1, :] == experts, 1.0, 0.0))
        logits = jnp.where(chosen > 0.5, dot(wr_t[...], x_all[j], 1, 1), -1e30)
        powers = jnp.exp(logits - jnp.max(logits, axis=0, keepdims=True))
        share = powers / jnp.sum(powers, axis=0, keepdims=True)
        sub = lax.broadcasted_iota(jnp.int32, (8, tree), 0)
        own_gates = jnp.zeros((8, tree), F32)
        for i in range(local):
            row = jnp.sum(jnp.where(experts == first + i, share, 0.0), axis=0, keepdims=True)
            own_gates = jnp.where(sub == i, row, own_gates)
        gates[j] = own_gates

    halves = width // 512

    def dispatch(j, src, dest):
        place = places(j)

        def body(n, carry):
            cols = pl.ds(pl.multiple_of(n * 512, 512), 512)
            picked = dot(place, src[:, cols]).astype(LOW)
            for i in range(local):
                dest[i, pl.ds(pl.multiple_of(j * SLOTS, SLOTS), SLOTS), cols] = picked[i * SLOTS : (i + 1) * SLOTS]
            return carry

        lax.fori_loop(0, halves, body, 0)

    def slot_gate(j, e):
        return jnp.sum(jnp.where(slot_ids == slots[j, pl.ds(e, 1), :], gates[j, pl.ds(e, 1), :], 0.0), axis=1, keepdims=True)

    def forward(chip):
        pair_rows = pl.ds(pl.multiple_of(chip * 2 * SLOTS, 2 * SLOTS), 2 * SLOTS)

        def one_tree(q, carry):
            j = 2 * chip + q
            find_gates(j)
            dispatch(j, x_all.at[j], sent)
            return carry

        lax.fori_loop(0, 2, one_tree, 0)

        def one_expert(e, carry):
            both = dot(sent[e, pair_rows, :], w_in[e])
            gu[e, pair_rows, :] = both.astype(LOW)
            a, b = both[:, :hidden_units], both[:, hidden_units:]
            act = (a / (1.0 + jnp.exp(-a)) * b).astype(LOW).astype(F32)
            gate = jnp.concatenate([slot_gate(2 * chip, e), slot_gate(2 * chip + 1, e)], axis=0)
            made = dot((act * gate).astype(LOW), w_out[e]).astype(LOW)
            for q in range(2):
                tmp[pl.ds(pl.multiple_of(q * rows_e + e * SLOTS, SLOTS), SLOTS), :] = made[q * SLOTS : (q + 1) * SLOTS]
            return carry

        lax.fori_loop(0, local, one_expert, 0)

    def combine_out(chip):
        def one_tree(q, carry):
            j = 2 * chip + q
            rows = pl.ds(pl.multiple_of(q * rows_e, rows_e), rows_e)
            x_all[j] = dot(places_t(j), tmp[rows, :]).astype(LOW)
            return carry

        lax.fori_loop(0, 2, one_tree, 0)

    def grad_rows(j, carry):
        pl.when(j + 1 < n_exp)(lambda: gy_copy(j + 1).start())
        gy_copy(j).wait()
        dispatch(j, gy_buf(j), grows)
        return carry

    events = gather.events()
    out = RingScatter(ring, lambda e: x_all.at[e], views((pair_buf, held, got)), out_sems)

    def chip_at(d):
        return lax.rem(ring.z + d, depth)

    def group(g, carry):
        d = jnp.where(g == 0, 0, jnp.where(g == 1, depth - 1, jnp.where(g == 2, 1, 2)))
        chip = chip_at(d)

        @pl.when(g == 0)
        def _():
            own.wait()
            gather.wait_pair(0, 0)
            gather.wait_pair(0, 1)
            for copy in weights:
                copy.wait()

        @pl.when(g == 1)
        def _():
            for event in events[:4]:
                gather.handle(event)
            gather.wait_pair(-1, 0)
            gather.wait_pair(-1, 1)

        @pl.when(g == 2)
        def _():
            gather.wait_pair(1, 0)
            gather.wait_pair(1, 1)

        @pl.when(g == 3)
        def _():
            for event in events[4:]:
                gather.handle(event)
            gather.wait_pair(2, 0)
            gather.wait_pair(2, 1)

        forward(chip)

        @pl.when(g == 0)
        def _():
            gather.finish_own()
            lax.fori_loop(0, n_exp, grad_rows, 0)

        for at, d in ((1, -1), (2, 1), (3, 2)):
            @pl.when(g == at)
            def _():
                for event in events:
                    if event[1] == abs(d) and (abs(d) == 2 or (event[0] == 0) == (d < 0)):
                        gather.finish_event(event)

        combine_out(chip)
        pl.when(g == 0)(lambda: out.start_pair(0))
        pl.when(g == 1)(lambda: out.start_pair(depth - 1))
        pl.when(g == 2)(lambda: out.start_pair(1))
        pl.when(g == 3)(lambda: out.start_pair(2))
        return carry

    lax.fori_loop(0, depth, group, 0)
    out.first()
    out.early()

    in_rows, out_rows = width // n_dp, hidden_units // n_dp
    cut = (in_rows + out_rows) // 2

    def grad_half(e, r, h):
        at = 2 * r + h
        return gu.at[e, pl.ds(at * cut, cut)] if at < 5 else stage.at[e, pl.ds((at - 5) * cut, cut)]

    def grad_land(e, k):
        return w_in.at[e, pl.ds(k * cut, cut)] if k < 5 else w_out.at[e, pl.ds(0, cut)]

    def grad_hop(e, step, h, which):
        bit = (1, 2)[h] if step == 0 else (2, 1)[h]
        r = bit if which == 0 else 3
        k = 2 * h + which if step == 0 else 4 + h
        return remote(grad_half(e, r, h), grad_land(e, k), dp_send.at[e, k], dp_recv.at[e, k], dp=me ^ bit)

    def grads_start(e):
        pl.semaphore_wait(dp_ready.at[e], 2)
        for which in (1, 0):
            for h in range(2):
                grad_hop(e, 0, h, which).start()

    def grads_turn(e):
        for which in (1, 0):
            for h in range(2):
                grad_hop(e, 0, h, which).wait_recv()
                kept = 0 if which == 0 else (2, 1)[h]
                add_rows(grad_half(e, kept, h), grad_half(e, kept, h), grad_land(e, 2 * h + which))
                if which == 1:
                    grad_hop(e, 1, h, 0).start()

    def wide_copies(e):
        return (
            pltpu.make_async_copy(wide.at[pl.ds(0, in_rows)], in_share.at[e], wide_sem.at[0]),
            pltpu.make_async_copy(wide.at[pl.ds(in_rows, out_rows)], out_share.at[e], wide_sem.at[1]),
        )

    def grads_end(e):
        for h in range(2):
            grad_hop(e, 1, h, 0).wait_recv()
            add_rows(wide.at[pl.ds(h * cut, cut)], grad_half(e, 0, h), grad_land(e, 4 + h))
        for copy in wide_copies(e):
            copy.start()
        for step, h, which in ((0, 0, 0), (0, 0, 1), (0, 1, 0), (0, 1, 1), (1, 0, 0), (1, 1, 0)):
            grad_hop(e, step, h, which).wait_send()
        for copy in wide_copies(e):
            copy.wait()

    block = 4 * SLOTS
    sub8 = lax.broadcasted_iota(jnp.int32, (8, tree), 0)

    def backward(e, carry):
        def one_block(m, inner):
            rows = pl.ds(pl.multiple_of(m * block, block), block)
            grad_act = dot(grows[e, rows, :], w_out[e], 1, 1)
            a = gu[e, rows, pl.ds(0, hidden_units)].astype(F32)
            b = gu[e, rows, pl.ds(hidden_units, hidden_units)].astype(F32)
            sg = 1.0 / (1.0 + jnp.exp(-a))
            sw = a * sg
            act = (sw * b).astype(LOW).astype(F32)
            gate = jnp.concatenate([slot_gate(4 * m + q, e) for q in range(4)], axis=0)
            told = jnp.sum(act * grad_act, axis=1, keepdims=True)
            acts[rows, :] = (act * gate).astype(LOW)
            grad_act = grad_act * gate
            tmp[rows, pl.ds(0, hidden_units)] = (grad_act * b * sg * (1.0 + a * (1.0 - sg))).astype(LOW)
            tmp[rows, pl.ds(hidden_units, hidden_units)] = (grad_act * sw).astype(LOW)
            for q in range(4):
                j = 4 * m + q
                row = jnp.sum(
                    jnp.where(slot_ids == slots[j, pl.ds(e, 1), :], told[q * SLOTS : (q + 1) * SLOTS], 0.0),
                    axis=0, keepdims=True)
                dots[j] = jnp.where(sub8 == e, row, dots[j])
            return inner

        lax.fori_loop(0, n_exp // 4, one_block, 0)
        pl.when(e > 0)(lambda: grads_start(e - 1))
        for r in range(n_dp):
            d = me ^ r
            grad_in = dot(sent[e, :, pl.ds(pl.multiple_of(d * in_rows, in_rows), in_rows)], tmp[...], 0, 0).astype(LOW)
            grad_out = dot(acts[:, pl.ds(pl.multiple_of(d * out_rows, out_rows), out_rows)], grows[e], 0, 0).astype(LOW)
            grad_half(e, r, 0)[...] = grad_in[:cut]
            half = grad_half(e, r, 1)
            half[pl.ds(0, in_rows - cut), :] = grad_in[cut:]
            half[pl.ds(in_rows - cut, out_rows), :] = grad_out

        def back_half(m, inner):
            rows = pl.ds(pl.multiple_of(m * 512, 512), 512)
            sent[e, rows, :] = dot(tmp[rows, :], w_in[e], 1, 1).astype(LOW)
            return inner

        lax.fori_loop(0, n_exp * SLOTS // 512, back_half, 0)
        for bit in (1, 2):
            pl.semaphore_signal(dp_ready.at[e], inc=1, device_id={"dp": me ^ bit}, device_id_type=MESH)
        pl.when(e == local // 2 - 1)(out.late)
        pl.when(e >= 2)(lambda: grads_turn(e - 2))
        return carry

    dots[...] = jnp.zeros(dots.shape, F32)
    middle_copy = pltpu.make_async_copy(middle, wide.at[pl.ds(0, tree)], wide_sem.at[0])
    middle_copy.start()
    lax.fori_loop(0, local, backward, 0)
    grads_start(local - 1)

    gate_copies = []
    for k, e in enumerate(peers):
        copy = remote(dots.at[e], gates_out.at[mine], gate_send.at[k], gate_recv.at[k], expert=e)
        copy.start()
        gate_copies.append(copy)
    gates_out[mine] = dots[mine]
    middle_copy.wait()
    out.last(block_out, wide.at[pl.ds(0, tree)])
    out.finish_sends()
    for partner in (ring.pair, ring.right, ring.left):
        pl.semaphore_signal(ready, inc=1, device_id={"expert": partner}, device_id_type=MESH)
    hid = RingScatter(ring, lambda e: x_all.at[e], views((pair_buf, held, got)), hid_sems)

    def combine_hid(g, carry):
        d = jnp.where(g == 0, 2, jnp.where(g == 1, 1, jnp.where(g == 2, depth - 1, 0)))
        chip = chip_at(d)

        def one_tree(q, inner):
            j = 2 * chip + q
            rows = pl.ds(pl.multiple_of(j * SLOTS, SLOTS), SLOTS)
            made = jnp.concatenate([sent[i, rows, :] for i in range(local)], axis=0)
            x_all[j] = dot(places_t(j), made).astype(LOW)
            return inner

        lax.fori_loop(0, 2, one_tree, 0)

        @pl.when(g == 0)
        def _():
            pl.semaphore_wait(ready, 3)
            hid.start_pair(2)

        pl.when(g == 1)(lambda: hid.start_pair(1))
        pl.when(g == 2)(lambda: hid.start_pair(depth - 1))
        pl.when(g == 3)(lambda: hid.start_pair(0))
        pl.when(g == 1)(hid.first)
        return carry

    lax.fori_loop(0, depth, combine_hid, 0)
    hid.early()
    grads_turn(local - 2)
    grads_end(0)
    hid.late()
    grads_end(1)
    grads_turn(local - 1)
    hid.last(wide.at[pl.ds(0, tree)])
    hid_copy = pltpu.make_async_copy(wide.at[pl.ds(0, tree)], hid_sum, wide_sem.at[0])
    hid_copy.start()
    hid_copy.wait()
    for e in range(2, local):
        grads_end(e)

    for k, copy in enumerate(gate_copies):
        copy.wait_send()
        source = lax.rem(mine + n_exp - 1 - k, n_exp)
        remote(dots.at[mine], gates_out.at[source], gate_send.at[k], gate_recv.at[k], expert=mine).wait_recv()
    hid.finish_sends()


def experts(n_dp, n_exp, hidden2, grad_y, routes_all, router, expert_in, expert_out, middle, collective_id):
    local, width, both = expert_in.shape
    units = expert_out.shape[1]
    tree = hidden2.shape[0]
    rows = n_exp * SLOTS
    sem = pltpu.SemaphoreType.DMA
    bufs, out_sems = RingScatter.scratch(n_exp, (tree, width), LOW)
    _, hid_sems = RingScatter.scratch(n_exp, (tree, width), LOW)
    shape = jax.ShapeDtypeStruct
    return pl.pallas_call(
        functools.partial(experts_body, n_dp, n_exp),
        out_shape=[
            shape((tree, width), LOW),
            shape((tree, width), F32),
            shape((n_exp, 8, tree), F32),
            shape((local, width // n_dp, width), F32),
            shape((local, units // n_dp, width), F32),
        ],
        in_specs=[pl.BlockSpec(memory_space=s) for s in (VMEM, ANY, VMEM, VMEM, ANY, ANY, ANY)],
        out_specs=[pl.BlockSpec(memory_space=s) for s in (VMEM, ANY, VMEM, ANY, ANY)],
        scratch_shapes=[
            pltpu.VMEM((n_exp, tree, width), LOW),
            pltpu.VMEM((local, width, both), LOW),
            pltpu.VMEM((local, units, width), LOW),
            pltpu.VMEM((local, rows, width), LOW),
            pltpu.VMEM((local, rows, width), LOW),
            pltpu.VMEM((local, rows, both), LOW),
            pltpu.VMEM((max(rows, 2 * local * SLOTS), width), LOW),
            pltpu.VMEM((rows, units), LOW),
            pltpu.VMEM((local, 3 * (width + units) // (2 * n_dp), width), LOW),
            pltpu.VMEM((n_exp, 8, tree), F32),
            pltpu.VMEM((n_exp, 8, tree), F32),
            pltpu.VMEM((n_exp, 8, tree), F32),
            pltpu.VMEM(((width + units) // n_dp, width), F32),
            *bufs,
            sem((2,)), sem((2,)), sem((2,)), sem, pltpu.SemaphoreType.REGULAR, sem((n_exp - 1,)), sem((n_exp - 1,)),
            pltpu.SemaphoreType.REGULAR((local,)), sem((local, 6)), sem((local, 6)),
            *RingGather.scratch(n_exp), *out_sems, *hid_sems,
        ],
        compiler_params=pltpu.CompilerParams(
            collective_id=collective_id, has_side_effects=True, vmem_limit_bytes=63 * MIB),
        name="experts",
    )(hidden2, grad_y, routes_all, router.T, expert_in, expert_out, middle)


def lanes_of(shape):
    return lax.broadcasted_iota(jnp.int32, shape, 1)


def turned(field):
    low_half = lax.rem(lanes_of(field.shape), HD) < HD // 2
    return jnp.where(low_half, -pltpu.roll(field, 128 - HD // 2, 1), pltpu.roll(field, HD // 2, 1))


def mask_bias(parents, tree):
    unit = tree // 20

    def segment(row):
        return jnp.where(row < 8 * unit, 0, jnp.where(row < 12 * unit, 1 + lax.div(row - 8 * unit, unit), 5 + lax.div(row - 12 * unit, unit)))

    count = parents.shape[1]
    names = parents[...].astype(F32)
    wide = (tree, count)
    seg = segment(lax.broadcasted_iota(jnp.int32, wide, 0)).astype(F32)
    lane = lanes_of(wide).astype(F32)
    own = seg[:, :1]
    parent = jnp.sum(jnp.where(lane == seg, names, 0.0), axis=1, keepdims=True)
    grand = jnp.sum(jnp.where(lane == parent, names, 0.0), axis=1, keepdims=True)
    square = (tree, tree)
    row, col = lax.broadcasted_iota(jnp.int32, square, 0), lanes_of(square)
    there = segment(col).astype(F32)
    hit = jnp.maximum(
        jnp.maximum(jnp.where(there == own, 1.0, 0.0), jnp.where(there == parent, 1.0, 0.0)), jnp.where(there == grand, 1.0, 0.0))
    hit = jnp.where(col <= row, hit, 0.0)
    return jnp.where(hit > 0.5, 0.0, -1e30)


def inverse_rms(field):
    return lax.rsqrt(jnp.mean(field * field, axis=-1, keepdims=True) + EPSILON)


class DpGather:
    def __init__(self, n_dp, mine, me, ins, outs, sems):
        self.n_dp, self.me, self.ins, self.outs = n_dp, me, ins, outs
        self.send, self.recv, self.pair_send, self.pair_recv, self.own_sem = sems
        self.core = lax.rem(mine, 2)
        self.pair = mine + 1 - 2 * self.core
        self.shard = ins[0].shape[0]
        half = self.shard // 2
        self.orders = bit_orders(n_dp)
        self.cuts = min(2, len(self.orders), half // 16)
        self.size = half // self.cuts

    @staticmethod
    def scratch(count, n_dp):
        sem = pltpu.SemaphoreType.DMA
        bits = max(1, n_dp.bit_length() - 1)
        return [sem((count, 2, n_dp, bits)), sem((count, 2, n_dp)), sem((count, 2, n_dp)), sem((count, 2, n_dp)), sem((count,))]

    def rows(self, start, side, p):
        return pl.ds(pl.multiple_of(start + side * (self.shard // 2) + p * self.size, 16), self.size)

    def hop(self, a, p, r, bit):
        there = self.outs[a].at[self.rows((self.me ^ r) * self.shard, self.core, p)]
        src = self.ins[a].at[self.rows(0, self.core, p)] if r == 0 else there
        return remote(src, there, self.send.at[a, p, r, bit.bit_length() - 1], self.recv.at[a, p, r ^ bit], dp=self.me ^ bit)

    def own(self, a):
        at = pl.ds(pl.multiple_of(self.me * self.shard, 16), self.shard)
        return pltpu.make_async_copy(self.ins[a], self.outs[a].at[at], self.own_sem.at[a])

    def across(self, a, p, r, side):
        here = self.outs[a].at[self.rows((self.me ^ r) * self.shard, side, p)]
        return remote(here, here, self.pair_send.at[a, p, r], self.pair_recv.at[a, p, r], expert=self.pair)

    def start(self, a):
        for p in range(self.cuts):
            for bit in self.orders[p]:
                self.hop(a, p, 0, bit).start()
        self.own(a).start()

    def stage(self, p, j):
        order = self.orders[p]
        blocks = [0]
        for bit in order[:j]:
            blocks = blocks + [r | bit for r in blocks]
        return [r | order[j] for r in blocks], order[j + 1 :]

    def turn(self, a, j):
        for p in range(self.cuts):
            blocks, onward = self.stage(p, j)
            for r in blocks:
                here = self.outs[a].at[self.rows((self.me ^ r) * self.shard, self.core, p)]
                remote(here, here, self.send.at[a, p, r, 0], self.recv.at[a, p, r], dp=self.me).wait_recv()
                for bit in onward:
                    self.hop(a, p, r, bit).start()
                self.across(a, p, r, self.core).start()

    def ready(self, a):
        self.own(a).wait()
        for p in range(self.cuts):
            for r in range(1, self.n_dp):
                self.across(a, p, r, 1 - self.core).wait_recv()

    def finish(self, a):
        for p in range(self.cuts):
            for bit in self.orders[p]:
                self.hop(a, p, 0, bit).wait_send()
            for j in range(len(self.orders[p])):
                blocks, onward = self.stage(p, j)
                for r in blocks:
                    for bit in onward:
                        self.hop(a, p, r, bit).wait_send()
                    self.across(a, p, r, self.core).wait_send()


def front_body(n_dp, n_exp, x_ref, gain1, gain2, router, w_query, w_keyval, w_output, routes_t, parents, cosine, sine,
               hidden, queries, keys, values, attended, middle, hidden2, log_total,
               query_full, keyval_full, output_full, router_full, gains, routes_all,
               router_pad, gain_pad, bias, *sems):
    gather_sems, (gain_send, gain_recv, route_send, route_recv) = sems[:5], sems[5:9]
    me, mine = lax.axis_index("dp"), lax.axis_index("expert")
    peers = [lax.rem(mine + k, n_exp) for k in range(1, n_exp)]
    greet([(None, {"expert": e}) for e in peers] + [(None, {"dp": me ^ k}) for k in range(1, n_dp)])
    tree, width = x_ref.shape
    shard = w_query.shape[0]

    router_pad[...] = jnp.zeros(router_pad.shape, LOW)
    router_pad[:, pl.ds(0, EXPERTS)] = router[...]
    sub = lax.broadcasted_iota(jnp.int32, (16, shard), 0)
    gain_pad[...] = jnp.where(sub == 0, gain1[...].astype(F32), jnp.where(sub == 1, gain2[...].astype(F32), 0.0)).astype(LOW)

    gather = DpGather(n_dp, mine, me, (w_query, w_keyval, w_output, router_pad),
                      (query_full, keyval_full, output_full, router_full), gather_sems)

    def gain_copy(k):
        return remote(gain_pad, gains.at[me], gain_send.at[k], gain_recv.at[k], dp=me ^ k)

    def route_copy(k, e):
        return remote(routes_t, routes_all.at[mine], route_send.at[k], route_recv.at[k], expert=e)

    for k in range(1, n_dp):
        gain_copy(k).start()
    for a in range(4):
        gather.start(a)
    for k, e in enumerate(peers):
        route_copy(k, e).start()
    gains[me] = gain_pad[...]
    routes_all[mine] = routes_t[...]
    bias[...] = mask_bias(parents, tree)
    log_total[...] = jnp.zeros(log_total.shape, F32)
    for k in range(1, n_dp):
        remote(gain_pad, gains.at[me ^ k], gain_send.at[k], gain_recv.at[k], dp=me).wait_recv()

    def gain_row(i):
        return jnp.concatenate([gains[d].astype(F32)[i : i + 1] for d in range(n_dp)], axis=1)

    x = x_ref[...].astype(F32)
    hidden[...] = (x * inverse_rms(x) * gain_row(0)).astype(LOW)
    stages = len(gather.orders[0])
    for j in range(stages):
        for a in range(4 if j + 1 < stages else 2):
            gather.turn(a, j)
    gather.ready(0)
    gather.ready(1)

    def rotate(field):
        return field * cosine[...] + turned(field) * sine[...]

    left = lanes_of((tree, 128)) < HD
    tile = 512

    def query_tile(n, carry):
        cols = pl.ds(pl.multiple_of(n * tile, tile), tile)
        pre = dot(hidden[...], query_full[:, cols])
        for i in range(tile // 128):
            at = pl.multiple_of(n * tile + i * 128, 128)
            queries[:, pl.ds(at, 128)] = rotate(pre[:, i * 128 : (i + 1) * 128]).astype(LOW)
        return carry

    lax.fori_loop(0, width // tile, query_tile, 0)

    def spread(field, out, i):
        other = pltpu.roll(field, HD, 1)
        out[2 * i] = jnp.where(left, field, other).astype(LOW)
        out[2 * i + 1] = jnp.where(left, other, field).astype(LOW)

    half = KV * HD
    pre = dot(hidden[...], keyval_full[:, pl.ds(0, half)])
    for i in range(half // 128):
        spread(rotate(pre[:, i * 128 : (i + 1) * 128]), keys, i)
    pre = dot(hidden[...], keyval_full[:, pl.ds(half, half)])
    for i in range(half // 128):
        spread(pre[:, i * 128 : (i + 1) * 128], values, i)
    for a in range(2, 4):
        gather.turn(a, stages - 1)

    def heads(c, carry):
        cols = pl.ds(pl.multiple_of(c * 128, 128), 128)
        pair = queries[:, cols]
        made = []
        for h in range(2):
            mine_lanes = left if h == 0 else jnp.logical_not(left)
            query = jnp.where(mine_lanes, pair, jnp.zeros_like(pair))
            scores = dot(query, keys[c], 1, 1) * HD**-0.5 + bias[...]
            top = jnp.max(scores, axis=1, keepdims=True)
            powers = jnp.exp(scores - top)
            total = jnp.sum(powers, axis=1, keepdims=True)
            made.append(dot((powers / total).astype(LOW), values[c]))
            log_total[...] = jnp.where(lanes_of((tree, 128)) == 2 * c + h, top + jnp.log(total), log_total[...])
        attended[:, cols] = jnp.where(left, made[0], made[1]).astype(LOW)
        return carry

    lax.fori_loop(0, KV, heads, 0)
    gather.ready(2)
    gather.ready(3)

    def middle_tile(n, carry):
        cols = pl.ds(pl.multiple_of(n * tile, tile), tile)
        middle[:, cols] = x_ref[:, cols].astype(F32) + dot(attended[...], output_full[:, cols])
        return carry

    lax.fori_loop(0, width // tile, middle_tile, 0)
    field = middle[...]
    hidden2[...] = (field * inverse_rms(field) * gain_row(1)).astype(LOW)
    for a in range(4):
        gather.finish(a)
    for k in range(1, n_dp):
        gain_copy(k).wait_send()
    for k, e in enumerate(peers):
        route_copy(k, e).wait_send()
        source = lax.rem(mine + n_exp - 1 - k, n_exp)
        remote(routes_t, routes_all.at[source], route_send.at[k], route_recv.at[k], expert=mine).wait_recv()


def front(n_dp, n_exp, tokens, gain1, gain2, router, w_query, w_keyval, w_output, routes_t, parents, tables, collective_id):
    tree, width = tokens.shape
    shard = w_query.shape[0]
    shape, sem = jax.ShapeDtypeStruct, pltpu.SemaphoreType.DMA
    low = shape((tree, width), LOW)
    spread = shape((KV, tree, 128), LOW)
    full = shape((n_dp * shard, width), LOW)
    return pl.pallas_call(
        functools.partial(front_body, n_dp, n_exp),
        out_shape=[
            low, low, spread, spread, low, shape((tree, width), F32), low, shape((tree, 128), F32),
            full, full, full, shape((n_dp * shard, 128), LOW), shape((n_dp, 16, shard), LOW),
            shape((n_exp,) + routes_t.shape, jnp.int32),
        ],
        in_specs=[pl.BlockSpec(memory_space=VMEM)] * 11,
        out_specs=[pl.BlockSpec(memory_space=VMEM)] * 14,
        scratch_shapes=[
            pltpu.VMEM((shard, 128), LOW), pltpu.VMEM((16, shard), LOW), pltpu.VMEM((tree, tree), F32),
            *DpGather.scratch(4, n_dp), sem((n_dp,)), sem((n_dp,)), sem((n_exp - 1,)), sem((n_exp - 1,)),
        ],
        compiler_params=pltpu.CompilerParams(
            collective_id=collective_id, has_side_effects=True, vmem_limit_bytes=56 * MIB),
        name="front",
    )(tokens, gain1[None], gain2[None], router, w_query, w_keyval, w_output, routes_t, parents, *tables)


class GradSum:
    def __init__(self, n_dp, n_exp, chunks, own, bufs, sems):
        self.n_dp, self.chunks, self.own = n_dp, chunks, own
        (self.pair_in, self.total, self.dp_in, self.prefix, self.suffix, self.go_r, self.go_l, self.final, self.other) = bufs
        (self.pair_send, self.pair_recv, self.dp_send, self.dp_recv,
         self.send_r, self.send_l, self.recv_r, self.recv_l, self.last_send, self.last_recv) = sems
        self.me, self.mine = lax.axis_index("dp"), lax.axis_index("expert")
        self.core = lax.rem(self.mine, 2)
        self.z = lax.div(self.mine, 2)
        self.depth = n_exp // 2
        self.pair = self.mine + 1 - 2 * self.core
        self.has_left, self.has_right = self.z > 0, self.z < self.depth - 1
        self.orders = bit_orders(n_dp)

    @staticmethod
    def scratch(n_dp, chunks, half, columns):
        sem = pltpu.SemaphoreType.DMA
        stages = max(1, n_dp.bit_length() - 1)
        one = pltpu.VMEM((chunks, half, columns), LOW)
        many = pltpu.VMEM((chunks, n_dp, half, columns), LOW)
        bufs = [many, many, many, one, one, one, one, one, one]
        sems = [sem((chunks, n_dp)), sem((chunks, n_dp)), sem((chunks, n_dp)), sem((chunks, n_dp))]
        return bufs, sems + [sem((chunks,))] * 6

    def partners(self):
        return ([(None, {"expert": self.pair})] + [(None, {"dp": self.me ^ bit}) for bit in self.orders[0]]
                + [(self.has_left, {"expert": self.mine - 2}), (self.has_right, {"expert": self.mine + 2})])

    def across(self, i, d):
        return remote(self.own.at[i, d, 1 - self.core], self.pair_in.at[i, d], self.pair_send.at[i, d],
                      self.pair_recv.at[i, d], expert=self.pair)

    def moved(self, i, j):
        order = self.orders[i % len(self.orders)]
        blocks = [0]
        for bit in order[j + 1 :]:
            blocks = blocks + [r | bit for r in blocks]
        return order[j], [r | order[j] for r in blocks]

    def dp_copy(self, i, r, bit):
        return remote(self.total.at[i, r], self.dp_in.at[i, r], self.dp_send.at[i, r], self.dp_recv.at[i, r], dp=self.me ^ bit)

    def start(self, i):
        for d in range(self.n_dp):
            self.across(i, d).start()

    def paired(self, i):
        for r in range(self.n_dp - 1, -1, -1):
            d = self.me ^ r
            self.across(i, d).wait_recv()
            add_rows(self.total.at[i, r], self.own.at[i, d, self.core], self.pair_in.at[i, d])
        self.leave(i, 0)

    def leave(self, i, j):
        if j < len(self.orders[0]):
            bit, blocks = self.moved(i, j)
            for r in blocks:
                self.dp_copy(i, r, bit).start()

    def met(self, i, j):
        bit, blocks = self.moved(i, j)
        for r in blocks:
            self.dp_copy(i, r, bit).wait_recv()
            add_rows(self.total.at[i, r ^ bit], self.total.at[i, r ^ bit], self.dp_in.at[i, r])
        self.leave(i, j + 1)

    def right(self, i):
        return remote(self.go_r.at[i], self.prefix.at[i], self.send_r.at[i], self.recv_r.at[i], expert=self.mine + 2)

    def left(self, i):
        return remote(self.go_l.at[i], self.suffix.at[i], self.send_l.at[i], self.recv_l.at[i], expert=self.mine - 2)

    def line(self, t):
        i = t - self.z
        has_left, has_right = self.has_left, self.has_right

        @pl.when(jnp.logical_and(i >= 0, i < self.chunks))
        def _():
            @pl.when(has_left)
            def _():
                remote(self.go_r.at[i], self.prefix.at[i], self.send_r.at[i], self.recv_r.at[i], expert=self.mine).wait_recv()

            @pl.when(jnp.logical_and(has_left, has_right))
            def _():
                add_rows(self.go_r.at[i], self.total.at[i, 0], self.prefix.at[i])

            @pl.when(jnp.logical_not(has_left))
            def _():
                add_rows(self.go_r.at[i], self.total.at[i, 0])

            pl.when(has_right)(lambda: self.right(i).start())

        k = t - (self.depth - 1 - self.z)

        @pl.when(jnp.logical_and(k >= 0, k < self.chunks))
        def _():
            @pl.when(has_right)
            def _():
                remote(self.go_l.at[k], self.suffix.at[k], self.send_l.at[k], self.recv_l.at[k], expert=self.mine).wait_recv()

            @pl.when(jnp.logical_and(has_left, has_right))
            def _():
                add_rows(self.go_l.at[k], self.total.at[k, 0], self.suffix.at[k])

            @pl.when(jnp.logical_not(has_right))
            def _():
                add_rows(self.go_l.at[k], self.total.at[k, 0])

            pl.when(has_left)(lambda: self.left(k).start())

    def last(self, i):
        return remote(self.final.at[i], self.other.at[i], self.last_send.at[i], self.last_recv.at[i], expert=self.pair)

    def close(self, i):
        has_left, has_right = self.has_left, self.has_right

        @pl.when(jnp.logical_and(has_left, has_right))
        def _():
            add_rows(self.final.at[i], self.total.at[i, 0], self.prefix.at[i], self.suffix.at[i])

        @pl.when(jnp.logical_not(has_left))
        def _():
            add_rows(self.final.at[i], self.total.at[i, 0], self.suffix.at[i])

        @pl.when(jnp.logical_not(has_right))
        def _():
            add_rows(self.final.at[i], self.total.at[i, 0], self.prefix.at[i])

        self.last(i).start()

    def finish(self, i):
        self.last(i).wait_send()
        pl.when(self.has_right)(lambda: self.right(i).wait_send())
        pl.when(self.has_left)(lambda: self.left(i).wait_send())
        for d in range(self.n_dp):
            self.across(i, d).wait_send()
        for j in range(len(self.orders[0])):
            bit, blocks = self.moved(i, j)
            for r in blocks:
                self.dp_copy(i, r, bit).wait_send()


def two_parts(field):
    high = field.astype(LOW)
    return high, (field - high.astype(F32)).astype(LOW)


def norm_back(field, gain, grad):
    r = inverse_rms(field)
    scaled = grad * gain
    back = r * scaled - field * (r * r * r) * jnp.mean(field * scaled, axis=-1, keepdims=True)
    return back, jnp.sum(field * r * grad, axis=0, keepdims=True)


def back_body(n_dp, n_exp, local, x_ref, cot, hid_sum, gates_in, routes, parents, cosine, sine,
              hidden, queries, keys, values, attended, middle, hidden2, log_total,
              query_full, keyval_full, output_full, router_full, gains,
              input_grad, grad_q, grad_kv, grad_o, grad_s,
              bias, branch, grad_att, grad_q_pre, grad_kv_pre, rhs, own, own_s, *rest):
    big = GradSum(n_dp, n_exp, own.shape[0], own, rest[:9], rest[9:19])
    little = GradSum(n_dp, n_exp, 1, own_s, rest[19:28], rest[28:38])
    tree, width = x_ref.shape
    greet(big.partners())
    shard = width // n_dp
    side = shard // 2
    tile = 512
    lane = lanes_of((tree, 128))
    left = lane < HD

    def gain_row(i):
        return jnp.concatenate([gains[d].astype(F32)[i : i + 1] for d in range(n_dp)], axis=1)

    bias[...] = mask_bias(parents, tree)

    chosen = jnp.zeros((tree, 128), F32)
    for k in range(routes.shape[1]):
        chosen = jnp.maximum(chosen, jnp.where(routes[:, k : k + 1] == lane, 1.0, 0.0))
    logits = jnp.where(chosen > 0.5, dot(hidden2[...], router_full[...]), -1e30)
    powers = jnp.exp(logits - jnp.max(logits, axis=1, keepdims=True))
    gate = powers / jnp.sum(powers, axis=1, keepdims=True)
    count = gates_in.shape[0]
    where_row = lax.broadcasted_iota(jnp.int32, (count, 128), 0)
    where_lane = lanes_of((count, 128))
    group_row = lax.rem(where_row, 8)
    target = lax.div(where_row, 8) * local + group_row
    pick = jnp.where(group_row < local, jnp.where(target == where_lane, 1.0, 0.0), 0.0).astype(LOW)
    high, low = two_parts(gates_in[...])
    gate_back = dot(high, pick, 0, 0) + dot(low, pick, 0, 0)
    grad_logits = (gate * (gate_back - jnp.sum(gate * gate_back, axis=1, keepdims=True))).astype(LOW)
    grad_router = dot(hidden2[...], grad_logits, 0, 0)
    grad_hidden2 = hid_sum[...] + dot(grad_logits, router_full[...], 1, 1)
    back, gain2_sum = norm_back(middle[...], gain_row(1), grad_hidden2)
    grad_middle = cot[...].astype(F32) + back
    input_grad[...] = grad_middle
    branch[...] = grad_middle.astype(LOW)

    def chunk_grads(i, lhs, rhs_ref):
        def part(n, carry):
            made = dot(lhs[:, pl.ds(pl.multiple_of(n * tile, tile), tile)], rhs_ref[...], 0, 0).astype(LOW)
            for k in range(tile // side):
                own[i, n * (tile // shard) + k // 2, k % 2] = made[k * side : (k + 1) * side]
            return carry

        if tile % shard == 0:
            lax.fori_loop(0, width // tile, part, 0)

    for i in range(2):
        rhs[...] = branch[:, pl.ds(i * tile, tile)]
        chunk_grads(i, attended, rhs)
        big.start(i)

    def att_tile(n, carry):
        rows = pl.ds(pl.multiple_of(n * tile, tile), tile)
        grad_att[:, rows] = dot(branch[...], output_full[rows, :], 1, 1).astype(LOW)
        return carry

    lax.fori_loop(0, width // tile, att_tile, 0)

    def unrotate(field):
        return field * cosine[...] - turned(field * sine[...])

    scale = HD**-0.5

    def group(c):
        cols = pl.ds(pl.multiple_of(c * 128, 128), 128)
        pair, grad_pair = queries[:, cols], grad_att[:, cols]
        zero = jnp.zeros_like(pair)
        key, value = keys[c], values[c]
        grad_query, grad_key, grad_value = [], 0.0, 0.0
        for h in range(2):
            here = left if h == 0 else jnp.logical_not(left)
            query, grad_out = jnp.where(here, pair, zero), jnp.where(here, grad_pair, zero)
            logs = jnp.sum(jnp.where(lane == 2 * c + h, log_total[...], 0.0), axis=1, keepdims=True)
            probs = jnp.exp(dot(query, key, 1, 1) * scale + bias[...] - logs)
            grad_probs = dot(grad_out, value, 1, 1)
            grad_scores = (probs * (grad_probs - jnp.sum(probs * grad_probs, axis=1, keepdims=True))).astype(LOW)
            grad_value = grad_value + dot(probs.astype(LOW), grad_out, 0, 0)
            grad_query.append(dot(grad_scores, key))
            grad_key = grad_key + dot(grad_scores, query, 0, 0)
        grad_q_pre[:, cols] = unrotate(jnp.where(left, grad_query[0], grad_query[1]) * scale).astype(LOW)
        grad_key = (grad_key + pltpu.roll(grad_key, HD, 1)) * scale
        return unrotate(grad_key), grad_value + pltpu.roll(grad_value, HD, 1)

    def two_groups(i):
        key_a, value_a = group(2 * i)
        key_b, value_b = group(2 * i + 1)
        at = pl.multiple_of(i * 128, 128)
        grad_kv_pre[:, pl.ds(at, 128)] = jnp.where(left, key_a, key_b).astype(LOW)
        at = pl.multiple_of(KV * HD + i * 128, 128)
        grad_kv_pre[:, pl.ds(at, 128)] = jnp.where(left, value_a, value_b).astype(LOW)

    def gather_rhs(i):
        rhs[:, pl.ds(0, 256)] = grad_q_pre[:, pl.ds(i * 256, 256)]
        rhs[:, pl.ds(256, 128)] = grad_kv_pre[:, pl.ds(i * 128, 128)]
        rhs[:, pl.ds(384, 128)] = grad_kv_pre[:, pl.ds(KV * HD + i * 128, 128)]

    for i in range(KV // 2):
        two_groups(i)
        if i == 0:
            big.paired(0)
            big.paired(1)
        if i == 1:
            big.met(0, 0)
            big.paired(2)
        if i == 2:
            big.met(1, 0)
            big.met(0, 1)
            big.paired(3)
        if i == 3:
            big.met(1, 1)
            big.met(2, 0)
            big.paired(4)
        gather_rhs(i)
        chunk_grads(2 + i, hidden, rhs)
        big.start(2 + i)

    def hidden_tile(n, carry):
        cols = pl.ds(pl.multiple_of(n * tile, tile), tile)
        grad = dot(grad_q_pre[...], query_full[cols, :], 1, 1) + dot(grad_kv_pre[...], keyval_full[cols, :], 1, 1)
        hid_sum_out[:, cols] = grad
        return carry

    hid_sum_out = rest[38]
    lax.fori_loop(0, width // tile, hidden_tile, 0)
    big.paired(5)
    back, gain1_sum = norm_back(x_ref[...].astype(F32), gain_row(0), hid_sum_out[...])
    input_grad[...] = input_grad[...] + back

    sub = lax.broadcasted_iota(jnp.int32, (16, width), 0)
    sums = jnp.zeros((16, width), F32)
    for k, row in enumerate((gain1_sum, gain2_sum)):
        first, second = two_parts(row)
        sums = jnp.where(sub == 2 * k, first.astype(F32), jnp.where(sub == 2 * k + 1, second.astype(F32), sums))
    line_at = lax.broadcasted_iota(jnp.int32, (16, 128), 0)
    column = jnp.where(lanes_of((16, 128)) == EXPERTS + lax.div(line_at, 2), jnp.where(line_at < 4, 1.0, 0.0), 0.0).astype(LOW)
    little_all = (grad_router + dot(sums.astype(LOW), column, 0, 0)).astype(LOW)
    for d in range(n_dp):
        for k in range(2):
            at = d * shard + k * side
            own_s[0, d, k] = little_all[at : at + side]
    little.start(0)

    big.met(2, 1)
    big.met(3, 0)
    big.met(4, 0)
    little.paired(0)
    big.met(3, 1)
    big.met(5, 0)
    little.met(0, 0)
    big.met(4, 1)
    little.met(0, 1)
    big.met(5, 1)
    steps = own.shape[0] + big.depth - 1

    def line(t, carry):
        big.line(t)
        return carry

    lax.fori_loop(0, steps, line, 0)

    def little_line(t, carry):
        little.line(t)
        return carry

    lax.fori_loop(0, little.depth, little_line, 0)

    def place(i, which, field):
        rows = pl.ds(pl.multiple_of(which * side, 16), side)
        if i < 2:
            add_rows(grad_o.at[rows, pl.ds(i * tile, tile)], field)
            return
        i = i - 2
        add_rows(grad_q.at[rows, pl.ds(i * 256, 256)], field.at[:, pl.ds(0, 256)])
        add_rows(grad_kv.at[rows, pl.ds(i * 128, 128)], field.at[:, pl.ds(256, 128)])
        add_rows(grad_kv.at[rows, pl.ds(KV * HD + i * 128, 128)], field.at[:, pl.ds(384, 128)])

    chunks = own.shape[0]
    for i in range(chunks):
        big.close(i)
    little.close(0)
    for i in range(chunks):
        place(i, big.core, big.final.at[i])
    add_rows(grad_s.at[pl.ds(pl.multiple_of(big.core * side, 16), side)], little.final.at[0])
    for i in range(chunks):
        big.last(i).wait_recv()
        place(i, 1 - big.core, big.other.at[i])
        big.finish(i)
    little.last(0).wait_recv()
    add_rows(grad_s.at[pl.ds(pl.multiple_of((1 - big.core) * side, 16), side)], little.other.at[0])
    little.finish(0)


def back(n_dp, n_exp, local, tokens, cotangent, hid_sum, gates_in, routes, parents, tables, saved, collective_id):
    tree, width = tokens.shape
    shard = width // n_dp
    shape = jax.ShapeDtypeStruct
    side, chunks, tile = shard // 2, 6, 512
    big_bufs, big_sems = GradSum.scratch(n_dp, chunks, side, tile)
    little_bufs, little_sems = GradSum.scratch(n_dp, 1, side, 128)
    vm = pltpu.VMEM
    args = (tokens, cotangent, hid_sum, gates_in, routes, parents, *tables, *saved)
    return pl.pallas_call(
        functools.partial(back_body, n_dp, n_exp, local),
        out_shape=[
            shape((tree, width), F32), shape((shard, width), F32), shape((shard, width), F32), shape((shard, width), F32),
            shape((shard, 128), F32),
        ],
        in_specs=[pl.BlockSpec(memory_space=VMEM)] * len(args),
        out_specs=[pl.BlockSpec(memory_space=VMEM)] * 5,
        scratch_shapes=[
            vm((tree, tree), F32), vm((tree, width), LOW), vm((tree, width), LOW), vm((tree, width), LOW), vm((tree, width), LOW),
            vm((tree, tile), LOW), vm((chunks, n_dp, 2, side, tile), LOW), vm((1, n_dp, 2, side, 128), LOW),
            *big_bufs, *big_sems, *little_bufs, *little_sems, vm((tree, width), F32),
        ],
        compiler_params=pltpu.CompilerParams(
            collective_id=collective_id, has_side_effects=True, vmem_limit_bytes=60 * MIB),
        name="back",
    )(*args)


def tree_layout(tree_rows):
    unit_rows = tree_rows // 20
    row_index = jnp.arange(tree_rows, dtype=jnp.int32)
    segment = jnp.where(
        row_index < 8 * unit_rows,
        0,
        jnp.where(
            row_index < 12 * unit_rows,
            1 + (row_index - 8 * unit_rows) // unit_rows,
            5 + (row_index - 12 * unit_rows) // unit_rows,
        ),
    )
    depth_start = jnp.where(segment == 0, 0, jnp.where(segment < 5, 8 * unit_rows, 9 * unit_rows))
    seg_start = jnp.where(
        segment == 0,
        0,
        jnp.where(
            segment < 5,
            8 * unit_rows + (segment - 1) * unit_rows,
            12 * unit_rows + (segment - 5) * unit_rows,
        ),
    )
    position = depth_start + row_index - seg_start
    return (segment, position)


def rope_tables(position):
    frequency = 10000.0 ** (-jnp.arange(0, HD, 2, dtype=jnp.float32) / HD)
    angles = position.astype(jnp.float32)[:, None] * frequency[None, :]
    return (jnp.concatenate([jnp.cos(angles)] * 2, -1), jnp.concatenate([jnp.sin(angles)] * 2, -1))


def gated_unit(gate_up):
    width_ff = gate_up.shape[-1] // 2
    gate_part = gate_up[..., :width_ff]
    return gate_part / (1.0 + jnp.exp(-gate_part)) * gate_up[..., width_ff:]


def experts_plain(
    n_dp, n_exp, hidden2, grad_y, routes_all, router_full, expert_in, expert_out, middle, collective_id
):
    tree_rows, width = hidden2.shape
    capacity = CAP
    routes_all = routes_all.transpose(0, 2, 1)
    expert_ids = jnp.arange(EXPERTS, dtype=jnp.int32)
    here = lax.axis_index("expert")
    local = expert_in.shape[0]
    first = here * local
    hidden_all = lax.all_gather(hidden2, "expert", axis=0, tiled=False)
    own_ids = first + jnp.arange(local, dtype=jnp.int32)
    hot_all = routes_all[:, :, :, None] == expert_ids[None, None, None, :]
    chosen_all = jnp.any(hot_all, axis=2)
    chosen = jnp.any(routes_all[:, :, :, None] == own_ids[None, None, None, :], axis=2)
    lower = jnp.tril(jnp.ones((tree_rows, tree_rows), jnp.bfloat16), -1)
    rank = jnp.einsum(
        "tu,jue->jet", lower, chosen.astype(jnp.bfloat16), preferred_element_type=jnp.float32
    ).astype(jnp.int32)
    slots = jnp.arange(capacity, dtype=jnp.int32)
    chosen_t = chosen.transpose(0, 2, 1)
    place = (rank[:, :, None, :] == slots[None, None, :, None]) & chosen_t[:, :, None, :]
    place = place.astype(jnp.bfloat16)
    logits_all = jnp.einsum(
        "jtd,de->jte", hidden_all, router_full, preferred_element_type=jnp.float32
    )
    masked = jnp.where(chosen_all, logits_all, -1e30)
    weight = jnp.exp(masked - jnp.max(masked, axis=-1, keepdims=True))
    weight = weight / jnp.sum(weight, axis=-1, keepdims=True)
    gates_own = lax.dynamic_slice_in_dim(weight, first, local, axis=2)
    gate_slot = jnp.einsum(
        "jest,jte->ejs", place.astype(jnp.float32), gates_own, precision=lax.Precision.HIGHEST
    )[..., None]
    sent = jnp.einsum("jest,jtd->ejsd", place, hidden_all, preferred_element_type=jnp.float32)
    sent = sent.astype(jnp.bfloat16)
    grad_rows = jnp.einsum("jest,jtd->ejsd", place, grad_y, preferred_element_type=jnp.float32)
    grad_rows = grad_rows.astype(jnp.bfloat16)
    gate_up = jnp.einsum("ejsd,edf->ejsf", sent, expert_in, preferred_element_type=jnp.float32)
    activated, glu_back = jax.vjp(gated_unit, gate_up)
    act_low = activated.astype(jnp.bfloat16).astype(jnp.float32)
    act_scaled = (act_low * gate_slot).astype(jnp.bfloat16)
    made = jnp.einsum(
        "ejsf,efd->ejsd", act_scaled, expert_out, preferred_element_type=jnp.float32
    ).astype(jnp.bfloat16)
    out_part = jnp.einsum("jest,ejsd->jtd", place, made, preferred_element_type=jnp.float32)
    out_sum = lax.psum_scatter(
        out_part.astype(jnp.bfloat16), "expert", scatter_dimension=0, tiled=False
    ).astype(jnp.float32)
    result = middle + out_sum
    block_out = result.astype(jnp.bfloat16)
    grad_act = jnp.einsum(
        "ejsd,efd->ejsf", grad_rows, expert_out, preferred_element_type=jnp.float32
    )
    gate_dot = jnp.sum(act_low * grad_act, axis=-1)
    gates_back = jnp.einsum(
        "jest,ejs->jte", place.astype(jnp.float32), gate_dot, precision=lax.Precision.HIGHEST
    )
    grad_out_w = jnp.einsum(
        "ejsf,ejsd->efd", act_scaled, grad_rows, preferred_element_type=jnp.float32
    )
    grad_gate_up = glu_back(grad_act * gate_slot)[0].astype(jnp.bfloat16)
    grad_sent = jnp.einsum(
        "ejsf,edf->ejsd", grad_gate_up, expert_in, preferred_element_type=jnp.float32
    ).astype(jnp.bfloat16)
    grad_in_w = jnp.einsum(
        "ejsd,ejsf->edf", sent, grad_gate_up, preferred_element_type=jnp.float32
    )
    hid_part = jnp.einsum("jest,ejsd->jtd", place, grad_sent, preferred_element_type=jnp.float32)
    gates_mine = lax.all_to_all(gates_back, "expert", split_axis=0, concat_axis=2, tiled=True)[0]
    hid_sum = lax.psum_scatter(
        hid_part.astype(jnp.bfloat16), "expert", scatter_dimension=0, tiled=False
    ).astype(jnp.float32)
    local, units = expert_in.shape[0], expert_out.shape[1]
    low = jnp.bfloat16
    grads = jnp.concatenate(
        [
            grad_in_w.astype(low).reshape(local, n_dp, width // n_dp, width),
            grad_out_w.astype(low).reshape(local, n_dp, units // n_dp, width),
        ],
        axis=2,
    ).reshape(local, width + units, width)
    share = lax.psum_scatter(grads, "dp", scatter_dimension=1, tiled=True).astype(jnp.float32)
    gates_mine = jnp.pad(gates_mine.T.reshape(n_exp, local, tree_rows), ((0, 0), (0, 8 - local), (0, 0)))
    return block_out, hid_sum, gates_mine, share[:, : width // n_dp], share[:, width // n_dp :]


def shards(
    tokens,
    attn_gain,
    w_query,
    w_keyval,
    w_output,
    moe_gain,
    w_router,
    expert_in,
    expert_out,
    cotangent,
    routes,
    parents,
):
    n_dp, n_exp = lax.axis_size("dp"), lax.axis_size("expert")
    local = expert_in.shape[0]
    tree_rows = tokens.shape[0]
    grad_y = lax.all_gather(cotangent, "expert", axis=0, tiled=False)
    _, position = tree_layout(tree_rows)
    tables = tuple(jnp.concatenate([table, table], axis=1) for table in rope_tables(position))
    (hidden, queries, keys, values, attended, middle, hidden2, log_total, *full, gains, routes_all) = front(
        n_dp, n_exp, tokens, attn_gain, moe_gain, w_router, w_query, w_keyval, w_output, routes.T, parents, tables, 1
    )
    run_experts = experts if (n_dp, n_exp) == (4, 8) else experts_plain
    block_out, hid_sum, gate_grads, expert_in_share, expert_out_share = run_experts(
        n_dp, n_exp, hidden2, grad_y, routes_all, full[3][:, :EXPERTS], expert_in, expert_out, middle, 2
    )
    saved = (hidden, queries, keys, values, attended, middle, hidden2, log_total, *full, gains)
    input_grad, grad_q, grad_kv, grad_o, grad_small = back(
        n_dp, n_exp, local, tokens, cotangent, hid_sum, gate_grads.reshape(n_exp * 8, tree_rows), routes, parents, tables, saved, 3
    )
    return (
        block_out,
        input_grad,
        grad_small[:, EXPERTS],
        grad_q,
        grad_kv,
        grad_o,
        grad_small[:, EXPERTS + 1],
        grad_small[:, :EXPERTS],
        expert_in_share,
        expert_out_share,
    )


def solution(mesh):
    in_specs = (
        P(("dp", "expert"), None),
        P("dp"),
        P("dp", None),
        P("dp", None),
        P("dp", None),
        P("dp"),
        P("dp", None),
        P("expert", None, None),
        P("expert", None, None),
        P(("dp", "expert"), None),
        P(("dp", "expert"), None),
        P(("dp", "expert"), None),
    )
    out_specs = (
        P(("dp", "expert"), None),
        P(("dp", "expert"), None),
        P("dp"),
        P("dp", None),
        P("dp", None),
        P("dp", None),
        P("dp"),
        P("dp", None),
        P("expert", "dp", None),
        P("expert", "dp", None),
    )
    return jax.shard_map(shards, mesh=mesh, in_specs=in_specs, out_specs=out_specs, check_vma=False)
```

```python
import functools

import jax
import jax.numpy as jnp
import numpy as np
from jax import lax
from jax.experimental import pallas as pl
from jax.experimental.pallas import tpu as pltpu
from jax.sharding import PartitionSpec as P

H = 16
KV = 8
HD = 64
EXPERTS = 32
TOPK = 8
CAP = 120


EPSILON = 1e-06


MESH = pl.DeviceIdType.MESH
MIB = 1024 * 1024
VMEM = pltpu.VMEM
ANY = pl.ANY


def remote(src, dst, send_sem, recv_sem, **where):
    return pltpu.make_async_remote_copy(
        src_ref=src, dst_ref=dst, send_sem=send_sem, recv_sem=recv_sem,
        device_id=where, device_id_type=MESH,
    )


def greet(partners):
    barrier = pltpu.get_barrier_semaphore()
    for condition, where in partners:
        def signal(where=where):
            pl.semaphore_signal(barrier, inc=1, device_id=where, device_id_type=MESH)
        if condition is None:
            signal()
        else:
            pl.when(condition)(signal)
    count = sum(1 if c is None else c.astype(jnp.int32) for c, _ in partners)
    pl.semaphore_wait(barrier, count)


def add_rows(out, *terms, step=16):
    rows = out.shape[0]

    def body(i, carry):
        at = pl.ds(pl.multiple_of(i * step, step), step)
        total = terms[0][at, :].astype(jnp.float32)
        for term in terms[1:]:
            total = total + term[at, :].astype(jnp.float32)
        out[at, :] = total.astype(out.dtype)
        return carry

    lax.fori_loop(0, rows // step, body, 0)


def bit_orders(n):
    bits = [1 << j for j in range(n.bit_length() - 1)]
    return [bits[p:] + bits[:p] for p in range(len(bits))] or [[]]


class Ring:
    def __init__(self, n_exp):
        self.mine = lax.axis_index("expert")
        self.core = lax.rem(self.mine, 2)
        self.z = lax.div(self.mine, 2)
        self.depth = n_exp // 2
        self.far = self.depth // 2
        self.pair = self.mine + 1 - 2 * self.core
        self.right, self.left = self.dev(1), self.dev(-1)

    def dev(self, d):
        return lax.rem(self.z + d + self.depth, self.depth) * 2 + self.core

    def partners(self):
        return [(None, {"expert": e}) for e in (self.pair, self.right, self.left)]


class RingGather:
    def __init__(self, ring, own, out, sems):
        self.ring, self.own, self.out = ring, own, out
        self.send, self.recv, self.pair_send, self.pair_recv = sems
        self.half = own.shape[0] // 2

    @staticmethod
    def scratch(n_exp):
        far, depth = n_exp // 4, n_exp // 2
        sem = pltpu.SemaphoreType.DMA
        return [sem((2, far + 1, 2)), sem((2, far + 1, 2)), sem((depth, 2)), sem((depth, 2))]

    def rows(self, h):
        return pl.ds(h * self.half, self.half)

    def goes(self, side, s, h):
        far = self.ring.far
        return s < far or (s == far and h == side)

    def block(self, d, h):
        return self.out.at[self.ring.dev(d), self.rows(h)]

    def hop(self, side, s, h):
        d = -s if side == 0 else s
        src = self.own.at[self.rows(h)] if s == 0 else self.block(d, h)
        to = self.ring.right if side == 0 else self.ring.left
        return remote(src, self.block(d, h), self.send.at[side, s, h], self.recv.at[side, s + 1, h], expert=to)

    def across(self, d, h):
        src = self.own.at[self.rows(h)] if d == 0 else self.block(d, h)
        slot = d % self.ring.depth
        return remote(src, self.block(d, h), self.pair_send.at[slot, h], self.pair_recv.at[slot, h], expert=self.ring.pair)

    ORDER = ((0, 0), (1, 1), (0, 1), (1, 0))

    def start(self):
        for side, h in self.ORDER:
            if self.goes(side, 1, h):
                self.hop(side, 0, h).start()
        self.across(0, 0).start()
        self.across(0, 1).start()

    def events(self):
        return [(side, s, h) for s in range(1, self.ring.far + 1) for side, h in self.ORDER if self.goes(side, s, h)]

    def handle(self, event):
        side, s, h = event
        d = -s if side == 0 else s
        here = self.block(d, h)
        remote(here, here, self.send.at[side, s, h], self.recv.at[side, s, h], expert=self.ring.mine).wait_recv()
        if self.goes(side, s + 1, h):
            self.hop(side, s, h).start()
        self.across(d, h).start()

    def wait_pair(self, d, h):
        slot = d % self.ring.depth
        here = self.out.at[self.ring.pair - self.ring.mine + self.ring.dev(d), self.rows(h)]
        remote(here, here, self.pair_send.at[slot, h], self.pair_recv.at[slot, h], expert=self.ring.mine).wait_recv()

    def finish_own(self):
        for side, h in self.ORDER:
            if self.goes(side, 1, h):
                self.hop(side, 0, h).wait_send()
        self.across(0, 0).wait_send()
        self.across(0, 1).wait_send()

    def finish_event(self, event):
        side, s, h = event
        if self.goes(side, s + 1, h):
            self.hop(side, s, h).wait_send()
        self.across(-s if side == 0 else s, h).wait_send()


class RingScatter:
    def __init__(self, ring, part, bufs, sems):
        self.ring, self.part = ring, part
        self.pair_buf, self.held, self.got = bufs
        self.pair_send, self.pair_recv, self.send, self.recv = sems
        self.half = self.held(0).shape[0] // 2

    @staticmethod
    def scratch(n_exp, block, dtype):
        far, depth = n_exp // 4, n_exp // 2
        sem = pltpu.SemaphoreType.DMA
        bufs = [pltpu.VMEM((depth,) + block, dtype), pltpu.VMEM((depth,) + block, dtype),
                pltpu.VMEM((2, far) + block, dtype)]
        return bufs, [sem((depth,)), sem((depth,)), sem((2, far + 1, 2)), sem((2, far + 1, 2))]

    def rows(self, h):
        return pl.ds(h * self.half, self.half)

    def order(self):
        far, depth = self.ring.far, self.ring.depth
        order = [far]
        for s in range(far - 1, 0, -1):
            order += [s, depth - s]
        return order + [0]

    def comes(self, side, d, h):
        far = self.ring.far
        return d + 1 < far or (d + 1 == far and h == side)

    def across(self, d):
        ring = self.ring
        return remote(self.part(ring.dev(d) + 1 - 2 * ring.core), self.pair_buf(d),
                      self.pair_send.at[d], self.pair_recv.at[d], expert=ring.pair)

    def start_pair(self, d):
        self.across(d).start()

    def wait_pair(self, d):
        self.across(d).wait_recv()

    def wait_got(self, side, d, h):
        here = self.got(side, d).at[self.rows(h)]
        remote(here, here, self.send.at[side, d, h], self.recv.at[side, d, h], expert=self.ring.mine).wait_recv()

    def hop(self, side, d, h):
        slot = d if side == 0 else self.ring.depth - d
        rows = self.rows(h)
        return remote(self.held(slot).at[rows], self.got(side, d - 1).at[rows], self.send.at[side, d, h],
                      self.recv.at[side, d - 1, h], expert=self.ring.right if side == 0 else self.ring.left)

    def push(self, side, d, h):
        ring = self.ring
        slot = d if side == 0 else ring.depth - d
        rows = self.rows(h)
        terms = [self.part(ring.dev(slot)).at[rows], self.pair_buf(slot).at[rows]]
        if self.comes(side, d, h):
            self.wait_got(side, d, h)
            terms.append(self.got(side, d).at[rows])
        add_rows(self.held(slot).at[rows], *terms)
        self.hop(side, d, h).start()

    def first(self):
        far = self.ring.far
        self.wait_pair(far)
        self.push(0, far, 0)
        self.push(1, far, 1)

    def early(self):
        for d in range(self.ring.far - 1, 0, -1):
            self.wait_pair(d)
            self.push(0, d, 1)
            self.wait_pair(self.ring.depth - d)
            self.push(1, d, 0)

    def late(self):
        for d in range(self.ring.far - 1, 0, -1):
            self.push(0, d, 0)
            self.push(1, d, 1)

    def last(self, out, *more):
        self.wait_pair(0)
        for h in range(2):
            rows = self.rows(h)
            terms = [self.part(self.ring.mine).at[rows], self.pair_buf(0).at[rows]] + [m.at[rows] for m in more]
            for side in range(2):
                if self.comes(side, 0, h):
                    self.wait_got(side, 0, h)
                    terms.append(self.got(side, 0).at[rows])
            add_rows(out.at[rows], *terms)

    def finish_sends(self):
        far = self.ring.far
        for side in range(2):
            for d in range(1, far + 1):
                for h in range(2):
                    if d < far or h == side:
                        self.hop(side, d, h).wait_send()
        for d in range(self.ring.depth):
            self.across(d).wait_send()


def views(bufs):
    pair_buf, held, got = bufs
    return (lambda d: pair_buf.at[d], lambda d: held.at[d], lambda side, d: got.at[side, d])


SLOTS = 128
F32, LOW = jnp.float32, jnp.bfloat16


def dot(a, b, over_a=1, over_b=0):
    return lax.dot_general(a, b, (((over_a,), (over_b,)), ((), ())), preferred_element_type=F32)


def experts_body(n_dp, n_exp, hid_ref, gy_hbm, routes_t, wr_t, w_in_hbm, w_out_hbm,
                 parts_hbm, hid_sum, gates_out, in_share, out_share, late,
                 x_all, w_in, w_out, sent, grows, gu, tmp, acts, stage, slots, gates, dots, wide,
                 pair_buf, held, got, *sems):
    w_sem, gy_sem, wide_sem, own_sem, part_sem, late_sem, gate_send, gate_recv, dp_ready, dp_send, dp_recv = sems[:11]
    gather_sems, hid_sems = sems[11:15], sems[15:19]
    me = lax.axis_index("dp")
    local, _, width = sent.shape
    tree, hidden_units = hid_ref.shape[0], w_out.shape[1]
    rows_e = local * SLOTS
    ring = Ring(n_exp)
    mine, core, depth = ring.mine, ring.core, ring.depth
    first = mine * local
    peers = [lax.rem(mine + k, n_exp) for k in range(1, n_exp)]
    greet([(None, {"expert": e}) for e in peers] + [(None, {"dp": me ^ bit}) for bit in (1, 2)])

    weights = [pltpu.make_async_copy(w_in_hbm, w_in, w_sem.at[0]), pltpu.make_async_copy(w_out_hbm, w_out, w_sem.at[1])]
    gather = RingGather(ring, hid_ref, x_all, gather_sems)
    gather.start()
    for copy in weights:
        copy.start()
    own = pltpu.make_async_copy(hid_ref, x_all.at[mine], own_sem)
    own.start()

    def gy_buf(j):
        return stage.at[lax.rem(j, 2), pl.ds(0, tree)]

    def gy_copy(j):
        return pltpu.make_async_copy(gy_hbm.at[j], gy_buf(j), gy_sem.at[lax.rem(j, 2)])

    gy_copy(0).start()

    below = (lax.broadcasted_iota(jnp.int32, (tree, tree), 0) < lax.broadcasted_iota(jnp.int32, (tree, tree), 1)).astype(LOW)
    sub16 = lax.broadcasted_iota(jnp.int32, (16, tree), 0)

    def find_slots(j, carry):
        names = routes_t[j]
        chosen = jnp.zeros((16, tree), F32)
        for k in range(names.shape[0]):
            chosen = jnp.maximum(chosen, jnp.where(names[k : k + 1, :] == first + sub16, 1.0, 0.0))
        chosen = jnp.where(sub16 < local, chosen, 0.0)
        rank = dot(chosen.astype(LOW), below)
        slots[j] = jnp.where(chosen > 0.5, rank, -1.0)[:8]
        return carry

    lax.fori_loop(0, n_exp, find_slots, 0)

    slot_ids = lax.broadcasted_iota(jnp.int32, (SLOTS, tree), 0).astype(F32)

    def places(j):
        return jnp.concatenate(
            [jnp.where(slot_ids == slots[j, i : i + 1, :], 1.0, 0.0).astype(LOW) for i in range(local)], axis=0)

    def places_t(j):
        lane = lax.broadcasted_iota(jnp.int32, (tree, 128), 1)
        pick = jnp.where(lax.broadcasted_iota(jnp.int32, (16, 128), 0) == lax.broadcasted_iota(jnp.int32, (16, 128), 1), 1.0, 0.0)
        slot = dot(jnp.concatenate([slots[j], jnp.zeros((8, tree), F32)], axis=0).astype(LOW), pick.astype(LOW), 0, 0)
        lanes = lane.astype(F32)
        return jnp.concatenate(
            [jnp.where(lanes == slot[:, i : i + 1], 1.0, 0.0).astype(LOW) for i in range(local)], axis=1)

    def find_gates(j):
        names = routes_t[j]
        experts = lax.broadcasted_iota(jnp.int32, (EXPERTS, tree), 0)
        chosen = jnp.zeros((EXPERTS, tree), F32)
        for k in range(names.shape[0]):
            chosen = jnp.maximum(chosen, jnp.where(names[k : k + 1, :] == experts, 1.0, 0.0))
        logits = jnp.where(chosen > 0.5, dot(wr_t[pl.ds(0, EXPERTS), :], x_all[j], 1, 1), -1e30)
        powers = jnp.exp(logits - jnp.max(logits, axis=0, keepdims=True))
        share = powers / jnp.sum(powers, axis=0, keepdims=True)
        sub = lax.broadcasted_iota(jnp.int32, (8, tree), 0)
        own_gates = jnp.zeros((8, tree), F32)
        for i in range(local):
            row = jnp.sum(jnp.where(experts == first + i, share, 0.0), axis=0, keepdims=True)
            own_gates = jnp.where(sub == i, row, own_gates)
        gates[j] = own_gates

    halves = width // 512

    def dispatch(j, src, dest):
        place = places(j)

        def body(n, carry):
            cols = pl.ds(pl.multiple_of(n * 512, 512), 512)
            picked = dot(place, src[:, cols]).astype(LOW)
            for i in range(local):
                dest[i, pl.ds(pl.multiple_of(j * SLOTS, SLOTS), SLOTS), cols] = picked[i * SLOTS : (i + 1) * SLOTS]
            return carry

        lax.fori_loop(0, halves, body, 0)

    def slot_gate(j, e):
        return jnp.sum(jnp.where(slot_ids == slots[j, pl.ds(e, 1), :], gates[j, pl.ds(e, 1), :], 0.0), axis=1, keepdims=True)

    def forward(chip):
        pair_rows = pl.ds(pl.multiple_of(chip * 2 * SLOTS, 2 * SLOTS), 2 * SLOTS)

        def one_tree(q, carry):
            j = 2 * chip + q
            find_gates(j)
            dispatch(j, x_all.at[j], sent)
            return carry

        lax.fori_loop(0, 2, one_tree, 0)

        def one_expert(e, carry):
            both = dot(sent[e, pair_rows, :], w_in[e])
            gu[e, pair_rows, :] = both.astype(LOW)
            a, b = both[:, :hidden_units], both[:, hidden_units:]
            act = (a / (1.0 + jnp.exp(-a)) * b).astype(LOW).astype(F32)
            gate = jnp.concatenate([slot_gate(2 * chip, e), slot_gate(2 * chip + 1, e)], axis=0)
            made = dot((act * gate).astype(LOW), w_out[e]).astype(LOW)
            for q in range(2):
                tmp[pl.ds(pl.multiple_of(q * rows_e + e * SLOTS, SLOTS), SLOTS), :] = made[q * SLOTS : (q + 1) * SLOTS]
            return carry

        lax.fori_loop(0, local, one_expert, 0)

    def part_copy(j):
        return pltpu.make_async_copy(x_all.at[j], parts_hbm.at[j], part_sem.at[j])

    def combine_out(chip):
        def one_tree(q, carry):
            j = 2 * chip + q
            rows = pl.ds(pl.multiple_of(q * rows_e, rows_e), rows_e)
            x_all[j] = dot(places_t(j), tmp[rows, :]).astype(LOW)
            part_copy(j).start()
            return carry

        lax.fori_loop(0, 2, one_tree, 0)

    def grad_rows(j, carry):
        pl.when(j + 1 < n_exp)(lambda: gy_copy(j + 1).start())
        gy_copy(j).wait()
        dispatch(j, gy_buf(j), grows)
        return carry

    events = gather.events()

    def chip_at(d):
        return lax.rem(ring.z + d, depth)

    def group(g, carry):
        d = jnp.where(g == 0, 0, jnp.where(g == 1, depth - 1, jnp.where(g == 2, 1, 2)))
        chip = chip_at(d)

        @pl.when(g == 0)
        def _():
            own.wait()
            gather.wait_pair(0, 0)
            gather.wait_pair(0, 1)
            for copy in weights:
                copy.wait()

        @pl.when(g == 1)
        def _():
            for event in events[:4]:
                gather.handle(event)
            gather.wait_pair(-1, 0)
            gather.wait_pair(-1, 1)

        @pl.when(g == 2)
        def _():
            gather.wait_pair(1, 0)
            gather.wait_pair(1, 1)

        @pl.when(g == 3)
        def _():
            for event in events[4:]:
                gather.handle(event)
            gather.wait_pair(2, 0)
            gather.wait_pair(2, 1)

        forward(chip)

        @pl.when(g == 0)
        def _():
            gather.finish_own()
            lax.fori_loop(0, n_exp, grad_rows, 0)

        for at, d in ((1, -1), (2, 1), (3, 2)):
            @pl.when(g == at)
            def _():
                for event in events:
                    if event[1] == abs(d) and (abs(d) == 2 or (event[0] == 0) == (d < 0)):
                        gather.finish_event(event)

        combine_out(chip)
        return carry

    lax.fori_loop(0, depth, group, 0)

    in_rows, out_rows = width // n_dp, hidden_units // n_dp
    cut = (in_rows + out_rows) // 2

    def grad_half(e, r, h):
        at = 2 * r + h
        return gu.at[e, pl.ds(at * cut, cut)] if at < 5 else stage.at[e, pl.ds((at - 5) * cut, cut)]

    def grad_land(e, k):
        return w_in.at[e, pl.ds(k * cut, cut)] if k < 5 else w_out.at[e, pl.ds(0, cut)]

    def grad_hop(e, step, h, which):
        bit = (1, 2)[h] if step == 0 else (2, 1)[h]
        r = bit if which == 0 else 3
        k = 2 * h + which if step == 0 else 4 + h
        return remote(grad_half(e, r, h), grad_land(e, k), dp_send.at[e, k], dp_recv.at[e, k], dp=me ^ bit)

    def grads_start(e):
        pl.semaphore_wait(dp_ready.at[e], 2)
        for which in (1, 0):
            for h in range(2):
                grad_hop(e, 0, h, which).start()

    def grads_turn(e):
        for which in (1, 0):
            for h in range(2):
                grad_hop(e, 0, h, which).wait_recv()
                kept = 0 if which == 0 else (2, 1)[h]
                add_rows(grad_half(e, kept, h), grad_half(e, kept, h), grad_land(e, 2 * h + which))
                if which == 1:
                    grad_hop(e, 1, h, 0).start()

    def wide_copies(e):
        return (
            pltpu.make_async_copy(wide.at[pl.ds(0, in_rows)], in_share.at[e], wide_sem.at[0]),
            pltpu.make_async_copy(wide.at[pl.ds(in_rows, out_rows)], out_share.at[e], wide_sem.at[1]),
        )

    def grads_end(e):
        for h in range(2):
            grad_hop(e, 1, h, 0).wait_recv()
            add_rows(wide.at[pl.ds(h * cut, cut)], grad_half(e, 0, h), grad_land(e, 4 + h))
        for copy in wide_copies(e):
            copy.start()
        for step, h, which in ((0, 0, 0), (0, 0, 1), (0, 1, 0), (0, 1, 1), (1, 0, 0), (1, 1, 0)):
            grad_hop(e, step, h, which).wait_send()
        for copy in wide_copies(e):
            copy.wait()

    block = 4 * SLOTS
    sub8 = lax.broadcasted_iota(jnp.int32, (8, tree), 0)

    def backward(e, carry):
        def one_block(m, inner):
            rows = pl.ds(pl.multiple_of(m * block, block), block)
            grad_act = dot(grows[e, rows, :], w_out[e], 1, 1)
            a = gu[e, rows, pl.ds(0, hidden_units)].astype(F32)
            b = gu[e, rows, pl.ds(hidden_units, hidden_units)].astype(F32)
            sg = 1.0 / (1.0 + jnp.exp(-a))
            sw = a * sg
            act = (sw * b).astype(LOW).astype(F32)
            gate = jnp.concatenate([slot_gate(4 * m + q, e) for q in range(4)], axis=0)
            told = jnp.sum(act * grad_act, axis=1, keepdims=True)
            acts[rows, :] = (act * gate).astype(LOW)
            grad_act = grad_act * gate
            tmp[rows, pl.ds(0, hidden_units)] = (grad_act * b * sg * (1.0 + a * (1.0 - sg))).astype(LOW)
            tmp[rows, pl.ds(hidden_units, hidden_units)] = (grad_act * sw).astype(LOW)
            for q in range(4):
                j = 4 * m + q
                row = jnp.sum(
                    jnp.where(slot_ids == slots[j, pl.ds(e, 1), :], told[q * SLOTS : (q + 1) * SLOTS], 0.0),
                    axis=0, keepdims=True)
                dots[j] = jnp.where(sub8 == e, row, dots[j])
            return inner

        lax.fori_loop(0, n_exp // 4, one_block, 0)
        pl.when(e > 0)(lambda: grads_start(e - 1))
        for r in range(n_dp):
            d = me ^ r
            grad_in = dot(sent[e, :, pl.ds(pl.multiple_of(d * in_rows, in_rows), in_rows)], tmp[...], 0, 0).astype(LOW)
            grad_out = dot(acts[:, pl.ds(pl.multiple_of(d * out_rows, out_rows), out_rows)], grows[e], 0, 0).astype(LOW)
            grad_half(e, r, 0)[...] = grad_in[:cut]
            half = grad_half(e, r, 1)
            half[pl.ds(0, in_rows - cut), :] = grad_in[cut:]
            half[pl.ds(in_rows - cut, out_rows), :] = grad_out

        def back_half(m, inner):
            rows = pl.ds(pl.multiple_of(m * 512, 512), 512)
            sent[e, rows, :] = dot(tmp[rows, :], w_in[e], 1, 1).astype(LOW)
            return inner

        lax.fori_loop(0, n_exp * SLOTS // 512, back_half, 0)
        @pl.when(e < local - 1)
        def _():
            for bit in (1, 2):
                pl.semaphore_signal(dp_ready.at[e], inc=1, device_id={"dp": me ^ bit}, device_id_type=MESH)

        pl.when(e >= 2)(lambda: grads_turn(e - 2))
        return carry

    dots[...] = jnp.zeros(dots.shape, F32)
    lax.fori_loop(0, local, backward, 0)

    def late_copy(r, h):
        at = pl.multiple_of((me ^ r) * 2 * cut + h * cut, 16)
        return pltpu.make_async_copy(grad_half(local - 1, r, h), late.at[pl.ds(at, cut)], late_sem.at[2 * r + h])

    for r in range(n_dp):
        for h in range(2):
            late_copy(r, h).start()

    gate_copies = []
    for k, e in enumerate(peers):
        copy = remote(dots.at[e], gates_out.at[mine], gate_send.at[k], gate_recv.at[k], expert=e)
        copy.start()
        gate_copies.append(copy)
    gates_out[mine] = dots[mine]
    for j in range(n_exp):
        part_copy(j).wait()
    hid = RingScatter(ring, lambda e: x_all.at[e], views((pair_buf, held, got)), hid_sems)

    def combine_hid(g, carry):
        d = jnp.where(g == 0, 2, jnp.where(g == 1, 1, jnp.where(g == 2, depth - 1, 0)))
        chip = chip_at(d)

        def one_tree(q, inner):
            j = 2 * chip + q
            rows = pl.ds(pl.multiple_of(j * SLOTS, SLOTS), SLOTS)
            made = jnp.concatenate([sent[i, rows, :] for i in range(local)], axis=0)
            x_all[j] = dot(places_t(j), made).astype(LOW)
            return inner

        lax.fori_loop(0, 2, one_tree, 0)

        pl.when(g == 0)(lambda: hid.start_pair(2))
        pl.when(g == 1)(lambda: hid.start_pair(1))
        pl.when(g == 2)(lambda: hid.start_pair(depth - 1))
        pl.when(g == 3)(lambda: hid.start_pair(0))
        pl.when(g == 1)(hid.first)
        return carry

    lax.fori_loop(0, depth, combine_hid, 0)
    hid.early()
    grads_end(0)
    grads_turn(local - 2)
    hid.late()
    grads_end(1)
    hid.last(wide.at[pl.ds(0, tree)])
    hid_copy = pltpu.make_async_copy(wide.at[pl.ds(0, tree)], hid_sum, wide_sem.at[0])
    hid_copy.start()
    hid_copy.wait()
    for e in range(2, local - 1):
        grads_end(e)
    for r in range(n_dp):
        for h in range(2):
            late_copy(r, h).wait()
    for k, copy in enumerate(gate_copies):
        copy.wait_send()
        source = lax.rem(mine + n_exp - 1 - k, n_exp)
        remote(dots.at[mine], gates_out.at[source], gate_send.at[k], gate_recv.at[k], expert=mine).wait_recv()
    hid.finish_sends()


def experts(n_dp, n_exp, hidden2, grad_y, routes_all, router_t, expert_in, expert_out, collective_id):
    local, width, both = expert_in.shape
    units = expert_out.shape[1]
    tree = hidden2.shape[0]
    rows = n_exp * SLOTS
    sem = pltpu.SemaphoreType.DMA
    bufs, hid_sems = RingScatter.scratch(n_exp, (tree, width), LOW)
    shape = jax.ShapeDtypeStruct
    return pl.pallas_call(
        functools.partial(experts_body, n_dp, n_exp),
        out_shape=[
            shape((n_exp, tree, width), LOW),
            shape((tree, width), F32),
            shape((n_exp, 8, tree), F32),
            shape((local - 1, width // n_dp, width), F32),
            shape((local - 1, units // n_dp, width), F32),
            shape((width + units, width), LOW),
        ],
        in_specs=[pl.BlockSpec(memory_space=s) for s in (VMEM, ANY, VMEM, VMEM, ANY, ANY)],
        out_specs=[pl.BlockSpec(memory_space=s) for s in (ANY, ANY, VMEM, ANY, ANY, ANY)],
        scratch_shapes=[
            pltpu.VMEM((n_exp, tree, width), LOW),
            pltpu.VMEM((local, width, both), LOW),
            pltpu.VMEM((local, units, width), LOW),
            pltpu.VMEM((local, rows, width), LOW),
            pltpu.VMEM((local, rows, width), LOW),
            pltpu.VMEM((local, rows, both), LOW),
            pltpu.VMEM((max(rows, 2 * local * SLOTS), width), LOW),
            pltpu.VMEM((rows, units), LOW),
            pltpu.VMEM((local, 3 * (width + units) // (2 * n_dp), width), LOW),
            pltpu.VMEM((n_exp, 8, tree), F32),
            pltpu.VMEM((n_exp, 8, tree), F32),
            pltpu.VMEM((n_exp, 8, tree), F32),
            pltpu.VMEM(((width + units) // n_dp, width), F32),
            *bufs,
            sem((2,)), sem((2,)), sem((2,)), sem, sem((n_exp,)), sem((2 * n_dp,)), sem((n_exp - 1,)), sem((n_exp - 1,)),
            pltpu.SemaphoreType.REGULAR((local,)), sem((local, 6)), sem((local, 6)),
            *RingGather.scratch(n_exp), *hid_sems,
        ],
        compiler_params=pltpu.CompilerParams(
            collective_id=collective_id, has_side_effects=True, vmem_limit_bytes=63 * MIB),
        name="experts",
    )(hidden2, grad_y, routes_all, router_t, expert_in, expert_out)


def lanes_of(shape):
    return lax.broadcasted_iota(jnp.int32, shape, 1)


def turned(field):
    low_half = lax.rem(lanes_of(field.shape), HD) < HD // 2
    return jnp.where(low_half, -pltpu.roll(field, 128 - HD // 2, 1), pltpu.roll(field, HD // 2, 1))


def mask_bias(parents, tree):
    unit = tree // 20

    def segment(row):
        return jnp.where(row < 8 * unit, 0, jnp.where(row < 12 * unit, 1 + lax.div(row - 8 * unit, unit), 5 + lax.div(row - 12 * unit, unit)))

    count = parents.shape[1]
    names = parents[...].astype(F32)
    wide = (tree, count)
    seg = segment(lax.broadcasted_iota(jnp.int32, wide, 0)).astype(F32)
    lane = lanes_of(wide).astype(F32)
    own = seg[:, :1]
    parent = jnp.sum(jnp.where(lane == seg, names, 0.0), axis=1, keepdims=True)
    grand = jnp.sum(jnp.where(lane == parent, names, 0.0), axis=1, keepdims=True)
    square = (tree, tree)
    row, col = lax.broadcasted_iota(jnp.int32, square, 0), lanes_of(square)
    there = segment(col).astype(F32)
    hit = jnp.maximum(
        jnp.maximum(jnp.where(there == own, 1.0, 0.0), jnp.where(there == parent, 1.0, 0.0)), jnp.where(there == grand, 1.0, 0.0))
    hit = jnp.where(col <= row, hit, 0.0)
    return jnp.where(hit > 0.5, 0.0, -1e30)


def inverse_rms(field):
    return lax.rsqrt(jnp.mean(field * field, axis=-1, keepdims=True) + EPSILON)


class DpGather:
    def __init__(self, n_dp, mine, me, ins, outs, sems):
        self.n_dp, self.me, self.ins, self.outs = n_dp, me, ins, outs
        self.send, self.recv, self.pair_send, self.pair_recv, self.own_sem = sems
        self.core = lax.rem(mine, 2)
        self.pair = mine + 1 - 2 * self.core
        self.shard = ins[0].shape[0]
        half = self.shard // 2
        self.orders = bit_orders(n_dp)
        self.cuts = min(2, len(self.orders), half // 16)
        self.size = half // self.cuts

    @staticmethod
    def scratch(count, n_dp):
        sem = pltpu.SemaphoreType.DMA
        bits = max(1, n_dp.bit_length() - 1)
        return [sem((count, 2, n_dp, bits)), sem((count, 2, n_dp)), sem((count, 2, n_dp)), sem((count, 2, n_dp)), sem((count,))]

    def rows(self, start, side, p):
        return pl.ds(pl.multiple_of(start + side * (self.shard // 2) + p * self.size, 16), self.size)

    def hop(self, a, p, r, bit):
        there = self.outs[a].at[self.rows((self.me ^ r) * self.shard, self.core, p)]
        src = self.ins[a].at[self.rows(0, self.core, p)] if r == 0 else there
        return remote(src, there, self.send.at[a, p, r, bit.bit_length() - 1], self.recv.at[a, p, r ^ bit], dp=self.me ^ bit)

    def own(self, a):
        at = pl.ds(pl.multiple_of(self.me * self.shard, 16), self.shard)
        return pltpu.make_async_copy(self.ins[a], self.outs[a].at[at], self.own_sem.at[a])

    def across(self, a, p, r, side):
        here = self.outs[a].at[self.rows((self.me ^ r) * self.shard, side, p)]
        return remote(here, here, self.pair_send.at[a, p, r], self.pair_recv.at[a, p, r], expert=self.pair)

    def start(self, a):
        for p in range(self.cuts):
            for bit in self.orders[p]:
                self.hop(a, p, 0, bit).start()
        self.own(a).start()

    def stage(self, p, j):
        order = self.orders[p]
        blocks = [0]
        for bit in order[:j]:
            blocks = blocks + [r | bit for r in blocks]
        return [r | order[j] for r in blocks], order[j + 1 :]

    def turn(self, a, j):
        for p in range(self.cuts):
            blocks, onward = self.stage(p, j)
            for r in blocks:
                here = self.outs[a].at[self.rows((self.me ^ r) * self.shard, self.core, p)]
                remote(here, here, self.send.at[a, p, r, 0], self.recv.at[a, p, r], dp=self.me).wait_recv()
                for bit in onward:
                    self.hop(a, p, r, bit).start()
                self.across(a, p, r, self.core).start()

    def ready(self, a):
        self.own(a).wait()
        for p in range(self.cuts):
            for r in range(1, self.n_dp):
                self.across(a, p, r, 1 - self.core).wait_recv()

    def finish(self, a):
        for p in range(self.cuts):
            for bit in self.orders[p]:
                self.hop(a, p, 0, bit).wait_send()
            for j in range(len(self.orders[p])):
                blocks, onward = self.stage(p, j)
                for r in blocks:
                    for bit in onward:
                        self.hop(a, p, r, bit).wait_send()
                    self.across(a, p, r, self.core).wait_send()


def front_body(n_dp, n_exp, x_ref, gain_pair, router_in, w_query, w_keyval, w_output, routes_t, parents, cosine, sine,
               hidden_hbm, queries_hbm, keys_hbm, values_hbm, attended, middle, hidden2, log_total,
               query_hbm, keyval_hbm, output_hbm, router_t, gains, routes_all,
               hidden, queries, keys, values, query_full, keyval_full, output_full, small, small_all, bias, *sems):
    gather_sems, (small_send, small_recv, route_send, route_recv, out_sem) = sems[:5], sems[5:10]
    me, mine = lax.axis_index("dp"), lax.axis_index("expert")
    peers = [lax.rem(mine + k, n_exp) for k in range(1, n_exp)]
    greet([(None, {"expert": e}) for e in peers] + [(None, {"dp": me ^ k}) for k in range(1, n_dp)])
    tree, width = x_ref.shape
    shard = w_query.shape[0]

    small[...] = jnp.zeros(small.shape, LOW)
    small[pl.ds(0, EXPERTS), :] = router_in[...]
    sub = lax.broadcasted_iota(jnp.int32, (16, shard), 0)
    gain_rows = gain_pair[...].astype(F32)
    small[pl.ds(EXPERTS, 16), :] = jnp.where(sub == 0, gain_rows[:1], jnp.where(sub == 1, gain_rows[1:], 0.0)).astype(LOW)

    gather = DpGather(n_dp, mine, me, (w_query, w_keyval, w_output), (query_full, keyval_full, output_full), gather_sems)

    def small_copy(k):
        return remote(small, small_all.at[me], small_send.at[k], small_recv.at[k], dp=me ^ k)

    def route_copy(k, e):
        return remote(routes_t, routes_all.at[mine], route_send.at[k], route_recv.at[k], expert=e)

    saves = [
        pltpu.make_async_copy(src, dst, out_sem.at[k])
        for k, (src, dst) in enumerate((
            (query_full, query_hbm), (keyval_full, keyval_hbm), (output_full, output_hbm), (hidden, hidden_hbm),
            (queries, queries_hbm), (keys, keys_hbm), (values, values_hbm)))
    ]
    for k in range(1, n_dp):
        small_copy(k).start()
    gather.start(0)
    gather.start(1)
    for k, e in enumerate(peers):
        route_copy(k, e).start()
    small_all[me] = small[...]
    routes_all[mine] = routes_t[...]
    bias[...] = mask_bias(parents, tree)
    log_total[...] = jnp.zeros(log_total.shape, F32)
    x = x_ref[...].astype(F32)
    scaled = x * inverse_rms(x)
    for k in range(1, n_dp):
        remote(small, small_all.at[me ^ k], small_send.at[k], small_recv.at[k], dp=me).wait_recv()
    joined = jnp.concatenate([small_all[d] for d in range(n_dp)], axis=1)
    router_t[...] = jnp.zeros(router_t.shape, LOW)
    router_t[pl.ds(0, EXPERTS), :] = joined[:EXPERTS]
    gains[...] = joined[EXPERTS:]
    gain_rows = joined[EXPERTS:].astype(F32)
    hidden[...] = (scaled * gain_rows[:1]).astype(LOW)
    saves[3].start()
    stages = len(gather.orders[0])
    for j in range(stages - 1):
        gather.turn(0, j)
        gather.turn(1, j)
    gather.start(2)
    gather.turn(0, stages - 1)
    gather.turn(1, stages - 1)
    gather.ready(0)
    saves[0].start()

    def rotate(field):
        return field * cosine[...] + turned(field) * sine[...]

    left = lanes_of((tree, 128)) < HD
    tile = 512

    def query_tile(n, carry):
        cols = pl.ds(pl.multiple_of(n * tile, tile), tile)
        pre = dot(hidden[...], query_full[:, cols])
        for i in range(tile // 128):
            at = pl.multiple_of(n * tile + i * 128, 128)
            queries[:, pl.ds(at, 128)] = rotate(pre[:, i * 128 : (i + 1) * 128]).astype(LOW)
        return carry

    lax.fori_loop(0, width // tile, query_tile, 0)
    saves[4].start()
    gather.ready(1)
    saves[1].start()

    def spread(field, out, i):
        other = pltpu.roll(field, HD, 1)
        out[2 * i] = jnp.where(left, field, other).astype(LOW)
        out[2 * i + 1] = jnp.where(left, other, field).astype(LOW)

    half = KV * HD
    pre = dot(hidden[...], keyval_full[:, pl.ds(0, half)])
    for i in range(half // 128):
        spread(rotate(pre[:, i * 128 : (i + 1) * 128]), keys, i)
    saves[5].start()
    pre = dot(hidden[...], keyval_full[:, pl.ds(half, half)])
    for i in range(half // 128):
        spread(pre[:, i * 128 : (i + 1) * 128], values, i)
    saves[6].start()
    for j in range(stages):
        gather.turn(2, j)

    def heads(c, carry):
        cols = pl.ds(pl.multiple_of(c * 128, 128), 128)
        pair = queries[:, cols]
        made = []
        for h in range(2):
            mine_lanes = left if h == 0 else jnp.logical_not(left)
            query = jnp.where(mine_lanes, pair, jnp.zeros_like(pair))
            scores = dot(query, keys[c], 1, 1) * HD**-0.5 + bias[...]
            top = jnp.max(scores, axis=1, keepdims=True)
            powers = jnp.exp(scores - top)
            total = jnp.sum(powers, axis=1, keepdims=True)
            made.append(dot((powers / total).astype(LOW), values[c]))
            log_total[...] = jnp.where(lanes_of((tree, 128)) == 2 * c + h, top + jnp.log(total), log_total[...])
        attended[:, cols] = jnp.where(left, made[0], made[1]).astype(LOW)
        return carry

    lax.fori_loop(0, KV, heads, 0)
    gather.ready(2)
    saves[2].start()

    def middle_tile(n, carry):
        cols = pl.ds(pl.multiple_of(n * tile, tile), tile)
        middle[:, cols] = x_ref[:, cols].astype(F32) + dot(attended[...], output_full[:, cols])
        return carry

    lax.fori_loop(0, width // tile, middle_tile, 0)
    field = middle[...]
    hidden2[...] = (field * inverse_rms(field) * gain_rows[1:2]).astype(LOW)
    for a in range(3):
        gather.finish(a)
    for k in range(1, n_dp):
        small_copy(k).wait_send()
    for k, e in enumerate(peers):
        route_copy(k, e).wait_send()
        source = lax.rem(mine + n_exp - 1 - k, n_exp)
        remote(routes_t, routes_all.at[source], route_send.at[k], route_recv.at[k], expert=mine).wait_recv()
    for copy in saves:
        copy.wait()


def front(n_dp, n_exp, tokens, gain_pair, router_in, w_query, w_keyval, w_output, routes_t, parents, tables, collective_id):
    tree, width = tokens.shape
    shard = w_query.shape[0]
    shape, sem, vm = jax.ShapeDtypeStruct, pltpu.SemaphoreType.DMA, pltpu.VMEM
    low = shape((tree, width), LOW)
    spread = shape((KV, tree, 128), LOW)
    full = shape((n_dp * shard, width), LOW)
    small = (EXPERTS + 16, shard)
    return pl.pallas_call(
        functools.partial(front_body, n_dp, n_exp),
        out_shape=[
            low, low, spread, spread, low, shape((tree, width), F32), low, shape((tree, 128), F32),
            full, full, full, shape((128, width), LOW), shape((16, width), LOW),
            shape((n_exp,) + routes_t.shape, jnp.int32),
        ],
        in_specs=[pl.BlockSpec(memory_space=VMEM)] * 10,
        out_specs=[pl.BlockSpec(memory_space=s) for s in [ANY] * 4 + [VMEM] * 4 + [ANY] * 3 + [VMEM] * 3],
        scratch_shapes=[
            vm((tree, width), LOW), vm((tree, width), LOW), vm(spread.shape, LOW), vm(spread.shape, LOW),
            vm(full.shape, LOW), vm(full.shape, LOW), vm(full.shape, LOW),
            vm(small, LOW), vm((n_dp,) + small, LOW), vm((tree, tree), F32),
            *DpGather.scratch(3, n_dp), sem((n_dp,)), sem((n_dp,)), sem((n_exp - 1,)), sem((n_exp - 1,)), sem((7,)),
        ],
        compiler_params=pltpu.CompilerParams(
            collective_id=collective_id, has_side_effects=True, vmem_limit_bytes=56 * MIB),
        name="front",
    )(tokens, gain_pair, router_in, w_query, w_keyval, w_output, routes_t, parents, *tables)


class GradSum:
    def __init__(self, n_dp, n_exp, chunks, own, bufs, sems):
        self.n_dp, self.chunks, self.own = n_dp, chunks, own
        (self.pair_in, self.dp_in, self.prefix, self.suffix, self.go_r, self.go_l, self.final, self.other) = bufs
        (self.pair_send, self.pair_recv, self.dp_send, self.dp_recv,
         self.send_r, self.send_l, self.recv_r, self.recv_l, self.last_send, self.last_recv) = sems
        self.me, self.mine = lax.axis_index("dp"), lax.axis_index("expert")
        self.core = lax.rem(self.mine, 2)
        self.z = lax.div(self.mine, 2)
        self.depth = n_exp // 2
        self.pair = self.mine + 1 - 2 * self.core
        self.has_left, self.has_right = self.z > 0, self.z < self.depth - 1
        self.orders = bit_orders(n_dp)

    @staticmethod
    def scratch(n_dp, chunks, half, columns):
        sem = pltpu.SemaphoreType.DMA
        stages = max(1, n_dp.bit_length() - 1)
        one = pltpu.VMEM((chunks, half, columns), LOW)
        many = pltpu.VMEM((chunks, n_dp, half, columns), LOW)
        bufs = [many, many, one, one, one, one, one, one]
        sems = [sem((chunks, n_dp)), sem((chunks, n_dp)), sem((chunks, n_dp)), sem((chunks, n_dp))]
        return bufs, sems + [sem((chunks,))] * 6

    def partners(self):
        return [(None, {"dp": self.me ^ bit}) for bit in self.orders[0]] + [
            (self.has_left, {"expert": self.mine - 2}), (self.has_right, {"expert": self.mine + 2})]

    def total(self, i, r):
        return self.own.at[i, self.me ^ r, self.core]

    def across(self, i, d):
        return remote(self.own.at[i, d, 1 - self.core], self.pair_in.at[i, d], self.pair_send.at[i, d],
                      self.pair_recv.at[i, d], expert=self.pair)

    def moved(self, i, j):
        order = self.orders[i % len(self.orders)]
        blocks = [0]
        for bit in order[j + 1 :]:
            blocks = blocks + [r | bit for r in blocks]
        return order[j], [r | order[j] for r in blocks]

    def dp_copy(self, i, r, bit):
        return remote(self.total(i, r), self.dp_in.at[i, r], self.dp_send.at[i, r], self.dp_recv.at[i, r], dp=self.me ^ bit)

    def start(self, i):
        for d in range(self.n_dp):
            self.across(i, d).start()

    def paired(self, i):
        for r in range(self.n_dp - 1, -1, -1):
            d = self.me ^ r
            self.across(i, d).wait_recv()
            add_rows(self.total(i, r), self.total(i, r), self.pair_in.at[i, d])
        self.leave(i, 0)

    def leave(self, i, j):
        if j < len(self.orders[0]):
            bit, blocks = self.moved(i, j)
            for r in blocks:
                self.dp_copy(i, r, bit).start()

    def met(self, i, j):
        bit, blocks = self.moved(i, j)
        for r in blocks:
            self.dp_copy(i, r, bit).wait_recv()
            add_rows(self.total(i, r ^ bit), self.total(i, r ^ bit), self.dp_in.at[i, r])
        self.leave(i, j + 1)

    def right(self, i):
        return remote(self.go_r.at[i], self.prefix.at[i], self.send_r.at[i], self.recv_r.at[i], expert=self.mine + 2)

    def left(self, i):
        return remote(self.go_l.at[i], self.suffix.at[i], self.send_l.at[i], self.recv_l.at[i], expert=self.mine - 2)

    def line(self, t):
        i = t - 2 * self.z
        has_left, has_right = self.has_left, self.has_right

        @pl.when(jnp.logical_and(i >= 0, i < self.chunks))
        def _():
            @pl.when(has_left)
            def _():
                remote(self.go_r.at[i], self.prefix.at[i], self.send_r.at[i], self.recv_r.at[i], expert=self.mine).wait_recv()

            @pl.when(jnp.logical_and(has_left, has_right))
            def _():
                add_rows(self.go_r.at[i], self.total(i, 0), self.prefix.at[i])

            @pl.when(jnp.logical_not(has_left))
            def _():
                add_rows(self.go_r.at[i], self.total(i, 0))

            pl.when(has_right)(lambda: self.right(i).start())

        k = t - 2 * (self.depth - 1 - self.z)

        @pl.when(jnp.logical_and(k >= 0, k < self.chunks))
        def _():
            @pl.when(has_right)
            def _():
                remote(self.go_l.at[k], self.suffix.at[k], self.send_l.at[k], self.recv_l.at[k], expert=self.mine).wait_recv()

            @pl.when(jnp.logical_and(has_left, has_right))
            def _():
                add_rows(self.go_l.at[k], self.total(k, 0), self.suffix.at[k])

            @pl.when(jnp.logical_not(has_right))
            def _():
                add_rows(self.go_l.at[k], self.total(k, 0))

            pl.when(has_left)(lambda: self.left(k).start())

    def last(self, i):
        return remote(self.final.at[i], self.other.at[i], self.last_send.at[i], self.last_recv.at[i], expert=self.pair)

    def close(self, i):
        has_left, has_right = self.has_left, self.has_right

        @pl.when(jnp.logical_and(has_left, has_right))
        def _():
            add_rows(self.final.at[i], self.total(i, 0), self.prefix.at[i], self.suffix.at[i])

        @pl.when(jnp.logical_not(has_left))
        def _():
            add_rows(self.final.at[i], self.total(i, 0), self.suffix.at[i])

        @pl.when(jnp.logical_not(has_right))
        def _():
            add_rows(self.final.at[i], self.total(i, 0), self.prefix.at[i])

        self.last(i).start()

    def finish(self, i):
        self.last(i).wait_send()
        pl.when(self.has_right)(lambda: self.right(i).wait_send())
        pl.when(self.has_left)(lambda: self.left(i).wait_send())
        for d in range(self.n_dp):
            self.across(i, d).wait_send()
        for j in range(len(self.orders[0])):
            bit, blocks = self.moved(i, j)
            for r in blocks:
                self.dp_copy(i, r, bit).wait_send()


def two_parts(field):
    high = field.astype(LOW)
    return high, (field - high.astype(F32)).astype(LOW)


def norm_back(field, gain, grad):
    r = inverse_rms(field)
    scaled = grad * gain
    back = r * scaled - field * (r * r * r) * jnp.mean(field * scaled, axis=-1, keepdims=True)
    return back, jnp.sum(field * r * grad, axis=0, keepdims=True)


def back_body(n_dp, n_exp, local, with_out, x_ref, cot, hid_sum, gates_in, routes_t, parents, cosine, sine,
              hidden, queries, keys, values, attended, middle, hidden2, log_total,
              query_hbm, keyval_hbm, output_hbm, router_t, gains, *refs):
    if with_out:
        parts_hbm, refs = refs[0], refs[1:]
    outs, refs = refs[: 5 + with_out], refs[5 + with_out :]
    input_grad, grad_q, grad_kv, grad_o, grad_s = outs[:5]
    (bias, branch, grad_att, grad_q_pre, grad_kv_pre, rhs, own, own_s, grad_hid, query_full, keyval_full, output_full,
     load_sem, *rest) = refs
    big = GradSum(n_dp, n_exp, own.shape[0], own, rest[:8], rest[8:18])
    little = GradSum(n_dp, n_exp, 1, own_s, rest[18:26], rest[26:36])
    tree, width = x_ref.shape
    ring = Ring(n_exp)
    greet(big.partners() + ring.partners())
    loads = [
        pltpu.make_async_copy(src, dst, load_sem.at[k])
        for k, (src, dst) in enumerate(((output_hbm, output_full), (query_hbm, query_full), (keyval_hbm, keyval_full)))
    ]
    if with_out:
        parts, part_sem = rest[36], rest[37]
        out = RingScatter(ring, lambda e: parts.at[e], views(rest[38:41]), rest[41:45])
        part_loads = [pltpu.make_async_copy(parts_hbm.at[j], parts.at[j], part_sem.at[j]) for j in range(n_exp)]
        for copy in part_loads:
            copy.start()
    for copy in loads:
        copy.start()
    shard = width // n_dp
    side = shard // 2
    tile = 512
    lane = lanes_of((tree, 128))
    left = lane < HD
    if with_out:
        for copy in part_loads:
            copy.wait()
        for d in out.order():
            out.start_pair(d)

    def gain_row(i):
        return gains[...].astype(F32)[i : i + 1]

    bias[...] = mask_bias(parents, tree)

    names = routes_t[...].astype(F32)
    pick = jnp.where(lax.broadcasted_iota(jnp.int32, (16, 128), 0) == lanes_of((16, 128)), 1.0, 0.0).astype(LOW)
    names = dot(jnp.concatenate([names, jnp.zeros_like(names)], axis=0).astype(LOW), pick, 0, 0)
    chosen = jnp.zeros((tree, 128), F32)
    for k in range(routes_t.shape[0]):
        chosen = jnp.maximum(chosen, jnp.where(names[:, k : k + 1] == lane.astype(F32), 1.0, 0.0))
    logits = jnp.where(chosen > 0.5, dot(hidden2[...], router_t[...], 1, 1), -1e30)
    powers = jnp.exp(logits - jnp.max(logits, axis=1, keepdims=True))
    gate = powers / jnp.sum(powers, axis=1, keepdims=True)
    count = gates_in.shape[0]
    where_row = lax.broadcasted_iota(jnp.int32, (count, 128), 0)
    where_lane = lanes_of((count, 128))
    group_row = lax.rem(where_row, 8)
    target = lax.div(where_row, 8) * local + group_row
    pick = jnp.where(group_row < local, jnp.where(target == where_lane, 1.0, 0.0), 0.0).astype(LOW)
    high, low = two_parts(gates_in[...])
    gate_back = dot(high, pick, 0, 0) + dot(low, pick, 0, 0)
    grad_logits = (gate * (gate_back - jnp.sum(gate * gate_back, axis=1, keepdims=True))).astype(LOW)
    grad_router = dot(grad_logits, hidden2[...], 0, 0)[:EXPERTS]
    grad_hidden2 = hid_sum[...] + dot(grad_logits, router_t[...])
    back, gain2_sum = norm_back(middle[...], gain_row(1), grad_hidden2)
    grad_middle = cot[...].astype(F32) + back
    input_grad[...] = grad_middle
    branch[...] = grad_middle.astype(LOW)

    def chunk_grads(i, lhs, rhs_ref):
        def part(n, carry):
            made = dot(lhs[:, pl.ds(pl.multiple_of(n * tile, tile), tile)], rhs_ref[...], 0, 0).astype(LOW)
            for k in range(tile // side):
                own[i, n * (tile // shard) + k // 2, k % 2] = made[k * side : (k + 1) * side]
            return carry

        if tile % shard == 0:
            lax.fori_loop(0, width // tile, part, 0)

    if with_out:
        out.first()
    for i in range(2):
        rhs[...] = branch[:, pl.ds(i * tile, tile)]
        chunk_grads(i, attended, rhs)
        big.start(i)

    if with_out:
        out.early()
    loads[0].wait()

    def att_tile(n, carry):
        rows = pl.ds(pl.multiple_of(n * tile, tile), tile)
        grad_att[:, rows] = dot(branch[...], output_full[rows, :], 1, 1).astype(LOW)
        return carry

    lax.fori_loop(0, width // tile, att_tile, 0)

    def unrotate(field):
        return field * cosine[...] - turned(field * sine[...])

    scale = HD**-0.5

    def group(c):
        cols = pl.ds(pl.multiple_of(c * 128, 128), 128)
        pair, grad_pair = queries[:, cols], grad_att[:, cols]
        zero = jnp.zeros_like(pair)
        key, value = keys[c], values[c]
        grad_query, grad_key, grad_value = [], 0.0, 0.0
        for h in range(2):
            here = left if h == 0 else jnp.logical_not(left)
            query, grad_out = jnp.where(here, pair, zero), jnp.where(here, grad_pair, zero)
            logs = jnp.sum(jnp.where(lane == 2 * c + h, log_total[...], 0.0), axis=1, keepdims=True)
            probs = jnp.exp(dot(query, key, 1, 1) * scale + bias[...] - logs)
            grad_probs = dot(grad_out, value, 1, 1)
            grad_scores = (probs * (grad_probs - jnp.sum(probs * grad_probs, axis=1, keepdims=True))).astype(LOW)
            grad_value = grad_value + dot(probs.astype(LOW), grad_out, 0, 0)
            grad_query.append(dot(grad_scores, key))
            grad_key = grad_key + dot(grad_scores, query, 0, 0)
        grad_q_pre[:, cols] = unrotate(jnp.where(left, grad_query[0], grad_query[1]) * scale).astype(LOW)
        grad_key = (grad_key + pltpu.roll(grad_key, HD, 1)) * scale
        return unrotate(grad_key), grad_value + pltpu.roll(grad_value, HD, 1)

    def two_groups(i):
        key_a, value_a = group(2 * i)
        key_b, value_b = group(2 * i + 1)
        at = pl.multiple_of(i * 128, 128)
        grad_kv_pre[:, pl.ds(at, 128)] = jnp.where(left, key_a, key_b).astype(LOW)
        at = pl.multiple_of(KV * HD + i * 128, 128)
        grad_kv_pre[:, pl.ds(at, 128)] = jnp.where(left, value_a, value_b).astype(LOW)

    def gather_rhs(i):
        rhs[:, pl.ds(0, 256)] = grad_q_pre[:, pl.ds(i * 256, 256)]
        rhs[:, pl.ds(256, 128)] = grad_kv_pre[:, pl.ds(i * 128, 128)]
        rhs[:, pl.ds(384, 128)] = grad_kv_pre[:, pl.ds(KV * HD + i * 128, 128)]

    for i in range(KV // 2):
        two_groups(i)
        gather_rhs(i)
        chunk_grads(2 + i, hidden, rhs)
        big.start(2 + i)
        if i == 0:
            big.paired(0)
            big.paired(1)
        if i == 1:
            if with_out:
                out.late()
            big.paired(2)
        if i == 2:
            big.met(0, 0)
            big.met(1, 0)
            big.paired(3)
        if i == 3:
            big.met(0, 1)
            big.met(1, 1)
            big.paired(4)
            big.met(2, 0)

    for copy in loads[1:]:
        copy.wait()
    big.line(0)

    def hidden_tile(n, carry):
        cols = pl.ds(pl.multiple_of(n * tile, tile), tile)
        grad_hid[:, cols] = dot(grad_q_pre[...], query_full[cols, :], 1, 1) + dot(grad_kv_pre[...], keyval_full[cols, :], 1, 1)
        return carry

    lax.fori_loop(0, width // tile, hidden_tile, 0)
    big.paired(5)
    big.met(3, 0)
    big.line(1)
    back, gain1_sum = norm_back(x_ref[...].astype(F32), gain_row(0), grad_hid[...])
    input_grad[...] = input_grad[...] + back

    sub = lax.broadcasted_iota(jnp.int32, (16, width), 0)
    sums = jnp.where(sub == 0, gain1_sum, jnp.where(sub == 1, gain2_sum, 0.0))
    little_all = jnp.concatenate([grad_router, sums], axis=0).astype(LOW)
    for d in range(n_dp):
        for k in range(2):
            at = d * shard + k * side
            own_s[0, d, k] = little_all[:, at : at + side]
    little.start(0)
    big.met(2, 1)
    big.line(2)
    big.met(4, 0)
    little.paired(0)
    big.met(3, 1)
    big.line(3)
    big.met(5, 0)
    little.met(0, 0)
    big.met(4, 1)
    big.line(4)
    little.met(0, 1)
    big.met(5, 1)
    big.line(5)
    if with_out:
        out.last(outs[5], middle)
    chunks = own.shape[0]
    hop = 2 * (big.depth - 1)
    for t in range(chunks, chunks + hop):
        big.line(t)
        if t >= hop:
            big.close(t - hop)

    def little_line(t, carry):
        little.line(t)
        return carry

    lax.fori_loop(0, hop + 1, little_line, 0)
    little.close(0)

    def place(i, which, field):
        rows = pl.ds(pl.multiple_of(which * side, 16), side)
        if i < 2:
            add_rows(grad_o.at[rows, pl.ds(i * tile, tile)], field)
            return
        i = i - 2
        add_rows(grad_q.at[rows, pl.ds(i * 256, 256)], field.at[:, pl.ds(0, 256)])
        add_rows(grad_kv.at[rows, pl.ds(i * 128, 128)], field.at[:, pl.ds(256, 128)])
        add_rows(grad_kv.at[rows, pl.ds(KV * HD + i * 128, 128)], field.at[:, pl.ds(384, 128)])

    for i in range(chunks):
        place(i, big.core, big.final.at[i])
    add_rows(grad_s.at[big.core], little.final.at[0])
    for i in range(chunks):
        big.last(i).wait_recv()
        place(i, 1 - big.core, big.other.at[i])
        big.finish(i)
    little.last(0).wait_recv()
    add_rows(grad_s.at[1 - big.core], little.other.at[0])
    little.finish(0)
    if with_out:
        out.finish_sends()


def back(n_dp, n_exp, local, tokens, cotangent, hid_sum, gates_in, routes_t, parents, tables, saved, parts, collective_id):
    tree, width = tokens.shape
    shard = width // n_dp
    shape, vm, sem = jax.ShapeDtypeStruct, pltpu.VMEM, pltpu.SemaphoreType.DMA
    side, chunks, tile, rows = shard // 2, 6, 512, EXPERTS + 16
    big_bufs, big_sems = GradSum.scratch(n_dp, chunks, side, tile)
    little_bufs, little_sems = GradSum.scratch(n_dp, 1, rows, side)
    args = (tokens, cotangent, hid_sum, gates_in, routes_t, parents, *tables, *saved)
    spaces = [VMEM] * len(args)
    spaces[16:19] = [ANY] * 3
    out_shape = [
        shape((tree, width), F32), shape((shard, width), F32), shape((shard, width), F32), shape((shard, width), F32),
        shape((2, rows, side), F32),
    ]
    extra = []
    if parts is not None:
        args, spaces = (*args, parts), spaces + [ANY]
        out_shape.append(shape((tree, width), LOW))
        bufs, sems = RingScatter.scratch(n_exp, (tree, width), LOW)
        extra = [vm(parts.shape, LOW), sem((n_exp,)), *bufs, *sems]
    return pl.pallas_call(
        functools.partial(back_body, n_dp, n_exp, local, parts is not None),
        out_shape=out_shape,
        in_specs=[pl.BlockSpec(memory_space=s) for s in spaces],
        out_specs=[pl.BlockSpec(memory_space=VMEM)] * len(out_shape),
        scratch_shapes=[
            vm((tree, tree), F32), vm((tree, width), LOW), vm((tree, width), LOW), vm((tree, width), LOW), vm((tree, width), LOW),
            vm((tree, tile), LOW), vm((chunks, n_dp, 2, side, tile), LOW), vm((1, n_dp, 2, rows, side), LOW),
            vm((tree, width), F32), vm((width, width), LOW), vm((width, width), LOW), vm((width, width), LOW), sem((3,)),
            *big_bufs, *big_sems, *little_bufs, *little_sems, *extra,
        ],
        compiler_params=pltpu.CompilerParams(
            collective_id=collective_id, has_side_effects=True, vmem_limit_bytes=63 * MIB),
        name="back",
    )(*args)


def rope_pairs(tree_rows):
    unit = tree_rows // 20
    row = np.arange(tree_rows)
    position = np.where(row < 8 * unit, row, np.where(row < 12 * unit, 8 * unit + row % unit, 9 * unit + row % unit))
    frequency = 10000.0 ** (-np.arange(0, HD, 2) / HD)
    angles = position[:, None] * frequency[None, :]
    return tuple(jnp.asarray(np.concatenate([table] * 4, axis=1), jnp.float32) for table in (np.cos(angles), np.sin(angles)))


def gated_unit(gate_up):
    width_ff = gate_up.shape[-1] // 2
    gate_part = gate_up[..., :width_ff]
    return gate_part / (1.0 + jnp.exp(-gate_part)) * gate_up[..., width_ff:]


def experts_plain(
    n_dp, n_exp, hidden2, grad_y, routes_all, router_full, expert_in, expert_out, middle
):
    tree_rows, width = hidden2.shape
    capacity = CAP
    routes_all = routes_all.transpose(0, 2, 1)
    expert_ids = jnp.arange(EXPERTS, dtype=jnp.int32)
    here = lax.axis_index("expert")
    local = expert_in.shape[0]
    first = here * local
    hidden_all = lax.all_gather(hidden2, "expert", axis=0, tiled=False)
    own_ids = first + jnp.arange(local, dtype=jnp.int32)
    hot_all = routes_all[:, :, :, None] == expert_ids[None, None, None, :]
    chosen_all = jnp.any(hot_all, axis=2)
    chosen = jnp.any(routes_all[:, :, :, None] == own_ids[None, None, None, :], axis=2)
    lower = jnp.tril(jnp.ones((tree_rows, tree_rows), jnp.bfloat16), -1)
    rank = jnp.einsum(
        "tu,jue->jet", lower, chosen.astype(jnp.bfloat16), preferred_element_type=jnp.float32
    ).astype(jnp.int32)
    slots = jnp.arange(capacity, dtype=jnp.int32)
    chosen_t = chosen.transpose(0, 2, 1)
    place = (rank[:, :, None, :] == slots[None, None, :, None]) & chosen_t[:, :, None, :]
    place = place.astype(jnp.bfloat16)
    logits_all = jnp.einsum(
        "jtd,de->jte", hidden_all, router_full, preferred_element_type=jnp.float32
    )
    masked = jnp.where(chosen_all, logits_all, -1e30)
    weight = jnp.exp(masked - jnp.max(masked, axis=-1, keepdims=True))
    weight = weight / jnp.sum(weight, axis=-1, keepdims=True)
    gates_own = lax.dynamic_slice_in_dim(weight, first, local, axis=2)
    gate_slot = jnp.einsum(
        "jest,jte->ejs", place.astype(jnp.float32), gates_own, precision=lax.Precision.HIGHEST
    )[..., None]
    sent = jnp.einsum("jest,jtd->ejsd", place, hidden_all, preferred_element_type=jnp.float32)
    sent = sent.astype(jnp.bfloat16)
    grad_rows = jnp.einsum("jest,jtd->ejsd", place, grad_y, preferred_element_type=jnp.float32)
    grad_rows = grad_rows.astype(jnp.bfloat16)
    gate_up = jnp.einsum("ejsd,edf->ejsf", sent, expert_in, preferred_element_type=jnp.float32)
    activated, glu_back = jax.vjp(gated_unit, gate_up)
    act_low = activated.astype(jnp.bfloat16).astype(jnp.float32)
    act_scaled = (act_low * gate_slot).astype(jnp.bfloat16)
    made = jnp.einsum(
        "ejsf,efd->ejsd", act_scaled, expert_out, preferred_element_type=jnp.float32
    ).astype(jnp.bfloat16)
    out_part = jnp.einsum("jest,ejsd->jtd", place, made, preferred_element_type=jnp.float32)
    out_sum = lax.psum_scatter(
        out_part.astype(jnp.bfloat16), "expert", scatter_dimension=0, tiled=False
    ).astype(jnp.float32)
    result = middle + out_sum
    block_out = result.astype(jnp.bfloat16)
    grad_act = jnp.einsum(
        "ejsd,efd->ejsf", grad_rows, expert_out, preferred_element_type=jnp.float32
    )
    gate_dot = jnp.sum(act_low * grad_act, axis=-1)
    gates_back = jnp.einsum(
        "jest,ejs->jte", place.astype(jnp.float32), gate_dot, precision=lax.Precision.HIGHEST
    )
    grad_out_w = jnp.einsum(
        "ejsf,ejsd->efd", act_scaled, grad_rows, preferred_element_type=jnp.float32
    )
    grad_gate_up = glu_back(grad_act * gate_slot)[0].astype(jnp.bfloat16)
    grad_sent = jnp.einsum(
        "ejsf,edf->ejsd", grad_gate_up, expert_in, preferred_element_type=jnp.float32
    ).astype(jnp.bfloat16)
    grad_in_w = jnp.einsum(
        "ejsd,ejsf->edf", sent, grad_gate_up, preferred_element_type=jnp.float32
    )
    hid_part = jnp.einsum("jest,ejsd->jtd", place, grad_sent, preferred_element_type=jnp.float32)
    gates_mine = lax.all_to_all(gates_back, "expert", split_axis=0, concat_axis=2, tiled=True)[0]
    hid_sum = lax.psum_scatter(
        hid_part.astype(jnp.bfloat16), "expert", scatter_dimension=0, tiled=False
    ).astype(jnp.float32)
    local, units = expert_in.shape[0], expert_out.shape[1]
    low = jnp.bfloat16
    grads = jnp.concatenate(
        [
            grad_in_w.astype(low).reshape(local, n_dp, width // n_dp, width),
            grad_out_w.astype(low).reshape(local, n_dp, units // n_dp, width),
        ],
        axis=2,
    ).reshape(local, width + units, width)
    share = lax.psum_scatter(grads, "dp", scatter_dimension=1, tiled=True).astype(jnp.float32)
    gates_mine = jnp.pad(gates_mine.T.reshape(n_exp, local, tree_rows), ((0, 0), (0, 8 - local), (0, 0)))
    return block_out, hid_sum, gates_mine, share[:, : width // n_dp], share[:, width // n_dp :]


def shards(
    tokens,
    attn_gain,
    w_query,
    w_keyval,
    w_output,
    moe_gain,
    w_router,
    expert_in,
    expert_out,
    cotangent,
    routes,
    parents,
):
    n_dp, n_exp = lax.axis_size("dp"), lax.axis_size("expert")
    local = expert_in.shape[0]
    tree_rows = tokens.shape[0]
    grad_y = lax.all_gather(cotangent, "expert", axis=0, tiled=False)
    tables = rope_pairs(tree_rows)
    routes_t = routes.T
    (hidden, queries, keys, values, attended, middle, hidden2, log_total, *full, gains, routes_all) = front(
        n_dp, n_exp, tokens, jnp.stack([attn_gain, moe_gain]), w_router.T, w_query, w_keyval, w_output, routes_t, parents, tables, 1
    )
    router_t = full[3]
    if (n_dp, n_exp) == (4, 8):
        parts, hid_sum, gate_grads, expert_in_share, expert_out_share, late = experts(
            n_dp, n_exp, hidden2, grad_y, routes_all, router_t, expert_in, expert_out, 2
        )
        late_share = lax.psum_scatter(late, "dp", scatter_dimension=0, tiled=True).astype(jnp.float32)[None]
        rows = expert_in_share.shape[1]
        expert_in_share = jnp.concatenate([expert_in_share, late_share[:, :rows]], axis=0)
        expert_out_share = jnp.concatenate([expert_out_share, late_share[:, rows:]], axis=0)
    else:
        parts = None
        block_out, hid_sum, gate_grads, expert_in_share, expert_out_share = experts_plain(
            n_dp, n_exp, hidden2, grad_y, routes_all, router_t[:EXPERTS].T, expert_in, expert_out, middle
        )
    saved = (hidden, queries, keys, values, attended, middle, hidden2, log_total, *full, gains)
    input_grad, grad_q, grad_kv, grad_o, grad_small, *made = back(
        n_dp, n_exp, local, tokens, cotangent, hid_sum, gate_grads.reshape(n_exp * 8, tree_rows), routes_t, parents, tables, saved, parts, 3
    )
    if parts is not None:
        block_out = made[0]
    return (
        block_out,
        input_grad,
        grad_small[:, EXPERTS].reshape(-1),
        grad_q,
        grad_kv,
        grad_o,
        grad_small[:, EXPERTS + 1].reshape(-1),
        jnp.concatenate([grad_small[0, :EXPERTS], grad_small[1, :EXPERTS]], axis=1).T,
        expert_in_share,
        expert_out_share,
    )


def solution(mesh):
    in_specs = (
        P(("dp", "expert"), None),
        P("dp"),
        P("dp", None),
        P("dp", None),
        P("dp", None),
        P("dp"),
        P("dp", None),
        P("expert", None, None),
        P("expert", None, None),
        P(("dp", "expert"), None),
        P(("dp", "expert"), None),
        P(("dp", "expert"), None),
    )
    out_specs = (
        P(("dp", "expert"), None),
        P(("dp", "expert"), None),
        P("dp"),
        P("dp", None),
        P("dp", None),
        P("dp", None),
        P("dp"),
        P("dp", None),
        P("expert", "dp", None),
        P("expert", "dp", None),
    )
    return jax.shard_map(shards, mesh=mesh, in_specs=in_specs, out_specs=out_specs, check_vma=False)
```

```python
import functools

import jax
import jax.numpy as jnp
import numpy as np
from jax import lax
from jax.experimental import pallas as pl
from jax.experimental.pallas import tpu as pltpu
from jax.sharding import PartitionSpec as P

H = 16
KV = 8
HD = 64
EXPERTS = 32
TOPK = 8
CAP = 120


EPSILON = 1e-06


MESH = pl.DeviceIdType.MESH
MIB = 1024 * 1024
VMEM = pltpu.VMEM
ANY = pl.ANY


def remote(src, dst, send_sem, recv_sem, **where):
    return pltpu.make_async_remote_copy(
        src_ref=src, dst_ref=dst, send_sem=send_sem, recv_sem=recv_sem,
        device_id=where, device_id_type=MESH,
    )


def greet(partners):
    barrier = pltpu.get_barrier_semaphore()
    for condition, where in partners:
        def signal(where=where):
            pl.semaphore_signal(barrier, inc=1, device_id=where, device_id_type=MESH)
        if condition is None:
            signal()
        else:
            pl.when(condition)(signal)
    count = sum(1 if c is None else c.astype(jnp.int32) for c, _ in partners)
    pl.semaphore_wait(barrier, count)


def add_rows(out, *terms, step=16):
    rows = out.shape[0]

    def body(i, carry):
        at = pl.ds(pl.multiple_of(i * step, step), step)
        total = terms[0][at, :].astype(jnp.float32)
        for term in terms[1:]:
            total = total + term[at, :].astype(jnp.float32)
        out[at, :] = total.astype(out.dtype)
        return carry

    lax.fori_loop(0, rows // step, body, 0)


def bit_orders(n):
    bits = [1 << j for j in range(n.bit_length() - 1)]
    return [bits[p:] + bits[:p] for p in range(len(bits))] or [[]]


class Ring:
    def __init__(self, n_exp):
        self.mine = lax.axis_index("expert")
        self.core = lax.rem(self.mine, 2)
        self.z = lax.div(self.mine, 2)
        self.depth = n_exp // 2
        self.far = self.depth // 2
        self.pair = self.mine + 1 - 2 * self.core
        self.right, self.left = self.dev(1), self.dev(-1)

    def dev(self, d):
        return lax.rem(self.z + d + self.depth, self.depth) * 2 + self.core

    def partners(self):
        return [(None, {"expert": e}) for e in (self.pair, self.right, self.left)]


class RingGather:
    def __init__(self, ring, own, out, sems):
        self.ring, self.own, self.out = ring, own, out
        self.send, self.recv, self.pair_send, self.pair_recv = sems
        self.half = own.shape[0] // 2

    @staticmethod
    def scratch(n_exp):
        far, depth = n_exp // 4, n_exp // 2
        sem = pltpu.SemaphoreType.DMA
        return [sem((2, far + 1, 2)), sem((2, far + 1, 2)), sem((depth, 2)), sem((depth, 2))]

    def rows(self, h):
        return pl.ds(h * self.half, self.half)

    def goes(self, side, s, h):
        far = self.ring.far
        return s < far or (s == far and h == side)

    def block(self, d, h):
        return self.out.at[self.ring.dev(d), self.rows(h)]

    def hop(self, side, s, h):
        d = -s if side == 0 else s
        src = self.own.at[self.rows(h)] if s == 0 else self.block(d, h)
        to = self.ring.right if side == 0 else self.ring.left
        return remote(src, self.block(d, h), self.send.at[side, s, h], self.recv.at[side, s + 1, h], expert=to)

    def across(self, d, h):
        src = self.own.at[self.rows(h)] if d == 0 else self.block(d, h)
        slot = d % self.ring.depth
        return remote(src, self.block(d, h), self.pair_send.at[slot, h], self.pair_recv.at[slot, h], expert=self.ring.pair)

    ORDER = ((0, 0), (1, 1), (0, 1), (1, 0))

    def start(self):
        for side, h in self.ORDER:
            if self.goes(side, 1, h):
                self.hop(side, 0, h).start()
        self.across(0, 0).start()
        self.across(0, 1).start()

    def events(self):
        return [(side, s, h) for s in range(1, self.ring.far + 1) for side, h in self.ORDER if self.goes(side, s, h)]

    def handle(self, event):
        side, s, h = event
        d = -s if side == 0 else s
        here = self.block(d, h)
        remote(here, here, self.send.at[side, s, h], self.recv.at[side, s, h], expert=self.ring.mine).wait_recv()
        if self.goes(side, s + 1, h):
            self.hop(side, s, h).start()
        self.across(d, h).start()

    def wait_pair(self, d, h):
        slot = d % self.ring.depth
        here = self.out.at[self.ring.pair - self.ring.mine + self.ring.dev(d), self.rows(h)]
        remote(here, here, self.pair_send.at[slot, h], self.pair_recv.at[slot, h], expert=self.ring.mine).wait_recv()

    def finish_own(self):
        for side, h in self.ORDER:
            if self.goes(side, 1, h):
                self.hop(side, 0, h).wait_send()
        self.across(0, 0).wait_send()
        self.across(0, 1).wait_send()

    def finish_event(self, event):
        side, s, h = event
        if self.goes(side, s + 1, h):
            self.hop(side, s, h).wait_send()
        self.across(-s if side == 0 else s, h).wait_send()


class RingScatter:
    def __init__(self, ring, part, bufs, sems):
        self.ring, self.part = ring, part
        self.pair_buf, self.held, self.got = bufs
        self.pair_send, self.pair_recv, self.send, self.recv = sems
        self.half = self.held(0).shape[0] // 2

    @staticmethod
    def scratch(n_exp, block, dtype):
        far, depth = n_exp // 4, n_exp // 2
        sem = pltpu.SemaphoreType.DMA
        bufs = [pltpu.VMEM((depth,) + block, dtype), pltpu.VMEM((depth,) + block, dtype),
                pltpu.VMEM((2, far) + block, dtype)]
        return bufs, [sem((depth,)), sem((depth,)), sem((2, far + 1, 2)), sem((2, far + 1, 2))]

    def rows(self, h):
        return pl.ds(h * self.half, self.half)

    def order(self):
        far, depth = self.ring.far, self.ring.depth
        order = [far]
        for s in range(far - 1, 0, -1):
            order += [s, depth - s]
        return order + [0]

    def comes(self, side, d, h):
        far = self.ring.far
        return d + 1 < far or (d + 1 == far and h == side)

    def across(self, d):
        ring = self.ring
        return remote(self.part(ring.dev(d) + 1 - 2 * ring.core), self.pair_buf(d),
                      self.pair_send.at[d], self.pair_recv.at[d], expert=ring.pair)

    def start_pair(self, d):
        self.across(d).start()

    def wait_pair(self, d):
        self.across(d).wait_recv()

    def wait_got(self, side, d, h):
        here = self.got(side, d).at[self.rows(h)]
        remote(here, here, self.send.at[side, d, h], self.recv.at[side, d, h], expert=self.ring.mine).wait_recv()

    def hop(self, side, d, h):
        slot = d if side == 0 else self.ring.depth - d
        rows = self.rows(h)
        return remote(self.held(slot).at[rows], self.got(side, d - 1).at[rows], self.send.at[side, d, h],
                      self.recv.at[side, d - 1, h], expert=self.ring.right if side == 0 else self.ring.left)

    def push(self, side, d, h):
        ring = self.ring
        slot = d if side == 0 else ring.depth - d
        rows = self.rows(h)
        terms = [self.part(ring.dev(slot)).at[rows], self.pair_buf(slot).at[rows]]
        if self.comes(side, d, h):
            self.wait_got(side, d, h)
            terms.append(self.got(side, d).at[rows])
        add_rows(self.held(slot).at[rows], *terms)
        self.hop(side, d, h).start()

    def first(self):
        far = self.ring.far
        self.wait_pair(far)
        self.push(0, far, 0)
        self.push(1, far, 1)

    def early(self):
        for d in range(self.ring.far - 1, 0, -1):
            self.wait_pair(d)
            self.push(0, d, 1)
            self.wait_pair(self.ring.depth - d)
            self.push(1, d, 0)

    def late(self):
        for d in range(self.ring.far - 1, 0, -1):
            self.push(0, d, 0)
            self.push(1, d, 1)

    def last(self, out, *more):
        self.wait_pair(0)
        for h in range(2):
            rows = self.rows(h)
            terms = [self.part(self.ring.mine).at[rows], self.pair_buf(0).at[rows]] + [m.at[rows] for m in more]
            for side in range(2):
                if self.comes(side, 0, h):
                    self.wait_got(side, 0, h)
                    terms.append(self.got(side, 0).at[rows])
            add_rows(out.at[rows], *terms)

    def finish_sends(self):
        far = self.ring.far
        for side in range(2):
            for d in range(1, far + 1):
                for h in range(2):
                    if d < far or h == side:
                        self.hop(side, d, h).wait_send()
        for d in range(self.ring.depth):
            self.across(d).wait_send()


def views(bufs):
    pair_buf, held, got = bufs
    return (lambda d: pair_buf.at[d], lambda d: held.at[d], lambda side, d: got.at[side, d])


SLOTS = 128
F32, LOW = jnp.float32, jnp.bfloat16


def dot(a, b, over_a=1, over_b=0):
    return lax.dot_general(a, b, (((over_a,), (over_b,)), ((), ())), preferred_element_type=F32)


class ExpertSum:
    def __init__(self, me, first, half, land, send, recv):
        self.me, self.first, self.half, self.land, self.send, self.recv = me, first, half, land, send, recv

    def hop(self, step, h, which):
        bit = (1, 2)[h] if step == 0 else (2, 1)[h]
        r = bit if which == 0 else 3
        k = 2 * h + which if step == 0 else 4 + h
        src = self.first(r, h) if step == 0 else self.half(r, h)
        return remote(src, self.land(k), self.send(k), self.recv(k), dp=self.me ^ bit)

    def start(self):
        for which in (1, 0):
            for h in range(2):
                self.hop(0, h, which).start()

    def turn(self):
        for which in (1, 0):
            for h in range(2):
                self.hop(0, h, which).wait_recv()
                kept = 0 if which == 0 else (2, 1)[h]
                add_rows(self.half(kept, h), self.half(kept, h), self.land(2 * h + which))
                if which == 1:
                    self.hop(1, h, 0).start()

    def end(self, h, out):
        self.hop(1, h, 0).wait_recv()
        add_rows(out, self.half(0, h), self.land(4 + h))

    def finish(self):
        for step, h, which in ((0, 0, 0), (0, 0, 1), (0, 1, 0), (0, 1, 1), (1, 0, 0), (1, 1, 0)):
            self.hop(step, h, which).wait_send()


def experts_body(n_dp, n_exp, hid_ref, gy_hbm, routes_t, wr_t, w_in_hbm, w_out_hbm,
                 parts_hbm, hid_sum, gates_out, in_share, out_share, late,
                 x_all, w_in, w_out, sent, grows, gu, tmp, acts, stage, slots, gates, dots, wide,
                 pair_buf, held, got, *sems):
    w_sem, gy_sem, wide_sem, own_sem, part_sem, late_sem, gate_send, gate_recv, dp_ready, dp_send, dp_recv = sems[:11]
    gather_sems, hid_sems = sems[11:15], sems[15:19]
    me = lax.axis_index("dp")
    local, _, width = sent.shape
    tree, hidden_units = hid_ref.shape[0], w_out.shape[1]
    rows_e = local * SLOTS
    ring = Ring(n_exp)
    mine, core, depth = ring.mine, ring.core, ring.depth
    first = mine * local
    peers = [lax.rem(mine + k, n_exp) for k in range(1, n_exp)]
    greet([(None, {"expert": e}) for e in peers] + [(None, {"dp": me ^ bit}) for bit in (1, 2)])

    weights = [pltpu.make_async_copy(w_in_hbm, w_in, w_sem.at[0]), pltpu.make_async_copy(w_out_hbm, w_out, w_sem.at[1])]
    gather = RingGather(ring, hid_ref, x_all, gather_sems)
    gather.start()
    for copy in weights:
        copy.start()
    own = pltpu.make_async_copy(hid_ref, x_all.at[mine], own_sem)
    own.start()

    def gy_buf(j):
        return stage.at[lax.rem(j, 2), pl.ds(0, tree)]

    def gy_copy(j):
        return pltpu.make_async_copy(gy_hbm.at[j], gy_buf(j), gy_sem.at[lax.rem(j, 2)])

    gy_copy(0).start()

    below = (lax.broadcasted_iota(jnp.int32, (tree, tree), 0) < lax.broadcasted_iota(jnp.int32, (tree, tree), 1)).astype(LOW)
    sub16 = lax.broadcasted_iota(jnp.int32, (16, tree), 0)

    def find_slots(j, carry):
        names = routes_t[j]
        chosen = jnp.zeros((16, tree), F32)
        for k in range(names.shape[0]):
            chosen = jnp.maximum(chosen, jnp.where(names[k : k + 1, :] == first + sub16, 1.0, 0.0))
        chosen = jnp.where(sub16 < local, chosen, 0.0)
        rank = dot(chosen.astype(LOW), below)
        slots[j] = jnp.where(chosen > 0.5, rank, -1.0)[:8]
        return carry

    lax.fori_loop(0, n_exp, find_slots, 0)

    slot_ids = lax.broadcasted_iota(jnp.int32, (SLOTS, tree), 0).astype(F32)

    def places(j):
        return jnp.concatenate(
            [jnp.where(slot_ids == slots[j, i : i + 1, :], 1.0, 0.0).astype(LOW) for i in range(local)], axis=0)

    def places_t(j):
        lane = lax.broadcasted_iota(jnp.int32, (tree, 128), 1)
        pick = jnp.where(lax.broadcasted_iota(jnp.int32, (16, 128), 0) == lax.broadcasted_iota(jnp.int32, (16, 128), 1), 1.0, 0.0)
        slot = dot(jnp.concatenate([slots[j], jnp.zeros((8, tree), F32)], axis=0).astype(LOW), pick.astype(LOW), 0, 0)
        lanes = lane.astype(F32)
        return jnp.concatenate(
            [jnp.where(lanes == slot[:, i : i + 1], 1.0, 0.0).astype(LOW) for i in range(local)], axis=1)

    def find_gates(j):
        names = routes_t[j]
        experts = lax.broadcasted_iota(jnp.int32, (EXPERTS, tree), 0)
        chosen = jnp.zeros((EXPERTS, tree), F32)
        for k in range(names.shape[0]):
            chosen = jnp.maximum(chosen, jnp.where(names[k : k + 1, :] == experts, 1.0, 0.0))
        logits = jnp.where(chosen > 0.5, dot(wr_t[pl.ds(0, EXPERTS), :], x_all[j], 1, 1), -1e30)
        powers = jnp.exp(logits - jnp.max(logits, axis=0, keepdims=True))
        share = powers / jnp.sum(powers, axis=0, keepdims=True)
        sub = lax.broadcasted_iota(jnp.int32, (8, tree), 0)
        own_gates = jnp.zeros((8, tree), F32)
        for i in range(local):
            row = jnp.sum(jnp.where(experts == first + i, share, 0.0), axis=0, keepdims=True)
            own_gates = jnp.where(sub == i, row, own_gates)
        gates[j] = own_gates

    halves = width // 512

    def dispatch(j, src, dest):
        place = places(j)

        def body(n, carry):
            cols = pl.ds(pl.multiple_of(n * 512, 512), 512)
            picked = dot(place, src[:, cols]).astype(LOW)
            for i in range(local):
                dest[i, pl.ds(pl.multiple_of(j * SLOTS, SLOTS), SLOTS), cols] = picked[i * SLOTS : (i + 1) * SLOTS]
            return carry

        lax.fori_loop(0, halves, body, 0)

    def slot_gate(j, e):
        return jnp.sum(jnp.where(slot_ids == slots[j, pl.ds(e, 1), :], gates[j, pl.ds(e, 1), :], 0.0), axis=1, keepdims=True)

    def forward(chip):
        pair_rows = pl.ds(pl.multiple_of(chip * 2 * SLOTS, 2 * SLOTS), 2 * SLOTS)

        def one_tree(q, carry):
            j = 2 * chip + q
            find_gates(j)
            dispatch(j, x_all.at[j], sent)
            return carry

        lax.fori_loop(0, 2, one_tree, 0)

        def one_expert(e, carry):
            both = dot(sent[e, pair_rows, :], w_in[e])
            gu[e, pair_rows, :] = both.astype(LOW)
            a, b = both[:, :hidden_units], both[:, hidden_units:]
            act = (a / (1.0 + jnp.exp(-a)) * b).astype(LOW).astype(F32)
            gate = jnp.concatenate([slot_gate(2 * chip, e), slot_gate(2 * chip + 1, e)], axis=0)
            made = dot((act * gate).astype(LOW), w_out[e]).astype(LOW)
            for q in range(2):
                tmp[pl.ds(pl.multiple_of(q * rows_e + e * SLOTS, SLOTS), SLOTS), :] = made[q * SLOTS : (q + 1) * SLOTS]
            return carry

        lax.fori_loop(0, local, one_expert, 0)

    def part_copy(j):
        return pltpu.make_async_copy(x_all.at[j], parts_hbm.at[j], part_sem.at[j])

    def combine_out(chip):
        def one_tree(q, carry):
            j = 2 * chip + q
            rows = pl.ds(pl.multiple_of(q * rows_e, rows_e), rows_e)
            x_all[j] = dot(places_t(j), tmp[rows, :]).astype(LOW)
            part_copy(j).start()
            return carry

        lax.fori_loop(0, 2, one_tree, 0)

    def grad_rows(j, carry):
        pl.when(j + 1 < n_exp)(lambda: gy_copy(j + 1).start())
        gy_copy(j).wait()
        dispatch(j, gy_buf(j), grows)
        return carry

    events = gather.events()

    def chip_at(d):
        return lax.rem(ring.z + d, depth)

    def group(g, carry):
        d = jnp.where(g == 0, 0, jnp.where(g == 1, depth - 1, jnp.where(g == 2, 1, 2)))
        chip = chip_at(d)

        @pl.when(g == 0)
        def _():
            own.wait()
            gather.wait_pair(0, 0)
            gather.wait_pair(0, 1)
            for copy in weights:
                copy.wait()

        @pl.when(g == 1)
        def _():
            for event in events[:4]:
                gather.handle(event)
            gather.wait_pair(-1, 0)
            gather.wait_pair(-1, 1)

        @pl.when(g == 2)
        def _():
            gather.wait_pair(1, 0)
            gather.wait_pair(1, 1)

        @pl.when(g == 3)
        def _():
            for event in events[4:]:
                gather.handle(event)
            gather.wait_pair(2, 0)
            gather.wait_pair(2, 1)

        forward(chip)

        @pl.when(g == 0)
        def _():
            gather.finish_own()
            lax.fori_loop(0, n_exp, grad_rows, 0)

        for at, d in ((1, -1), (2, 1), (3, 2)):
            @pl.when(g == at)
            def _():
                for event in events:
                    if event[1] == abs(d) and (abs(d) == 2 or (event[0] == 0) == (d < 0)):
                        gather.finish_event(event)

        combine_out(chip)
        return carry

    lax.fori_loop(0, depth, group, 0)

    in_rows, out_rows = width // n_dp, hidden_units // n_dp
    cut = (in_rows + out_rows) // 2

    def grad_half(e, r, h):
        at = 2 * r + h
        return gu.at[e, pl.ds(at * cut, cut)] if at < 5 else stage.at[e, pl.ds((at - 5) * cut, cut)]

    def grad_land(e, k):
        return w_in.at[e, pl.ds(k * cut, cut)] if k < 5 else w_out.at[e, pl.ds(0, cut)]

    def grad_sum(e):
        half = lambda r, h: grad_half(e, r, h)
        return ExpertSum(me, half, half, lambda k: grad_land(e, k), lambda k: dp_send.at[e, k], lambda k: dp_recv.at[e, k])

    def grads_start(e):
        pl.semaphore_wait(dp_ready.at[e], 2)
        grad_sum(e).start()

    def grads_turn(e):
        grad_sum(e).turn()

    def wide_copies(e):
        return (
            pltpu.make_async_copy(wide.at[pl.ds(0, in_rows)], in_share.at[e], wide_sem.at[0]),
            pltpu.make_async_copy(wide.at[pl.ds(in_rows, out_rows)], out_share.at[e], wide_sem.at[1]),
        )

    def grads_end(e):
        for h in range(2):
            grad_sum(e).end(h, wide.at[pl.ds(h * cut, cut)])
        for copy in wide_copies(e):
            copy.start()
        grad_sum(e).finish()
        for copy in wide_copies(e):
            copy.wait()

    block = 4 * SLOTS
    sub8 = lax.broadcasted_iota(jnp.int32, (8, tree), 0)

    def back_units(e):
        def one_block(m, inner):
            rows = pl.ds(pl.multiple_of(m * block, block), block)
            grad_act = dot(grows[e, rows, :], w_out[e], 1, 1)
            a = gu[e, rows, pl.ds(0, hidden_units)].astype(F32)
            b = gu[e, rows, pl.ds(hidden_units, hidden_units)].astype(F32)
            sg = 1.0 / (1.0 + jnp.exp(-a))
            sw = a * sg
            act = (sw * b).astype(LOW).astype(F32)
            gate = jnp.concatenate([slot_gate(4 * m + q, e) for q in range(4)], axis=0)
            told = jnp.sum(act * grad_act, axis=1, keepdims=True)
            acts[rows, :] = (act * gate).astype(LOW)
            grad_act = grad_act * gate
            tmp[rows, pl.ds(0, hidden_units)] = (grad_act * b * sg * (1.0 + a * (1.0 - sg))).astype(LOW)
            tmp[rows, pl.ds(hidden_units, hidden_units)] = (grad_act * sw).astype(LOW)
            for q in range(4):
                j = 4 * m + q
                row = jnp.sum(
                    jnp.where(slot_ids == slots[j, pl.ds(e, 1), :], told[q * SLOTS : (q + 1) * SLOTS], 0.0),
                    axis=0, keepdims=True)
                dots[j] = jnp.where(sub8 == e, row, dots[j])
            return inner

        lax.fori_loop(0, n_exp // 4, one_block, 0)

    def back_weights(e):
        for r in range(n_dp):
            d = me ^ r
            grad_in = dot(sent[e, :, pl.ds(pl.multiple_of(d * in_rows, in_rows), in_rows)], tmp[...], 0, 0).astype(LOW)
            grad_out = dot(acts[:, pl.ds(pl.multiple_of(d * out_rows, out_rows), out_rows)], grows[e], 0, 0).astype(LOW)
            grad_half(e, r, 0)[...] = grad_in[:cut]
            half = grad_half(e, r, 1)
            half[pl.ds(0, in_rows - cut), :] = grad_in[cut:]
            half[pl.ds(in_rows - cut, out_rows), :] = grad_out

    def back_rows(e, dest):
        def back_half(m, inner):
            rows = pl.ds(pl.multiple_of(m * 512, 512), 512)
            dest[rows, :] = dot(tmp[rows, :], w_in[e], 1, 1).astype(LOW)
            return inner

        lax.fori_loop(0, n_exp * SLOTS // 512, back_half, 0)

    end = local - 1

    def backward(e, carry):
        back_units(e)
        pl.when(e > 0)(lambda: grads_start(e - 1))
        back_weights(e)
        back_rows(e, sent.at[e])
        for bit in (1, 2):
            pl.semaphore_signal(dp_ready.at[e], inc=1, device_id={"dp": me ^ bit}, device_id_type=MESH)
        pl.when(e >= 2)(lambda: grads_turn(e - 2))
        return carry

    dots[...] = jnp.zeros(dots.shape, F32)
    lax.fori_loop(0, end, backward, 0)
    back_units(end)
    grads_start(end - 1)
    back_rows(end, grows.at[end - 1])

    gate_copies = []
    for k, e in enumerate(peers):
        copy = remote(dots.at[e], gates_out.at[mine], gate_send.at[k], gate_recv.at[k], expert=e)
        copy.start()
        gate_copies.append(copy)
    gates_out[mine] = dots[mine]
    for j in range(n_exp):
        part_copy(j).wait()
    hid = RingScatter(ring, lambda e: x_all.at[e], views((pair_buf, held, got)), hid_sems)

    def combine_hid(g, carry):
        d = jnp.where(g == 0, 2, jnp.where(g == 1, 1, jnp.where(g == 2, depth - 1, 0)))
        chip = chip_at(d)

        def one_tree(q, inner):
            j = 2 * chip + q
            rows = pl.ds(pl.multiple_of(j * SLOTS, SLOTS), SLOTS)
            made = jnp.concatenate([sent[i, rows, :] for i in range(end)] + [grows[end - 1, rows, :]], axis=0)
            x_all[j] = dot(places_t(j), made).astype(LOW)
            return inner

        lax.fori_loop(0, 2, one_tree, 0)

        pl.when(g == 0)(lambda: hid.start_pair(2))
        pl.when(g == 1)(lambda: hid.start_pair(1))
        pl.when(g == 2)(lambda: hid.start_pair(depth - 1))
        pl.when(g == 3)(lambda: hid.start_pair(0))
        pl.when(g == 1)(hid.first)
        return carry

    lax.fori_loop(0, depth, combine_hid, 0)
    hid.early()
    grads_turn(end - 2)
    back_weights(end)
    def late_copy(r, h):
        at = pl.multiple_of((me ^ r) * 2 * cut + h * cut, 16)
        return pltpu.make_async_copy(grad_half(end, r, h), late.at[pl.ds(at, cut)], late_sem.at[2 * r + h])

    for r in range(n_dp):
        for h in range(2):
            late_copy(r, h).start()

    hid.late()
    grads_end(0)
    grads_turn(end - 1)
    grads_end(1)
    hid.last(wide.at[pl.ds(0, tree)])
    hid_copy = pltpu.make_async_copy(wide.at[pl.ds(0, tree)], hid_sum, wide_sem.at[0])
    hid_copy.start()
    hid_copy.wait()
    for e in range(2, end):
        grads_end(e)
    for r in range(n_dp):
        for h in range(2):
            late_copy(r, h).wait()
    for k, copy in enumerate(gate_copies):
        copy.wait_send()
        source = lax.rem(mine + n_exp - 1 - k, n_exp)
        remote(dots.at[mine], gates_out.at[source], gate_send.at[k], gate_recv.at[k], expert=mine).wait_recv()
    hid.finish_sends()


def experts(n_dp, n_exp, hidden2, grad_y, routes_all, router_t, expert_in, expert_out, collective_id):
    local, width, both = expert_in.shape
    units = expert_out.shape[1]
    tree = hidden2.shape[0]
    rows = n_exp * SLOTS
    sem = pltpu.SemaphoreType.DMA
    bufs, hid_sems = RingScatter.scratch(n_exp, (tree, width), LOW)
    shape = jax.ShapeDtypeStruct
    return pl.pallas_call(
        functools.partial(experts_body, n_dp, n_exp),
        out_shape=[
            shape((n_exp, tree, width), LOW),
            shape((tree, width), F32),
            shape((n_exp, 8, tree), F32),
            shape((local - 1, width // n_dp, width), F32),
            shape((local - 1, units // n_dp, width), F32),
            shape((width + units, width), LOW),
        ],
        in_specs=[pl.BlockSpec(memory_space=s) for s in (VMEM, ANY, VMEM, VMEM, ANY, ANY)],
        out_specs=[pl.BlockSpec(memory_space=s) for s in (ANY, ANY, VMEM, ANY, ANY, ANY)],
        scratch_shapes=[
            pltpu.VMEM((n_exp, tree, width), LOW),
            pltpu.VMEM((local, width, both), LOW),
            pltpu.VMEM((local, units, width), LOW),
            pltpu.VMEM((local, rows, width), LOW),
            pltpu.VMEM((local, rows, width), LOW),
            pltpu.VMEM((local, rows, both), LOW),
            pltpu.VMEM((max(rows, 2 * local * SLOTS), width), LOW),
            pltpu.VMEM((rows, units), LOW),
            pltpu.VMEM((local, 3 * (width + units) // (2 * n_dp), width), LOW),
            pltpu.VMEM((n_exp, 8, tree), F32),
            pltpu.VMEM((n_exp, 8, tree), F32),
            pltpu.VMEM((n_exp, 8, tree), F32),
            pltpu.VMEM(((width + units) // n_dp, width), F32),
            *bufs,
            sem((2,)), sem((2,)), sem((2,)), sem, sem((n_exp,)), sem((2 * n_dp,)), sem((n_exp - 1,)), sem((n_exp - 1,)),
            pltpu.SemaphoreType.REGULAR((local,)), sem((local, 6)), sem((local, 6)),
            *RingGather.scratch(n_exp), *hid_sems,
        ],
        compiler_params=pltpu.CompilerParams(
            collective_id=collective_id, has_side_effects=True, vmem_limit_bytes=63 * MIB),
        name="experts",
    )(hidden2, grad_y, routes_all, router_t, expert_in, expert_out)


def lanes_of(shape):
    return lax.broadcasted_iota(jnp.int32, shape, 1)


def turned(field):
    low_half = lax.rem(lanes_of(field.shape), HD) < HD // 2
    return jnp.where(low_half, -pltpu.roll(field, 128 - HD // 2, 1), pltpu.roll(field, HD // 2, 1))


def mask_bias(parents, tree):
    unit = tree // 20

    def segment(row):
        return jnp.where(row < 8 * unit, 0, jnp.where(row < 12 * unit, 1 + lax.div(row - 8 * unit, unit), 5 + lax.div(row - 12 * unit, unit)))

    count = parents.shape[1]
    names = parents[...].astype(F32)
    wide = (tree, count)
    seg = segment(lax.broadcasted_iota(jnp.int32, wide, 0)).astype(F32)
    lane = lanes_of(wide).astype(F32)
    own = seg[:, :1]
    parent = jnp.sum(jnp.where(lane == seg, names, 0.0), axis=1, keepdims=True)
    grand = jnp.sum(jnp.where(lane == parent, names, 0.0), axis=1, keepdims=True)
    square = (tree, tree)
    row, col = lax.broadcasted_iota(jnp.int32, square, 0), lanes_of(square)
    there = segment(col).astype(F32)
    hit = jnp.maximum(
        jnp.maximum(jnp.where(there == own, 1.0, 0.0), jnp.where(there == parent, 1.0, 0.0)), jnp.where(there == grand, 1.0, 0.0))
    hit = jnp.where(col <= row, hit, 0.0)
    return jnp.where(hit > 0.5, 0.0, -1e30)


def inverse_rms(field):
    return lax.rsqrt(jnp.mean(field * field, axis=-1, keepdims=True) + EPSILON)


class DpGather:
    def __init__(self, n_dp, mine, me, ins, outs, sems):
        self.n_dp, self.me, self.ins, self.outs = n_dp, me, ins, outs
        self.send, self.recv, self.pair_send, self.pair_recv, self.own_sem = sems
        self.core = lax.rem(mine, 2)
        self.pair = mine + 1 - 2 * self.core
        self.shard = ins[0].shape[0]
        half = self.shard // 2
        self.orders = bit_orders(n_dp)
        self.cuts = min(2, len(self.orders), half // 16)
        self.size = half // self.cuts

    @staticmethod
    def scratch(count, n_dp):
        sem = pltpu.SemaphoreType.DMA
        bits = max(1, n_dp.bit_length() - 1)
        return [sem((count, 2, n_dp, bits)), sem((count, 2, n_dp)), sem((count, 2, n_dp)), sem((count, 2, n_dp)), sem((count,))]

    def rows(self, start, side, p):
        return pl.ds(pl.multiple_of(start + side * (self.shard // 2) + p * self.size, 16), self.size)

    def hop(self, a, p, r, bit):
        there = self.outs[a].at[self.rows((self.me ^ r) * self.shard, self.core, p)]
        src = self.ins[a].at[self.rows(0, self.core, p)] if r == 0 else there
        return remote(src, there, self.send.at[a, p, r, bit.bit_length() - 1], self.recv.at[a, p, r ^ bit], dp=self.me ^ bit)

    def own(self, a):
        at = pl.ds(pl.multiple_of(self.me * self.shard, 16), self.shard)
        return pltpu.make_async_copy(self.ins[a], self.outs[a].at[at], self.own_sem.at[a])

    def across(self, a, p, r, side):
        here = self.outs[a].at[self.rows((self.me ^ r) * self.shard, side, p)]
        return remote(here, here, self.pair_send.at[a, p, r], self.pair_recv.at[a, p, r], expert=self.pair)

    def start(self, a):
        for p in range(self.cuts):
            for bit in self.orders[p]:
                self.hop(a, p, 0, bit).start()
        self.own(a).start()

    def stage(self, p, j):
        order = self.orders[p]
        blocks = [0]
        for bit in order[:j]:
            blocks = blocks + [r | bit for r in blocks]
        return [r | order[j] for r in blocks], order[j + 1 :]

    def turn(self, a, j):
        for p in range(self.cuts):
            blocks, onward = self.stage(p, j)
            for r in blocks:
                here = self.outs[a].at[self.rows((self.me ^ r) * self.shard, self.core, p)]
                remote(here, here, self.send.at[a, p, r, 0], self.recv.at[a, p, r], dp=self.me).wait_recv()
                for bit in onward:
                    self.hop(a, p, r, bit).start()
                self.across(a, p, r, self.core).start()

    def ready(self, a):
        self.own(a).wait()
        for p in range(self.cuts):
            for r in range(1, self.n_dp):
                self.across(a, p, r, 1 - self.core).wait_recv()

    def finish(self, a):
        for p in range(self.cuts):
            for bit in self.orders[p]:
                self.hop(a, p, 0, bit).wait_send()
            for j in range(len(self.orders[p])):
                blocks, onward = self.stage(p, j)
                for r in blocks:
                    for bit in onward:
                        self.hop(a, p, r, bit).wait_send()
                    self.across(a, p, r, self.core).wait_send()


def front_body(n_dp, n_exp, x_ref, gain_pair, router_in, w_query, w_keyval, w_output, routes_t, parents, cosine, sine, cot,
               hidden_hbm, queries_hbm, keys_hbm, values_hbm, attended, middle, hidden2, log_total,
               query_hbm, keyval_hbm, output_hbm, router_t, gains, routes_all, grad_y,
               hidden, queries, keys, values, query_full, keyval_full, output_full, small, small_all, bias, *sems):
    gather_sems, (small_send, small_recv, route_send, route_recv, out_sem), ring_sems = sems[:5], sems[5:10], sems[10:14]
    me, mine = lax.axis_index("dp"), lax.axis_index("expert")
    peers = [lax.rem(mine + k, n_exp) for k in range(1, n_exp)]
    greet([(None, {"expert": e}) for e in peers] + [(None, {"dp": me ^ k}) for k in range(1, n_dp)])
    tree, width = x_ref.shape
    shard = w_query.shape[0]

    small[...] = jnp.zeros(small.shape, LOW)
    small[pl.ds(0, EXPERTS), :] = router_in[...]
    sub = lax.broadcasted_iota(jnp.int32, (16, shard), 0)
    gain_rows = gain_pair[...].astype(F32)
    small[pl.ds(EXPERTS, 16), :] = jnp.where(sub == 0, gain_rows[:1], jnp.where(sub == 1, gain_rows[1:], 0.0)).astype(LOW)

    gather = DpGather(n_dp, mine, me, (w_query, w_keyval, w_output), (query_full, keyval_full, output_full), gather_sems)

    def small_copy(k):
        return remote(small, small_all.at[me], small_send.at[k], small_recv.at[k], dp=me ^ k)

    def route_copy(k, e):
        return remote(routes_t, routes_all.at[mine], route_send.at[k], route_recv.at[k], expert=e)

    saves = [
        pltpu.make_async_copy(src, dst, out_sem.at[k])
        for k, (src, dst) in enumerate((
            (query_full, query_hbm), (keyval_full, keyval_hbm), (output_full, output_hbm), (hidden, hidden_hbm),
            (queries, queries_hbm), (keys, keys_hbm), (values, values_hbm), (cot, grad_y.at[mine])))
    ]
    ring = RingGather(Ring(n_exp), cot, grad_y, ring_sems)
    events = ring.events()
    for k in range(1, n_dp):
        small_copy(k).start()
    gather.start(0)
    gather.start(1)
    ring.start()
    saves[7].start()
    for k, e in enumerate(peers):
        route_copy(k, e).start()
    small_all[me] = small[...]
    routes_all[mine] = routes_t[...]
    bias[...] = mask_bias(parents, tree)
    log_total[...] = jnp.zeros(log_total.shape, F32)
    x = x_ref[...].astype(F32)
    scaled = x * inverse_rms(x)
    for k in range(1, n_dp):
        remote(small, small_all.at[me ^ k], small_send.at[k], small_recv.at[k], dp=me).wait_recv()
    joined = jnp.concatenate([small_all[d] for d in range(n_dp)], axis=1)
    router_t[...] = jnp.zeros(router_t.shape, LOW)
    router_t[pl.ds(0, EXPERTS), :] = joined[:EXPERTS]
    gains[...] = joined[EXPERTS:]
    gain_rows = joined[EXPERTS:].astype(F32)
    hidden[...] = (scaled * gain_rows[:1]).astype(LOW)
    saves[3].start()
    stages = len(gather.orders[0])
    for j in range(stages - 1):
        gather.turn(0, j)
        gather.turn(1, j)
    gather.start(2)
    gather.turn(0, stages - 1)
    gather.turn(1, stages - 1)
    for event in events[:2]:
        ring.handle(event)
    gather.ready(0)
    saves[0].start()

    def rotate(field):
        return field * cosine[...] + turned(field) * sine[...]

    left = lanes_of((tree, 128)) < HD
    tile = 512

    def query_tile(n, carry):
        cols = pl.ds(pl.multiple_of(n * tile, tile), tile)
        pre = dot(hidden[...], query_full[:, cols])
        for i in range(tile // 128):
            at = pl.multiple_of(n * tile + i * 128, 128)
            queries[:, pl.ds(at, 128)] = rotate(pre[:, i * 128 : (i + 1) * 128]).astype(LOW)
        return carry

    lax.fori_loop(0, width // tile, query_tile, 0)
    saves[4].start()
    gather.ready(1)
    saves[1].start()

    def spread(field, out, i):
        other = pltpu.roll(field, HD, 1)
        out[2 * i] = jnp.where(left, field, other).astype(LOW)
        out[2 * i + 1] = jnp.where(left, other, field).astype(LOW)

    half = KV * HD
    pre = dot(hidden[...], keyval_full[:, pl.ds(0, half)])
    for i in range(half // 128):
        spread(rotate(pre[:, i * 128 : (i + 1) * 128]), keys, i)
    saves[5].start()
    pre = dot(hidden[...], keyval_full[:, pl.ds(half, half)])
    for i in range(half // 128):
        spread(pre[:, i * 128 : (i + 1) * 128], values, i)
    saves[6].start()
    for j in range(stages):
        gather.turn(2, j)

    def heads(c, carry):
        cols = pl.ds(pl.multiple_of(c * 128, 128), 128)
        pair = queries[:, cols]
        made = []
        for h in range(2):
            mine_lanes = left if h == 0 else jnp.logical_not(left)
            query = jnp.where(mine_lanes, pair, jnp.zeros_like(pair))
            scores = dot(query, keys[c], 1, 1) * HD**-0.5 + bias[...]
            top = jnp.max(scores, axis=1, keepdims=True)
            powers = jnp.exp(scores - top)
            total = jnp.sum(powers, axis=1, keepdims=True)
            made.append(dot((powers / total).astype(LOW), values[c]))
            log_total[...] = jnp.where(lanes_of((tree, 128)) == 2 * c + h, top + jnp.log(total), log_total[...])
        attended[:, cols] = jnp.where(left, made[0], made[1]).astype(LOW)
        return carry

    lax.fori_loop(0, KV, heads, 0)
    for event in events[2:4]:
        ring.handle(event)
    gather.ready(2)
    saves[2].start()

    def middle_tile(n, carry):
        cols = pl.ds(pl.multiple_of(n * tile, tile), tile)
        middle[:, cols] = x_ref[:, cols].astype(F32) + dot(attended[...], output_full[:, cols])
        return carry

    lax.fori_loop(0, width // tile, middle_tile, 0)
    field = middle[...]
    hidden2[...] = (field * inverse_rms(field) * gain_rows[1:2]).astype(LOW)
    for a in range(3):
        gather.finish(a)
    for k in range(1, n_dp):
        small_copy(k).wait_send()
    for k, e in enumerate(peers):
        route_copy(k, e).wait_send()
        source = lax.rem(mine + n_exp - 1 - k, n_exp)
        remote(routes_t, routes_all.at[source], route_send.at[k], route_recv.at[k], expert=mine).wait_recv()
    for event in events[4:]:
        ring.handle(event)
    ring.finish_own()
    for h in range(2):
        ring.wait_pair(0, h)
    for event in events:
        ring.finish_event(event)
        ring.wait_pair(-event[1] if event[0] == 0 else event[1], event[2])
    for copy in saves:
        copy.wait()


def front(n_dp, n_exp, tokens, gain_pair, router_in, w_query, w_keyval, w_output, routes_t, parents, tables, cot, collective_id):
    tree, width = tokens.shape
    shard = w_query.shape[0]
    shape, sem, vm = jax.ShapeDtypeStruct, pltpu.SemaphoreType.DMA, pltpu.VMEM
    low = shape((tree, width), LOW)
    spread = shape((KV, tree, 128), LOW)
    full = shape((n_dp * shard, width), LOW)
    small = (EXPERTS + 16, shard)
    return pl.pallas_call(
        functools.partial(front_body, n_dp, n_exp),
        out_shape=[
            low, low, spread, spread, low, shape((tree, width), F32), low, shape((tree, 128), F32),
            full, full, full, shape((128, width), LOW), shape((16, width), LOW),
            shape((n_exp,) + routes_t.shape, jnp.int32), shape((n_exp, tree, width), LOW),
        ],
        in_specs=[pl.BlockSpec(memory_space=VMEM)] * 11,
        out_specs=[pl.BlockSpec(memory_space=s) for s in [ANY] * 4 + [VMEM] * 4 + [ANY] * 3 + [VMEM] * 3 + [ANY]],
        scratch_shapes=[
            vm((tree, width), LOW), vm((tree, width), LOW), vm(spread.shape, LOW), vm(spread.shape, LOW),
            vm(full.shape, LOW), vm(full.shape, LOW), vm(full.shape, LOW),
            vm(small, LOW), vm((n_dp,) + small, LOW), vm((tree, tree), F32),
            *DpGather.scratch(3, n_dp), sem((n_dp,)), sem((n_dp,)), sem((n_exp - 1,)), sem((n_exp - 1,)), sem((8,)),
            *RingGather.scratch(n_exp),
        ],
        compiler_params=pltpu.CompilerParams(
            collective_id=collective_id, has_side_effects=True, vmem_limit_bytes=56 * MIB),
        name="front",
    )(tokens, gain_pair, router_in, w_query, w_keyval, w_output, routes_t, parents, *tables, cot)


class GradSum:
    def __init__(self, n_dp, n_exp, chunks, own, bufs, sems):
        self.n_dp, self.chunks, self.own = n_dp, chunks, own
        (self.pair_in, self.dp_in, self.prefix, self.suffix, self.go_r, self.go_l, self.final, self.other) = bufs
        (self.pair_send, self.pair_recv, self.dp_send, self.dp_recv,
         self.send_r, self.send_l, self.recv_r, self.recv_l, self.last_send, self.last_recv) = sems
        self.me, self.mine = lax.axis_index("dp"), lax.axis_index("expert")
        self.core = lax.rem(self.mine, 2)
        self.z = lax.div(self.mine, 2)
        self.depth = n_exp // 2
        self.pair = self.mine + 1 - 2 * self.core
        self.has_left, self.has_right = self.z > 0, self.z < self.depth - 1
        self.orders = bit_orders(n_dp)

    @staticmethod
    def scratch(n_dp, chunks, half, columns):
        sem = pltpu.SemaphoreType.DMA
        stages = max(1, n_dp.bit_length() - 1)
        one = pltpu.VMEM((chunks, half, columns), LOW)
        many = pltpu.VMEM((chunks, n_dp, half, columns), LOW)
        bufs = [many, many, one, one, one, one, one, one]
        sems = [sem((chunks, n_dp)), sem((chunks, n_dp)), sem((chunks, n_dp)), sem((chunks, n_dp))]
        return bufs, sems + [sem((chunks,))] * 6

    def partners(self):
        return [(None, {"dp": self.me ^ bit}) for bit in self.orders[0]] + [
            (self.has_left, {"expert": self.mine - 2}), (self.has_right, {"expert": self.mine + 2})]

    def total(self, i, r):
        return self.own.at[i, self.me ^ r, self.core]

    def across(self, i, d):
        return remote(self.own.at[i, d, 1 - self.core], self.pair_in.at[i, d], self.pair_send.at[i, d],
                      self.pair_recv.at[i, d], expert=self.pair)

    def moved(self, i, j):
        order = self.orders[i % len(self.orders)]
        blocks = [0]
        for bit in order[j + 1 :]:
            blocks = blocks + [r | bit for r in blocks]
        return order[j], [r | order[j] for r in blocks]

    def dp_copy(self, i, r, bit):
        return remote(self.total(i, r), self.dp_in.at[i, r], self.dp_send.at[i, r], self.dp_recv.at[i, r], dp=self.me ^ bit)

    def start(self, i):
        for d in range(self.n_dp):
            self.across(i, d).start()

    def paired(self, i):
        for r in range(self.n_dp - 1, -1, -1):
            d = self.me ^ r
            self.across(i, d).wait_recv()
            add_rows(self.total(i, r), self.total(i, r), self.pair_in.at[i, d])
        self.leave(i, 0)

    def leave(self, i, j):
        if j < len(self.orders[0]):
            bit, blocks = self.moved(i, j)
            for r in blocks:
                self.dp_copy(i, r, bit).start()

    def met(self, i, j):
        bit, blocks = self.moved(i, j)
        for r in blocks:
            self.dp_copy(i, r, bit).wait_recv()
            add_rows(self.total(i, r ^ bit), self.total(i, r ^ bit), self.dp_in.at[i, r])
        self.leave(i, j + 1)

    def right(self, i):
        return remote(self.go_r.at[i], self.prefix.at[i], self.send_r.at[i], self.recv_r.at[i], expert=self.mine + 2)

    def left(self, i):
        return remote(self.go_l.at[i], self.suffix.at[i], self.send_l.at[i], self.recv_l.at[i], expert=self.mine - 2)

    def line(self, t):
        i = t - 2 * self.z
        has_left, has_right = self.has_left, self.has_right

        @pl.when(jnp.logical_and(i >= 0, i < self.chunks))
        def _():
            @pl.when(has_left)
            def _():
                remote(self.go_r.at[i], self.prefix.at[i], self.send_r.at[i], self.recv_r.at[i], expert=self.mine).wait_recv()

            @pl.when(jnp.logical_and(has_left, has_right))
            def _():
                add_rows(self.go_r.at[i], self.total(i, 0), self.prefix.at[i])

            @pl.when(jnp.logical_not(has_left))
            def _():
                add_rows(self.go_r.at[i], self.total(i, 0))

            pl.when(has_right)(lambda: self.right(i).start())

        k = t - 2 * (self.depth - 1 - self.z)

        @pl.when(jnp.logical_and(k >= 0, k < self.chunks))
        def _():
            @pl.when(has_right)
            def _():
                remote(self.go_l.at[k], self.suffix.at[k], self.send_l.at[k], self.recv_l.at[k], expert=self.mine).wait_recv()

            @pl.when(jnp.logical_and(has_left, has_right))
            def _():
                add_rows(self.go_l.at[k], self.total(k, 0), self.suffix.at[k])

            @pl.when(jnp.logical_not(has_right))
            def _():
                add_rows(self.go_l.at[k], self.total(k, 0))

            pl.when(has_left)(lambda: self.left(k).start())

    def last(self, i):
        return remote(self.final.at[i], self.other.at[i], self.last_send.at[i], self.last_recv.at[i], expert=self.pair)

    def close(self, i):
        has_left, has_right = self.has_left, self.has_right

        @pl.when(jnp.logical_and(has_left, has_right))
        def _():
            add_rows(self.final.at[i], self.total(i, 0), self.prefix.at[i], self.suffix.at[i])

        @pl.when(jnp.logical_not(has_left))
        def _():
            add_rows(self.final.at[i], self.total(i, 0), self.suffix.at[i])

        @pl.when(jnp.logical_not(has_right))
        def _():
            add_rows(self.final.at[i], self.total(i, 0), self.prefix.at[i])

        self.last(i).start()

    def finish(self, i):
        self.last(i).wait_send()
        pl.when(self.has_right)(lambda: self.right(i).wait_send())
        pl.when(self.has_left)(lambda: self.left(i).wait_send())
        for d in range(self.n_dp):
            self.across(i, d).wait_send()
        for j in range(len(self.orders[0])):
            bit, blocks = self.moved(i, j)
            for r in blocks:
                self.dp_copy(i, r, bit).wait_send()


def two_parts(field):
    high = field.astype(LOW)
    return high, (field - high.astype(F32)).astype(LOW)


def norm_back(field, gain, grad):
    r = inverse_rms(field)
    scaled = grad * gain
    back = r * scaled - field * (r * r * r) * jnp.mean(field * scaled, axis=-1, keepdims=True)
    return back, jnp.sum(field * r * grad, axis=0, keepdims=True)


def back_body(n_dp, n_exp, local, with_out, x_ref, cot, hid_sum, gates_in, routes_t, parents, cosine, sine,
              hidden, queries, keys, values, attended, middle, hidden2, log_total,
              query_hbm, keyval_hbm, output_hbm, router_t, gains, *refs):
    if with_out:
        parts_hbm, late_hbm, refs = refs[0], refs[1], refs[2:]
    outs, refs = refs[: 5 + 3 * with_out], refs[5 + 3 * with_out :]
    input_grad, grad_q, grad_kv, grad_o, grad_s = outs[:5]
    (bias, branch, grad_att, grad_q_pre, grad_kv_pre, rhs, own, own_s, grad_hid, query_full, keyval_full, output_full,
     load_sem, *rest) = refs
    big = GradSum(n_dp, n_exp, own.shape[0], own, rest[:8], rest[8:18])
    little = GradSum(n_dp, n_exp, 1, own_s, rest[18:26], rest[26:36])
    tree, width = x_ref.shape
    ring = Ring(n_exp)
    greet(big.partners() + ring.partners())
    loads = [
        pltpu.make_async_copy(src, dst, load_sem.at[k])
        for k, (src, dst) in enumerate(((output_hbm, output_full), (query_hbm, query_full), (keyval_hbm, keyval_full)))
    ]
    if with_out:
        parts, part_sem = rest[36], rest[37]
        out = RingScatter(ring, lambda e: parts.at[e], views(rest[38:41]), rest[41:45])
        late_sem, late_send, late_recv, wide_sem = rest[45:49]
        cut = late_hbm.shape[0] // (2 * n_dp)
        kept = {(0, 0): 0, (0, 1): 1, (2, 0): 2, (1, 1): 3}

        def late_rows(r, h):
            return late_hbm.at[pl.ds(pl.multiple_of((big.me ^ r) * 2 * cut + h * cut, 16), cut)]

        def late_half(r, h):
            return keyval_full.at[pl.ds(kept[r, h] * cut, cut)]

        def late_land(k):
            return query_full.at[pl.ds(k * cut, cut)] if k < 5 else keyval_full.at[pl.ds(4 * cut, cut)]

        late = ExpertSum(big.me, late_rows, late_half, late_land, lambda k: late_send.at[k], lambda k: late_recv.at[k])
        late.start()
        late_loads = [pltpu.make_async_copy(late_rows(r, h), late_half(r, h), late_sem.at[k]) for (r, h), k in kept.items()]
        for copy in late_loads:
            copy.start()
        in_rows = outs[6].shape[0]

        def late_end():
            for h in range(2):
                late.end(h, grad_hid.at[pl.ds(0, cut)])
                if h == 0:
                    copies = [pltpu.make_async_copy(grad_hid.at[pl.ds(0, cut)], outs[6].at[pl.ds(0, cut)], wide_sem.at[0])]
                else:
                    copies = [
                        pltpu.make_async_copy(grad_hid.at[pl.ds(0, in_rows - cut)], outs[6].at[pl.ds(cut, in_rows - cut)], wide_sem.at[0]),
                        pltpu.make_async_copy(grad_hid.at[pl.ds(in_rows - cut, 2 * cut - in_rows)], outs[7], wide_sem.at[1])]
                for copy in copies:
                    copy.start()
                for copy in copies:
                    copy.wait()
            late.finish()

        part_loads = [pltpu.make_async_copy(parts_hbm.at[j], parts.at[j], part_sem.at[j]) for j in range(n_exp)]
        for copy in part_loads:
            copy.start()
    loads[0].start()
    if not with_out:
        for copy in loads[1:]:
            copy.start()
    shard = width // n_dp
    side = shard // 2
    tile = 512
    lane = lanes_of((tree, 128))
    left = lane < HD
    if with_out:
        for copy in part_loads:
            copy.wait()
        for d in out.order():
            out.start_pair(d)

    def gain_row(i):
        return gains[...].astype(F32)[i : i + 1]

    bias[...] = mask_bias(parents, tree)

    names = routes_t[...].astype(F32)
    pick = jnp.where(lax.broadcasted_iota(jnp.int32, (16, 128), 0) == lanes_of((16, 128)), 1.0, 0.0).astype(LOW)
    names = dot(jnp.concatenate([names, jnp.zeros_like(names)], axis=0).astype(LOW), pick, 0, 0)
    chosen = jnp.zeros((tree, 128), F32)
    for k in range(routes_t.shape[0]):
        chosen = jnp.maximum(chosen, jnp.where(names[:, k : k + 1] == lane.astype(F32), 1.0, 0.0))
    logits = jnp.where(chosen > 0.5, dot(hidden2[...], router_t[...], 1, 1), -1e30)
    powers = jnp.exp(logits - jnp.max(logits, axis=1, keepdims=True))
    gate = powers / jnp.sum(powers, axis=1, keepdims=True)
    count = gates_in.shape[0]
    where_row = lax.broadcasted_iota(jnp.int32, (count, 128), 0)
    where_lane = lanes_of((count, 128))
    group_row = lax.rem(where_row, 8)
    target = lax.div(where_row, 8) * local + group_row
    pick = jnp.where(group_row < local, jnp.where(target == where_lane, 1.0, 0.0), 0.0).astype(LOW)
    high, low = two_parts(gates_in[...])
    gate_back = dot(high, pick, 0, 0) + dot(low, pick, 0, 0)
    grad_logits = (gate * (gate_back - jnp.sum(gate * gate_back, axis=1, keepdims=True))).astype(LOW)
    grad_router = dot(grad_logits, hidden2[...], 0, 0)[:EXPERTS]
    grad_hidden2 = hid_sum[...] + dot(grad_logits, router_t[...])
    back, gain2_sum = norm_back(middle[...], gain_row(1), grad_hidden2)
    grad_middle = cot[...].astype(F32) + back
    input_grad[...] = grad_middle
    branch[...] = grad_middle.astype(LOW)

    def chunk_grads(i, lhs, rhs_ref):
        def part(n, carry):
            made = dot(lhs[:, pl.ds(pl.multiple_of(n * tile, tile), tile)], rhs_ref[...], 0, 0).astype(LOW)
            for k in range(tile // side):
                own[i, n * (tile // shard) + k // 2, k % 2] = made[k * side : (k + 1) * side]
            return carry

        if tile % shard == 0:
            lax.fori_loop(0, width // tile, part, 0)

    if with_out:
        out.first()
    for i in range(2):
        rhs[...] = branch[:, pl.ds(i * tile, tile)]
        chunk_grads(i, attended, rhs)
        big.start(i)

    if with_out:
        out.early()
    loads[0].wait()

    def att_tile(n, carry):
        rows = pl.ds(pl.multiple_of(n * tile, tile), tile)
        grad_att[:, rows] = dot(branch[...], output_full[rows, :], 1, 1).astype(LOW)
        return carry

    lax.fori_loop(0, width // tile, att_tile, 0)

    def unrotate(field):
        return field * cosine[...] - turned(field * sine[...])

    scale = HD**-0.5

    def group(c):
        cols = pl.ds(pl.multiple_of(c * 128, 128), 128)
        pair, grad_pair = queries[:, cols], grad_att[:, cols]
        zero = jnp.zeros_like(pair)
        key, value = keys[c], values[c]
        grad_query, grad_key, grad_value = [], 0.0, 0.0
        for h in range(2):
            here = left if h == 0 else jnp.logical_not(left)
            query, grad_out = jnp.where(here, pair, zero), jnp.where(here, grad_pair, zero)
            logs = jnp.sum(jnp.where(lane == 2 * c + h, log_total[...], 0.0), axis=1, keepdims=True)
            probs = jnp.exp(dot(query, key, 1, 1) * scale + bias[...] - logs)
            grad_probs = dot(grad_out, value, 1, 1)
            grad_scores = (probs * (grad_probs - jnp.sum(probs * grad_probs, axis=1, keepdims=True))).astype(LOW)
            grad_value = grad_value + dot(probs.astype(LOW), grad_out, 0, 0)
            grad_query.append(dot(grad_scores, key))
            grad_key = grad_key + dot(grad_scores, query, 0, 0)
        grad_q_pre[:, cols] = unrotate(jnp.where(left, grad_query[0], grad_query[1]) * scale).astype(LOW)
        grad_key = (grad_key + pltpu.roll(grad_key, HD, 1)) * scale
        return unrotate(grad_key), grad_value + pltpu.roll(grad_value, HD, 1)

    def two_groups(i):
        key_a, value_a = group(2 * i)
        key_b, value_b = group(2 * i + 1)
        at = pl.multiple_of(i * 128, 128)
        grad_kv_pre[:, pl.ds(at, 128)] = jnp.where(left, key_a, key_b).astype(LOW)
        at = pl.multiple_of(KV * HD + i * 128, 128)
        grad_kv_pre[:, pl.ds(at, 128)] = jnp.where(left, value_a, value_b).astype(LOW)

    def gather_rhs(i):
        rhs[:, pl.ds(0, 256)] = grad_q_pre[:, pl.ds(i * 256, 256)]
        rhs[:, pl.ds(256, 128)] = grad_kv_pre[:, pl.ds(i * 128, 128)]
        rhs[:, pl.ds(384, 128)] = grad_kv_pre[:, pl.ds(KV * HD + i * 128, 128)]

    for i in range(KV // 2):
        two_groups(i)
        gather_rhs(i)
        chunk_grads(2 + i, hidden, rhs)
        big.start(2 + i)
        if i == 0:
            big.paired(0)
            big.paired(1)
        if i == 1:
            if with_out:
                out.late()
                for copy in late_loads:
                    copy.wait()
                late.turn()
            big.paired(2)
        if i == 2:
            if with_out:
                late_end()
                for copy in loads[1:]:
                    copy.start()
            big.met(0, 0)
            big.met(1, 0)
            big.paired(3)
        if i == 3:
            big.met(0, 1)
            big.met(1, 1)
            big.paired(4)
            big.met(2, 0)

    for copy in loads[1:]:
        copy.wait()
    big.line(0)

    def hidden_tile(n, carry):
        cols = pl.ds(pl.multiple_of(n * tile, tile), tile)
        grad_hid[:, cols] = dot(grad_q_pre[...], query_full[cols, :], 1, 1) + dot(grad_kv_pre[...], keyval_full[cols, :], 1, 1)
        return carry

    lax.fori_loop(0, width // tile, hidden_tile, 0)
    big.paired(5)
    big.met(3, 0)
    big.line(1)
    back, gain1_sum = norm_back(x_ref[...].astype(F32), gain_row(0), grad_hid[...])
    input_grad[...] = input_grad[...] + back

    sub = lax.broadcasted_iota(jnp.int32, (16, width), 0)
    sums = jnp.where(sub == 0, gain1_sum, jnp.where(sub == 1, gain2_sum, 0.0))
    little_all = jnp.concatenate([grad_router, sums], axis=0).astype(LOW)
    for d in range(n_dp):
        for k in range(2):
            at = d * shard + k * side
            own_s[0, d, k] = little_all[:, at : at + side]
    little.start(0)
    big.met(2, 1)
    big.line(2)
    big.met(4, 0)
    little.paired(0)
    big.met(3, 1)
    big.line(3)
    big.met(5, 0)
    little.met(0, 0)
    big.met(4, 1)
    big.line(4)
    little.met(0, 1)
    big.met(5, 1)
    big.line(5)
    if with_out:
        out.last(outs[5], middle)
    chunks = own.shape[0]
    hop = 2 * (big.depth - 1)
    for t in range(chunks, chunks + hop):
        big.line(t)
        if t >= hop:
            big.close(t - hop)

    def little_line(t, carry):
        little.line(t)
        return carry

    lax.fori_loop(0, hop + 1, little_line, 0)
    little.close(0)

    def place(i, which, field):
        rows = pl.ds(pl.multiple_of(which * side, 16), side)
        if i < 2:
            add_rows(grad_o.at[rows, pl.ds(i * tile, tile)], field)
            return
        i = i - 2
        add_rows(grad_q.at[rows, pl.ds(i * 256, 256)], field.at[:, pl.ds(0, 256)])
        add_rows(grad_kv.at[rows, pl.ds(i * 128, 128)], field.at[:, pl.ds(256, 128)])
        add_rows(grad_kv.at[rows, pl.ds(KV * HD + i * 128, 128)], field.at[:, pl.ds(384, 128)])

    for i in range(chunks):
        place(i, big.core, big.final.at[i])
    add_rows(grad_s.at[big.core], little.final.at[0])
    for i in range(chunks):
        big.last(i).wait_recv()
        place(i, 1 - big.core, big.other.at[i])
        big.finish(i)
    little.last(0).wait_recv()
    add_rows(grad_s.at[1 - big.core], little.other.at[0])
    little.finish(0)
    if with_out:
        out.finish_sends()


def back(n_dp, n_exp, local, tokens, cotangent, hid_sum, gates_in, routes_t, parents, tables, saved, parts, late, collective_id):
    tree, width = tokens.shape
    shard = width // n_dp
    shape, vm, sem = jax.ShapeDtypeStruct, pltpu.VMEM, pltpu.SemaphoreType.DMA
    side, chunks, tile, rows = shard // 2, 6, 512, EXPERTS + 16
    big_bufs, big_sems = GradSum.scratch(n_dp, chunks, side, tile)
    little_bufs, little_sems = GradSum.scratch(n_dp, 1, rows, side)
    args = (tokens, cotangent, hid_sum, gates_in, routes_t, parents, *tables, *saved)
    spaces = [VMEM] * len(args)
    spaces[16:19] = [ANY] * 3
    out_shape = [
        shape((tree, width), F32), shape((shard, width), F32), shape((shard, width), F32), shape((shard, width), F32),
        shape((2, rows, side), F32),
    ]
    extra = []
    if parts is not None:
        args, spaces = (*args, parts, late), spaces + [ANY] * 2
        out_rows = late.shape[0] // n_dp - shard
        out_shape += [shape((tree, width), LOW), shape((shard, width), F32), shape((out_rows, width), F32)]
        bufs, sems = RingScatter.scratch(n_exp, (tree, width), LOW)
        extra = [vm(parts.shape, LOW), sem((n_exp,)), *bufs, *sems, sem((4,)), sem((6,)), sem((6,)), sem((2,))]
    return pl.pallas_call(
        functools.partial(back_body, n_dp, n_exp, local, parts is not None),
        out_shape=out_shape,
        in_specs=[pl.BlockSpec(memory_space=s) for s in spaces],
        out_specs=[pl.BlockSpec(memory_space=s) for s in ([VMEM] * 6 + [ANY] * 2)[: len(out_shape)]],
        scratch_shapes=[
            vm((tree, tree), F32), vm((tree, width), LOW), vm((tree, width), LOW), vm((tree, width), LOW), vm((tree, width), LOW),
            vm((tree, tile), LOW), vm((chunks, n_dp, 2, side, tile), LOW), vm((1, n_dp, 2, rows, side), LOW),
            vm((tree, width), F32), vm((width, width), LOW), vm((width, width), LOW), vm((width, width), LOW), sem((3,)),
            *big_bufs, *big_sems, *little_bufs, *little_sems, *extra,
        ],
        compiler_params=pltpu.CompilerParams(
            collective_id=collective_id, has_side_effects=True, vmem_limit_bytes=63 * MIB),
        name="back",
    )(*args)


def rope_pairs(tree_rows):
    unit = tree_rows // 20
    row = np.arange(tree_rows)
    position = np.where(row < 8 * unit, row, np.where(row < 12 * unit, 8 * unit + row % unit, 9 * unit + row % unit))
    frequency = 10000.0 ** (-np.arange(0, HD, 2) / HD)
    angles = position[:, None] * frequency[None, :]
    return tuple(jnp.asarray(np.concatenate([table] * 4, axis=1), jnp.float32) for table in (np.cos(angles), np.sin(angles)))


def gated_unit(gate_up):
    width_ff = gate_up.shape[-1] // 2
    gate_part = gate_up[..., :width_ff]
    return gate_part / (1.0 + jnp.exp(-gate_part)) * gate_up[..., width_ff:]


def experts_plain(
    n_dp, n_exp, hidden2, grad_y, routes_all, router_full, expert_in, expert_out, middle
):
    tree_rows, width = hidden2.shape
    capacity = CAP
    routes_all = routes_all.transpose(0, 2, 1)
    expert_ids = jnp.arange(EXPERTS, dtype=jnp.int32)
    here = lax.axis_index("expert")
    local = expert_in.shape[0]
    first = here * local
    hidden_all = lax.all_gather(hidden2, "expert", axis=0, tiled=False)
    own_ids = first + jnp.arange(local, dtype=jnp.int32)
    hot_all = routes_all[:, :, :, None] == expert_ids[None, None, None, :]
    chosen_all = jnp.any(hot_all, axis=2)
    chosen = jnp.any(routes_all[:, :, :, None] == own_ids[None, None, None, :], axis=2)
    lower = jnp.tril(jnp.ones((tree_rows, tree_rows), jnp.bfloat16), -1)
    rank = jnp.einsum(
        "tu,jue->jet", lower, chosen.astype(jnp.bfloat16), preferred_element_type=jnp.float32
    ).astype(jnp.int32)
    slots = jnp.arange(capacity, dtype=jnp.int32)
    chosen_t = chosen.transpose(0, 2, 1)
    place = (rank[:, :, None, :] == slots[None, None, :, None]) & chosen_t[:, :, None, :]
    place = place.astype(jnp.bfloat16)
    logits_all = jnp.einsum(
        "jtd,de->jte", hidden_all, router_full, preferred_element_type=jnp.float32
    )
    masked = jnp.where(chosen_all, logits_all, -1e30)
    weight = jnp.exp(masked - jnp.max(masked, axis=-1, keepdims=True))
    weight = weight / jnp.sum(weight, axis=-1, keepdims=True)
    gates_own = lax.dynamic_slice_in_dim(weight, first, local, axis=2)
    gate_slot = jnp.einsum(
        "jest,jte->ejs", place.astype(jnp.float32), gates_own, precision=lax.Precision.HIGHEST
    )[..., None]
    sent = jnp.einsum("jest,jtd->ejsd", place, hidden_all, preferred_element_type=jnp.float32)
    sent = sent.astype(jnp.bfloat16)
    grad_rows = jnp.einsum("jest,jtd->ejsd", place, grad_y, preferred_element_type=jnp.float32)
    grad_rows = grad_rows.astype(jnp.bfloat16)
    gate_up = jnp.einsum("ejsd,edf->ejsf", sent, expert_in, preferred_element_type=jnp.float32)
    activated, glu_back = jax.vjp(gated_unit, gate_up)
    act_low = activated.astype(jnp.bfloat16).astype(jnp.float32)
    act_scaled = (act_low * gate_slot).astype(jnp.bfloat16)
    made = jnp.einsum(
        "ejsf,efd->ejsd", act_scaled, expert_out, preferred_element_type=jnp.float32
    ).astype(jnp.bfloat16)
    out_part = jnp.einsum("jest,ejsd->jtd", place, made, preferred_element_type=jnp.float32)
    out_sum = lax.psum_scatter(
        out_part.astype(jnp.bfloat16), "expert", scatter_dimension=0, tiled=False
    ).astype(jnp.float32)
    result = middle + out_sum
    block_out = result.astype(jnp.bfloat16)
    grad_act = jnp.einsum(
        "ejsd,efd->ejsf", grad_rows, expert_out, preferred_element_type=jnp.float32
    )
    gate_dot = jnp.sum(act_low * grad_act, axis=-1)
    gates_back = jnp.einsum(
        "jest,ejs->jte", place.astype(jnp.float32), gate_dot, precision=lax.Precision.HIGHEST
    )
    grad_out_w = jnp.einsum(
        "ejsf,ejsd->efd", act_scaled, grad_rows, preferred_element_type=jnp.float32
    )
    grad_gate_up = glu_back(grad_act * gate_slot)[0].astype(jnp.bfloat16)
    grad_sent = jnp.einsum(
        "ejsf,edf->ejsd", grad_gate_up, expert_in, preferred_element_type=jnp.float32
    ).astype(jnp.bfloat16)
    grad_in_w = jnp.einsum(
        "ejsd,ejsf->edf", sent, grad_gate_up, preferred_element_type=jnp.float32
    )
    hid_part = jnp.einsum("jest,ejsd->jtd", place, grad_sent, preferred_element_type=jnp.float32)
    gates_mine = lax.all_to_all(gates_back, "expert", split_axis=0, concat_axis=2, tiled=True)[0]
    hid_sum = lax.psum_scatter(
        hid_part.astype(jnp.bfloat16), "expert", scatter_dimension=0, tiled=False
    ).astype(jnp.float32)
    local, units = expert_in.shape[0], expert_out.shape[1]
    low = jnp.bfloat16
    grads = jnp.concatenate(
        [
            grad_in_w.astype(low).reshape(local, n_dp, width // n_dp, width),
            grad_out_w.astype(low).reshape(local, n_dp, units // n_dp, width),
        ],
        axis=2,
    ).reshape(local, width + units, width)
    share = lax.psum_scatter(grads, "dp", scatter_dimension=1, tiled=True).astype(jnp.float32)
    gates_mine = jnp.pad(gates_mine.T.reshape(n_exp, local, tree_rows), ((0, 0), (0, 8 - local), (0, 0)))
    return block_out, hid_sum, gates_mine, share[:, : width // n_dp], share[:, width // n_dp :]


def shards(
    tokens,
    attn_gain,
    w_query,
    w_keyval,
    w_output,
    moe_gain,
    w_router,
    expert_in,
    expert_out,
    cotangent,
    routes,
    parents,
):
    n_dp, n_exp = lax.axis_size("dp"), lax.axis_size("expert")
    local = expert_in.shape[0]
    tree_rows = tokens.shape[0]
    tables = rope_pairs(tree_rows)
    routes_t = routes.T
    (hidden, queries, keys, values, attended, middle, hidden2, log_total, *full, gains, routes_all, grad_y) = front(
        n_dp, n_exp, tokens, jnp.stack([attn_gain, moe_gain]), w_router.T, w_query, w_keyval, w_output, routes_t, parents, tables, cotangent, 1
    )
    router_t = full[3]
    if (n_dp, n_exp) == (4, 8):
        parts, hid_sum, gate_grads, expert_in_share, expert_out_share, late = experts(
            n_dp, n_exp, hidden2, grad_y, routes_all, router_t, expert_in, expert_out, 2
        )
    else:
        parts = late = None
        block_out, hid_sum, gate_grads, expert_in_share, expert_out_share = experts_plain(
            n_dp, n_exp, hidden2, grad_y, routes_all, router_t[:EXPERTS].T, expert_in, expert_out, middle
        )
    saved = (hidden, queries, keys, values, attended, middle, hidden2, log_total, *full, gains)
    input_grad, grad_q, grad_kv, grad_o, grad_small, *made = back(
        n_dp, n_exp, local, tokens, cotangent, hid_sum, gate_grads.reshape(n_exp * 8, tree_rows), routes_t, parents, tables, saved, parts, late, 3
    )
    if parts is not None:
        block_out = made[0]
        expert_in_share = jnp.concatenate([expert_in_share, made[1][None]], axis=0)
        expert_out_share = jnp.concatenate([expert_out_share, made[2][None]], axis=0)
    return (
        block_out,
        input_grad,
        grad_small[:, EXPERTS].reshape(-1),
        grad_q,
        grad_kv,
        grad_o,
        grad_small[:, EXPERTS + 1].reshape(-1),
        jnp.concatenate([grad_small[0, :EXPERTS], grad_small[1, :EXPERTS]], axis=1).T,
        expert_in_share,
        expert_out_share,
    )


def solution(mesh):
    in_specs = (
        P(("dp", "expert"), None),
        P("dp"),
        P("dp", None),
        P("dp", None),
        P("dp", None),
        P("dp"),
        P("dp", None),
        P("expert", None, None),
        P("expert", None, None),
        P(("dp", "expert"), None),
        P(("dp", "expert"), None),
        P(("dp", "expert"), None),
    )
    out_specs = (
        P(("dp", "expert"), None),
        P(("dp", "expert"), None),
        P("dp"),
        P("dp", None),
        P("dp", None),
        P("dp", None),
        P("dp"),
        P("dp", None),
        P("expert", "dp", None),
        P("expert", "dp", None),
    )
    return jax.shard_map(shards, mesh=mesh, in_specs=in_specs, out_specs=out_specs, check_vma=False)
```

```python
import functools

import jax
import jax.numpy as jnp
import numpy as np
from jax import lax
from jax.experimental import pallas as pl
from jax.experimental.pallas import tpu as pltpu
from jax.sharding import PartitionSpec as P

H = 16
KV = 8
HD = 64
EXPERTS = 32
TOPK = 8
CAP = 120


EPSILON = 1e-06


MESH = pl.DeviceIdType.MESH
MIB = 1024 * 1024
VMEM = pltpu.VMEM
ANY = pl.ANY


def remote(src, dst, send_sem, recv_sem, **where):
    return pltpu.make_async_remote_copy(
        src_ref=src, dst_ref=dst, send_sem=send_sem, recv_sem=recv_sem,
        device_id=where, device_id_type=MESH,
    )


def greet(partners):
    barrier = pltpu.get_barrier_semaphore()
    for condition, where in partners:
        def signal(where=where):
            pl.semaphore_signal(barrier, inc=1, device_id=where, device_id_type=MESH)
        if condition is None:
            signal()
        else:
            pl.when(condition)(signal)
    count = sum(1 if c is None else c.astype(jnp.int32) for c, _ in partners)
    pl.semaphore_wait(barrier, count)


def add_rows(out, *terms, step=16):
    rows = out.shape[0]

    def body(i, carry):
        at = pl.ds(pl.multiple_of(i * step, step), step)
        total = terms[0][at, :].astype(jnp.float32)
        for term in terms[1:]:
            total = total + term[at, :].astype(jnp.float32)
        out[at, :] = total.astype(out.dtype)
        return carry

    lax.fori_loop(0, rows // step, body, 0)


def bit_orders(n):
    bits = [1 << j for j in range(n.bit_length() - 1)]
    return [bits[p:] + bits[:p] for p in range(len(bits))] or [[]]


class Ring:
    def __init__(self, n_exp):
        self.mine = lax.axis_index("expert")
        self.core = lax.rem(self.mine, 2)
        self.z = lax.div(self.mine, 2)
        self.depth = n_exp // 2
        self.far = self.depth // 2
        self.pair = self.mine + 1 - 2 * self.core
        self.right, self.left = self.dev(1), self.dev(-1)

    def dev(self, d):
        return lax.rem(self.z + d + self.depth, self.depth) * 2 + self.core

    def partners(self):
        return [(None, {"expert": e}) for e in (self.pair, self.right, self.left)]


class RingGather:
    def __init__(self, ring, own, out, sems):
        self.ring, self.own, self.out = ring, own, out
        self.send, self.recv, self.pair_send, self.pair_recv = sems
        self.half = own.shape[0] // 2

    @staticmethod
    def scratch(n_exp):
        far, depth = n_exp // 4, n_exp // 2
        sem = pltpu.SemaphoreType.DMA
        return [sem((2, far + 1, 2)), sem((2, far + 1, 2)), sem((depth, 2)), sem((depth, 2))]

    def rows(self, h):
        return pl.ds(h * self.half, self.half)

    def goes(self, side, s, h):
        far = self.ring.far
        return s < far or (s == far and h == side)

    def block(self, d, h):
        return self.out.at[self.ring.dev(d), self.rows(h)]

    def hop(self, side, s, h):
        d = -s if side == 0 else s
        src = self.own.at[self.rows(h)] if s == 0 else self.block(d, h)
        to = self.ring.right if side == 0 else self.ring.left
        return remote(src, self.block(d, h), self.send.at[side, s, h], self.recv.at[side, s + 1, h], expert=to)

    def across(self, d, h):
        src = self.own.at[self.rows(h)] if d == 0 else self.block(d, h)
        slot = d % self.ring.depth
        return remote(src, self.block(d, h), self.pair_send.at[slot, h], self.pair_recv.at[slot, h], expert=self.ring.pair)

    ORDER = ((0, 0), (1, 1), (0, 1), (1, 0))

    def start(self):
        for side, h in self.ORDER:
            if self.goes(side, 1, h):
                self.hop(side, 0, h).start()
        self.across(0, 0).start()
        self.across(0, 1).start()

    def events(self):
        return [(side, s, h) for s in range(1, self.ring.far + 1) for side, h in self.ORDER if self.goes(side, s, h)]

    def handle(self, event):
        side, s, h = event
        d = -s if side == 0 else s
        here = self.block(d, h)
        remote(here, here, self.send.at[side, s, h], self.recv.at[side, s, h], expert=self.ring.mine).wait_recv()
        if self.goes(side, s + 1, h):
            self.hop(side, s, h).start()
        self.across(d, h).start()

    def wait_pair(self, d, h):
        slot = d % self.ring.depth
        here = self.out.at[self.ring.pair - self.ring.mine + self.ring.dev(d), self.rows(h)]
        remote(here, here, self.pair_send.at[slot, h], self.pair_recv.at[slot, h], expert=self.ring.mine).wait_recv()

    def finish_own(self):
        for side, h in self.ORDER:
            if self.goes(side, 1, h):
                self.hop(side, 0, h).wait_send()
        self.across(0, 0).wait_send()
        self.across(0, 1).wait_send()

    def finish_event(self, event):
        side, s, h = event
        if self.goes(side, s + 1, h):
            self.hop(side, s, h).wait_send()
        self.across(-s if side == 0 else s, h).wait_send()


class RingScatter:
    def __init__(self, ring, part, bufs, sems):
        self.ring, self.part = ring, part
        self.pair_buf, self.held, self.got = bufs
        self.pair_send, self.pair_recv, self.send, self.recv = sems
        self.half = self.held(0).shape[0] // 2

    @staticmethod
    def scratch(n_exp, block, dtype):
        far, depth = n_exp // 4, n_exp // 2
        sem = pltpu.SemaphoreType.DMA
        bufs = [pltpu.VMEM((depth,) + block, dtype), pltpu.VMEM((depth,) + block, dtype),
                pltpu.VMEM((2, far) + block, dtype)]
        return bufs, [sem((depth,)), sem((depth,)), sem((2, far + 1, 2)), sem((2, far + 1, 2))]

    def rows(self, h):
        return pl.ds(h * self.half, self.half)

    def order(self):
        far, depth = self.ring.far, self.ring.depth
        order = [far]
        for s in range(far - 1, 0, -1):
            order += [s, depth - s]
        return order + [0]

    def comes(self, side, d, h):
        far = self.ring.far
        return d + 1 < far or (d + 1 == far and h == side)

    def across(self, d):
        ring = self.ring
        return remote(self.part(d, 1), self.pair_buf(d),
                      self.pair_send.at[d], self.pair_recv.at[d], expert=ring.pair)

    def start_pair(self, d):
        self.across(d).start()

    def wait_pair(self, d):
        self.across(d).wait_recv()

    def wait_got(self, side, d, h):
        here = self.got(side, d).at[self.rows(h)]
        remote(here, here, self.send.at[side, d, h], self.recv.at[side, d, h], expert=self.ring.mine).wait_recv()

    def hop(self, side, d, h):
        slot = d if side == 0 else self.ring.depth - d
        rows = self.rows(h)
        return remote(self.held(slot).at[rows], self.got(side, d - 1).at[rows], self.send.at[side, d, h],
                      self.recv.at[side, d - 1, h], expert=self.ring.right if side == 0 else self.ring.left)

    def push(self, side, d, h):
        ring = self.ring
        slot = d if side == 0 else ring.depth - d
        rows = self.rows(h)
        terms = [self.part(slot, 0).at[rows], self.pair_buf(slot).at[rows]]
        if self.comes(side, d, h):
            self.wait_got(side, d, h)
            terms.append(self.got(side, d).at[rows])
        add_rows(self.held(slot).at[rows], *terms)
        self.hop(side, d, h).start()

    def first(self):
        far = self.ring.far
        self.wait_pair(far)
        self.push(0, far, 0)
        self.push(1, far, 1)

    def early(self):
        for d in range(self.ring.far - 1, 0, -1):
            self.wait_pair(d)
            self.push(0, d, 1)
            self.wait_pair(self.ring.depth - d)
            self.push(1, d, 0)

    def late(self):
        for d in range(self.ring.far - 1, 0, -1):
            self.push(0, d, 0)
            self.push(1, d, 1)

    def last(self, out, *more):
        self.wait_pair(0)
        for h in range(2):
            rows = self.rows(h)
            terms = [self.part(0, 0).at[rows], self.pair_buf(0).at[rows]] + [m.at[rows] for m in more]
            for side in range(2):
                if self.comes(side, 0, h):
                    self.wait_got(side, 0, h)
                    terms.append(self.got(side, 0).at[rows])
            add_rows(out.at[rows], *terms)

    def finish_sends(self):
        far = self.ring.far
        for side in range(2):
            for d in range(1, far + 1):
                for h in range(2):
                    if d < far or h == side:
                        self.hop(side, d, h).wait_send()
        for d in range(self.ring.depth):
            self.across(d).wait_send()


def views(bufs):
    pair_buf, held, got = bufs
    return (lambda d: pair_buf.at[d], lambda d: held.at[d], lambda side, d: got.at[side, d])


SLOTS = 128
F32, LOW = jnp.float32, jnp.bfloat16


def dot(a, b, over_a=1, over_b=0):
    return lax.dot_general(a, b, (((over_a,), (over_b,)), ((), ())), preferred_element_type=F32)


class ExpertSum:
    def __init__(self, me, first, half, land, send, recv):
        self.me, self.first, self.half, self.land, self.send, self.recv = me, first, half, land, send, recv

    def hop(self, step, h, which):
        bit = (1, 2)[h] if step == 0 else (2, 1)[h]
        r = bit if which == 0 else 3
        k = 2 * h + which if step == 0 else 4 + h
        src = self.first(r, h) if step == 0 else self.half(r, h)
        return remote(src, self.land(k), self.send(k), self.recv(k), dp=self.me ^ bit)

    def start(self, blocks=(1, 0)):
        for which in blocks:
            for h in range(2):
                self.hop(0, h, which).start()

    def turn(self, blocks=(1, 0)):
        for which in blocks:
            for h in range(2):
                self.hop(0, h, which).wait_recv()
                kept = 0 if which == 0 else (2, 1)[h]
                add_rows(self.half(kept, h), self.half(kept, h), self.land(2 * h + which))
                if which == 1:
                    self.hop(1, h, 0).start()

    def end(self, h, out):
        self.hop(1, h, 0).wait_recv()
        add_rows(out, self.half(0, h), self.land(4 + h))

    def finish(self):
        for step, h, which in ((0, 0, 0), (0, 0, 1), (0, 1, 0), (0, 1, 1), (1, 0, 0), (1, 1, 0)):
            self.hop(step, h, which).wait_send()


def experts_body(n_dp, n_exp, hid_ref, gy_hbm, routes_t, wr_t, w_in_hbm, w_out_hbm, middle,
                 block_out, hid_sum, gates_out, in_share, out_share, late,
                 x_all, w_in, w_out, sent, grows, gu, tmp, acts, stage, slots, gates, dots, wide,
                 pair_buf, held, got, *sems):
    w_sem, gy_sem, wide_sem, own_sem, ready, late_sem, gate_send, gate_recv, dp_ready, dp_send, dp_recv = sems[:11]
    gather_sems, out_sems, hid_sems = sems[11:15], sems[15:19], sems[19:23]
    me = lax.axis_index("dp")
    local, _, width = sent.shape
    tree, hidden_units = hid_ref.shape[0], w_out.shape[1]
    rows_e = local * SLOTS
    ring = Ring(n_exp)
    mine, core, depth = ring.mine, ring.core, ring.depth
    first = mine * local
    peers = [lax.rem(mine + k, n_exp) for k in range(1, n_exp)]
    greet([(None, {"expert": e}) for e in peers] + [(None, {"dp": me ^ bit}) for bit in (1, 2)])

    weights = [pltpu.make_async_copy(w_in_hbm, w_in, w_sem.at[0]), pltpu.make_async_copy(w_out_hbm, w_out, w_sem.at[1])]
    gather = RingGather(ring, hid_ref, x_all, gather_sems)
    gather.start()
    for copy in weights:
        copy.start()
    own = pltpu.make_async_copy(hid_ref, x_all.at[mine], own_sem)
    own.start()

    def gy_buf(j):
        return stage.at[lax.rem(j, 2), pl.ds(0, tree)]

    def gy_copy(j):
        return pltpu.make_async_copy(gy_hbm.at[j], gy_buf(j), gy_sem.at[lax.rem(j, 2)])

    gy_copy(0).start()

    below = (lax.broadcasted_iota(jnp.int32, (tree, tree), 0) < lax.broadcasted_iota(jnp.int32, (tree, tree), 1)).astype(LOW)
    sub16 = lax.broadcasted_iota(jnp.int32, (16, tree), 0)

    def find_slots(j, carry):
        names = routes_t[j]
        chosen = jnp.zeros((16, tree), F32)
        for k in range(names.shape[0]):
            chosen = jnp.maximum(chosen, jnp.where(names[k : k + 1, :] == first + sub16, 1.0, 0.0))
        chosen = jnp.where(sub16 < local, chosen, 0.0)
        rank = dot(chosen.astype(LOW), below)
        slots[j] = jnp.where(chosen > 0.5, rank, -1.0)[:8]
        return carry

    lax.fori_loop(0, n_exp, find_slots, 0)

    slot_ids = lax.broadcasted_iota(jnp.int32, (SLOTS, tree), 0).astype(F32)

    def places(j):
        return jnp.concatenate(
            [jnp.where(slot_ids == slots[j, i : i + 1, :], 1.0, 0.0).astype(LOW) for i in range(local)], axis=0)

    def places_t(j):
        lane = lax.broadcasted_iota(jnp.int32, (tree, 128), 1)
        pick = jnp.where(lax.broadcasted_iota(jnp.int32, (16, 128), 0) == lax.broadcasted_iota(jnp.int32, (16, 128), 1), 1.0, 0.0)
        slot = dot(jnp.concatenate([slots[j], jnp.zeros((8, tree), F32)], axis=0).astype(LOW), pick.astype(LOW), 0, 0)
        lanes = lane.astype(F32)
        return jnp.concatenate(
            [jnp.where(lanes == slot[:, i : i + 1], 1.0, 0.0).astype(LOW) for i in range(local)], axis=1)

    def find_gates(j):
        names = routes_t[j]
        experts = lax.broadcasted_iota(jnp.int32, (EXPERTS, tree), 0)
        chosen = jnp.zeros((EXPERTS, tree), F32)
        for k in range(names.shape[0]):
            chosen = jnp.maximum(chosen, jnp.where(names[k : k + 1, :] == experts, 1.0, 0.0))
        logits = jnp.where(chosen > 0.5, dot(wr_t[pl.ds(0, EXPERTS), :], x_all[j], 1, 1), -1e30)
        powers = jnp.exp(logits - jnp.max(logits, axis=0, keepdims=True))
        share = powers / jnp.sum(powers, axis=0, keepdims=True)
        sub = lax.broadcasted_iota(jnp.int32, (8, tree), 0)
        own_gates = jnp.zeros((8, tree), F32)
        for i in range(local):
            row = jnp.sum(jnp.where(experts == first + i, share, 0.0), axis=0, keepdims=True)
            own_gates = jnp.where(sub == i, row, own_gates)
        gates[j] = own_gates

    halves = width // 512

    def dispatch(j, src, dest):
        place = places(j)

        def body(n, carry):
            cols = pl.ds(pl.multiple_of(n * 512, 512), 512)
            picked = dot(place, src[:, cols]).astype(LOW)
            for i in range(local):
                dest[i, pl.ds(pl.multiple_of(j * SLOTS, SLOTS), SLOTS), cols] = picked[i * SLOTS : (i + 1) * SLOTS]
            return carry

        lax.fori_loop(0, halves, body, 0)

    def slot_gate(j, e):
        return jnp.sum(jnp.where(slot_ids == slots[j, pl.ds(e, 1), :], gates[j, pl.ds(e, 1), :], 0.0), axis=1, keepdims=True)

    def forward(chip):
        pair_rows = pl.ds(pl.multiple_of(chip * 2 * SLOTS, 2 * SLOTS), 2 * SLOTS)

        def one_tree(q, carry):
            j = 2 * chip + q
            find_gates(j)
            dispatch(j, x_all.at[j], sent)
            return carry

        lax.fori_loop(0, 2, one_tree, 0)

        def one_expert(e, carry):
            both = dot(sent[e, pair_rows, :], w_in[e])
            gu[e, pair_rows, :] = both.astype(LOW)
            a, b = both[:, :hidden_units], both[:, hidden_units:]
            act = (a / (1.0 + jnp.exp(-a)) * b).astype(LOW).astype(F32)
            gate = jnp.concatenate([slot_gate(2 * chip, e), slot_gate(2 * chip + 1, e)], axis=0)
            made = dot((act * gate).astype(LOW), w_out[e]).astype(LOW)
            for q in range(2):
                tmp[pl.ds(pl.multiple_of(q * rows_e + e * SLOTS, SLOTS), SLOTS), :] = made[q * SLOTS : (q + 1) * SLOTS]
            return carry

        lax.fori_loop(0, local, one_expert, 0)

    def combine_out(chip):
        def one_tree(q, carry):
            j = 2 * chip + q
            rows = pl.ds(pl.multiple_of(q * rows_e, rows_e), rows_e)
            x_all[j] = dot(places_t(j), tmp[rows, :]).astype(LOW)
            return carry

        lax.fori_loop(0, 2, one_tree, 0)

    def grad_rows(j, carry):
        pl.when(j + 1 < n_exp)(lambda: gy_copy(j + 1).start())
        gy_copy(j).wait()
        dispatch(j, gy_buf(j), grows)
        return carry

    events = gather.events()

    def out_part(d, other):
        return x_all.at[ring.dev(d) + other * (1 - 2 * core)]

    out = RingScatter(ring, out_part, views((pair_buf, held, got)), out_sems)

    def chip_at(d):
        return lax.rem(ring.z + d, depth)

    def group(g, carry):
        d = jnp.where(g == 0, 0, jnp.where(g == 1, depth - 1, jnp.where(g == 2, 1, 2)))
        chip = chip_at(d)

        @pl.when(g == 0)
        def _():
            own.wait()
            gather.wait_pair(0, 0)
            gather.wait_pair(0, 1)
            for copy in weights:
                copy.wait()

        @pl.when(g == 1)
        def _():
            for event in events[:4]:
                gather.handle(event)
            gather.wait_pair(-1, 0)
            gather.wait_pair(-1, 1)

        @pl.when(g == 2)
        def _():
            gather.wait_pair(1, 0)
            gather.wait_pair(1, 1)

        @pl.when(g == 3)
        def _():
            for event in events[4:]:
                gather.handle(event)
            gather.wait_pair(2, 0)
            gather.wait_pair(2, 1)

        forward(chip)

        @pl.when(g == 0)
        def _():
            gather.finish_own()
            lax.fori_loop(0, n_exp, grad_rows, 0)

        for at, d in ((1, -1), (2, 1), (3, 2)):
            @pl.when(g == at)
            def _():
                for event in events:
                    if event[1] == abs(d) and (abs(d) == 2 or (event[0] == 0) == (d < 0)):
                        gather.finish_event(event)

        combine_out(chip)
        pl.when(g == 0)(lambda: out.start_pair(0))
        pl.when(g == 1)(lambda: out.start_pair(depth - 1))
        pl.when(g == 2)(lambda: out.start_pair(1))
        pl.when(g == 3)(lambda: out.start_pair(2))
        return carry

    lax.fori_loop(0, depth, group, 0)
    out.first()
    out.early()
    middle_copy = pltpu.make_async_copy(middle, wide.at[pl.ds(0, tree)], wide_sem.at[0])
    middle_copy.start()

    in_rows, out_rows = width // n_dp, hidden_units // n_dp
    cut = (in_rows + out_rows) // 2

    def grad_half(e, r, h):
        at = 2 * r + h
        return gu.at[e, pl.ds(at * cut, cut)] if at < 5 else stage.at[e, pl.ds((at - 5) * cut, cut)]

    def grad_land(e, k):
        return w_in.at[e, pl.ds(k * cut, cut)] if k < 5 else w_out.at[e, pl.ds(0, cut)]

    def grad_sum(e):
        half = lambda r, h: grad_half(e, r, h)
        return ExpertSum(me, half, half, lambda k: grad_land(e, k), lambda k: dp_send.at[e, k], lambda k: dp_recv.at[e, k])

    def grads_start(e):
        pl.semaphore_wait(dp_ready.at[e], 2)
        grad_sum(e).start()

    def grads_turn(e):
        grad_sum(e).turn()

    def wide_copies(e):
        return (
            pltpu.make_async_copy(wide.at[pl.ds(0, in_rows)], in_share.at[e], wide_sem.at[0]),
            pltpu.make_async_copy(wide.at[pl.ds(in_rows, out_rows)], out_share.at[e], wide_sem.at[1]),
        )

    def grads_end(e):
        for h in range(2):
            grad_sum(e).end(h, wide.at[pl.ds(h * cut, cut)])
        for copy in wide_copies(e):
            copy.start()
        grad_sum(e).finish()
        for copy in wide_copies(e):
            copy.wait()

    block = 4 * SLOTS
    sub8 = lax.broadcasted_iota(jnp.int32, (8, tree), 0)

    def back_units(e):
        def one_block(m, inner):
            rows = pl.ds(pl.multiple_of(m * block, block), block)
            grad_act = dot(grows[e, rows, :], w_out[e], 1, 1)
            a = gu[e, rows, pl.ds(0, hidden_units)].astype(F32)
            b = gu[e, rows, pl.ds(hidden_units, hidden_units)].astype(F32)
            sg = 1.0 / (1.0 + jnp.exp(-a))
            sw = a * sg
            act = (sw * b).astype(LOW).astype(F32)
            gate = jnp.concatenate([slot_gate(4 * m + q, e) for q in range(4)], axis=0)
            told = jnp.sum(act * grad_act, axis=1, keepdims=True)
            acts[rows, :] = (act * gate).astype(LOW)
            grad_act = grad_act * gate
            tmp[rows, pl.ds(0, hidden_units)] = (grad_act * b * sg * (1.0 + a * (1.0 - sg))).astype(LOW)
            tmp[rows, pl.ds(hidden_units, hidden_units)] = (grad_act * sw).astype(LOW)
            for q in range(4):
                j = 4 * m + q
                row = jnp.sum(
                    jnp.where(slot_ids == slots[j, pl.ds(e, 1), :], told[q * SLOTS : (q + 1) * SLOTS], 0.0),
                    axis=0, keepdims=True)
                dots[j] = jnp.where(sub8 == e, row, dots[j])
            return inner

        lax.fori_loop(0, n_exp // 4, one_block, 0)

    def back_weights(e):
        for r in range(n_dp):
            d = me ^ r
            grad_in = dot(sent[e, :, pl.ds(pl.multiple_of(d * in_rows, in_rows), in_rows)], tmp[...], 0, 0).astype(LOW)
            grad_out = dot(acts[:, pl.ds(pl.multiple_of(d * out_rows, out_rows), out_rows)], grows[e], 0, 0).astype(LOW)
            grad_half(e, r, 0)[...] = grad_in[:cut]
            half = grad_half(e, r, 1)
            half[pl.ds(0, in_rows - cut), :] = grad_in[cut:]
            half[pl.ds(in_rows - cut, out_rows), :] = grad_out

    def back_rows(e, dest):
        def back_half(m, inner):
            rows = pl.ds(pl.multiple_of(m * 512, 512), 512)
            dest[rows, :] = dot(tmp[rows, :], w_in[e], 1, 1).astype(LOW)
            return inner

        lax.fori_loop(0, n_exp * SLOTS // 512, back_half, 0)

    end = local - 1

    def backward(e, carry):
        back_units(e)
        pl.when(e > 0)(lambda: grads_start(e - 1))
        back_weights(e)
        back_rows(e, sent.at[e])
        for bit in (1, 2):
            pl.semaphore_signal(dp_ready.at[e], inc=1, device_id={"dp": me ^ bit}, device_id_type=MESH)
        pl.when(e == 1)(out.late)
        pl.when(e >= 2)(lambda: grads_turn(e - 2))
        return carry

    dots[...] = jnp.zeros(dots.shape, F32)
    lax.fori_loop(0, end, backward, 0)
    back_units(end)
    grads_start(end - 1)
    back_rows(end, grows.at[end - 1])


    def hid_part(d, other):
        if d == 0:
            return x_all.at[mine + other * (1 - 2 * core)]
        k = 2 * (d - 1) + other
        return grows.at[k // 3, pl.ds((k % 3) * tree, tree)]

    hid = RingScatter(ring, hid_part, views((pair_buf, held, got)), hid_sems)

    def combine_hid(d):
        for other in range(2):
            j = ring.dev(d) + other * (1 - 2 * core)
            rows = pl.ds(pl.multiple_of(j * SLOTS, SLOTS), SLOTS)
            made = jnp.concatenate([sent[i, rows, :] for i in range(end)] + [grows[end - 1, rows, :]], axis=0)
            hid_part(d, other)[...] = dot(places_t(j), made).astype(LOW)

    for d in (2, 1, depth - 1):
        combine_hid(d)

    gate_copies = []
    for k, e in enumerate(peers):
        copy = remote(dots.at[e], gates_out.at[mine], gate_send.at[k], gate_recv.at[k], expert=e)
        copy.start()
        gate_copies.append(copy)
    gates_out[mine] = dots[mine]
    middle_copy.wait()
    out.last(block_out, wide.at[pl.ds(0, tree)])
    out.finish_sends()
    for partner in (ring.pair, ring.right, ring.left):
        pl.semaphore_signal(ready, inc=1, device_id={"expert": partner}, device_id_type=MESH)
    pl.semaphore_wait(ready, 3)
    for d in (2, 1, depth - 1):
        hid.start_pair(d)
    hid.first()
    combine_hid(0)
    hid.start_pair(0)
    hid.early()
    back_weights(end)

    def late_copy(r, h):
        at = pl.multiple_of((me ^ r) * 2 * cut + h * cut, 16)
        return pltpu.make_async_copy(grad_half(end, r, h), late.at[pl.ds(at, cut)], late_sem.at[2 * r + h])

    for r in range(n_dp):
        for h in range(2):
            late_copy(r, h).start()
    hid.late()
    grads_turn(end - 2)
    grads_end(0)
    grads_turn(end - 1)
    grads_end(1)
    hid.last(wide.at[pl.ds(0, tree)])
    hid_copy = pltpu.make_async_copy(wide.at[pl.ds(0, tree)], hid_sum, wide_sem.at[0])
    hid_copy.start()
    hid_copy.wait()
    for e in range(2, end):
        grads_end(e)
    for r in range(n_dp):
        for h in range(2):
            late_copy(r, h).wait()
    for k, copy in enumerate(gate_copies):
        copy.wait_send()
        source = lax.rem(mine + n_exp - 1 - k, n_exp)
        remote(dots.at[mine], gates_out.at[source], gate_send.at[k], gate_recv.at[k], expert=mine).wait_recv()
    hid.finish_sends()


def experts(n_dp, n_exp, hidden2, grad_y, routes_all, router_t, expert_in, expert_out, middle, collective_id):
    local, width, both = expert_in.shape
    units = expert_out.shape[1]
    tree = hidden2.shape[0]
    rows = n_exp * SLOTS
    sem = pltpu.SemaphoreType.DMA
    bufs, out_sems = RingScatter.scratch(n_exp, (tree, width), LOW)
    _, hid_sems = RingScatter.scratch(n_exp, (tree, width), LOW)
    shape = jax.ShapeDtypeStruct
    return pl.pallas_call(
        functools.partial(experts_body, n_dp, n_exp),
        out_shape=[
            shape((tree, width), LOW),
            shape((tree, width), F32),
            shape((n_exp, 8, tree), F32),
            shape((local - 1, width // n_dp, width), F32),
            shape((local - 1, units // n_dp, width), F32),
            shape((width + units, width), LOW),
        ],
        in_specs=[pl.BlockSpec(memory_space=s) for s in (VMEM, ANY, VMEM, VMEM, ANY, ANY, ANY)],
        out_specs=[pl.BlockSpec(memory_space=s) for s in (VMEM, ANY, VMEM, ANY, ANY, ANY)],
        scratch_shapes=[
            pltpu.VMEM((n_exp, tree, width), LOW),
            pltpu.VMEM((local, width, both), LOW),
            pltpu.VMEM((local, units, width), LOW),
            pltpu.VMEM((local, rows, width), LOW),
            pltpu.VMEM((local, rows, width), LOW),
            pltpu.VMEM((local, rows, both), LOW),
            pltpu.VMEM((max(rows, 2 * local * SLOTS), width), LOW),
            pltpu.VMEM((rows, units), LOW),
            pltpu.VMEM((local, 3 * (width + units) // (2 * n_dp), width), LOW),
            pltpu.VMEM((n_exp, 8, tree), F32),
            pltpu.VMEM((n_exp, 8, tree), F32),
            pltpu.VMEM((n_exp, 8, tree), F32),
            pltpu.VMEM(((width + units) // n_dp, width), F32),
            *bufs,
            sem((2,)), sem((2,)), sem((2,)), sem, pltpu.SemaphoreType.REGULAR, sem((2 * n_dp,)), sem((n_exp - 1,)), sem((n_exp - 1,)),
            pltpu.SemaphoreType.REGULAR((local,)), sem((local, 6)), sem((local, 6)),
            *RingGather.scratch(n_exp), *out_sems, *hid_sems,
        ],
        compiler_params=pltpu.CompilerParams(
            collective_id=collective_id, has_side_effects=True, vmem_limit_bytes=63 * MIB),
        name="experts",
    )(hidden2, grad_y, routes_all, router_t, expert_in, expert_out, middle)


def lanes_of(shape):
    return lax.broadcasted_iota(jnp.int32, shape, 1)


def turned(field):
    low_half = lax.rem(lanes_of(field.shape), HD) < HD // 2
    return jnp.where(low_half, -pltpu.roll(field, 128 - HD // 2, 1), pltpu.roll(field, HD // 2, 1))


def mask_bias(parents, tree):
    unit = tree // 20

    def segment(row):
        return jnp.where(row < 8 * unit, 0, jnp.where(row < 12 * unit, 1 + lax.div(row - 8 * unit, unit), 5 + lax.div(row - 12 * unit, unit)))

    count = parents.shape[1]
    names = parents[...].astype(F32)
    wide = (tree, count)
    seg = segment(lax.broadcasted_iota(jnp.int32, wide, 0)).astype(F32)
    lane = lanes_of(wide).astype(F32)
    own = seg[:, :1]
    parent = jnp.sum(jnp.where(lane == seg, names, 0.0), axis=1, keepdims=True)
    grand = jnp.sum(jnp.where(lane == parent, names, 0.0), axis=1, keepdims=True)
    square = (tree, tree)
    row, col = lax.broadcasted_iota(jnp.int32, square, 0), lanes_of(square)
    there = segment(col).astype(F32)
    hit = jnp.maximum(
        jnp.maximum(jnp.where(there == own, 1.0, 0.0), jnp.where(there == parent, 1.0, 0.0)), jnp.where(there == grand, 1.0, 0.0))
    hit = jnp.where(col <= row, hit, 0.0)
    return jnp.where(hit > 0.5, 0.0, -1e30)


def inverse_rms(field):
    return lax.rsqrt(jnp.mean(field * field, axis=-1, keepdims=True) + EPSILON)


class DpGather:
    def __init__(self, n_dp, mine, me, ins, outs, sems):
        self.n_dp, self.me, self.ins, self.outs = n_dp, me, ins, outs
        self.send, self.recv, self.pair_send, self.pair_recv, self.own_sem = sems
        self.core = lax.rem(mine, 2)
        self.pair = mine + 1 - 2 * self.core
        self.shard = ins[0].shape[0]
        half = self.shard // 2
        self.orders = bit_orders(n_dp)
        self.cuts = min(2, len(self.orders), half // 16)
        self.size = half // self.cuts

    @staticmethod
    def scratch(count, n_dp):
        sem = pltpu.SemaphoreType.DMA
        bits = max(1, n_dp.bit_length() - 1)
        return [sem((count, 2, n_dp, bits)), sem((count, 2, n_dp)), sem((count, 2, n_dp)), sem((count, 2, n_dp)), sem((count,))]

    def rows(self, start, side, p):
        return pl.ds(pl.multiple_of(start + side * (self.shard // 2) + p * self.size, 16), self.size)

    def hop(self, a, p, r, bit):
        there = self.outs[a].at[self.rows((self.me ^ r) * self.shard, self.core, p)]
        src = self.ins[a].at[self.rows(0, self.core, p)] if r == 0 else there
        return remote(src, there, self.send.at[a, p, r, bit.bit_length() - 1], self.recv.at[a, p, r ^ bit], dp=self.me ^ bit)

    def own(self, a):
        at = pl.ds(pl.multiple_of(self.me * self.shard, 16), self.shard)
        return pltpu.make_async_copy(self.ins[a], self.outs[a].at[at], self.own_sem.at[a])

    def across(self, a, p, r, side):
        here = self.outs[a].at[self.rows((self.me ^ r) * self.shard, side, p)]
        return remote(here, here, self.pair_send.at[a, p, r], self.pair_recv.at[a, p, r], expert=self.pair)

    def start(self, a):
        for p in range(self.cuts):
            for bit in self.orders[p]:
                self.hop(a, p, 0, bit).start()
        self.own(a).start()

    def stage(self, p, j):
        order = self.orders[p]
        blocks = [0]
        for bit in order[:j]:
            blocks = blocks + [r | bit for r in blocks]
        return [r | order[j] for r in blocks], order[j + 1 :]

    def turn(self, a, j):
        for p in range(self.cuts):
            blocks, onward = self.stage(p, j)
            for r in blocks:
                here = self.outs[a].at[self.rows((self.me ^ r) * self.shard, self.core, p)]
                remote(here, here, self.send.at[a, p, r, 0], self.recv.at[a, p, r], dp=self.me).wait_recv()
                for bit in onward:
                    self.hop(a, p, r, bit).start()
                self.across(a, p, r, self.core).start()

    def ready(self, a):
        self.own(a).wait()
        for p in range(self.cuts):
            for r in range(1, self.n_dp):
                self.across(a, p, r, 1 - self.core).wait_recv()

    def finish(self, a):
        for p in range(self.cuts):
            for bit in self.orders[p]:
                self.hop(a, p, 0, bit).wait_send()
            for j in range(len(self.orders[p])):
                blocks, onward = self.stage(p, j)
                for r in blocks:
                    for bit in onward:
                        self.hop(a, p, r, bit).wait_send()
                    self.across(a, p, r, self.core).wait_send()


def front_body(n_dp, n_exp, x_ref, gain_pair, router_in, w_query, w_keyval, w_output, routes_t, parents, cosine, sine, cot,
               hidden_hbm, queries_hbm, keys_hbm, values_hbm, attended, middle, hidden2, log_total,
               query_hbm, keyval_hbm, output_hbm, router_t, gains, routes_all, grad_y,
               hidden, queries, keys, values, query_full, keyval_full, output_full, small, small_all, bias, *sems):
    gather_sems, (small_send, small_recv, route_send, route_recv, out_sem), ring_sems = sems[:5], sems[5:10], sems[10:14]
    me, mine = lax.axis_index("dp"), lax.axis_index("expert")
    peers = [lax.rem(mine + k, n_exp) for k in range(1, n_exp)]
    greet([(None, {"expert": e}) for e in peers] + [(None, {"dp": me ^ k}) for k in range(1, n_dp)])
    tree, width = x_ref.shape
    shard = w_query.shape[0]

    small[...] = jnp.zeros(small.shape, LOW)
    small[pl.ds(0, EXPERTS), :] = router_in[...]
    sub = lax.broadcasted_iota(jnp.int32, (16, shard), 0)
    gain_rows = gain_pair[...].astype(F32)
    small[pl.ds(EXPERTS, 16), :] = jnp.where(sub == 0, gain_rows[:1], jnp.where(sub == 1, gain_rows[1:], 0.0)).astype(LOW)

    gather = DpGather(n_dp, mine, me, (w_query, w_keyval, w_output), (query_full, keyval_full, output_full), gather_sems)

    def small_copy(k):
        return remote(small, small_all.at[me], small_send.at[k], small_recv.at[k], dp=me ^ k)

    def route_copy(k, e):
        return remote(routes_t, routes_all.at[mine], route_send.at[k], route_recv.at[k], expert=e)

    saves = [
        pltpu.make_async_copy(src, dst, out_sem.at[k])
        for k, (src, dst) in enumerate((
            (query_full, query_hbm), (keyval_full, keyval_hbm), (output_full, output_hbm), (hidden, hidden_hbm),
            (queries, queries_hbm), (keys, keys_hbm), (values, values_hbm), (cot, grad_y.at[mine])))
    ]
    ring = RingGather(Ring(n_exp), cot, grad_y, ring_sems)
    events = ring.events()
    for k in range(1, n_dp):
        small_copy(k).start()
    ring.start()
    gather.start(0)
    gather.start(1)
    saves[7].start()
    for k, e in enumerate(peers):
        route_copy(k, e).start()
    small_all[me] = small[...]
    routes_all[mine] = routes_t[...]
    bias[...] = mask_bias(parents, tree)
    log_total[...] = jnp.zeros(log_total.shape, F32)
    x = x_ref[...].astype(F32)
    scaled = x * inverse_rms(x)
    for k in range(1, n_dp):
        remote(small, small_all.at[me ^ k], small_send.at[k], small_recv.at[k], dp=me).wait_recv()
    joined = jnp.concatenate([small_all[d] for d in range(n_dp)], axis=1)
    router_t[...] = jnp.zeros(router_t.shape, LOW)
    router_t[pl.ds(0, EXPERTS), :] = joined[:EXPERTS]
    gains[...] = joined[EXPERTS:]
    gain_rows = joined[EXPERTS:].astype(F32)
    hidden[...] = (scaled * gain_rows[:1]).astype(LOW)
    saves[3].start()
    stages = len(gather.orders[0])
    for j in range(stages - 1):
        gather.turn(0, j)
        gather.turn(1, j)
    gather.start(2)
    gather.turn(0, stages - 1)
    gather.turn(1, stages - 1)
    for event in events[:2]:
        ring.handle(event)
    gather.ready(0)
    saves[0].start()

    def rotate(field):
        return field * cosine[...] + turned(field) * sine[...]

    left = lanes_of((tree, 128)) < HD
    tile = 512

    def query_tile(n, carry):
        cols = pl.ds(pl.multiple_of(n * tile, tile), tile)
        pre = dot(hidden[...], query_full[:, cols])
        for i in range(tile // 128):
            at = pl.multiple_of(n * tile + i * 128, 128)
            queries[:, pl.ds(at, 128)] = rotate(pre[:, i * 128 : (i + 1) * 128]).astype(LOW)
        return carry

    lax.fori_loop(0, width // tile, query_tile, 0)
    saves[4].start()
    gather.ready(1)
    saves[1].start()

    def spread(field, out, i):
        other = pltpu.roll(field, HD, 1)
        out[2 * i] = jnp.where(left, field, other).astype(LOW)
        out[2 * i + 1] = jnp.where(left, other, field).astype(LOW)

    half = KV * HD
    pre = dot(hidden[...], keyval_full[:, pl.ds(0, half)])
    for i in range(half // 128):
        spread(rotate(pre[:, i * 128 : (i + 1) * 128]), keys, i)
    saves[5].start()
    pre = dot(hidden[...], keyval_full[:, pl.ds(half, half)])
    for i in range(half // 128):
        spread(pre[:, i * 128 : (i + 1) * 128], values, i)
    saves[6].start()
    for j in range(stages):
        gather.turn(2, j)

    def heads(c, carry):
        cols = pl.ds(pl.multiple_of(c * 128, 128), 128)
        pair = queries[:, cols]
        made = []
        for h in range(2):
            mine_lanes = left if h == 0 else jnp.logical_not(left)
            query = jnp.where(mine_lanes, pair, jnp.zeros_like(pair))
            scores = dot(query, keys[c], 1, 1) * HD**-0.5 + bias[...]
            top = jnp.max(scores, axis=1, keepdims=True)
            powers = jnp.exp(scores - top)
            total = jnp.sum(powers, axis=1, keepdims=True)
            made.append(dot((powers / total).astype(LOW), values[c]))
            log_total[...] = jnp.where(lanes_of((tree, 128)) == 2 * c + h, top + jnp.log(total), log_total[...])
        attended[:, cols] = jnp.where(left, made[0], made[1]).astype(LOW)
        return carry

    lax.fori_loop(0, KV, heads, 0)
    for event in events[2:4]:
        ring.handle(event)
    gather.ready(2)
    saves[2].start()

    def middle_tile(n, carry):
        cols = pl.ds(pl.multiple_of(n * tile, tile), tile)
        middle[:, cols] = x_ref[:, cols].astype(F32) + dot(attended[...], output_full[:, cols])
        return carry

    lax.fori_loop(0, width // tile, middle_tile, 0)
    field = middle[...]
    hidden2[...] = (field * inverse_rms(field) * gain_rows[1:2]).astype(LOW)
    for a in range(3):
        gather.finish(a)
    for k in range(1, n_dp):
        small_copy(k).wait_send()
    for k, e in enumerate(peers):
        route_copy(k, e).wait_send()
        source = lax.rem(mine + n_exp - 1 - k, n_exp)
        remote(routes_t, routes_all.at[source], route_send.at[k], route_recv.at[k], expert=mine).wait_recv()
    for event in events[4:]:
        ring.handle(event)
    ring.finish_own()
    for h in range(2):
        ring.wait_pair(0, h)
    for event in events:
        ring.finish_event(event)
        ring.wait_pair(-event[1] if event[0] == 0 else event[1], event[2])
    for copy in saves:
        copy.wait()


def front(n_dp, n_exp, tokens, gain_pair, router_in, w_query, w_keyval, w_output, routes_t, parents, tables, cot, collective_id):
    tree, width = tokens.shape
    shard = w_query.shape[0]
    shape, sem, vm = jax.ShapeDtypeStruct, pltpu.SemaphoreType.DMA, pltpu.VMEM
    low = shape((tree, width), LOW)
    spread = shape((KV, tree, 128), LOW)
    full = shape((n_dp * shard, width), LOW)
    small = (EXPERTS + 16, shard)
    return pl.pallas_call(
        functools.partial(front_body, n_dp, n_exp),
        out_shape=[
            low, low, spread, spread, low, shape((tree, width), F32), low, shape((tree, 128), F32),
            full, full, full, shape((128, width), LOW), shape((16, width), LOW),
            shape((n_exp,) + routes_t.shape, jnp.int32), shape((n_exp, tree, width), LOW),
        ],
        in_specs=[pl.BlockSpec(memory_space=VMEM)] * 11,
        out_specs=[pl.BlockSpec(memory_space=s) for s in [ANY] * 4 + [VMEM] * 4 + [ANY] * 3 + [VMEM] * 3 + [ANY]],
        scratch_shapes=[
            vm((tree, width), LOW), vm((tree, width), LOW), vm(spread.shape, LOW), vm(spread.shape, LOW),
            vm(full.shape, LOW), vm(full.shape, LOW), vm(full.shape, LOW),
            vm(small, LOW), vm((n_dp,) + small, LOW), vm((tree, tree), F32),
            *DpGather.scratch(3, n_dp), sem((n_dp,)), sem((n_dp,)), sem((n_exp - 1,)), sem((n_exp - 1,)), sem((8,)),
            *RingGather.scratch(n_exp),
        ],
        compiler_params=pltpu.CompilerParams(
            collective_id=collective_id, has_side_effects=True, vmem_limit_bytes=56 * MIB),
        name="front",
    )(tokens, gain_pair, router_in, w_query, w_keyval, w_output, routes_t, parents, *tables, cot)


class GradSum:
    def __init__(self, n_dp, n_exp, chunks, own, bufs, sems):
        self.n_dp, self.chunks, self.own = n_dp, chunks, own
        (self.pair_in, self.dp_in, self.prefix, self.suffix, self.go_r, self.go_l, self.final, self.other) = bufs
        (self.pair_send, self.pair_recv, self.dp_send, self.dp_recv,
         self.send_r, self.send_l, self.recv_r, self.recv_l, self.last_send, self.last_recv) = sems
        self.me, self.mine = lax.axis_index("dp"), lax.axis_index("expert")
        self.core = lax.rem(self.mine, 2)
        self.z = lax.div(self.mine, 2)
        self.depth = n_exp // 2
        self.pair = self.mine + 1 - 2 * self.core
        self.has_left, self.has_right = self.z > 0, self.z < self.depth - 1
        self.orders = bit_orders(n_dp)

    @staticmethod
    def scratch(n_dp, chunks, half, columns):
        sem = pltpu.SemaphoreType.DMA
        stages = max(1, n_dp.bit_length() - 1)
        one = pltpu.VMEM((chunks, half, columns), LOW)
        many = pltpu.VMEM((chunks, n_dp, half, columns), LOW)
        bufs = [many, many, one, one, one, one, one, one]
        sems = [sem((chunks, n_dp)), sem((chunks, n_dp)), sem((chunks, n_dp)), sem((chunks, n_dp))]
        return bufs, sems + [sem((chunks,))] * 6

    def partners(self):
        return [(None, {"dp": self.me ^ bit}) for bit in self.orders[0]] + [
            (self.has_left, {"expert": self.mine - 2}), (self.has_right, {"expert": self.mine + 2})]

    def total(self, i, r):
        return self.own.at[i, self.me ^ r, self.core]

    def across(self, i, d):
        return remote(self.own.at[i, d, 1 - self.core], self.pair_in.at[i, d], self.pair_send.at[i, d],
                      self.pair_recv.at[i, d], expert=self.pair)

    def moved(self, i, j):
        order = self.orders[i % len(self.orders)]
        blocks = [0]
        for bit in order[j + 1 :]:
            blocks = blocks + [r | bit for r in blocks]
        return order[j], [r | order[j] for r in blocks]

    def dp_copy(self, i, r, bit):
        return remote(self.total(i, r), self.dp_in.at[i, r], self.dp_send.at[i, r], self.dp_recv.at[i, r], dp=self.me ^ bit)

    def start(self, i):
        for d in range(self.n_dp):
            self.across(i, d).start()

    def paired(self, i):
        for r in range(self.n_dp - 1, -1, -1):
            d = self.me ^ r
            self.across(i, d).wait_recv()
            add_rows(self.total(i, r), self.total(i, r), self.pair_in.at[i, d])
        self.leave(i, 0)

    def leave(self, i, j):
        if j < len(self.orders[0]):
            bit, blocks = self.moved(i, j)
            for r in blocks:
                self.dp_copy(i, r, bit).start()

    def met(self, i, j):
        bit, blocks = self.moved(i, j)
        for r in blocks:
            self.dp_copy(i, r, bit).wait_recv()
            add_rows(self.total(i, r ^ bit), self.total(i, r ^ bit), self.dp_in.at[i, r])
        self.leave(i, j + 1)

    def right(self, i):
        return remote(self.go_r.at[i], self.prefix.at[i], self.send_r.at[i], self.recv_r.at[i], expert=self.mine + 2)

    def left(self, i):
        return remote(self.go_l.at[i], self.suffix.at[i], self.send_l.at[i], self.recv_l.at[i], expert=self.mine - 2)

    def line(self, t):
        i = t - 2 * self.z
        has_left, has_right = self.has_left, self.has_right

        @pl.when(jnp.logical_and(i >= 0, i < self.chunks))
        def _():
            @pl.when(has_left)
            def _():
                remote(self.go_r.at[i], self.prefix.at[i], self.send_r.at[i], self.recv_r.at[i], expert=self.mine).wait_recv()

            @pl.when(jnp.logical_and(has_left, has_right))
            def _():
                add_rows(self.go_r.at[i], self.total(i, 0), self.prefix.at[i])

            @pl.when(jnp.logical_not(has_left))
            def _():
                add_rows(self.go_r.at[i], self.total(i, 0))

            pl.when(has_right)(lambda: self.right(i).start())

        k = t - 2 * (self.depth - 1 - self.z)

        @pl.when(jnp.logical_and(k >= 0, k < self.chunks))
        def _():
            @pl.when(has_right)
            def _():
                remote(self.go_l.at[k], self.suffix.at[k], self.send_l.at[k], self.recv_l.at[k], expert=self.mine).wait_recv()

            @pl.when(jnp.logical_and(has_left, has_right))
            def _():
                add_rows(self.go_l.at[k], self.total(k, 0), self.suffix.at[k])

            @pl.when(jnp.logical_not(has_right))
            def _():
                add_rows(self.go_l.at[k], self.total(k, 0))

            pl.when(has_left)(lambda: self.left(k).start())

    def last(self, i):
        return remote(self.final.at[i], self.other.at[i], self.last_send.at[i], self.last_recv.at[i], expert=self.pair)

    def close(self, i):
        has_left, has_right = self.has_left, self.has_right

        @pl.when(jnp.logical_and(has_left, has_right))
        def _():
            add_rows(self.final.at[i], self.total(i, 0), self.prefix.at[i], self.suffix.at[i])

        @pl.when(jnp.logical_not(has_left))
        def _():
            add_rows(self.final.at[i], self.total(i, 0), self.suffix.at[i])

        @pl.when(jnp.logical_not(has_right))
        def _():
            add_rows(self.final.at[i], self.total(i, 0), self.prefix.at[i])

        self.last(i).start()

    def finish(self, i):
        self.last(i).wait_send()
        pl.when(self.has_right)(lambda: self.right(i).wait_send())
        pl.when(self.has_left)(lambda: self.left(i).wait_send())
        for d in range(self.n_dp):
            self.across(i, d).wait_send()
        for j in range(len(self.orders[0])):
            bit, blocks = self.moved(i, j)
            for r in blocks:
                self.dp_copy(i, r, bit).wait_send()


def two_parts(field):
    high = field.astype(LOW)
    return high, (field - high.astype(F32)).astype(LOW)


def norm_back(field, gain, grad):
    r = inverse_rms(field)
    scaled = grad * gain
    back = r * scaled - field * (r * r * r) * jnp.mean(field * scaled, axis=-1, keepdims=True)
    return back, jnp.sum(field * r * grad, axis=0, keepdims=True)


def back_body(n_dp, n_exp, local, with_late, x_ref, cot, hid_sum, gates_in, routes_t, parents, cosine, sine,
              hidden, queries, keys, values, attended, middle, hidden2, log_total,
              query_hbm, keyval_hbm, output_hbm, router_t, gains, *refs):
    if with_late:
        late_hbm, refs = refs[0], refs[1:]
    outs, refs = refs[: 5 + 2 * with_late], refs[5 + 2 * with_late :]
    input_grad, grad_q, grad_kv, grad_o, grad_s = outs[:5]
    (bias, branch, grad_att, grad_q_pre, grad_kv_pre, rhs, own, own_s, grad_hid, query_full, keyval_full, output_full,
     load_sem, *rest) = refs
    big = GradSum(n_dp, n_exp, own.shape[0], own, rest[:8], rest[8:18])
    little = GradSum(n_dp, n_exp, 1, own_s, rest[18:26], rest[26:36])
    tree, width = x_ref.shape
    ring = Ring(n_exp)
    greet(big.partners() + [(None, {"expert": ring.pair})])
    loads = [
        pltpu.make_async_copy(src, dst, load_sem.at[k])
        for k, (src, dst) in enumerate(((output_hbm, output_full), (query_hbm, query_full), (keyval_hbm, keyval_full)))
    ]
    if with_late:
        late_sem, late_send, late_recv, wide_sem, late_buf = rest[36:41]
        cut = late_hbm.shape[0] // (2 * n_dp)
        kept = {(0, 0): 0, (0, 1): 1, (2, 0): 2, (1, 1): 3}

        def late_rows(r, h):
            return late_hbm.at[pl.ds(pl.multiple_of((big.me ^ r) * 2 * cut + h * cut, 16), cut)]

        def late_half(r, h):
            return late_buf.at[pl.ds(kept[r, h] * cut, cut)]

        def late_land(k):
            return late_buf.at[pl.ds((4 + k) * cut, cut)]

        late = ExpertSum(big.me, late_rows, late_half, late_land, lambda k: late_send.at[k], lambda k: late_recv.at[k])
        late.start()
        late_loads = [pltpu.make_async_copy(late_rows(r, h), late_half(r, h), late_sem.at[k]) for (r, h), k in kept.items()]
        for copy in late_loads:
            copy.start()
        in_rows = outs[5].shape[0]

        def late_end():
            for h in range(2):
                late.end(h, grad_hid.at[pl.ds(0, cut)])
                if h == 0:
                    copies = [pltpu.make_async_copy(grad_hid.at[pl.ds(0, cut)], outs[5].at[pl.ds(0, cut)], wide_sem.at[0])]
                else:
                    copies = [
                        pltpu.make_async_copy(grad_hid.at[pl.ds(0, in_rows - cut)], outs[5].at[pl.ds(cut, in_rows - cut)], wide_sem.at[0]),
                        pltpu.make_async_copy(grad_hid.at[pl.ds(in_rows - cut, 2 * cut - in_rows)], outs[6], wide_sem.at[1])]
                for copy in copies:
                    copy.start()
                for copy in copies:
                    copy.wait()
            late.finish()

    for copy in loads:
        copy.start()
    shard = width // n_dp
    side = shard // 2
    tile = 512
    lane = lanes_of((tree, 128))
    left = lane < HD

    def gain_row(i):
        return gains[...].astype(F32)[i : i + 1]

    bias[...] = mask_bias(parents, tree)

    names = routes_t[...].astype(F32)
    pick = jnp.where(lax.broadcasted_iota(jnp.int32, (16, 128), 0) == lanes_of((16, 128)), 1.0, 0.0).astype(LOW)
    names = dot(jnp.concatenate([names, jnp.zeros_like(names)], axis=0).astype(LOW), pick, 0, 0)
    chosen = jnp.zeros((tree, 128), F32)
    for k in range(routes_t.shape[0]):
        chosen = jnp.maximum(chosen, jnp.where(names[:, k : k + 1] == lane.astype(F32), 1.0, 0.0))
    logits = jnp.where(chosen > 0.5, dot(hidden2[...], router_t[...], 1, 1), -1e30)
    powers = jnp.exp(logits - jnp.max(logits, axis=1, keepdims=True))
    gate = powers / jnp.sum(powers, axis=1, keepdims=True)
    count = gates_in.shape[0]
    where_row = lax.broadcasted_iota(jnp.int32, (count, 128), 0)
    where_lane = lanes_of((count, 128))
    group_row = lax.rem(where_row, 8)
    target = lax.div(where_row, 8) * local + group_row
    pick = jnp.where(group_row < local, jnp.where(target == where_lane, 1.0, 0.0), 0.0).astype(LOW)
    high, low = two_parts(gates_in[...])
    gate_back = dot(high, pick, 0, 0) + dot(low, pick, 0, 0)
    grad_logits = (gate * (gate_back - jnp.sum(gate * gate_back, axis=1, keepdims=True))).astype(LOW)
    grad_router = dot(grad_logits, hidden2[...], 0, 0)[:EXPERTS]
    grad_hidden2 = hid_sum[...] + dot(grad_logits, router_t[...])
    back, gain2_sum = norm_back(middle[...], gain_row(1), grad_hidden2)
    grad_middle = cot[...].astype(F32) + back
    input_grad[...] = grad_middle
    branch[...] = grad_middle.astype(LOW)

    def chunk_grads(i, lhs, rhs_ref):
        def part(n, carry):
            made = dot(lhs[:, pl.ds(pl.multiple_of(n * tile, tile), tile)], rhs_ref[...], 0, 0).astype(LOW)
            for k in range(tile // side):
                own[i, n * (tile // shard) + k // 2, k % 2] = made[k * side : (k + 1) * side]
            return carry

        if tile % shard == 0:
            lax.fori_loop(0, width // tile, part, 0)

    for i in range(2):
        rhs[...] = branch[:, pl.ds(i * tile, tile)]
        chunk_grads(i, attended, rhs)
        big.start(i)

    loads[0].wait()

    def att_tile(n, carry):
        rows = pl.ds(pl.multiple_of(n * tile, tile), tile)
        grad_att[:, rows] = dot(branch[...], output_full[rows, :], 1, 1).astype(LOW)
        return carry

    lax.fori_loop(0, width // tile, att_tile, 0)

    def unrotate(field):
        return field * cosine[...] - turned(field * sine[...])

    scale = HD**-0.5

    def group(c):
        cols = pl.ds(pl.multiple_of(c * 128, 128), 128)
        pair, grad_pair = queries[:, cols], grad_att[:, cols]
        zero = jnp.zeros_like(pair)
        key, value = keys[c], values[c]
        grad_query, grad_key, grad_value = [], 0.0, 0.0
        for h in range(2):
            here = left if h == 0 else jnp.logical_not(left)
            query, grad_out = jnp.where(here, pair, zero), jnp.where(here, grad_pair, zero)
            logs = jnp.sum(jnp.where(lane == 2 * c + h, log_total[...], 0.0), axis=1, keepdims=True)
            probs = jnp.exp(dot(query, key, 1, 1) * scale + bias[...] - logs)
            grad_probs = dot(grad_out, value, 1, 1)
            grad_scores = (probs * (grad_probs - jnp.sum(probs * grad_probs, axis=1, keepdims=True))).astype(LOW)
            grad_value = grad_value + dot(probs.astype(LOW), grad_out, 0, 0)
            grad_query.append(dot(grad_scores, key))
            grad_key = grad_key + dot(grad_scores, query, 0, 0)
        grad_q_pre[:, cols] = unrotate(jnp.where(left, grad_query[0], grad_query[1]) * scale).astype(LOW)
        grad_key = (grad_key + pltpu.roll(grad_key, HD, 1)) * scale
        return unrotate(grad_key), grad_value + pltpu.roll(grad_value, HD, 1)

    def two_groups(i):
        key_a, value_a = group(2 * i)
        key_b, value_b = group(2 * i + 1)
        at = pl.multiple_of(i * 128, 128)
        grad_kv_pre[:, pl.ds(at, 128)] = jnp.where(left, key_a, key_b).astype(LOW)
        at = pl.multiple_of(KV * HD + i * 128, 128)
        grad_kv_pre[:, pl.ds(at, 128)] = jnp.where(left, value_a, value_b).astype(LOW)

    def gather_rhs(i):
        rhs[:, pl.ds(0, 256)] = grad_q_pre[:, pl.ds(i * 256, 256)]
        rhs[:, pl.ds(256, 128)] = grad_kv_pre[:, pl.ds(i * 128, 128)]
        rhs[:, pl.ds(384, 128)] = grad_kv_pre[:, pl.ds(KV * HD + i * 128, 128)]

    for i in range(KV // 2):
        two_groups(i)
        gather_rhs(i)
        chunk_grads(2 + i, hidden, rhs)
        big.start(2 + i)
        if i == 0:
            big.paired(0)
            big.paired(1)
        if i == 1:
            big.paired(2)
        if i == 2:
            big.paired(3)
        if i == 3:
            big.met(0, 0)
            big.met(1, 0)
            big.paired(4)
            big.met(2, 0)

    for copy in loads[1:]:
        copy.wait()

    def hidden_tile(n, carry):
        cols = pl.ds(pl.multiple_of(n * tile, tile), tile)
        grad_hid[:, cols] = dot(grad_q_pre[...], query_full[cols, :], 1, 1) + dot(grad_kv_pre[...], keyval_full[cols, :], 1, 1)
        return carry

    lax.fori_loop(0, width // tile, hidden_tile, 0)
    big.paired(5)
    big.met(3, 0)
    big.met(0, 1)
    big.line(0)
    big.met(1, 1)
    big.line(1)
    back, gain1_sum = norm_back(x_ref[...].astype(F32), gain_row(0), grad_hid[...])
    input_grad[...] = input_grad[...] + back

    sub = lax.broadcasted_iota(jnp.int32, (16, width), 0)
    sums = jnp.where(sub == 0, gain1_sum, jnp.where(sub == 1, gain2_sum, 0.0))
    little_all = jnp.concatenate([grad_router, sums], axis=0).astype(LOW)
    for d in range(n_dp):
        for k in range(2):
            at = d * shard + k * side
            own_s[0, d, k] = little_all[:, at : at + side]
    little.start(0)
    big.met(2, 1)
    big.line(2)
    big.met(4, 0)
    little.paired(0)
    big.met(3, 1)
    big.line(3)
    big.met(5, 0)
    if with_late:
        for copy in late_loads:
            copy.wait()
        late.turn()
    little.met(0, 0)
    big.met(4, 1)
    big.line(4)
    little.met(0, 1)
    big.met(5, 1)
    big.line(5)
    def place(i, which, field):
        rows = pl.ds(pl.multiple_of(which * side, 16), side)
        if i < 2:
            add_rows(grad_o.at[rows, pl.ds(i * tile, tile)], field)
            return
        i = i - 2
        add_rows(grad_q.at[rows, pl.ds(i * 256, 256)], field.at[:, pl.ds(0, 256)])
        add_rows(grad_kv.at[rows, pl.ds(i * 128, 128)], field.at[:, pl.ds(256, 128)])
        add_rows(grad_kv.at[rows, pl.ds(KV * HD + i * 128, 128)], field.at[:, pl.ds(384, 128)])

    def settle(i):
        big.last(i).wait_recv()
        place(i, 1 - big.core, big.other.at[i])

    chunks = own.shape[0]
    hop = 2 * (big.depth - 1)
    for t in range(chunks, chunks + hop):
        big.line(t)
        little.line(t - chunks)
        if t >= hop:
            big.close(t - hop)
            place(t - hop, big.core, big.final.at[t - hop])
        if t > hop:
            settle(t - hop - 1)
        if with_late and t == chunks + hop // 2:
            late_end()
    little.line(hop)
    little.close(0)
    add_rows(grad_s.at[big.core], little.final.at[0])
    settle(chunks - 1)
    for i in range(chunks):
        big.finish(i)
    little.last(0).wait_recv()
    add_rows(grad_s.at[1 - big.core], little.other.at[0])
    little.finish(0)


def back(n_dp, n_exp, local, tokens, cotangent, hid_sum, gates_in, routes_t, parents, tables, saved, late, collective_id):
    tree, width = tokens.shape
    shard = width // n_dp
    shape, vm, sem = jax.ShapeDtypeStruct, pltpu.VMEM, pltpu.SemaphoreType.DMA
    side, chunks, tile, rows = shard // 2, 6, 512, EXPERTS + 16
    big_bufs, big_sems = GradSum.scratch(n_dp, chunks, side, tile)
    little_bufs, little_sems = GradSum.scratch(n_dp, 1, rows, side)
    args = (tokens, cotangent, hid_sum, gates_in, routes_t, parents, *tables, *saved)
    spaces = [VMEM] * len(args)
    spaces[16:19] = [ANY] * 3
    out_shape = [
        shape((tree, width), F32), shape((shard, width), F32), shape((shard, width), F32), shape((shard, width), F32),
        shape((2, rows, side), F32),
    ]
    extra = []
    if late is not None:
        args, spaces = (*args, late), spaces + [ANY]
        out_rows = late.shape[0] // n_dp - shard
        out_shape += [shape((shard, width), F32), shape((out_rows, width), F32)]
        extra = [sem((4,)), sem((6,)), sem((6,)), sem((2,)), vm((10 * late.shape[0] // (2 * n_dp), width), LOW)]
    return pl.pallas_call(
        functools.partial(back_body, n_dp, n_exp, local, late is not None),
        out_shape=out_shape,
        in_specs=[pl.BlockSpec(memory_space=s) for s in spaces],
        out_specs=[pl.BlockSpec(memory_space=s) for s in ([VMEM] * 5 + [ANY] * 2)[: len(out_shape)]],
        scratch_shapes=[
            vm((tree, tree), F32), vm((tree, width), LOW), vm((tree, width), LOW), vm((tree, width), LOW), vm((tree, width), LOW),
            vm((tree, tile), LOW), vm((chunks, n_dp, 2, side, tile), LOW), vm((1, n_dp, 2, rows, side), LOW),
            vm((tree, width), F32), vm((width, width), LOW), vm((width, width), LOW), vm((width, width), LOW), sem((3,)),
            *big_bufs, *big_sems, *little_bufs, *little_sems, *extra,
        ],
        compiler_params=pltpu.CompilerParams(
            collective_id=collective_id, has_side_effects=True, vmem_limit_bytes=63 * MIB),
        name="back",
    )(*args)


def rope_pairs(tree_rows):
    unit = tree_rows // 20
    row = np.arange(tree_rows)
    position = np.where(row < 8 * unit, row, np.where(row < 12 * unit, 8 * unit + row % unit, 9 * unit + row % unit))
    frequency = 10000.0 ** (-np.arange(0, HD, 2) / HD)
    angles = position[:, None] * frequency[None, :]
    return tuple(jnp.asarray(np.concatenate([table] * 4, axis=1), jnp.float32) for table in (np.cos(angles), np.sin(angles)))


def gated_unit(gate_up):
    width_ff = gate_up.shape[-1] // 2
    gate_part = gate_up[..., :width_ff]
    return gate_part / (1.0 + jnp.exp(-gate_part)) * gate_up[..., width_ff:]


def experts_plain(
    n_dp, n_exp, hidden2, grad_y, routes_all, router_full, expert_in, expert_out, middle
):
    tree_rows, width = hidden2.shape
    capacity = CAP
    routes_all = routes_all.transpose(0, 2, 1)
    expert_ids = jnp.arange(EXPERTS, dtype=jnp.int32)
    here = lax.axis_index("expert")
    local = expert_in.shape[0]
    first = here * local
    hidden_all = lax.all_gather(hidden2, "expert", axis=0, tiled=False)
    own_ids = first + jnp.arange(local, dtype=jnp.int32)
    hot_all = routes_all[:, :, :, None] == expert_ids[None, None, None, :]
    chosen_all = jnp.any(hot_all, axis=2)
    chosen = jnp.any(routes_all[:, :, :, None] == own_ids[None, None, None, :], axis=2)
    lower = jnp.tril(jnp.ones((tree_rows, tree_rows), jnp.bfloat16), -1)
    rank = jnp.einsum(
        "tu,jue->jet", lower, chosen.astype(jnp.bfloat16), preferred_element_type=jnp.float32
    ).astype(jnp.int32)
    slots = jnp.arange(capacity, dtype=jnp.int32)
    chosen_t = chosen.transpose(0, 2, 1)
    place = (rank[:, :, None, :] == slots[None, None, :, None]) & chosen_t[:, :, None, :]
    place = place.astype(jnp.bfloat16)
    logits_all = jnp.einsum(
        "jtd,de->jte", hidden_all, router_full, preferred_element_type=jnp.float32
    )
    masked = jnp.where(chosen_all, logits_all, -1e30)
    weight = jnp.exp(masked - jnp.max(masked, axis=-1, keepdims=True))
    weight = weight / jnp.sum(weight, axis=-1, keepdims=True)
    gates_own = lax.dynamic_slice_in_dim(weight, first, local, axis=2)
    gate_slot = jnp.einsum(
        "jest,jte->ejs", place.astype(jnp.float32), gates_own, precision=lax.Precision.HIGHEST
    )[..., None]
    sent = jnp.einsum("jest,jtd->ejsd", place, hidden_all, preferred_element_type=jnp.float32)
    sent = sent.astype(jnp.bfloat16)
    grad_rows = jnp.einsum("jest,jtd->ejsd", place, grad_y, preferred_element_type=jnp.float32)
    grad_rows = grad_rows.astype(jnp.bfloat16)
    gate_up = jnp.einsum("ejsd,edf->ejsf", sent, expert_in, preferred_element_type=jnp.float32)
    activated, glu_back = jax.vjp(gated_unit, gate_up)
    act_low = activated.astype(jnp.bfloat16).astype(jnp.float32)
    act_scaled = (act_low * gate_slot).astype(jnp.bfloat16)
    made = jnp.einsum(
        "ejsf,efd->ejsd", act_scaled, expert_out, preferred_element_type=jnp.float32
    ).astype(jnp.bfloat16)
    out_part = jnp.einsum("jest,ejsd->jtd", place, made, preferred_element_type=jnp.float32)
    out_sum = lax.psum_scatter(
        out_part.astype(jnp.bfloat16), "expert", scatter_dimension=0, tiled=False
    ).astype(jnp.float32)
    result = middle + out_sum
    block_out = result.astype(jnp.bfloat16)
    grad_act = jnp.einsum(
        "ejsd,efd->ejsf", grad_rows, expert_out, preferred_element_type=jnp.float32
    )
    gate_dot = jnp.sum(act_low * grad_act, axis=-1)
    gates_back = jnp.einsum(
        "jest,ejs->jte", place.astype(jnp.float32), gate_dot, precision=lax.Precision.HIGHEST
    )
    grad_out_w = jnp.einsum(
        "ejsf,ejsd->efd", act_scaled, grad_rows, preferred_element_type=jnp.float32
    )
    grad_gate_up = glu_back(grad_act * gate_slot)[0].astype(jnp.bfloat16)
    grad_sent = jnp.einsum(
        "ejsf,edf->ejsd", grad_gate_up, expert_in, preferred_element_type=jnp.float32
    ).astype(jnp.bfloat16)
    grad_in_w = jnp.einsum(
        "ejsd,ejsf->edf", sent, grad_gate_up, preferred_element_type=jnp.float32
    )
    hid_part = jnp.einsum("jest,ejsd->jtd", place, grad_sent, preferred_element_type=jnp.float32)
    gates_mine = lax.all_to_all(gates_back, "expert", split_axis=0, concat_axis=2, tiled=True)[0]
    hid_sum = lax.psum_scatter(
        hid_part.astype(jnp.bfloat16), "expert", scatter_dimension=0, tiled=False
    ).astype(jnp.float32)
    local, units = expert_in.shape[0], expert_out.shape[1]
    low = jnp.bfloat16
    grads = jnp.concatenate(
        [
            grad_in_w.astype(low).reshape(local, n_dp, width // n_dp, width),
            grad_out_w.astype(low).reshape(local, n_dp, units // n_dp, width),
        ],
        axis=2,
    ).reshape(local, width + units, width)
    share = lax.psum_scatter(grads, "dp", scatter_dimension=1, tiled=True).astype(jnp.float32)
    gates_mine = jnp.pad(gates_mine.T.reshape(n_exp, local, tree_rows), ((0, 0), (0, 8 - local), (0, 0)))
    return block_out, hid_sum, gates_mine, share[:, : width // n_dp], share[:, width // n_dp :]


def shards(
    tokens,
    attn_gain,
    w_query,
    w_keyval,
    w_output,
    moe_gain,
    w_router,
    expert_in,
    expert_out,
    cotangent,
    routes,
    parents,
):
    n_dp, n_exp = lax.axis_size("dp"), lax.axis_size("expert")
    local = expert_in.shape[0]
    tree_rows = tokens.shape[0]
    tables = rope_pairs(tree_rows)
    routes_t = routes.T
    (hidden, queries, keys, values, attended, middle, hidden2, log_total, *full, gains, routes_all, grad_y) = front(
        n_dp, n_exp, tokens, jnp.stack([attn_gain, moe_gain]), w_router.T, w_query, w_keyval, w_output, routes_t, parents, tables, cotangent, 1
    )
    router_t = full[3]
    if (n_dp, n_exp) == (4, 8):
        block_out, hid_sum, gate_grads, expert_in_share, expert_out_share, late = experts(
            n_dp, n_exp, hidden2, grad_y, routes_all, router_t, expert_in, expert_out, middle, 2
        )
    else:
        late = None
        block_out, hid_sum, gate_grads, expert_in_share, expert_out_share = experts_plain(
            n_dp, n_exp, hidden2, grad_y, routes_all, router_t[:EXPERTS].T, expert_in, expert_out, middle
        )
    saved = (hidden, queries, keys, values, attended, middle, hidden2, log_total, *full, gains)
    input_grad, grad_q, grad_kv, grad_o, grad_small, *made = back(
        n_dp, n_exp, local, tokens, cotangent, hid_sum, gate_grads.reshape(n_exp * 8, tree_rows), routes_t, parents, tables, saved, late, 3
    )
    if late is not None:
        expert_in_share = jnp.concatenate([expert_in_share, made[0][None]], axis=0)
        expert_out_share = jnp.concatenate([expert_out_share, made[1][None]], axis=0)
    return (
        block_out,
        input_grad,
        grad_small[:, EXPERTS].reshape(-1),
        grad_q,
        grad_kv,
        grad_o,
        grad_small[:, EXPERTS + 1].reshape(-1),
        jnp.concatenate([grad_small[0, :EXPERTS], grad_small[1, :EXPERTS]], axis=1).T,
        expert_in_share,
        expert_out_share,
    )


def solution(mesh):
    in_specs = (
        P(("dp", "expert"), None),
        P("dp"),
        P("dp", None),
        P("dp", None),
        P("dp", None),
        P("dp"),
        P("dp", None),
        P("expert", None, None),
        P("expert", None, None),
        P(("dp", "expert"), None),
        P(("dp", "expert"), None),
        P(("dp", "expert"), None),
    )
    out_specs = (
        P(("dp", "expert"), None),
        P(("dp", "expert"), None),
        P("dp"),
        P("dp", None),
        P("dp", None),
        P("dp", None),
        P("dp"),
        P("dp", None),
        P("expert", "dp", None),
        P("expert", "dp", None),
    )
    return jax.shard_map(shards, mesh=mesh, in_specs=in_specs, out_specs=out_specs, check_vma=False)
```

```python
import functools

import jax
import jax.numpy as jnp
import numpy as np
from jax import lax
from jax.experimental import pallas as pl
from jax.experimental.pallas import tpu as pltpu
from jax.sharding import PartitionSpec as P

H = 16
KV = 8
HD = 64
EXPERTS = 32
TOPK = 8
CAP = 120


EPSILON = 1e-06


MESH = pl.DeviceIdType.MESH
MIB = 1024 * 1024
VMEM = pltpu.VMEM
ANY = pl.ANY


def remote(src, dst, send_sem, recv_sem, **where):
    return pltpu.make_async_remote_copy(
        src_ref=src, dst_ref=dst, send_sem=send_sem, recv_sem=recv_sem,
        device_id=where, device_id_type=MESH,
    )


def greet(partners):
    barrier = pltpu.get_barrier_semaphore()
    for condition, where in partners:
        def signal(where=where):
            pl.semaphore_signal(barrier, inc=1, device_id=where, device_id_type=MESH)
        if condition is None:
            signal()
        else:
            pl.when(condition)(signal)
    count = sum(1 if c is None else c.astype(jnp.int32) for c, _ in partners)
    pl.semaphore_wait(barrier, count)


def add_rows(out, *terms, step=16):
    rows = out.shape[0]

    def body(i, carry):
        at = pl.ds(pl.multiple_of(i * step, step), step)
        total = terms[0][at, :].astype(jnp.float32)
        for term in terms[1:]:
            total = total + term[at, :].astype(jnp.float32)
        out[at, :] = total.astype(out.dtype)
        return carry

    lax.fori_loop(0, rows // step, body, 0)


def bit_orders(n):
    bits = [1 << j for j in range(n.bit_length() - 1)]
    return [bits[p:] + bits[:p] for p in range(len(bits))] or [[]]


class Ring:
    def __init__(self, n_exp):
        self.mine = lax.axis_index("expert")
        self.core = lax.rem(self.mine, 2)
        self.z = lax.div(self.mine, 2)
        self.depth = n_exp // 2
        self.far = self.depth // 2
        self.pair = self.mine + 1 - 2 * self.core
        self.right, self.left = self.dev(1), self.dev(-1)

    def dev(self, d):
        return lax.rem(self.z + d + self.depth, self.depth) * 2 + self.core

    def partners(self):
        return [(None, {"expert": e}) for e in (self.pair, self.right, self.left)]


class RingGather:
    def __init__(self, ring, own, out, sems):
        self.ring, self.own, self.out = ring, own, out
        self.send, self.recv, self.pair_send, self.pair_recv = sems
        self.half = own.shape[0] // 2

    @staticmethod
    def scratch(n_exp):
        far, depth = n_exp // 4, n_exp // 2
        sem = pltpu.SemaphoreType.DMA
        return [sem((2, far + 1, 2)), sem((2, far + 1, 2)), sem((depth, 2)), sem((depth, 2))]

    def rows(self, h):
        return pl.ds(h * self.half, self.half)

    def goes(self, side, s, h):
        far = self.ring.far
        return s < far or (s == far and h == side)

    def block(self, d, h):
        return self.out.at[self.ring.dev(d), self.rows(h)]

    def hop(self, side, s, h):
        d = -s if side == 0 else s
        src = self.own.at[self.rows(h)] if s == 0 else self.block(d, h)
        to = self.ring.right if side == 0 else self.ring.left
        return remote(src, self.block(d, h), self.send.at[side, s, h], self.recv.at[side, s + 1, h], expert=to)

    def across(self, d, h):
        src = self.own.at[self.rows(h)] if d == 0 else self.block(d, h)
        slot = d % self.ring.depth
        return remote(src, self.block(d, h), self.pair_send.at[slot, h], self.pair_recv.at[slot, h], expert=self.ring.pair)

    ORDER = ((0, 0), (1, 1), (0, 1), (1, 0))

    def start(self):
        for side, h in self.ORDER:
            if self.goes(side, 1, h):
                self.hop(side, 0, h).start()
        self.across(0, 0).start()
        self.across(0, 1).start()

    def events(self):
        return [(side, s, h) for s in range(1, self.ring.far + 1) for side, h in self.ORDER if self.goes(side, s, h)]

    def handle(self, event):
        side, s, h = event
        d = -s if side == 0 else s
        here = self.block(d, h)
        remote(here, here, self.send.at[side, s, h], self.recv.at[side, s, h], expert=self.ring.mine).wait_recv()
        if self.goes(side, s + 1, h):
            self.hop(side, s, h).start()
        self.across(d, h).start()

    def wait_pair(self, d, h):
        slot = d % self.ring.depth
        here = self.out.at[self.ring.pair - self.ring.mine + self.ring.dev(d), self.rows(h)]
        remote(here, here, self.pair_send.at[slot, h], self.pair_recv.at[slot, h], expert=self.ring.mine).wait_recv()

    def finish_own(self):
        for side, h in self.ORDER:
            if self.goes(side, 1, h):
                self.hop(side, 0, h).wait_send()
        self.across(0, 0).wait_send()
        self.across(0, 1).wait_send()

    def finish_event(self, event):
        side, s, h = event
        if self.goes(side, s + 1, h):
            self.hop(side, s, h).wait_send()
        self.across(-s if side == 0 else s, h).wait_send()


class RingScatter:
    def __init__(self, ring, part, bufs, sems):
        self.ring, self.part = ring, part
        self.pair_buf, self.held, self.got = bufs
        self.pair_send, self.pair_recv, self.send, self.recv = sems
        self.half = self.held(0).shape[0] // 2

    @staticmethod
    def scratch(n_exp, block, dtype):
        far, depth = n_exp // 4, n_exp // 2
        sem = pltpu.SemaphoreType.DMA
        bufs = [pltpu.VMEM((depth,) + block, dtype), pltpu.VMEM((depth,) + block, dtype),
                pltpu.VMEM((2, far) + block, dtype)]
        return bufs, [sem((depth,)), sem((depth,)), sem((2, far + 1, 2)), sem((2, far + 1, 2))]

    def rows(self, h):
        return pl.ds(h * self.half, self.half)

    def order(self):
        far, depth = self.ring.far, self.ring.depth
        order = [far]
        for s in range(far - 1, 0, -1):
            order += [s, depth - s]
        return order + [0]

    def comes(self, side, d, h):
        far = self.ring.far
        return d + 1 < far or (d + 1 == far and h == side)

    def across(self, d):
        ring = self.ring
        return remote(self.part(d, 1), self.pair_buf(d),
                      self.pair_send.at[d], self.pair_recv.at[d], expert=ring.pair)

    def start_pair(self, d):
        self.across(d).start()

    def wait_pair(self, d):
        self.across(d).wait_recv()

    def wait_got(self, side, d, h):
        here = self.got(side, d).at[self.rows(h)]
        remote(here, here, self.send.at[side, d, h], self.recv.at[side, d, h], expert=self.ring.mine).wait_recv()

    def hop(self, side, d, h):
        slot = d if side == 0 else self.ring.depth - d
        rows = self.rows(h)
        return remote(self.held(slot).at[rows], self.got(side, d - 1).at[rows], self.send.at[side, d, h],
                      self.recv.at[side, d - 1, h], expert=self.ring.right if side == 0 else self.ring.left)

    def push(self, side, d, h):
        ring = self.ring
        slot = d if side == 0 else ring.depth - d
        rows = self.rows(h)
        terms = [self.part(slot, 0).at[rows], self.pair_buf(slot).at[rows]]
        if self.comes(side, d, h):
            self.wait_got(side, d, h)
            terms.append(self.got(side, d).at[rows])
        add_rows(self.held(slot).at[rows], *terms)
        self.hop(side, d, h).start()

    def first(self):
        far = self.ring.far
        self.wait_pair(far)
        self.push(0, far, 0)
        self.push(1, far, 1)

    def early(self):
        for d in range(self.ring.far - 1, 0, -1):
            self.wait_pair(d)
            self.push(0, d, 1)
            self.wait_pair(self.ring.depth - d)
            self.push(1, d, 0)

    def late(self):
        for d in range(self.ring.far - 1, 0, -1):
            self.push(0, d, 0)
            self.push(1, d, 1)

    def last(self, out, *more):
        self.wait_pair(0)
        for h in range(2):
            rows = self.rows(h)
            terms = [self.part(0, 0).at[rows], self.pair_buf(0).at[rows]] + [m.at[rows] for m in more]
            for side in range(2):
                if self.comes(side, 0, h):
                    self.wait_got(side, 0, h)
                    terms.append(self.got(side, 0).at[rows])
            add_rows(out.at[rows], *terms)

    def finish_sends(self):
        far = self.ring.far
        for side in range(2):
            for d in range(1, far + 1):
                for h in range(2):
                    if d < far or h == side:
                        self.hop(side, d, h).wait_send()
        for d in range(self.ring.depth):
            self.across(d).wait_send()


def views(bufs):
    pair_buf, held, got = bufs
    return (lambda d: pair_buf.at[d], lambda d: held.at[d], lambda side, d: got.at[side, d])


SLOTS = 128
F32, LOW = jnp.float32, jnp.bfloat16


def dot(a, b, over_a=1, over_b=0):
    return lax.dot_general(a, b, (((over_a,), (over_b,)), ((), ())), preferred_element_type=F32)


class ExpertSum:
    def __init__(self, me, first, half, land, send, recv):
        self.me, self.first, self.half, self.land, self.send, self.recv = me, first, half, land, send, recv

    def hop(self, step, h, which):
        bit = (1, 2)[h] if step == 0 else (2, 1)[h]
        r = bit if which == 0 else 3
        k = 2 * h + which if step == 0 else 4 + h
        src = self.first(r, h) if step == 0 else self.half(r, h)
        return remote(src, self.land(k), self.send(k), self.recv(k), dp=self.me ^ bit)

    def start(self, blocks=(1, 0)):
        for which in blocks:
            for h in range(2):
                self.hop(0, h, which).start()

    def turn(self, blocks=(1, 0)):
        for which in blocks:
            for h in range(2):
                self.hop(0, h, which).wait_recv()
                kept = 0 if which == 0 else (2, 1)[h]
                add_rows(self.half(kept, h), self.half(kept, h), self.land(2 * h + which))
                if which == 1:
                    self.hop(1, h, 0).start()

    def end(self, h, out):
        self.hop(1, h, 0).wait_recv()
        add_rows(out, self.half(0, h), self.land(4 + h))

    def finish(self):
        for step, h, which in ((0, 0, 0), (0, 0, 1), (0, 1, 0), (0, 1, 1), (1, 0, 0), (1, 1, 0)):
            self.hop(step, h, which).wait_send()


def experts_body(n_dp, n_exp, hid_ref, gy_hbm, routes_t, wr_t, w_in_hbm, w_out_hbm, middle,
                 block_out, hid_sum, gates_out, in_share, out_share, late,
                 x_all, w_in, w_out, sent, grows, gu, tmp, acts, stage, slots, gates, dots, wide,
                 pair_buf, held, got, *sems):
    w_sem, gy_sem, wide_sem, own_sem, ready, late_sem, gate_send, gate_recv, dp_ready, dp_send, dp_recv = sems[:11]
    gather_sems, out_sems, hid_sems = sems[11:15], sems[15:19], sems[19:23]
    me = lax.axis_index("dp")
    local, _, width = sent.shape
    tree, hidden_units = hid_ref.shape[0], w_out.shape[1]
    rows_e = local * SLOTS
    ring = Ring(n_exp)
    mine, core, depth = ring.mine, ring.core, ring.depth
    first = mine * local
    peers = [lax.rem(mine + k, n_exp) for k in range(1, n_exp)]
    greet([(None, {"expert": e}) for e in peers] + [(None, {"dp": me ^ bit}) for bit in (1, 2)])

    weights = [pltpu.make_async_copy(w_in_hbm, w_in, w_sem.at[0]), pltpu.make_async_copy(w_out_hbm, w_out, w_sem.at[1])]
    gather = RingGather(ring, hid_ref, x_all, gather_sems)
    gather.start()
    for copy in weights:
        copy.start()
    own = pltpu.make_async_copy(hid_ref, x_all.at[mine], own_sem)
    own.start()

    def gy_buf(j):
        return stage.at[lax.rem(j, 2), pl.ds(0, tree)]

    def gy_copy(j):
        return pltpu.make_async_copy(gy_hbm.at[j], gy_buf(j), gy_sem.at[lax.rem(j, 2)])

    gy_copy(0).start()

    below = (lax.broadcasted_iota(jnp.int32, (tree, tree), 0) < lax.broadcasted_iota(jnp.int32, (tree, tree), 1)).astype(LOW)
    sub16 = lax.broadcasted_iota(jnp.int32, (16, tree), 0)

    def find_slots(j, carry):
        names = routes_t[j]
        chosen = jnp.zeros((16, tree), F32)
        for k in range(names.shape[0]):
            chosen = jnp.maximum(chosen, jnp.where(names[k : k + 1, :] == first + sub16, 1.0, 0.0))
        chosen = jnp.where(sub16 < local, chosen, 0.0)
        rank = dot(chosen.astype(LOW), below)
        slots[j] = jnp.where(chosen > 0.5, rank, -1.0)[:8]
        return carry

    lax.fori_loop(0, n_exp, find_slots, 0)

    slot_ids = lax.broadcasted_iota(jnp.int32, (SLOTS, tree), 0).astype(F32)

    def places(j):
        return jnp.concatenate(
            [jnp.where(slot_ids == slots[j, i : i + 1, :], 1.0, 0.0).astype(LOW) for i in range(local)], axis=0)

    def places_t(j):
        lane = lax.broadcasted_iota(jnp.int32, (tree, 128), 1)
        pick = jnp.where(lax.broadcasted_iota(jnp.int32, (16, 128), 0) == lax.broadcasted_iota(jnp.int32, (16, 128), 1), 1.0, 0.0)
        slot = dot(jnp.concatenate([slots[j], jnp.zeros((8, tree), F32)], axis=0).astype(LOW), pick.astype(LOW), 0, 0)
        lanes = lane.astype(F32)
        return jnp.concatenate(
            [jnp.where(lanes == slot[:, i : i + 1], 1.0, 0.0).astype(LOW) for i in range(local)], axis=1)

    def find_gates(j):
        names = routes_t[j]
        experts = lax.broadcasted_iota(jnp.int32, (EXPERTS, tree), 0)
        chosen = jnp.zeros((EXPERTS, tree), F32)
        for k in range(names.shape[0]):
            chosen = jnp.maximum(chosen, jnp.where(names[k : k + 1, :] == experts, 1.0, 0.0))
        logits = jnp.where(chosen > 0.5, dot(wr_t[pl.ds(0, EXPERTS), :], x_all[j], 1, 1), -1e30)
        powers = jnp.exp(logits - jnp.max(logits, axis=0, keepdims=True))
        share = powers / jnp.sum(powers, axis=0, keepdims=True)
        sub = lax.broadcasted_iota(jnp.int32, (8, tree), 0)
        own_gates = jnp.zeros((8, tree), F32)
        for i in range(local):
            row = jnp.sum(jnp.where(experts == first + i, share, 0.0), axis=0, keepdims=True)
            own_gates = jnp.where(sub == i, row, own_gates)
        gates[j] = own_gates

    halves = width // 512

    def dispatch(j, src, dest):
        place = places(j)

        def body(n, carry):
            cols = pl.ds(pl.multiple_of(n * 512, 512), 512)
            picked = dot(place, src[:, cols]).astype(LOW)
            for i in range(local):
                dest[i, pl.ds(pl.multiple_of(j * SLOTS, SLOTS), SLOTS), cols] = picked[i * SLOTS : (i + 1) * SLOTS]
            return carry

        lax.fori_loop(0, halves, body, 0)

    def slot_gate(j, e):
        return jnp.sum(jnp.where(slot_ids == slots[j, pl.ds(e, 1), :], gates[j, pl.ds(e, 1), :], 0.0), axis=1, keepdims=True)

    def forward(chip):
        pair_rows = pl.ds(pl.multiple_of(chip * 2 * SLOTS, 2 * SLOTS), 2 * SLOTS)

        def one_tree(q, carry):
            j = 2 * chip + q
            find_gates(j)
            dispatch(j, x_all.at[j], sent)
            return carry

        lax.fori_loop(0, 2, one_tree, 0)

        def one_expert(e, carry):
            both = dot(sent[e, pair_rows, :], w_in[e])
            gu[e, pair_rows, :] = both.astype(LOW)
            a, b = both[:, :hidden_units], both[:, hidden_units:]
            act = (a / (1.0 + jnp.exp(-a)) * b).astype(LOW).astype(F32)
            gate = jnp.concatenate([slot_gate(2 * chip, e), slot_gate(2 * chip + 1, e)], axis=0)
            made = dot((act * gate).astype(LOW), w_out[e]).astype(LOW)
            for q in range(2):
                tmp[pl.ds(pl.multiple_of(q * rows_e + e * SLOTS, SLOTS), SLOTS), :] = made[q * SLOTS : (q + 1) * SLOTS]
            return carry

        lax.fori_loop(0, local, one_expert, 0)

    def combine_out(chip):
        def one_tree(q, carry):
            j = 2 * chip + q
            rows = pl.ds(pl.multiple_of(q * rows_e, rows_e), rows_e)
            x_all[j] = dot(places_t(j), tmp[rows, :]).astype(LOW)
            return carry

        lax.fori_loop(0, 2, one_tree, 0)

    def grad_rows(j, carry):
        pl.when(j + 1 < n_exp)(lambda: gy_copy(j + 1).start())
        gy_copy(j).wait()
        dispatch(j, gy_buf(j), grows)
        return carry

    events = gather.events()

    def out_part(d, other):
        return x_all.at[ring.dev(d) + other * (1 - 2 * core)]

    out = RingScatter(ring, out_part, views((pair_buf, held, got)), out_sems)

    def chip_at(d):
        return lax.rem(ring.z + d, depth)

    def group(g, carry):
        d = jnp.where(g == 0, 0, jnp.where(g == 1, depth - 1, jnp.where(g == 2, 1, 2)))
        chip = chip_at(d)

        @pl.when(g == 0)
        def _():
            own.wait()
            gather.wait_pair(0, 0)
            gather.wait_pair(0, 1)
            for copy in weights:
                copy.wait()

        @pl.when(g == 1)
        def _():
            for event in events[:4]:
                gather.handle(event)
            gather.wait_pair(-1, 0)
            gather.wait_pair(-1, 1)

        @pl.when(g == 2)
        def _():
            gather.wait_pair(1, 0)
            gather.wait_pair(1, 1)

        @pl.when(g == 3)
        def _():
            for event in events[4:]:
                gather.handle(event)
            out.early()
            gather.wait_pair(2, 0)
            gather.wait_pair(2, 1)

        forward(chip)

        @pl.when(g == 0)
        def _():
            gather.finish_own()
            lax.fori_loop(0, n_exp, grad_rows, 0)

        for at, d in ((1, -1), (2, 1), (3, 2)):
            @pl.when(g == at)
            def _():
                for event in events:
                    if event[1] == abs(d) and (abs(d) == 2 or (event[0] == 0) == (d < 0)):
                        gather.finish_event(event)

        combine_out(chip)
        pl.when(g == 0)(lambda: out.start_pair(0))
        pl.when(g == 1)(lambda: out.start_pair(depth - 1))
        pl.when(g == 2)(lambda: out.start_pair(1))
        pl.when(g == 3)(lambda: out.start_pair(2))
        return carry

    lax.fori_loop(0, depth, group, 0)
    out.first()
    middle_copy = pltpu.make_async_copy(middle, wide.at[pl.ds(0, tree)], wide_sem.at[0])
    middle_copy.start()

    in_rows, out_rows = width // n_dp, hidden_units // n_dp
    cut = (in_rows + out_rows) // 2

    def grad_half(e, r, h):
        at = 2 * r + h
        return gu.at[e, pl.ds(at * cut, cut)] if at < 5 else stage.at[e, pl.ds((at - 5) * cut, cut)]

    def grad_land(e, k):
        return w_in.at[e, pl.ds(k * cut, cut)] if k < 5 else w_out.at[e, pl.ds(0, cut)]

    def grad_sum(e):
        half = lambda r, h: grad_half(e, r, h)
        return ExpertSum(me, half, half, lambda k: grad_land(e, k), lambda k: dp_send.at[e, k], lambda k: dp_recv.at[e, k])

    def grads_start(e):
        pl.semaphore_wait(dp_ready.at[e], 2)
        grad_sum(e).start()

    def grads_turn(e):
        grad_sum(e).turn()

    def wide_copies(e):
        return (
            pltpu.make_async_copy(wide.at[pl.ds(0, in_rows)], in_share.at[e], wide_sem.at[0]),
            pltpu.make_async_copy(wide.at[pl.ds(in_rows, out_rows)], out_share.at[e], wide_sem.at[1]),
        )

    def grads_end(e):
        for h in range(2):
            grad_sum(e).end(h, wide.at[pl.ds(h * cut, cut)])
        for copy in wide_copies(e):
            copy.start()
        grad_sum(e).finish()
        for copy in wide_copies(e):
            copy.wait()

    block = 4 * SLOTS
    sub8 = lax.broadcasted_iota(jnp.int32, (8, tree), 0)

    def back_units(e):
        def one_block(m, inner):
            rows = pl.ds(pl.multiple_of(m * block, block), block)
            grad_act = dot(grows[e, rows, :], w_out[e], 1, 1)
            a = gu[e, rows, pl.ds(0, hidden_units)].astype(F32)
            b = gu[e, rows, pl.ds(hidden_units, hidden_units)].astype(F32)
            sg = 1.0 / (1.0 + jnp.exp(-a))
            sw = a * sg
            act = (sw * b).astype(LOW).astype(F32)
            gate = jnp.concatenate([slot_gate(4 * m + q, e) for q in range(4)], axis=0)
            told = jnp.sum(act * grad_act, axis=1, keepdims=True)
            acts[rows, :] = (act * gate).astype(LOW)
            grad_act = grad_act * gate
            tmp[rows, pl.ds(0, hidden_units)] = (grad_act * b * sg * (1.0 + a * (1.0 - sg))).astype(LOW)
            tmp[rows, pl.ds(hidden_units, hidden_units)] = (grad_act * sw).astype(LOW)
            for q in range(4):
                j = 4 * m + q
                row = jnp.sum(
                    jnp.where(slot_ids == slots[j, pl.ds(e, 1), :], told[q * SLOTS : (q + 1) * SLOTS], 0.0),
                    axis=0, keepdims=True)
                dots[j] = jnp.where(sub8 == e, row, dots[j])
            return inner

        lax.fori_loop(0, n_exp // 4, one_block, 0)

    def back_weights(e):
        for r in range(n_dp):
            d = me ^ r
            grad_in = dot(sent[e, :, pl.ds(pl.multiple_of(d * in_rows, in_rows), in_rows)], tmp[...], 0, 0).astype(LOW)
            grad_out = dot(acts[:, pl.ds(pl.multiple_of(d * out_rows, out_rows), out_rows)], grows[e], 0, 0).astype(LOW)
            grad_half(e, r, 0)[...] = grad_in[:cut]
            half = grad_half(e, r, 1)
            half[pl.ds(0, in_rows - cut), :] = grad_in[cut:]
            half[pl.ds(in_rows - cut, out_rows), :] = grad_out

    def back_rows(e, dest):
        def back_half(m, inner):
            rows = pl.ds(pl.multiple_of(m * 512, 512), 512)
            dest[rows, :] = dot(tmp[rows, :], w_in[e], 1, 1).astype(LOW)
            return inner

        lax.fori_loop(0, n_exp * SLOTS // 512, back_half, 0)

    end = local - 1

    def backward(e, carry):
        back_units(e)
        pl.when(e > 0)(lambda: grads_start(e - 1))
        back_weights(e)
        back_rows(e, sent.at[e])
        for bit in (1, 2):
            pl.semaphore_signal(dp_ready.at[e], inc=1, device_id={"dp": me ^ bit}, device_id_type=MESH)
        pl.when(e == 1)(out.late)
        pl.when(e >= 2)(lambda: grads_turn(e - 2))
        return carry

    dots[...] = jnp.zeros(dots.shape, F32)
    lax.fori_loop(0, end, backward, 0)
    back_units(end)
    grads_start(end - 1)
    back_rows(end, grows.at[end - 1])


    def hid_part(d, other):
        if d == 0:
            return x_all.at[mine + other * (1 - 2 * core)]
        k = 2 * (d - 1) + other
        return grows.at[k // 3, pl.ds((k % 3) * tree, tree)]

    hid = RingScatter(ring, hid_part, views((pair_buf, held, got)), hid_sems)

    def combine_hid(d):
        for other in range(2):
            j = ring.dev(d) + other * (1 - 2 * core)
            rows = pl.ds(pl.multiple_of(j * SLOTS, SLOTS), SLOTS)
            made = jnp.concatenate([sent[i, rows, :] for i in range(end)] + [grows[end - 1, rows, :]], axis=0)
            hid_part(d, other)[...] = dot(places_t(j), made).astype(LOW)

    for d in (2, 1, depth - 1):
        combine_hid(d)

    gate_copies = []
    for k, e in enumerate(peers):
        copy = remote(dots.at[e], gates_out.at[mine], gate_send.at[k], gate_recv.at[k], expert=e)
        copy.start()
        gate_copies.append(copy)
    gates_out[mine] = dots[mine]
    middle_copy.wait()
    out.last(block_out, wide.at[pl.ds(0, tree)])
    out.finish_sends()
    for partner in (ring.pair, ring.right, ring.left):
        pl.semaphore_signal(ready, inc=1, device_id={"expert": partner}, device_id_type=MESH)
    pl.semaphore_wait(ready, 3)
    for d in (2, 1, depth - 1):
        hid.start_pair(d)
    hid.first()
    combine_hid(0)
    hid.start_pair(0)
    hid.early()
    back_weights(end)

    def late_copy(r, h):
        at = pl.multiple_of((me ^ r) * 2 * cut + h * cut, 16)
        return pltpu.make_async_copy(grad_half(end, r, h), late.at[pl.ds(at, cut)], late_sem.at[2 * r + h])

    for r in range(n_dp):
        for h in range(2):
            late_copy(r, h).start()
    hid.late()
    grads_turn(end - 2)
    grads_end(0)
    grads_turn(end - 1)
    grads_end(1)
    hid.last(wide.at[pl.ds(0, tree)])
    hid_copy = pltpu.make_async_copy(wide.at[pl.ds(0, tree)], hid_sum, wide_sem.at[0])
    hid_copy.start()
    hid_copy.wait()
    for e in range(2, end):
        grads_end(e)
    for r in range(n_dp):
        for h in range(2):
            late_copy(r, h).wait()
    for k, copy in enumerate(gate_copies):
        copy.wait_send()
        source = lax.rem(mine + n_exp - 1 - k, n_exp)
        remote(dots.at[mine], gates_out.at[source], gate_send.at[k], gate_recv.at[k], expert=mine).wait_recv()
    hid.finish_sends()


def experts(n_dp, n_exp, hidden2, grad_y, routes_all, router_t, expert_in, expert_out, middle, collective_id):
    local, width, both = expert_in.shape
    units = expert_out.shape[1]
    tree = hidden2.shape[0]
    rows = n_exp * SLOTS
    sem = pltpu.SemaphoreType.DMA
    bufs, out_sems = RingScatter.scratch(n_exp, (tree, width), LOW)
    _, hid_sems = RingScatter.scratch(n_exp, (tree, width), LOW)
    shape = jax.ShapeDtypeStruct
    return pl.pallas_call(
        functools.partial(experts_body, n_dp, n_exp),
        out_shape=[
            shape((tree, width), LOW),
            shape((tree, width), F32),
            shape((n_exp, 8, tree), F32),
            shape((local - 1, width // n_dp, width), F32),
            shape((local - 1, units // n_dp, width), F32),
            shape((width + units, width), LOW),
        ],
        in_specs=[pl.BlockSpec(memory_space=s) for s in (VMEM, ANY, VMEM, VMEM, ANY, ANY, ANY)],
        out_specs=[pl.BlockSpec(memory_space=s) for s in (VMEM, ANY, VMEM, ANY, ANY, ANY)],
        scratch_shapes=[
            pltpu.VMEM((n_exp, tree, width), LOW),
            pltpu.VMEM((local, width, both), LOW),
            pltpu.VMEM((local, units, width), LOW),
            pltpu.VMEM((local, rows, width), LOW),
            pltpu.VMEM((local, rows, width), LOW),
            pltpu.VMEM((local, rows, both), LOW),
            pltpu.VMEM((max(rows, 2 * local * SLOTS), width), LOW),
            pltpu.VMEM((rows, units), LOW),
            pltpu.VMEM((local, 3 * (width + units) // (2 * n_dp), width), LOW),
            pltpu.VMEM((n_exp, 8, tree), F32),
            pltpu.VMEM((n_exp, 8, tree), F32),
            pltpu.VMEM((n_exp, 8, tree), F32),
            pltpu.VMEM(((width + units) // n_dp, width), F32),
            *bufs,
            sem((2,)), sem((2,)), sem((2,)), sem, pltpu.SemaphoreType.REGULAR, sem((2 * n_dp,)), sem((n_exp - 1,)), sem((n_exp - 1,)),
            pltpu.SemaphoreType.REGULAR((local,)), sem((local, 6)), sem((local, 6)),
            *RingGather.scratch(n_exp), *out_sems, *hid_sems,
        ],
        compiler_params=pltpu.CompilerParams(
            collective_id=collective_id, has_side_effects=True, vmem_limit_bytes=63 * MIB),
        name="experts",
    )(hidden2, grad_y, routes_all, router_t, expert_in, expert_out, middle)


def lanes_of(shape):
    return lax.broadcasted_iota(jnp.int32, shape, 1)


def turned(field):
    low_half = lax.rem(lanes_of(field.shape), HD) < HD // 2
    return jnp.where(low_half, -pltpu.roll(field, 128 - HD // 2, 1), pltpu.roll(field, HD // 2, 1))


def mask_bias(parents, tree):
    unit = tree // 20

    def segment(row):
        return jnp.where(row < 8 * unit, 0, jnp.where(row < 12 * unit, 1 + lax.div(row - 8 * unit, unit), 5 + lax.div(row - 12 * unit, unit)))

    count = parents.shape[1]
    names = parents[...].astype(F32)
    wide = (tree, count)
    seg = segment(lax.broadcasted_iota(jnp.int32, wide, 0)).astype(F32)
    lane = lanes_of(wide).astype(F32)
    own = seg[:, :1]
    parent = jnp.sum(jnp.where(lane == seg, names, 0.0), axis=1, keepdims=True)
    grand = jnp.sum(jnp.where(lane == parent, names, 0.0), axis=1, keepdims=True)
    square = (tree, tree)
    row, col = lax.broadcasted_iota(jnp.int32, square, 0), lanes_of(square)
    there = segment(col).astype(F32)
    hit = jnp.maximum(
        jnp.maximum(jnp.where(there == own, 1.0, 0.0), jnp.where(there == parent, 1.0, 0.0)), jnp.where(there == grand, 1.0, 0.0))
    hit = jnp.where(col <= row, hit, 0.0)
    return jnp.where(hit > 0.5, 0.0, -1e30)


def inverse_rms(field):
    return lax.rsqrt(jnp.mean(field * field, axis=-1, keepdims=True) + EPSILON)


class DpGather:
    def __init__(self, n_dp, mine, me, ins, outs, sems):
        self.n_dp, self.me, self.ins, self.outs = n_dp, me, ins, outs
        self.send, self.recv, self.pair_send, self.pair_recv, self.own_sem = sems
        self.core = lax.rem(mine, 2)
        self.pair = mine + 1 - 2 * self.core
        self.shard = ins[0].shape[0]
        half = self.shard // 2
        self.orders = bit_orders(n_dp)
        self.cuts = min(2, len(self.orders), half // 16)
        self.size = half // self.cuts

    @staticmethod
    def scratch(count, n_dp):
        sem = pltpu.SemaphoreType.DMA
        bits = max(1, n_dp.bit_length() - 1)
        return [sem((count, 2, n_dp, bits)), sem((count, 2, n_dp)), sem((count, 2, n_dp)), sem((count, 2, n_dp)), sem((count,))]

    def rows(self, start, side, p):
        return pl.ds(pl.multiple_of(start + side * (self.shard // 2) + p * self.size, 16), self.size)

    def hop(self, a, p, r, bit):
        there = self.outs[a].at[self.rows((self.me ^ r) * self.shard, self.core, p)]
        src = self.ins[a].at[self.rows(0, self.core, p)] if r == 0 else there
        return remote(src, there, self.send.at[a, p, r, bit.bit_length() - 1], self.recv.at[a, p, r ^ bit], dp=self.me ^ bit)

    def own(self, a):
        at = pl.ds(pl.multiple_of(self.me * self.shard, 16), self.shard)
        return pltpu.make_async_copy(self.ins[a], self.outs[a].at[at], self.own_sem.at[a])

    def across(self, a, p, r, side):
        here = self.outs[a].at[self.rows((self.me ^ r) * self.shard, side, p)]
        return remote(here, here, self.pair_send.at[a, p, r], self.pair_recv.at[a, p, r], expert=self.pair)

    def start(self, a):
        for p in range(self.cuts):
            for bit in self.orders[p]:
                self.hop(a, p, 0, bit).start()
        self.own(a).start()

    def stage(self, p, j):
        order = self.orders[p]
        blocks = [0]
        for bit in order[:j]:
            blocks = blocks + [r | bit for r in blocks]
        return [r | order[j] for r in blocks], order[j + 1 :]

    def turn(self, a, j):
        for p in range(self.cuts):
            blocks, onward = self.stage(p, j)
            for r in blocks:
                here = self.outs[a].at[self.rows((self.me ^ r) * self.shard, self.core, p)]
                remote(here, here, self.send.at[a, p, r, 0], self.recv.at[a, p, r], dp=self.me).wait_recv()
                for bit in onward:
                    self.hop(a, p, r, bit).start()
                self.across(a, p, r, self.core).start()

    def ready(self, a):
        self.own(a).wait()
        for p in range(self.cuts):
            for r in range(1, self.n_dp):
                self.across(a, p, r, 1 - self.core).wait_recv()

    def finish(self, a):
        for p in range(self.cuts):
            for bit in self.orders[p]:
                self.hop(a, p, 0, bit).wait_send()
            for j in range(len(self.orders[p])):
                blocks, onward = self.stage(p, j)
                for r in blocks:
                    for bit in onward:
                        self.hop(a, p, r, bit).wait_send()
                    self.across(a, p, r, self.core).wait_send()


def front_body(n_dp, n_exp, x_ref, gain_pair, router_in, w_query, w_keyval, w_output, routes_t, parents, cosine, sine, cot,
               hidden_hbm, queries_hbm, keys_hbm, values_hbm, attended, middle, hidden2, log_total,
               query_hbm, keyval_hbm, output_hbm, router_t, gains, routes_all, grad_y,
               hidden, queries, keys, values, query_full, keyval_full, output_full, small, small_all, bias, *sems):
    gather_sems, (small_send, small_recv, route_send, route_recv, out_sem), ring_sems = sems[:5], sems[5:10], sems[10:14]
    me, mine = lax.axis_index("dp"), lax.axis_index("expert")
    peers = [lax.rem(mine + k, n_exp) for k in range(1, n_exp)]
    greet([(None, {"expert": e}) for e in peers] + [(None, {"dp": me ^ k}) for k in range(1, n_dp)])
    tree, width = x_ref.shape
    shard = w_query.shape[0]

    small[...] = jnp.zeros(small.shape, LOW)
    small[pl.ds(0, EXPERTS), :] = router_in[...]
    sub = lax.broadcasted_iota(jnp.int32, (16, shard), 0)
    gain_rows = gain_pair[...].astype(F32)
    small[pl.ds(EXPERTS, 16), :] = jnp.where(sub == 0, gain_rows[:1], jnp.where(sub == 1, gain_rows[1:], 0.0)).astype(LOW)

    gather = DpGather(n_dp, mine, me, (w_query, w_keyval, w_output), (query_full, keyval_full, output_full), gather_sems)

    def small_copy(k):
        return remote(small, small_all.at[me], small_send.at[k], small_recv.at[k], dp=me ^ k)

    def route_copy(k, e):
        return remote(routes_t, routes_all.at[mine], route_send.at[k], route_recv.at[k], expert=e)

    saves = [
        pltpu.make_async_copy(src, dst, out_sem.at[k])
        for k, (src, dst) in enumerate((
            (query_full, query_hbm), (keyval_full, keyval_hbm), (output_full, output_hbm), (hidden, hidden_hbm),
            (queries, queries_hbm), (keys, keys_hbm), (values, values_hbm), (cot, grad_y.at[mine])))
    ]
    ring = RingGather(Ring(n_exp), cot, grad_y, ring_sems)
    events = ring.events()
    for k in range(1, n_dp):
        small_copy(k).start()
    ring.start()
    gather.start(0)
    gather.start(1)
    saves[7].start()
    for k, e in enumerate(peers):
        route_copy(k, e).start()
    small_all[me] = small[...]
    routes_all[mine] = routes_t[...]
    bias[...] = mask_bias(parents, tree)
    log_total[...] = jnp.zeros(log_total.shape, F32)
    x = x_ref[...].astype(F32)
    scaled = x * inverse_rms(x)
    for k in range(1, n_dp):
        remote(small, small_all.at[me ^ k], small_send.at[k], small_recv.at[k], dp=me).wait_recv()
    joined = jnp.concatenate([small_all[d] for d in range(n_dp)], axis=1)
    router_t[...] = jnp.zeros(router_t.shape, LOW)
    router_t[pl.ds(0, EXPERTS), :] = joined[:EXPERTS]
    gains[...] = joined[EXPERTS:]
    gain_rows = joined[EXPERTS:].astype(F32)
    hidden[...] = (scaled * gain_rows[:1]).astype(LOW)
    saves[3].start()
    stages = len(gather.orders[0])
    for j in range(stages - 1):
        gather.turn(0, j)
        gather.turn(1, j)
    gather.start(2)
    for event in events[:2]:
        ring.handle(event)
    gather.turn(0, stages - 1)
    gather.turn(1, stages - 1)
    gather.ready(0)
    saves[0].start()

    def rotate(field):
        return field * cosine[...] + turned(field) * sine[...]

    left = lanes_of((tree, 128)) < HD
    tile = 512

    def query_tile(n, carry):
        cols = pl.ds(pl.multiple_of(n * tile, tile), tile)
        pre = dot(hidden[...], query_full[:, cols])
        for i in range(tile // 128):
            at = pl.multiple_of(n * tile + i * 128, 128)
            queries[:, pl.ds(at, 128)] = rotate(pre[:, i * 128 : (i + 1) * 128]).astype(LOW)
        return carry

    lax.fori_loop(0, width // tile, query_tile, 0)
    saves[4].start()
    gather.ready(1)
    saves[1].start()

    def spread(field, out, i):
        other = pltpu.roll(field, HD, 1)
        out[2 * i] = jnp.where(left, field, other).astype(LOW)
        out[2 * i + 1] = jnp.where(left, other, field).astype(LOW)

    half = KV * HD
    pre = dot(hidden[...], keyval_full[:, pl.ds(0, half)])
    for i in range(half // 128):
        spread(rotate(pre[:, i * 128 : (i + 1) * 128]), keys, i)
    saves[5].start()
    pre = dot(hidden[...], keyval_full[:, pl.ds(half, half)])
    for i in range(half // 128):
        spread(pre[:, i * 128 : (i + 1) * 128], values, i)
    saves[6].start()
    for j in range(stages):
        gather.turn(2, j)

    def heads(c, carry):
        cols = pl.ds(pl.multiple_of(c * 128, 128), 128)
        pair = queries[:, cols]
        made = []
        for h in range(2):
            mine_lanes = left if h == 0 else jnp.logical_not(left)
            query = jnp.where(mine_lanes, pair, jnp.zeros_like(pair))
            scores = dot(query, keys[c], 1, 1) * HD**-0.5 + bias[...]
            top = jnp.max(scores, axis=1, keepdims=True)
            powers = jnp.exp(scores - top)
            total = jnp.sum(powers, axis=1, keepdims=True)
            made.append(dot((powers / total).astype(LOW), values[c]))
            log_total[...] = jnp.where(lanes_of((tree, 128)) == 2 * c + h, top + jnp.log(total), log_total[...])
        attended[:, cols] = jnp.where(left, made[0], made[1]).astype(LOW)
        return carry

    lax.fori_loop(0, KV, heads, 0)
    for event in events[2:4]:
        ring.handle(event)
    gather.ready(2)
    saves[2].start()

    def middle_tile(n, carry):
        cols = pl.ds(pl.multiple_of(n * tile, tile), tile)
        middle[:, cols] = x_ref[:, cols].astype(F32) + dot(attended[...], output_full[:, cols])
        return carry

    lax.fori_loop(0, width // tile, middle_tile, 0)
    field = middle[...]
    hidden2[...] = (field * inverse_rms(field) * gain_rows[1:2]).astype(LOW)
    for a in range(3):
        gather.finish(a)
    for k in range(1, n_dp):
        small_copy(k).wait_send()
    for k, e in enumerate(peers):
        route_copy(k, e).wait_send()
        source = lax.rem(mine + n_exp - 1 - k, n_exp)
        remote(routes_t, routes_all.at[source], route_send.at[k], route_recv.at[k], expert=mine).wait_recv()
    for event in events[4:]:
        ring.handle(event)
    ring.finish_own()
    for h in range(2):
        ring.wait_pair(0, h)
    for event in events:
        ring.finish_event(event)
        ring.wait_pair(-event[1] if event[0] == 0 else event[1], event[2])
    for copy in saves:
        copy.wait()


def front(n_dp, n_exp, tokens, gain_pair, router_in, w_query, w_keyval, w_output, routes_t, parents, tables, cot, collective_id):
    tree, width = tokens.shape
    shard = w_query.shape[0]
    shape, sem, vm = jax.ShapeDtypeStruct, pltpu.SemaphoreType.DMA, pltpu.VMEM
    low = shape((tree, width), LOW)
    spread = shape((KV, tree, 128), LOW)
    full = shape((n_dp * shard, width), LOW)
    small = (EXPERTS + 16, shard)
    return pl.pallas_call(
        functools.partial(front_body, n_dp, n_exp),
        out_shape=[
            low, low, spread, spread, low, shape((tree, width), F32), low, shape((tree, 128), F32),
            full, full, full, shape((128, width), LOW), shape((16, width), LOW),
            shape((n_exp,) + routes_t.shape, jnp.int32), shape((n_exp, tree, width), LOW),
        ],
        in_specs=[pl.BlockSpec(memory_space=VMEM)] * 11,
        out_specs=[pl.BlockSpec(memory_space=s) for s in [ANY] * 4 + [VMEM] * 4 + [ANY] * 3 + [VMEM] * 3 + [ANY]],
        scratch_shapes=[
            vm((tree, width), LOW), vm((tree, width), LOW), vm(spread.shape, LOW), vm(spread.shape, LOW),
            vm(full.shape, LOW), vm(full.shape, LOW), vm(full.shape, LOW),
            vm(small, LOW), vm((n_dp,) + small, LOW), vm((tree, tree), F32),
            *DpGather.scratch(3, n_dp), sem((n_dp,)), sem((n_dp,)), sem((n_exp - 1,)), sem((n_exp - 1,)), sem((8,)),
            *RingGather.scratch(n_exp),
        ],
        compiler_params=pltpu.CompilerParams(
            collective_id=collective_id, has_side_effects=True, vmem_limit_bytes=56 * MIB),
        name="front",
    )(tokens, gain_pair, router_in, w_query, w_keyval, w_output, routes_t, parents, *tables, cot)


class GradSum:
    def __init__(self, n_dp, n_exp, chunks, own, bufs, sems):
        self.n_dp, self.chunks, self.own = n_dp, chunks, own
        (self.pair_in, self.dp_in, self.prefix, self.suffix, self.go_r, self.go_l, self.final, self.other) = bufs
        (self.pair_send, self.pair_recv, self.dp_send, self.dp_recv,
         self.send_r, self.send_l, self.recv_r, self.recv_l, self.last_send, self.last_recv) = sems
        self.me, self.mine = lax.axis_index("dp"), lax.axis_index("expert")
        self.core = lax.rem(self.mine, 2)
        self.z = lax.div(self.mine, 2)
        self.depth = n_exp // 2
        self.pair = self.mine + 1 - 2 * self.core
        self.has_left, self.has_right = self.z > 0, self.z < self.depth - 1
        self.orders = bit_orders(n_dp)

    @staticmethod
    def scratch(n_dp, chunks, half, columns):
        sem = pltpu.SemaphoreType.DMA
        stages = max(1, n_dp.bit_length() - 1)
        one = pltpu.VMEM((chunks, half, columns), LOW)
        many = pltpu.VMEM((chunks, n_dp, half, columns), LOW)
        bufs = [many, many, one, one, one, one, one, one]
        sems = [sem((chunks, n_dp)), sem((chunks, n_dp)), sem((chunks, n_dp)), sem((chunks, n_dp))]
        return bufs, sems + [sem((chunks,))] * 6

    def partners(self):
        return [(None, {"dp": self.me ^ bit}) for bit in self.orders[0]] + [
            (self.has_left, {"expert": self.mine - 2}), (self.has_right, {"expert": self.mine + 2})]

    def total(self, i, r):
        return self.own.at[i, self.me ^ r, self.core]

    def across(self, i, d):
        return remote(self.own.at[i, d, 1 - self.core], self.pair_in.at[i, d], self.pair_send.at[i, d],
                      self.pair_recv.at[i, d], expert=self.pair)

    def moved(self, i, j):
        order = self.orders[i % len(self.orders)]
        blocks = [0]
        for bit in order[j + 1 :]:
            blocks = blocks + [r | bit for r in blocks]
        return order[j], [r | order[j] for r in blocks]

    def dp_copy(self, i, r, bit):
        return remote(self.total(i, r), self.dp_in.at[i, r], self.dp_send.at[i, r], self.dp_recv.at[i, r], dp=self.me ^ bit)

    def start(self, i):
        for d in range(self.n_dp):
            self.across(i, d).start()

    def paired(self, i):
        for r in range(self.n_dp - 1, -1, -1):
            d = self.me ^ r
            self.across(i, d).wait_recv()
            add_rows(self.total(i, r), self.total(i, r), self.pair_in.at[i, d])
        self.leave(i, 0)

    def leave(self, i, j):
        if j < len(self.orders[0]):
            bit, blocks = self.moved(i, j)
            for r in blocks:
                self.dp_copy(i, r, bit).start()

    def met(self, i, j):
        bit, blocks = self.moved(i, j)
        for r in blocks:
            self.dp_copy(i, r, bit).wait_recv()
            add_rows(self.total(i, r ^ bit), self.total(i, r ^ bit), self.dp_in.at[i, r])
        self.leave(i, j + 1)

    def right(self, i):
        return remote(self.go_r.at[i], self.prefix.at[i], self.send_r.at[i], self.recv_r.at[i], expert=self.mine + 2)

    def left(self, i):
        return remote(self.go_l.at[i], self.suffix.at[i], self.send_l.at[i], self.recv_l.at[i], expert=self.mine - 2)

    def line(self, t):
        i = t - 2 * self.z
        has_left, has_right = self.has_left, self.has_right

        @pl.when(jnp.logical_and(i >= 0, i < self.chunks))
        def _():
            @pl.when(has_left)
            def _():
                remote(self.go_r.at[i], self.prefix.at[i], self.send_r.at[i], self.recv_r.at[i], expert=self.mine).wait_recv()

            @pl.when(jnp.logical_and(has_left, has_right))
            def _():
                add_rows(self.go_r.at[i], self.total(i, 0), self.prefix.at[i])

            @pl.when(jnp.logical_not(has_left))
            def _():
                add_rows(self.go_r.at[i], self.total(i, 0))

            pl.when(has_right)(lambda: self.right(i).start())

        k = t - 2 * (self.depth - 1 - self.z)

        @pl.when(jnp.logical_and(k >= 0, k < self.chunks))
        def _():
            @pl.when(has_right)
            def _():
                remote(self.go_l.at[k], self.suffix.at[k], self.send_l.at[k], self.recv_l.at[k], expert=self.mine).wait_recv()

            @pl.when(jnp.logical_and(has_left, has_right))
            def _():
                add_rows(self.go_l.at[k], self.total(k, 0), self.suffix.at[k])

            @pl.when(jnp.logical_not(has_right))
            def _():
                add_rows(self.go_l.at[k], self.total(k, 0))

            pl.when(has_left)(lambda: self.left(k).start())

    def last(self, i):
        return remote(self.final.at[i], self.other.at[i], self.last_send.at[i], self.last_recv.at[i], expert=self.pair)

    def close(self, i):
        has_left, has_right = self.has_left, self.has_right

        @pl.when(jnp.logical_and(has_left, has_right))
        def _():
            add_rows(self.final.at[i], self.total(i, 0), self.prefix.at[i], self.suffix.at[i])

        @pl.when(jnp.logical_not(has_left))
        def _():
            add_rows(self.final.at[i], self.total(i, 0), self.suffix.at[i])

        @pl.when(jnp.logical_not(has_right))
        def _():
            add_rows(self.final.at[i], self.total(i, 0), self.prefix.at[i])

        self.last(i).start()

    def finish(self, i):
        self.last(i).wait_send()
        pl.when(self.has_right)(lambda: self.right(i).wait_send())
        pl.when(self.has_left)(lambda: self.left(i).wait_send())
        for d in range(self.n_dp):
            self.across(i, d).wait_send()
        for j in range(len(self.orders[0])):
            bit, blocks = self.moved(i, j)
            for r in blocks:
                self.dp_copy(i, r, bit).wait_send()


def two_parts(field):
    high = field.astype(LOW)
    return high, (field - high.astype(F32)).astype(LOW)


def norm_back(field, gain, grad):
    r = inverse_rms(field)
    scaled = grad * gain
    back = r * scaled - field * (r * r * r) * jnp.mean(field * scaled, axis=-1, keepdims=True)
    return back, jnp.sum(field * r * grad, axis=0, keepdims=True)


def back_body(n_dp, n_exp, local, with_late, x_ref, cot, hid_sum, gates_in, routes_t, parents, cosine, sine,
              hidden, queries, keys, values, attended, middle, hidden2, log_total,
              query_hbm, keyval_hbm, output_hbm, router_t, gains, *refs):
    if with_late:
        late_hbm, refs = refs[0], refs[1:]
    outs, refs = refs[: 5 + 2 * with_late], refs[5 + 2 * with_late :]
    input_grad, grad_q, grad_kv, grad_o, grad_s = outs[:5]
    (bias, branch, grad_att, grad_q_pre, grad_kv_pre, rhs, own, own_s, grad_hid, query_full, keyval_full, output_full,
     load_sem, *rest) = refs
    big = GradSum(n_dp, n_exp, own.shape[0], own, rest[:8], rest[8:18])
    little = GradSum(n_dp, n_exp, 1, own_s, rest[18:26], rest[26:36])
    tree, width = x_ref.shape
    ring = Ring(n_exp)
    greet(big.partners() + [(None, {"expert": ring.pair})])
    loads = [
        pltpu.make_async_copy(src, dst, load_sem.at[k])
        for k, (src, dst) in enumerate(((output_hbm, output_full), (query_hbm, query_full), (keyval_hbm, keyval_full)))
    ]
    if with_late:
        late_sem, late_send, late_recv, wide_sem, late_buf = rest[36:41]
        cut = late_hbm.shape[0] // (2 * n_dp)
        kept = {(0, 0): 0, (0, 1): 1, (2, 0): 2, (1, 1): 3}

        def late_rows(r, h):
            return late_hbm.at[pl.ds(pl.multiple_of((big.me ^ r) * 2 * cut + h * cut, 16), cut)]

        def late_half(r, h):
            return late_buf.at[pl.ds(kept[r, h] * cut, cut)]

        def late_land(k):
            return late_buf.at[pl.ds((4 + k) * cut, cut)]

        late = ExpertSum(big.me, late_rows, late_half, late_land, lambda k: late_send.at[k], lambda k: late_recv.at[k])
        late.start()
        late_loads = [pltpu.make_async_copy(late_rows(r, h), late_half(r, h), late_sem.at[k]) for (r, h), k in kept.items()]
        for copy in late_loads:
            copy.start()
        in_rows = outs[5].shape[0]

        def late_end():
            for h in range(2):
                late.end(h, grad_hid.at[pl.ds(0, cut)])
                if h == 0:
                    copies = [pltpu.make_async_copy(grad_hid.at[pl.ds(0, cut)], outs[5].at[pl.ds(0, cut)], wide_sem.at[0])]
                else:
                    copies = [
                        pltpu.make_async_copy(grad_hid.at[pl.ds(0, in_rows - cut)], outs[5].at[pl.ds(cut, in_rows - cut)], wide_sem.at[0]),
                        pltpu.make_async_copy(grad_hid.at[pl.ds(in_rows - cut, 2 * cut - in_rows)], outs[6], wide_sem.at[1])]
                for copy in copies:
                    copy.start()
                for copy in copies:
                    copy.wait()
            late.finish()

    for copy in loads:
        copy.start()
    shard = width // n_dp
    side = shard // 2
    tile = 512
    lane = lanes_of((tree, 128))
    left = lane < HD

    def gain_row(i):
        return gains[...].astype(F32)[i : i + 1]

    bias[...] = mask_bias(parents, tree)

    names = routes_t[...].astype(F32)
    pick = jnp.where(lax.broadcasted_iota(jnp.int32, (16, 128), 0) == lanes_of((16, 128)), 1.0, 0.0).astype(LOW)
    names = dot(jnp.concatenate([names, jnp.zeros_like(names)], axis=0).astype(LOW), pick, 0, 0)
    chosen = jnp.zeros((tree, 128), F32)
    for k in range(routes_t.shape[0]):
        chosen = jnp.maximum(chosen, jnp.where(names[:, k : k + 1] == lane.astype(F32), 1.0, 0.0))
    logits = jnp.where(chosen > 0.5, dot(hidden2[...], router_t[...], 1, 1), -1e30)
    powers = jnp.exp(logits - jnp.max(logits, axis=1, keepdims=True))
    gate = powers / jnp.sum(powers, axis=1, keepdims=True)
    count = gates_in.shape[0]
    where_row = lax.broadcasted_iota(jnp.int32, (count, 128), 0)
    where_lane = lanes_of((count, 128))
    group_row = lax.rem(where_row, 8)
    target = lax.div(where_row, 8) * local + group_row
    pick = jnp.where(group_row < local, jnp.where(target == where_lane, 1.0, 0.0), 0.0).astype(LOW)
    high, low = two_parts(gates_in[...])
    gate_back = dot(high, pick, 0, 0) + dot(low, pick, 0, 0)
    grad_logits = (gate * (gate_back - jnp.sum(gate * gate_back, axis=1, keepdims=True))).astype(LOW)
    grad_router = dot(grad_logits, hidden2[...], 0, 0)[:EXPERTS]
    grad_hidden2 = hid_sum[...] + dot(grad_logits, router_t[...])
    back, gain2_sum = norm_back(middle[...], gain_row(1), grad_hidden2)
    grad_middle = cot[...].astype(F32) + back
    input_grad[...] = grad_middle
    branch[...] = grad_middle.astype(LOW)

    def chunk_grads(i, lhs, rhs_ref):
        def part(n, carry):
            made = dot(lhs[:, pl.ds(pl.multiple_of(n * tile, tile), tile)], rhs_ref[...], 0, 0).astype(LOW)
            for k in range(tile // side):
                own[i, n * (tile // shard) + k // 2, k % 2] = made[k * side : (k + 1) * side]
            return carry

        if tile % shard == 0:
            lax.fori_loop(0, width // tile, part, 0)

    for i in range(2):
        rhs[...] = branch[:, pl.ds(i * tile, tile)]
        chunk_grads(i, attended, rhs)
        big.start(i)

    loads[0].wait()

    def att_tile(n, carry):
        rows = pl.ds(pl.multiple_of(n * tile, tile), tile)
        grad_att[:, rows] = dot(branch[...], output_full[rows, :], 1, 1).astype(LOW)
        return carry

    lax.fori_loop(0, width // tile, att_tile, 0)

    def unrotate(field):
        return field * cosine[...] - turned(field * sine[...])

    scale = HD**-0.5

    def group(c):
        cols = pl.ds(pl.multiple_of(c * 128, 128), 128)
        pair, grad_pair = queries[:, cols], grad_att[:, cols]
        zero = jnp.zeros_like(pair)
        key, value = keys[c], values[c]
        grad_query, grad_key, grad_value = [], 0.0, 0.0
        for h in range(2):
            here = left if h == 0 else jnp.logical_not(left)
            query, grad_out = jnp.where(here, pair, zero), jnp.where(here, grad_pair, zero)
            logs = jnp.sum(jnp.where(lane == 2 * c + h, log_total[...], 0.0), axis=1, keepdims=True)
            probs = jnp.exp(dot(query, key, 1, 1) * scale + bias[...] - logs)
            grad_probs = dot(grad_out, value, 1, 1)
            grad_scores = (probs * (grad_probs - jnp.sum(probs * grad_probs, axis=1, keepdims=True))).astype(LOW)
            grad_value = grad_value + dot(probs.astype(LOW), grad_out, 0, 0)
            grad_query.append(dot(grad_scores, key))
            grad_key = grad_key + dot(grad_scores, query, 0, 0)
        grad_q_pre[:, cols] = unrotate(jnp.where(left, grad_query[0], grad_query[1]) * scale).astype(LOW)
        grad_key = (grad_key + pltpu.roll(grad_key, HD, 1)) * scale
        return unrotate(grad_key), grad_value + pltpu.roll(grad_value, HD, 1)

    def two_groups(i):
        key_a, value_a = group(2 * i)
        key_b, value_b = group(2 * i + 1)
        at = pl.multiple_of(i * 128, 128)
        grad_kv_pre[:, pl.ds(at, 128)] = jnp.where(left, key_a, key_b).astype(LOW)
        at = pl.multiple_of(KV * HD + i * 128, 128)
        grad_kv_pre[:, pl.ds(at, 128)] = jnp.where(left, value_a, value_b).astype(LOW)

    def gather_rhs(i):
        rhs[:, pl.ds(0, 256)] = grad_q_pre[:, pl.ds(i * 256, 256)]
        rhs[:, pl.ds(256, 128)] = grad_kv_pre[:, pl.ds(i * 128, 128)]
        rhs[:, pl.ds(384, 128)] = grad_kv_pre[:, pl.ds(KV * HD + i * 128, 128)]

    for i in range(KV // 2):
        two_groups(i)
        gather_rhs(i)
        chunk_grads(2 + i, hidden, rhs)
        big.start(2 + i)
        if i == 0:
            big.paired(0)
            big.paired(1)
        if i == 1:
            big.paired(2)
        if i == 2:
            big.paired(3)
        if i == 3:
            big.met(0, 0)
            big.met(1, 0)
            big.paired(4)
            big.met(2, 0)

    for copy in loads[1:]:
        copy.wait()

    def hidden_tile(n, carry):
        cols = pl.ds(pl.multiple_of(n * tile, tile), tile)
        grad_hid[:, cols] = dot(grad_q_pre[...], query_full[cols, :], 1, 1) + dot(grad_kv_pre[...], keyval_full[cols, :], 1, 1)
        return carry

    lax.fori_loop(0, width // tile, hidden_tile, 0)
    big.paired(5)
    big.met(3, 0)
    big.met(0, 1)
    big.line(0)
    big.met(1, 1)
    big.line(1)
    back, gain1_sum = norm_back(x_ref[...].astype(F32), gain_row(0), grad_hid[...])
    input_grad[...] = input_grad[...] + back

    sub = lax.broadcasted_iota(jnp.int32, (16, width), 0)
    sums = jnp.where(sub == 0, gain1_sum, jnp.where(sub == 1, gain2_sum, 0.0))
    little_all = jnp.concatenate([grad_router, sums], axis=0).astype(LOW)
    for d in range(n_dp):
        for k in range(2):
            at = d * shard + k * side
            own_s[0, d, k] = little_all[:, at : at + side]
    little.start(0)
    big.met(2, 1)
    big.line(2)
    big.met(4, 0)
    little.paired(0)
    big.met(3, 1)
    big.line(3)
    big.met(5, 0)
    if with_late:
        for copy in late_loads:
            copy.wait()
        late.turn()
    little.met(0, 0)
    big.met(4, 1)
    big.line(4)
    little.met(0, 1)
    big.met(5, 1)
    big.line(5)
    def place(i, which, field):
        rows = pl.ds(pl.multiple_of(which * side, 16), side)
        if i < 2:
            add_rows(grad_o.at[rows, pl.ds(i * tile, tile)], field)
            return
        i = i - 2
        add_rows(grad_q.at[rows, pl.ds(i * 256, 256)], field.at[:, pl.ds(0, 256)])
        add_rows(grad_kv.at[rows, pl.ds(i * 128, 128)], field.at[:, pl.ds(256, 128)])
        add_rows(grad_kv.at[rows, pl.ds(KV * HD + i * 128, 128)], field.at[:, pl.ds(384, 128)])

    def settle(i):
        big.last(i).wait_recv()
        place(i, 1 - big.core, big.other.at[i])

    chunks = own.shape[0]
    hop = 2 * (big.depth - 1)
    for t in range(chunks, chunks + hop):
        big.line(t)
        little.line(t - chunks)
        if t >= hop:
            big.close(t - hop)
            place(t - hop, big.core, big.final.at[t - hop])
        if t > hop:
            settle(t - hop - 1)
        if with_late and t == chunks + hop // 2:
            late_end()
    little.line(hop)
    little.close(0)
    add_rows(grad_s.at[big.core], little.final.at[0])
    settle(chunks - 1)
    for i in range(chunks):
        big.finish(i)
    little.last(0).wait_recv()
    add_rows(grad_s.at[1 - big.core], little.other.at[0])
    little.finish(0)


def back(n_dp, n_exp, local, tokens, cotangent, hid_sum, gates_in, routes_t, parents, tables, saved, late, collective_id):
    tree, width = tokens.shape
    shard = width // n_dp
    shape, vm, sem = jax.ShapeDtypeStruct, pltpu.VMEM, pltpu.SemaphoreType.DMA
    side, chunks, tile, rows = shard // 2, 6, 512, EXPERTS + 16
    big_bufs, big_sems = GradSum.scratch(n_dp, chunks, side, tile)
    little_bufs, little_sems = GradSum.scratch(n_dp, 1, rows, side)
    args = (tokens, cotangent, hid_sum, gates_in, routes_t, parents, *tables, *saved)
    spaces = [VMEM] * len(args)
    spaces[16:19] = [ANY] * 3
    out_shape = [
        shape((tree, width), F32), shape((shard, width), F32), shape((shard, width), F32), shape((shard, width), F32),
        shape((2, rows, side), F32),
    ]
    extra = []
    if late is not None:
        args, spaces = (*args, late), spaces + [ANY]
        out_rows = late.shape[0] // n_dp - shard
        out_shape += [shape((shard, width), F32), shape((out_rows, width), F32)]
        extra = [sem((4,)), sem((6,)), sem((6,)), sem((2,)), vm((10 * late.shape[0] // (2 * n_dp), width), LOW)]
    return pl.pallas_call(
        functools.partial(back_body, n_dp, n_exp, local, late is not None),
        out_shape=out_shape,
        in_specs=[pl.BlockSpec(memory_space=s) for s in spaces],
        out_specs=[pl.BlockSpec(memory_space=s) for s in ([VMEM] * 5 + [ANY] * 2)[: len(out_shape)]],
        scratch_shapes=[
            vm((tree, tree), F32), vm((tree, width), LOW), vm((tree, width), LOW), vm((tree, width), LOW), vm((tree, width), LOW),
            vm((tree, tile), LOW), vm((chunks, n_dp, 2, side, tile), LOW), vm((1, n_dp, 2, rows, side), LOW),
            vm((tree, width), F32), vm((width, width), LOW), vm((width, width), LOW), vm((width, width), LOW), sem((3,)),
            *big_bufs, *big_sems, *little_bufs, *little_sems, *extra,
        ],
        compiler_params=pltpu.CompilerParams(
            collective_id=collective_id, has_side_effects=True, vmem_limit_bytes=63 * MIB),
        name="back",
    )(*args)


def rope_pairs(tree_rows):
    unit = tree_rows // 20
    row = np.arange(tree_rows)
    position = np.where(row < 8 * unit, row, np.where(row < 12 * unit, 8 * unit + row % unit, 9 * unit + row % unit))
    frequency = 10000.0 ** (-np.arange(0, HD, 2) / HD)
    angles = position[:, None] * frequency[None, :]
    return tuple(jnp.asarray(np.concatenate([table] * 4, axis=1), jnp.float32) for table in (np.cos(angles), np.sin(angles)))


def gated_unit(gate_up):
    width_ff = gate_up.shape[-1] // 2
    gate_part = gate_up[..., :width_ff]
    return gate_part / (1.0 + jnp.exp(-gate_part)) * gate_up[..., width_ff:]


def experts_plain(
    n_dp, n_exp, hidden2, grad_y, routes_all, router_full, expert_in, expert_out, middle
):
    tree_rows, width = hidden2.shape
    capacity = CAP
    routes_all = routes_all.transpose(0, 2, 1)
    expert_ids = jnp.arange(EXPERTS, dtype=jnp.int32)
    here = lax.axis_index("expert")
    local = expert_in.shape[0]
    first = here * local
    hidden_all = lax.all_gather(hidden2, "expert", axis=0, tiled=False)
    own_ids = first + jnp.arange(local, dtype=jnp.int32)
    hot_all = routes_all[:, :, :, None] == expert_ids[None, None, None, :]
    chosen_all = jnp.any(hot_all, axis=2)
    chosen = jnp.any(routes_all[:, :, :, None] == own_ids[None, None, None, :], axis=2)
    lower = jnp.tril(jnp.ones((tree_rows, tree_rows), jnp.bfloat16), -1)
    rank = jnp.einsum(
        "tu,jue->jet", lower, chosen.astype(jnp.bfloat16), preferred_element_type=jnp.float32
    ).astype(jnp.int32)
    slots = jnp.arange(capacity, dtype=jnp.int32)
    chosen_t = chosen.transpose(0, 2, 1)
    place = (rank[:, :, None, :] == slots[None, None, :, None]) & chosen_t[:, :, None, :]
    place = place.astype(jnp.bfloat16)
    logits_all = jnp.einsum(
        "jtd,de->jte", hidden_all, router_full, preferred_element_type=jnp.float32
    )
    masked = jnp.where(chosen_all, logits_all, -1e30)
    weight = jnp.exp(masked - jnp.max(masked, axis=-1, keepdims=True))
    weight = weight / jnp.sum(weight, axis=-1, keepdims=True)
    gates_own = lax.dynamic_slice_in_dim(weight, first, local, axis=2)
    gate_slot = jnp.einsum(
        "jest,jte->ejs", place.astype(jnp.float32), gates_own, precision=lax.Precision.HIGHEST
    )[..., None]
    sent = jnp.einsum("jest,jtd->ejsd", place, hidden_all, preferred_element_type=jnp.float32)
    sent = sent.astype(jnp.bfloat16)
    grad_rows = jnp.einsum("jest,jtd->ejsd", place, grad_y, preferred_element_type=jnp.float32)
    grad_rows = grad_rows.astype(jnp.bfloat16)
    gate_up = jnp.einsum("ejsd,edf->ejsf", sent, expert_in, preferred_element_type=jnp.float32)
    activated, glu_back = jax.vjp(gated_unit, gate_up)
    act_low = activated.astype(jnp.bfloat16).astype(jnp.float32)
    act_scaled = (act_low * gate_slot).astype(jnp.bfloat16)
    made = jnp.einsum(
        "ejsf,efd->ejsd", act_scaled, expert_out, preferred_element_type=jnp.float32
    ).astype(jnp.bfloat16)
    out_part = jnp.einsum("jest,ejsd->jtd", place, made, preferred_element_type=jnp.float32)
    out_sum = lax.psum_scatter(
        out_part.astype(jnp.bfloat16), "expert", scatter_dimension=0, tiled=False
    ).astype(jnp.float32)
    result = middle + out_sum
    block_out = result.astype(jnp.bfloat16)
    grad_act = jnp.einsum(
        "ejsd,efd->ejsf", grad_rows, expert_out, preferred_element_type=jnp.float32
    )
    gate_dot = jnp.sum(act_low * grad_act, axis=-1)
    gates_back = jnp.einsum(
        "jest,ejs->jte", place.astype(jnp.float32), gate_dot, precision=lax.Precision.HIGHEST
    )
    grad_out_w = jnp.einsum(
        "ejsf,ejsd->efd", act_scaled, grad_rows, preferred_element_type=jnp.float32
    )
    grad_gate_up = glu_back(grad_act * gate_slot)[0].astype(jnp.bfloat16)
    grad_sent = jnp.einsum(
        "ejsf,edf->ejsd", grad_gate_up, expert_in, preferred_element_type=jnp.float32
    ).astype(jnp.bfloat16)
    grad_in_w = jnp.einsum(
        "ejsd,ejsf->edf", sent, grad_gate_up, preferred_element_type=jnp.float32
    )
    hid_part = jnp.einsum("jest,ejsd->jtd", place, grad_sent, preferred_element_type=jnp.float32)
    gates_mine = lax.all_to_all(gates_back, "expert", split_axis=0, concat_axis=2, tiled=True)[0]
    hid_sum = lax.psum_scatter(
        hid_part.astype(jnp.bfloat16), "expert", scatter_dimension=0, tiled=False
    ).astype(jnp.float32)
    local, units = expert_in.shape[0], expert_out.shape[1]
    low = jnp.bfloat16
    grads = jnp.concatenate(
        [
            grad_in_w.astype(low).reshape(local, n_dp, width // n_dp, width),
            grad_out_w.astype(low).reshape(local, n_dp, units // n_dp, width),
        ],
        axis=2,
    ).reshape(local, width + units, width)
    share = lax.psum_scatter(grads, "dp", scatter_dimension=1, tiled=True).astype(jnp.float32)
    gates_mine = jnp.pad(gates_mine.T.reshape(n_exp, local, tree_rows), ((0, 0), (0, 8 - local), (0, 0)))
    return block_out, hid_sum, gates_mine, share[:, : width // n_dp], share[:, width // n_dp :]


def shards(
    tokens,
    attn_gain,
    w_query,
    w_keyval,
    w_output,
    moe_gain,
    w_router,
    expert_in,
    expert_out,
    cotangent,
    routes,
    parents,
):
    n_dp, n_exp = lax.axis_size("dp"), lax.axis_size("expert")
    local = expert_in.shape[0]
    tree_rows = tokens.shape[0]
    tables = rope_pairs(tree_rows)
    routes_t = routes.T
    (hidden, queries, keys, values, attended, middle, hidden2, log_total, *full, gains, routes_all, grad_y) = front(
        n_dp, n_exp, tokens, jnp.stack([attn_gain, moe_gain]), w_router.T, w_query, w_keyval, w_output, routes_t, parents, tables, cotangent, 1
    )
    router_t = full[3]
    if (n_dp, n_exp) == (4, 8):
        block_out, hid_sum, gate_grads, expert_in_share, expert_out_share, late = experts(
            n_dp, n_exp, hidden2, grad_y, routes_all, router_t, expert_in, expert_out, middle, 2
        )
    else:
        late = None
        block_out, hid_sum, gate_grads, expert_in_share, expert_out_share = experts_plain(
            n_dp, n_exp, hidden2, grad_y, routes_all, router_t[:EXPERTS].T, expert_in, expert_out, middle
        )
    saved = (hidden, queries, keys, values, attended, middle, hidden2, log_total, *full, gains)
    input_grad, grad_q, grad_kv, grad_o, grad_small, *made = back(
        n_dp, n_exp, local, tokens, cotangent, hid_sum, gate_grads.reshape(n_exp * 8, tree_rows), routes_t, parents, tables, saved, late, 3
    )
    if late is not None:
        expert_in_share = jnp.concatenate([expert_in_share, made[0][None]], axis=0)
        expert_out_share = jnp.concatenate([expert_out_share, made[1][None]], axis=0)
    return (
        block_out,
        input_grad,
        grad_small[:, EXPERTS].reshape(-1),
        grad_q,
        grad_kv,
        grad_o,
        grad_small[:, EXPERTS + 1].reshape(-1),
        jnp.concatenate([grad_small[0, :EXPERTS], grad_small[1, :EXPERTS]], axis=1).T,
        expert_in_share,
        expert_out_share,
    )


def solution(mesh):
    in_specs = (
        P(("dp", "expert"), None),
        P("dp"),
        P("dp", None),
        P("dp", None),
        P("dp", None),
        P("dp"),
        P("dp", None),
        P("expert", None, None),
        P("expert", None, None),
        P(("dp", "expert"), None),
        P(("dp", "expert"), None),
        P(("dp", "expert"), None),
    )
    out_specs = (
        P(("dp", "expert"), None),
        P(("dp", "expert"), None),
        P("dp"),
        P("dp", None),
        P("dp", None),
        P("dp", None),
        P("dp"),
        P("dp", None),
        P("expert", "dp", None),
        P("expert", "dp", None),
    )
    return jax.shard_map(shards, mesh=mesh, in_specs=in_specs, out_specs=out_specs, check_vma=False)
```

```python
import functools

import jax
import jax.numpy as jnp
import numpy as np
from jax import lax
from jax.experimental import pallas as pl
from jax.experimental.pallas import tpu as pltpu
from jax.sharding import PartitionSpec as P

H = 16
KV = 8
HD = 64
EXPERTS = 32
TOPK = 8
CAP = 120


EPSILON = 1e-06


MESH = pl.DeviceIdType.MESH
MIB = 1024 * 1024
VMEM = pltpu.VMEM
ANY = pl.ANY


def remote(src, dst, send_sem, recv_sem, **where):
    return pltpu.make_async_remote_copy(
        src_ref=src, dst_ref=dst, send_sem=send_sem, recv_sem=recv_sem,
        device_id=where, device_id_type=MESH,
    )


def greet(partners):
    barrier = pltpu.get_barrier_semaphore()
    for condition, where in partners:
        def signal(where=where):
            pl.semaphore_signal(barrier, inc=1, device_id=where, device_id_type=MESH)
        if condition is None:
            signal()
        else:
            pl.when(condition)(signal)
    count = sum(1 if c is None else c.astype(jnp.int32) for c, _ in partners)
    pl.semaphore_wait(barrier, count)


def add_rows(out, *terms):
    rows = out.shape[0]
    step = 32 if rows % 32 == 0 else 16

    def body(i, carry):
        at = pl.ds(pl.multiple_of(i * step, step), step)
        total = terms[0][at, :].astype(jnp.float32)
        for term in terms[1:]:
            total = total + term[at, :].astype(jnp.float32)
        out[at, :] = total.astype(out.dtype)
        return carry

    lax.fori_loop(0, rows // step, body, 0)


def bit_orders(n):
    bits = [1 << j for j in range(n.bit_length() - 1)]
    return [bits[p:] + bits[:p] for p in range(len(bits))] or [[]]


class Ring:
    def __init__(self, n_exp):
        self.mine = lax.axis_index("expert")
        self.core = lax.rem(self.mine, 2)
        self.z = lax.div(self.mine, 2)
        self.depth = n_exp // 2
        self.far = self.depth // 2
        self.pair = self.mine + 1 - 2 * self.core
        self.right, self.left = self.dev(1), self.dev(-1)

    def dev(self, d):
        return lax.rem(self.z + d + self.depth, self.depth) * 2 + self.core

    def partners(self):
        return [(None, {"expert": e}) for e in (self.pair, self.right, self.left)]


class RingGather:
    def __init__(self, ring, own, out, sems):
        self.ring, self.own, self.out = ring, own, out
        self.send, self.recv, self.pair_send, self.pair_recv = sems
        self.half = own.shape[0] // 2

    @staticmethod
    def scratch(n_exp):
        far, depth = n_exp // 4, n_exp // 2
        sem = pltpu.SemaphoreType.DMA
        return [sem((2, far + 1, 2)), sem((2, far + 1, 2)), sem((depth, 2)), sem((depth, 2))]

    def rows(self, h):
        return pl.ds(h * self.half, self.half)

    def goes(self, side, s, h):
        far = self.ring.far
        return s < far or (s == far and h == side)

    def block(self, d, h):
        return self.out.at[self.ring.dev(d), self.rows(h)]

    def hop(self, side, s, h):
        d = -s if side == 0 else s
        src = self.own.at[self.rows(h)] if s == 0 else self.block(d, h)
        to = self.ring.right if side == 0 else self.ring.left
        return remote(src, self.block(d, h), self.send.at[side, s, h], self.recv.at[side, s + 1, h], expert=to)

    def across(self, d, h):
        src = self.own.at[self.rows(h)] if d == 0 else self.block(d, h)
        slot = d % self.ring.depth
        return remote(src, self.block(d, h), self.pair_send.at[slot, h], self.pair_recv.at[slot, h], expert=self.ring.pair)

    ORDER = ((0, 0), (1, 1), (0, 1), (1, 0))

    def start(self):
        for side, h in self.ORDER:
            if self.goes(side, 1, h):
                self.hop(side, 0, h).start()
        self.across(0, 0).start()
        self.across(0, 1).start()

    def events(self):
        return [(side, s, h) for s in range(1, self.ring.far + 1) for side, h in self.ORDER if self.goes(side, s, h)]

    def handle(self, event):
        side, s, h = event
        d = -s if side == 0 else s
        here = self.block(d, h)
        remote(here, here, self.send.at[side, s, h], self.recv.at[side, s, h], expert=self.ring.mine).wait_recv()
        if self.goes(side, s + 1, h):
            self.hop(side, s, h).start()
        self.across(d, h).start()

    def wait_pair(self, d, h):
        slot = d % self.ring.depth
        here = self.out.at[self.ring.pair - self.ring.mine + self.ring.dev(d), self.rows(h)]
        remote(here, here, self.pair_send.at[slot, h], self.pair_recv.at[slot, h], expert=self.ring.mine).wait_recv()

    def finish_own(self):
        for side, h in self.ORDER:
            if self.goes(side, 1, h):
                self.hop(side, 0, h).wait_send()
        self.across(0, 0).wait_send()
        self.across(0, 1).wait_send()

    def finish_event(self, event):
        side, s, h = event
        if self.goes(side, s + 1, h):
            self.hop(side, s, h).wait_send()
        self.across(-s if side == 0 else s, h).wait_send()


class RingScatter:
    def __init__(self, ring, part, bufs, sems):
        self.ring, self.part = ring, part
        self.pair_buf, self.held, self.got = bufs
        self.pair_send, self.pair_recv, self.send, self.recv = sems
        self.half = self.held(0).shape[0] // 2

    @staticmethod
    def scratch(n_exp, block, dtype):
        far, depth = n_exp // 4, n_exp // 2
        sem = pltpu.SemaphoreType.DMA
        bufs = [pltpu.VMEM((depth,) + block, dtype), pltpu.VMEM((depth,) + block, dtype),
                pltpu.VMEM((2, far) + block, dtype)]
        return bufs, [sem((depth,)), sem((depth,)), sem((2, far + 1, 2)), sem((2, far + 1, 2))]

    def rows(self, h):
        return pl.ds(h * self.half, self.half)

    def order(self):
        far, depth = self.ring.far, self.ring.depth
        order = [far]
        for s in range(far - 1, 0, -1):
            order += [s, depth - s]
        return order + [0]

    def comes(self, side, d, h):
        far = self.ring.far
        return d + 1 < far or (d + 1 == far and h == side)

    def across(self, d):
        ring = self.ring
        return remote(self.part(d, 1), self.pair_buf(d),
                      self.pair_send.at[d], self.pair_recv.at[d], expert=ring.pair)

    def start_pair(self, d):
        self.across(d).start()

    def wait_pair(self, d):
        self.across(d).wait_recv()

    def wait_got(self, side, d, h):
        here = self.got(side, d).at[self.rows(h)]
        remote(here, here, self.send.at[side, d, h], self.recv.at[side, d, h], expert=self.ring.mine).wait_recv()

    def hop(self, side, d, h):
        slot = d if side == 0 else self.ring.depth - d
        rows = self.rows(h)
        return remote(self.held(slot).at[rows], self.got(side, d - 1).at[rows], self.send.at[side, d, h],
                      self.recv.at[side, d - 1, h], expert=self.ring.right if side == 0 else self.ring.left)

    def push(self, side, d, h):
        ring = self.ring
        slot = d if side == 0 else ring.depth - d
        rows = self.rows(h)
        terms = [self.part(slot, 0).at[rows], self.pair_buf(slot).at[rows]]
        if self.comes(side, d, h):
            self.wait_got(side, d, h)
            terms.append(self.got(side, d).at[rows])
        add_rows(self.held(slot).at[rows], *terms)
        self.hop(side, d, h).start()

    def first(self):
        far = self.ring.far
        self.wait_pair(far)
        self.push(0, far, 0)
        self.push(1, far, 1)

    def early(self):
        for d in range(self.ring.far - 1, 0, -1):
            self.wait_pair(d)
            self.push(0, d, 1)
            self.wait_pair(self.ring.depth - d)
            self.push(1, d, 0)

    def late(self):
        for d in range(self.ring.far - 1, 0, -1):
            self.push(0, d, 0)
            self.push(1, d, 1)

    def last(self, out, *more):
        self.wait_pair(0)
        for h in range(2):
            rows = self.rows(h)
            terms = [self.part(0, 0).at[rows], self.pair_buf(0).at[rows]] + [m.at[rows] for m in more]
            for side in range(2):
                if self.comes(side, 0, h):
                    self.wait_got(side, 0, h)
                    terms.append(self.got(side, 0).at[rows])
            add_rows(out.at[rows], *terms)

    def finish_sends(self):
        far = self.ring.far
        for side in range(2):
            for d in range(1, far + 1):
                for h in range(2):
                    if d < far or h == side:
                        self.hop(side, d, h).wait_send()
        for d in range(self.ring.depth):
            self.across(d).wait_send()


def views(bufs):
    pair_buf, held, got = bufs
    return (lambda d: pair_buf.at[d], lambda d: held.at[d], lambda side, d: got.at[side, d])


SLOTS = 128
F32, LOW = jnp.float32, jnp.bfloat16


def dot(a, b, over_a=1, over_b=0):
    return lax.dot_general(a, b, (((over_a,), (over_b,)), ((), ())), preferred_element_type=F32)


class ExpertSum:
    def __init__(self, me, first, half, land, send, recv):
        self.me, self.first, self.half, self.land, self.send, self.recv = me, first, half, land, send, recv

    def hop(self, step, h, which):
        bit = (1, 2)[h] if step == 0 else (2, 1)[h]
        r = bit if which == 0 else 3
        k = 2 * h + which if step == 0 else 4 + h
        src = self.first(r, h) if step == 0 else self.half(r, h)
        return remote(src, self.land(k), self.send(k), self.recv(k), dp=self.me ^ bit)

    def start(self, blocks=(1, 0)):
        for which in blocks:
            for h in range(2):
                self.hop(0, h, which).start()

    def turn(self, blocks=(1, 0)):
        for which in blocks:
            for h in range(2):
                self.hop(0, h, which).wait_recv()
                kept = 0 if which == 0 else (2, 1)[h]
                add_rows(self.half(kept, h), self.half(kept, h), self.land(2 * h + which))
                if which == 1:
                    self.hop(1, h, 0).start()

    def end(self, h, out):
        self.hop(1, h, 0).wait_recv()
        add_rows(out, self.half(0, h), self.land(4 + h))

    def finish(self):
        for step, h, which in ((0, 0, 0), (0, 0, 1), (0, 1, 0), (0, 1, 1), (1, 0, 0), (1, 1, 0)):
            self.hop(step, h, which).wait_send()


def experts_body(n_dp, n_exp, hid_ref, gy_hbm, routes_t, wr_t, w_in_hbm, w_out_hbm, middle,
                 block_out, hid_sum, gates_out, in_share, out_share, late,
                 x_all, w_in, w_out, sent, grows, gu, tmp, acts, stage, slots, gates, dots, wide,
                 pair_buf, held, got, *sems):
    w_sem, gy_sem, wide_sem, own_sem, ready, late_sem, gate_send, gate_recv, dp_ready, dp_send, dp_recv = sems[:11]
    gather_sems, out_sems, hid_sems = sems[11:15], sems[15:19], sems[19:23]
    me = lax.axis_index("dp")
    local, _, width = sent.shape
    tree, hidden_units = hid_ref.shape[0], w_out.shape[1]
    rows_e = local * SLOTS
    ring = Ring(n_exp)
    mine, core, depth = ring.mine, ring.core, ring.depth
    first = mine * local
    peers = [lax.rem(mine + k, n_exp) for k in range(1, n_exp)]
    greet([(None, {"expert": e}) for e in peers] + [(None, {"dp": me ^ bit}) for bit in (1, 2)])

    weights = [pltpu.make_async_copy(w_in_hbm, w_in, w_sem.at[0]), pltpu.make_async_copy(w_out_hbm, w_out, w_sem.at[1])]
    gather = RingGather(ring, hid_ref, x_all, gather_sems)
    gather.start()
    for copy in weights:
        copy.start()
    own = pltpu.make_async_copy(hid_ref, x_all.at[mine], own_sem)
    own.start()

    def gy_buf(j):
        return stage.at[lax.rem(j, 2), pl.ds(0, tree)]

    def gy_copy(j):
        return pltpu.make_async_copy(gy_hbm.at[j], gy_buf(j), gy_sem.at[lax.rem(j, 2)])

    gy_copy(0).start()

    below = (lax.broadcasted_iota(jnp.int32, (tree, tree), 0) < lax.broadcasted_iota(jnp.int32, (tree, tree), 1)).astype(LOW)
    sub16 = lax.broadcasted_iota(jnp.int32, (16, tree), 0)

    def find_slots(j, carry):
        names = routes_t[j]
        chosen = jnp.zeros((16, tree), F32)
        for k in range(names.shape[0]):
            chosen = jnp.maximum(chosen, jnp.where(names[k : k + 1, :] == first + sub16, 1.0, 0.0))
        chosen = jnp.where(sub16 < local, chosen, 0.0)
        rank = dot(chosen.astype(LOW), below)
        slots[j] = jnp.where(chosen > 0.5, rank, -1.0)[:8]
        return carry

    lax.fori_loop(0, n_exp, find_slots, 0)

    slot_ids = lax.broadcasted_iota(jnp.int32, (SLOTS, tree), 0).astype(F32)

    def places(j):
        return jnp.concatenate(
            [jnp.where(slot_ids == slots[j, i : i + 1, :], 1.0, 0.0).astype(LOW) for i in range(local)], axis=0)

    def places_t(j):
        lane = lax.broadcasted_iota(jnp.int32, (tree, 128), 1)
        pick = jnp.where(lax.broadcasted_iota(jnp.int32, (16, 128), 0) == lax.broadcasted_iota(jnp.int32, (16, 128), 1), 1.0, 0.0)
        slot = dot(jnp.concatenate([slots[j], jnp.zeros((8, tree), F32)], axis=0).astype(LOW), pick.astype(LOW), 0, 0)
        lanes = lane.astype(F32)
        return jnp.concatenate(
            [jnp.where(lanes == slot[:, i : i + 1], 1.0, 0.0).astype(LOW) for i in range(local)], axis=1)

    def find_gates(j):
        names = routes_t[j]
        experts = lax.broadcasted_iota(jnp.int32, (EXPERTS, tree), 0)
        chosen = jnp.zeros((EXPERTS, tree), F32)
        for k in range(names.shape[0]):
            chosen = jnp.maximum(chosen, jnp.where(names[k : k + 1, :] == experts, 1.0, 0.0))
        logits = jnp.where(chosen > 0.5, dot(wr_t[pl.ds(0, EXPERTS), :], x_all[j], 1, 1), -1e30)
        powers = jnp.exp(logits - jnp.max(logits, axis=0, keepdims=True))
        share = powers / jnp.sum(powers, axis=0, keepdims=True)
        sub = lax.broadcasted_iota(jnp.int32, (8, tree), 0)
        own_gates = jnp.zeros((8, tree), F32)
        for i in range(local):
            row = jnp.sum(jnp.where(experts == first + i, share, 0.0), axis=0, keepdims=True)
            own_gates = jnp.where(sub == i, row, own_gates)
        gates[j] = own_gates

    halves = width // 512

    def dispatch(j, src, dest):
        place = places(j)

        def body(n, carry):
            cols = pl.ds(pl.multiple_of(n * 512, 512), 512)
            picked = dot(place, src[:, cols]).astype(LOW)
            for i in range(local):
                dest[i, pl.ds(pl.multiple_of(j * SLOTS, SLOTS), SLOTS), cols] = picked[i * SLOTS : (i + 1) * SLOTS]
            return carry

        lax.fori_loop(0, halves, body, 0)

    def slot_gate(j, e):
        return jnp.sum(jnp.where(slot_ids == slots[j, pl.ds(e, 1), :], gates[j, pl.ds(e, 1), :], 0.0), axis=1, keepdims=True)

    def forward(chip):
        pair_rows = pl.ds(pl.multiple_of(chip * 2 * SLOTS, 2 * SLOTS), 2 * SLOTS)

        def one_tree(q, carry):
            j = 2 * chip + q
            find_gates(j)
            dispatch(j, x_all.at[j], sent)
            return carry

        lax.fori_loop(0, 2, one_tree, 0)

        def one_expert(e, carry):
            both = dot(sent[e, pair_rows, :], w_in[e])
            gu[e, pair_rows, :] = both.astype(LOW)
            a, b = both[:, :hidden_units], both[:, hidden_units:]
            act = (a / (1.0 + jnp.exp(-a)) * b).astype(LOW).astype(F32)
            gate = jnp.concatenate([slot_gate(2 * chip, e), slot_gate(2 * chip + 1, e)], axis=0)
            made = dot((act * gate).astype(LOW), w_out[e]).astype(LOW)
            for q in range(2):
                tmp[pl.ds(pl.multiple_of(q * rows_e + e * SLOTS, SLOTS), SLOTS), :] = made[q * SLOTS : (q + 1) * SLOTS]
            return carry

        lax.fori_loop(0, local, one_expert, 0)

    def combine_out(chip, q):
        rows = pl.ds(pl.multiple_of(q * rows_e, rows_e), rows_e)
        x_all[2 * chip + q] = dot(places_t(2 * chip + q), tmp[rows, :]).astype(LOW)

    def grad_rows(j, carry):
        pl.when(j + 1 < n_exp)(lambda: gy_copy(j + 1).start())
        gy_copy(j).wait()
        dispatch(j, gy_buf(j), grows)
        return carry

    events = gather.events()

    def out_part(d, other):
        return x_all.at[ring.dev(d) + other * (1 - 2 * core)]

    out = RingScatter(ring, out_part, views((pair_buf, held, got)), out_sems)

    def chip_at(d):
        return lax.rem(ring.z + d, depth)

    def group(g, carry):
        d = jnp.where(g == 0, 0, jnp.where(g == 1, depth - 1, jnp.where(g == 2, 1, 2)))
        chip = chip_at(d)

        @pl.when(g == 0)
        def _():
            own.wait()
            gather.wait_pair(0, 0)
            gather.wait_pair(0, 1)
            for copy in weights:
                copy.wait()

        @pl.when(g == 1)
        def _():
            for event in events[:4]:
                gather.handle(event)
            gather.wait_pair(-1, 0)
            gather.wait_pair(-1, 1)

        @pl.when(g == 2)
        def _():
            gather.wait_pair(1, 0)
            gather.wait_pair(1, 1)

        @pl.when(g == 3)
        def _():
            for event in events[4:]:
                gather.handle(event)
            out.early()
            gather.wait_pair(2, 0)
            gather.wait_pair(2, 1)

        forward(chip)

        @pl.when(g == 0)
        def _():
            gather.finish_own()
            lax.fori_loop(0, n_exp, grad_rows, 0)

        for at, d in ((1, -1), (2, 1), (3, 2)):
            @pl.when(g == at)
            def _():
                for event in events:
                    if event[1] == abs(d) and (abs(d) == 2 or (event[0] == 0) == (d < 0)):
                        gather.finish_event(event)

        combine_out(chip, 1 - core)
        pl.when(g == 0)(lambda: out.start_pair(0))
        pl.when(g == 1)(lambda: out.start_pair(depth - 1))
        pl.when(g == 2)(lambda: out.start_pair(1))
        pl.when(g == 3)(lambda: out.start_pair(2))
        combine_out(chip, core)
        return carry

    lax.fori_loop(0, depth, group, 0)
    out.first()
    middle_copy = pltpu.make_async_copy(middle, wide.at[pl.ds(0, tree)], wide_sem.at[0])
    middle_copy.start()

    in_rows, out_rows = width // n_dp, hidden_units // n_dp
    cut = (in_rows + out_rows) // 2

    def grad_half(e, r, h):
        at = 2 * r + h
        return gu.at[e, pl.ds(at * cut, cut)] if at < 5 else stage.at[e, pl.ds((at - 5) * cut, cut)]

    def grad_land(e, k):
        return w_in.at[e, pl.ds(k * cut, cut)] if k < 5 else w_out.at[e, pl.ds(0, cut)]

    def grad_sum(e):
        half = lambda r, h: grad_half(e, r, h)
        return ExpertSum(me, half, half, lambda k: grad_land(e, k), lambda k: dp_send.at[e, k], lambda k: dp_recv.at[e, k])

    def grads_start(e):
        pl.semaphore_wait(dp_ready.at[e], 2)
        grad_sum(e).start()

    def grads_turn(e):
        grad_sum(e).turn()

    def wide_copies(e):
        return (
            pltpu.make_async_copy(wide.at[pl.ds(0, in_rows)], in_share.at[e], wide_sem.at[0]),
            pltpu.make_async_copy(wide.at[pl.ds(in_rows, out_rows)], out_share.at[e], wide_sem.at[1]),
        )

    def grads_end(e):
        for h in range(2):
            grad_sum(e).end(h, wide.at[pl.ds(h * cut, cut)])
        for copy in wide_copies(e):
            copy.start()
        grad_sum(e).finish()
        for copy in wide_copies(e):
            copy.wait()

    block = 4 * SLOTS
    sub8 = lax.broadcasted_iota(jnp.int32, (8, tree), 0)

    def back_units(e):
        def one_block(m, inner):
            rows = pl.ds(pl.multiple_of(m * block, block), block)
            grad_act = dot(grows[e, rows, :], w_out[e], 1, 1)
            a = gu[e, rows, pl.ds(0, hidden_units)].astype(F32)
            b = gu[e, rows, pl.ds(hidden_units, hidden_units)].astype(F32)
            sg = 1.0 / (1.0 + jnp.exp(-a))
            sw = a * sg
            act = (sw * b).astype(LOW).astype(F32)
            gate = jnp.concatenate([slot_gate(4 * m + q, e) for q in range(4)], axis=0)
            told = jnp.sum(act * grad_act, axis=1, keepdims=True)
            acts[rows, :] = (act * gate).astype(LOW)
            grad_act = grad_act * gate
            tmp[rows, pl.ds(0, hidden_units)] = (grad_act * b * sg * (1.0 + a * (1.0 - sg))).astype(LOW)
            tmp[rows, pl.ds(hidden_units, hidden_units)] = (grad_act * sw).astype(LOW)
            for q in range(4):
                j = 4 * m + q
                row = jnp.sum(
                    jnp.where(slot_ids == slots[j, pl.ds(e, 1), :], told[q * SLOTS : (q + 1) * SLOTS], 0.0),
                    axis=0, keepdims=True)
                dots[j] = jnp.where(sub8 == e, row, dots[j])
            return inner

        lax.fori_loop(0, n_exp // 4, one_block, 0)

    def back_weights(e):
        for r in range(n_dp):
            d = me ^ r
            grad_in = dot(sent[e, :, pl.ds(pl.multiple_of(d * in_rows, in_rows), in_rows)], tmp[...], 0, 0).astype(LOW)
            grad_out = dot(acts[:, pl.ds(pl.multiple_of(d * out_rows, out_rows), out_rows)], grows[e], 0, 0).astype(LOW)
            grad_half(e, r, 0)[...] = grad_in[:cut]
            half = grad_half(e, r, 1)
            half[pl.ds(0, in_rows - cut), :] = grad_in[cut:]
            half[pl.ds(in_rows - cut, out_rows), :] = grad_out

    def back_rows(e, dest):
        def back_half(m, inner):
            rows = pl.ds(pl.multiple_of(m * 512, 512), 512)
            dest[rows, :] = dot(tmp[rows, :], w_in[e], 1, 1).astype(LOW)
            return inner

        lax.fori_loop(0, n_exp * SLOTS // 512, back_half, 0)

    end = local - 1

    def backward(e, carry):
        back_units(e)
        pl.when(e > 0)(lambda: grads_start(e - 1))
        back_weights(e)
        back_rows(e, sent.at[e])
        for bit in (1, 2):
            pl.semaphore_signal(dp_ready.at[e], inc=1, device_id={"dp": me ^ bit}, device_id_type=MESH)
        pl.when(e == 1)(out.late)
        return carry

    dots[...] = jnp.zeros(dots.shape, F32)
    lax.fori_loop(0, end, backward, 0)
    back_units(end)
    grads_start(end - 1)
    back_rows(end, grows.at[end - 1])


    def hid_part(d, other):
        if d == 0:
            return x_all.at[mine + other * (1 - 2 * core)]
        k = 2 * (d - 1) + other
        return grows.at[k // 3, pl.ds((k % 3) * tree, tree)]

    hid = RingScatter(ring, hid_part, views((pair_buf, held, got)), hid_sems)

    def combine_hid(d):
        for other in range(2):
            j = ring.dev(d) + other * (1 - 2 * core)
            rows = pl.ds(pl.multiple_of(j * SLOTS, SLOTS), SLOTS)
            made = jnp.concatenate([sent[i, rows, :] for i in range(end)] + [grows[end - 1, rows, :]], axis=0)
            hid_part(d, other)[...] = dot(places_t(j), made).astype(LOW)

    for d in (2, 1, depth - 1):
        combine_hid(d)

    gate_copies = []
    for k, e in enumerate(peers):
        copy = remote(dots.at[e], gates_out.at[mine], gate_send.at[k], gate_recv.at[k], expert=e)
        copy.start()
        gate_copies.append(copy)
    gates_out[mine] = dots[mine]
    middle_copy.wait()
    out.last(block_out, wide.at[pl.ds(0, tree)])
    out.finish_sends()
    for partner in (ring.pair, ring.right, ring.left):
        pl.semaphore_signal(ready, inc=1, device_id={"expert": partner}, device_id_type=MESH)
    pl.semaphore_wait(ready, 3)
    for d in (2, 1, depth - 1):
        hid.start_pair(d)
    hid.first()
    combine_hid(0)
    hid.start_pair(0)
    hid.early()
    back_weights(end)

    def late_copy(r, h):
        at = pl.multiple_of((me ^ r) * 2 * cut + h * cut, 16)
        return pltpu.make_async_copy(grad_half(end, r, h), late.at[pl.ds(at, cut)], late_sem.at[2 * r + h])

    for r in range(n_dp):
        for h in range(2):
            late_copy(r, h).start()
    hid.late()
    grads_turn(0)
    grads_turn(end - 2)
    grads_end(0)
    grads_turn(end - 1)
    grads_end(1)
    hid.last(wide.at[pl.ds(0, tree)])
    hid_copy = pltpu.make_async_copy(wide.at[pl.ds(0, tree)], hid_sum, wide_sem.at[0])
    hid_copy.start()
    hid_copy.wait()
    for e in range(2, end):
        grads_end(e)
    for r in range(n_dp):
        for h in range(2):
            late_copy(r, h).wait()
    for k, copy in enumerate(gate_copies):
        copy.wait_send()
        source = lax.rem(mine + n_exp - 1 - k, n_exp)
        remote(dots.at[mine], gates_out.at[source], gate_send.at[k], gate_recv.at[k], expert=mine).wait_recv()
    hid.finish_sends()


def experts(n_dp, n_exp, hidden2, grad_y, routes_all, router_t, expert_in, expert_out, middle, collective_id):
    local, width, both = expert_in.shape
    units = expert_out.shape[1]
    tree = hidden2.shape[0]
    rows = n_exp * SLOTS
    sem = pltpu.SemaphoreType.DMA
    bufs, out_sems = RingScatter.scratch(n_exp, (tree, width), LOW)
    _, hid_sems = RingScatter.scratch(n_exp, (tree, width), LOW)
    shape = jax.ShapeDtypeStruct
    return pl.pallas_call(
        functools.partial(experts_body, n_dp, n_exp),
        out_shape=[
            shape((tree, width), LOW),
            shape((tree, width), F32),
            shape((n_exp, 8, tree), F32),
            shape((local - 1, width // n_dp, width), F32),
            shape((local - 1, units // n_dp, width), F32),
            shape((width + units, width), LOW),
        ],
        in_specs=[pl.BlockSpec(memory_space=s) for s in (VMEM, ANY, VMEM, VMEM, ANY, ANY, ANY)],
        out_specs=[pl.BlockSpec(memory_space=s) for s in (VMEM, ANY, VMEM, ANY, ANY, ANY)],
        scratch_shapes=[
            pltpu.VMEM((n_exp, tree, width), LOW),
            pltpu.VMEM((local, width, both), LOW),
            pltpu.VMEM((local, units, width), LOW),
            pltpu.VMEM((local, rows, width), LOW),
            pltpu.VMEM((local, rows, width), LOW),
            pltpu.VMEM((local, rows, both), LOW),
            pltpu.VMEM((max(rows, 2 * local * SLOTS), width), LOW),
            pltpu.VMEM((rows, units), LOW),
            pltpu.VMEM((local, 3 * (width + units) // (2 * n_dp), width), LOW),
            pltpu.VMEM((n_exp, 8, tree), F32),
            pltpu.VMEM((n_exp, 8, tree), F32),
            pltpu.VMEM((n_exp, 8, tree), F32),
            pltpu.VMEM(((width + units) // n_dp, width), F32),
            *bufs,
            sem((2,)), sem((2,)), sem((2,)), sem, pltpu.SemaphoreType.REGULAR, sem((2 * n_dp,)), sem((n_exp - 1,)), sem((n_exp - 1,)),
            pltpu.SemaphoreType.REGULAR((local,)), sem((local, 6)), sem((local, 6)),
            *RingGather.scratch(n_exp), *out_sems, *hid_sems,
        ],
        compiler_params=pltpu.CompilerParams(
            collective_id=collective_id, has_side_effects=True, vmem_limit_bytes=63 * MIB),
        name="experts",
    )(hidden2, grad_y, routes_all, router_t, expert_in, expert_out, middle)


def lanes_of(shape):
    return lax.broadcasted_iota(jnp.int32, shape, 1)


def turned(field):
    low_half = lax.rem(lanes_of(field.shape), HD) < HD // 2
    return jnp.where(low_half, -pltpu.roll(field, 128 - HD // 2, 1), pltpu.roll(field, HD // 2, 1))


def mask_bias(parents, tree):
    unit = tree // 20

    def segment(row):
        return jnp.where(row < 8 * unit, 0, jnp.where(row < 12 * unit, 1 + lax.div(row - 8 * unit, unit), 5 + lax.div(row - 12 * unit, unit)))

    count = parents.shape[1]
    names = parents[...].astype(F32)
    wide = (tree, count)
    seg = segment(lax.broadcasted_iota(jnp.int32, wide, 0)).astype(F32)
    lane = lanes_of(wide).astype(F32)
    own = seg[:, :1]
    parent = jnp.sum(jnp.where(lane == seg, names, 0.0), axis=1, keepdims=True)
    grand = jnp.sum(jnp.where(lane == parent, names, 0.0), axis=1, keepdims=True)
    square = (tree, tree)
    row, col = lax.broadcasted_iota(jnp.int32, square, 0), lanes_of(square)
    there = segment(col).astype(F32)
    hit = jnp.maximum(
        jnp.maximum(jnp.where(there == own, 1.0, 0.0), jnp.where(there == parent, 1.0, 0.0)), jnp.where(there == grand, 1.0, 0.0))
    hit = jnp.where(col <= row, hit, 0.0)
    return jnp.where(hit > 0.5, 0.0, -1e30)


def inverse_rms(field):
    return lax.rsqrt(jnp.mean(field * field, axis=-1, keepdims=True) + EPSILON)


class DpGather:
    def __init__(self, n_dp, mine, me, ins, outs, sems):
        self.n_dp, self.me, self.ins, self.outs = n_dp, me, ins, outs
        self.send, self.recv, self.pair_send, self.pair_recv, self.own_sem = sems
        self.core = lax.rem(mine, 2)
        self.pair = mine + 1 - 2 * self.core
        self.shard = ins[0].shape[0]
        half = self.shard // 2
        self.orders = bit_orders(n_dp)
        self.cuts = min(2, len(self.orders), half // 16)
        self.size = half // self.cuts

    @staticmethod
    def scratch(count, n_dp):
        sem = pltpu.SemaphoreType.DMA
        bits = max(1, n_dp.bit_length() - 1)
        return [sem((count, 2, n_dp, bits)), sem((count, 2, n_dp)), sem((count, 2, n_dp)), sem((count, 2, n_dp)), sem((count,))]

    def rows(self, start, side, p):
        return pl.ds(pl.multiple_of(start + side * (self.shard // 2) + p * self.size, 16), self.size)

    def hop(self, a, p, r, bit):
        there = self.outs[a].at[self.rows((self.me ^ r) * self.shard, self.core, p)]
        src = self.ins[a].at[self.rows(0, self.core, p)] if r == 0 else there
        return remote(src, there, self.send.at[a, p, r, bit.bit_length() - 1], self.recv.at[a, p, r ^ bit], dp=self.me ^ bit)

    def own(self, a):
        at = pl.ds(pl.multiple_of(self.me * self.shard, 16), self.shard)
        return pltpu.make_async_copy(self.ins[a], self.outs[a].at[at], self.own_sem.at[a])

    def across(self, a, p, r, side):
        here = self.outs[a].at[self.rows((self.me ^ r) * self.shard, side, p)]
        return remote(here, here, self.pair_send.at[a, p, r], self.pair_recv.at[a, p, r], expert=self.pair)

    def start(self, a):
        for p in range(self.cuts):
            for bit in self.orders[p]:
                self.hop(a, p, 0, bit).start()
        self.own(a).start()

    def stage(self, p, j):
        order = self.orders[p]
        blocks = [0]
        for bit in order[:j]:
            blocks = blocks + [r | bit for r in blocks]
        return [r | order[j] for r in blocks], order[j + 1 :]

    def turn(self, a, j):
        for p in range(self.cuts):
            blocks, onward = self.stage(p, j)
            for r in blocks:
                here = self.outs[a].at[self.rows((self.me ^ r) * self.shard, self.core, p)]
                remote(here, here, self.send.at[a, p, r, 0], self.recv.at[a, p, r], dp=self.me).wait_recv()
                for bit in onward:
                    self.hop(a, p, r, bit).start()
                self.across(a, p, r, self.core).start()

    def ready(self, a):
        self.own(a).wait()
        for p in range(self.cuts):
            for r in range(1, self.n_dp):
                self.across(a, p, r, 1 - self.core).wait_recv()

    def finish(self, a):
        for p in range(self.cuts):
            for bit in self.orders[p]:
                self.hop(a, p, 0, bit).wait_send()
            for j in range(len(self.orders[p])):
                blocks, onward = self.stage(p, j)
                for r in blocks:
                    for bit in onward:
                        self.hop(a, p, r, bit).wait_send()
                    self.across(a, p, r, self.core).wait_send()


def front_body(n_dp, n_exp, x_ref, gain_pair, router_in, w_query, w_keyval, w_output, routes_t, parents, cosine, sine, cot,
               hidden_hbm, queries_hbm, keys_hbm, values_hbm, attended_hbm, middle_hbm, hidden2_hbm, log_hbm,
               query_hbm, keyval_hbm, output_hbm, router_t, gains, routes_all, grad_y,
               hidden, queries, keys, values, query_full, keyval_full, output_full, small, small_all, bias,
               attended, middle, hidden2, log_total, *sems):
    gather_sems, (small_send, small_recv, route_send, route_recv, out_sem), ring_sems = sems[:5], sems[5:10], sems[10:14]
    me, mine = lax.axis_index("dp"), lax.axis_index("expert")
    peers = [lax.rem(mine + k, n_exp) for k in range(1, n_exp)]
    greet([(None, {"expert": e}) for e in peers] + [(None, {"dp": me ^ k}) for k in range(1, n_dp)])
    tree, width = x_ref.shape
    shard = w_query.shape[0]

    small[...] = jnp.zeros(small.shape, LOW)
    small[pl.ds(0, EXPERTS), :] = router_in[...]
    sub = lax.broadcasted_iota(jnp.int32, (16, shard), 0)
    gain_rows = gain_pair[...].astype(F32)
    small[pl.ds(EXPERTS, 16), :] = jnp.where(sub == 0, gain_rows[:1], jnp.where(sub == 1, gain_rows[1:], 0.0)).astype(LOW)

    gather = DpGather(n_dp, mine, me, (w_query, w_keyval, w_output), (query_full, keyval_full, output_full), gather_sems)

    def small_copy(k):
        return remote(small, small_all.at[me], small_send.at[k], small_recv.at[k], dp=me ^ k)

    def route_copy(k, e):
        return remote(routes_t, routes_all.at[mine], route_send.at[k], route_recv.at[k], expert=e)

    saves = [
        pltpu.make_async_copy(src, dst, out_sem.at[k])
        for k, (src, dst) in enumerate((
            (query_full, query_hbm), (keyval_full, keyval_hbm), (output_full, output_hbm), (hidden, hidden_hbm),
            (queries, queries_hbm), (keys, keys_hbm), (values, values_hbm), (cot, grad_y.at[mine]),
            (attended, attended_hbm), (log_total, log_hbm), (middle, middle_hbm), (hidden2, hidden2_hbm)))
    ]
    ring = RingGather(Ring(n_exp), cot, grad_y, ring_sems)
    events = ring.events()
    for k in range(1, n_dp):
        small_copy(k).start()
    ring.start()
    gather.start(0)
    gather.start(1)
    saves[7].start()
    for k, e in enumerate(peers):
        route_copy(k, e).start()
    small_all[me] = small[...]
    routes_all[mine] = routes_t[...]
    bias[...] = mask_bias(parents, tree)
    log_total[...] = jnp.zeros(log_total.shape, F32)
    x = x_ref[...].astype(F32)
    scaled = x * inverse_rms(x)
    for k in range(1, n_dp):
        remote(small, small_all.at[me ^ k], small_send.at[k], small_recv.at[k], dp=me).wait_recv()
    joined = jnp.concatenate([small_all[d] for d in range(n_dp)], axis=1)
    router_t[...] = jnp.zeros(router_t.shape, LOW)
    router_t[pl.ds(0, EXPERTS), :] = joined[:EXPERTS]
    gains[...] = joined[EXPERTS:]
    gain_rows = joined[EXPERTS:].astype(F32)
    hidden[...] = (scaled * gain_rows[:1]).astype(LOW)
    saves[3].start()
    stages = len(gather.orders[0])
    for j in range(stages - 1):
        gather.turn(0, j)
        gather.turn(1, j)
    gather.start(2)
    for event in events[:2]:
        ring.handle(event)
    gather.turn(0, stages - 1)
    gather.turn(1, stages - 1)
    gather.ready(0)
    saves[0].start()

    def rotate(field):
        return field * cosine[...] + turned(field) * sine[...]

    left = lanes_of((tree, 128)) < HD
    tile = 512

    def query_tile(n, carry):
        cols = pl.ds(pl.multiple_of(n * tile, tile), tile)
        pre = dot(hidden[...], query_full[:, cols])
        for i in range(tile // 128):
            at = pl.multiple_of(n * tile + i * 128, 128)
            queries[:, pl.ds(at, 128)] = rotate(pre[:, i * 128 : (i + 1) * 128]).astype(LOW)
        return carry

    lax.fori_loop(0, width // tile, query_tile, 0)
    saves[4].start()
    gather.ready(1)
    saves[1].start()

    def spread(field, out, i):
        other = pltpu.roll(field, HD, 1)
        out[2 * i] = jnp.where(left, field, other).astype(LOW)
        out[2 * i + 1] = jnp.where(left, other, field).astype(LOW)

    half = KV * HD
    pre = dot(hidden[...], keyval_full[:, pl.ds(0, half)])
    for i in range(half // 128):
        spread(rotate(pre[:, i * 128 : (i + 1) * 128]), keys, i)
    saves[5].start()
    pre = dot(hidden[...], keyval_full[:, pl.ds(half, half)])
    for i in range(half // 128):
        spread(pre[:, i * 128 : (i + 1) * 128], values, i)
    saves[6].start()
    for j in range(stages):
        gather.turn(2, j)

    def heads(c, carry):
        cols = pl.ds(pl.multiple_of(c * 128, 128), 128)
        pair = queries[:, cols]
        made = []
        for h in range(2):
            mine_lanes = left if h == 0 else jnp.logical_not(left)
            query = jnp.where(mine_lanes, pair, jnp.zeros_like(pair))
            scores = dot(query, keys[c], 1, 1) * HD**-0.5 + bias[...]
            top = jnp.max(scores, axis=1, keepdims=True)
            powers = jnp.exp(scores - top)
            total = jnp.sum(powers, axis=1, keepdims=True)
            made.append(dot((powers / total).astype(LOW), values[c]))
            log_total[...] = jnp.where(lanes_of((tree, 128)) == 2 * c + h, top + jnp.log(total), log_total[...])
        attended[:, cols] = jnp.where(left, made[0], made[1]).astype(LOW)
        return carry

    lax.fori_loop(0, KV, heads, 0)
    saves[8].start()
    saves[9].start()
    for event in events[2:4]:
        ring.handle(event)
    gather.ready(2)
    saves[2].start()

    def middle_tile(n, carry):
        cols = pl.ds(pl.multiple_of(n * tile, tile), tile)
        middle[:, cols] = x_ref[:, cols].astype(F32) + dot(attended[...], output_full[:, cols])
        return carry

    lax.fori_loop(0, width // tile, middle_tile, 0)
    saves[10].start()
    field = middle[...]
    hidden2[...] = (field * inverse_rms(field) * gain_rows[1:2]).astype(LOW)
    saves[11].start()
    for a in range(3):
        gather.finish(a)
    for k in range(1, n_dp):
        small_copy(k).wait_send()
    for k, e in enumerate(peers):
        route_copy(k, e).wait_send()
        source = lax.rem(mine + n_exp - 1 - k, n_exp)
        remote(routes_t, routes_all.at[source], route_send.at[k], route_recv.at[k], expert=mine).wait_recv()
    for event in events[4:]:
        ring.handle(event)
    ring.finish_own()
    for h in range(2):
        ring.wait_pair(0, h)
    for event in events:
        ring.finish_event(event)
        ring.wait_pair(-event[1] if event[0] == 0 else event[1], event[2])
    for copy in saves:
        copy.wait()


def front(n_dp, n_exp, tokens, gain_pair, router_in, w_query, w_keyval, w_output, routes_t, parents, tables, cot, collective_id):
    tree, width = tokens.shape
    shard = w_query.shape[0]
    shape, sem, vm = jax.ShapeDtypeStruct, pltpu.SemaphoreType.DMA, pltpu.VMEM
    low = shape((tree, width), LOW)
    spread = shape((KV, tree, 128), LOW)
    full = shape((n_dp * shard, width), LOW)
    small = (EXPERTS + 16, shard)
    return pl.pallas_call(
        functools.partial(front_body, n_dp, n_exp),
        out_shape=[
            low, low, spread, spread, low, shape((tree, width), F32), low, shape((tree, 128), F32),
            full, full, full, shape((128, width), LOW), shape((16, width), LOW),
            shape((n_exp,) + routes_t.shape, jnp.int32), shape((n_exp, tree, width), LOW),
        ],
        in_specs=[pl.BlockSpec(memory_space=VMEM)] * 11,
        out_specs=[pl.BlockSpec(memory_space=s) for s in [ANY] * 11 + [VMEM] * 3 + [ANY]],
        scratch_shapes=[
            vm((tree, width), LOW), vm((tree, width), LOW), vm(spread.shape, LOW), vm(spread.shape, LOW),
            vm(full.shape, LOW), vm(full.shape, LOW), vm(full.shape, LOW),
            vm(small, LOW), vm((n_dp,) + small, LOW), vm((tree, tree), F32),
            vm((tree, width), LOW), vm((tree, width), F32), vm((tree, width), LOW), vm((tree, 128), F32),
            *DpGather.scratch(3, n_dp), sem((n_dp,)), sem((n_dp,)), sem((n_exp - 1,)), sem((n_exp - 1,)), sem((12,)),
            *RingGather.scratch(n_exp),
        ],
        compiler_params=pltpu.CompilerParams(
            collective_id=collective_id, has_side_effects=True, vmem_limit_bytes=56 * MIB),
        name="front",
    )(tokens, gain_pair, router_in, w_query, w_keyval, w_output, routes_t, parents, *tables, cot)


class GradSum:
    def __init__(self, n_dp, n_exp, chunks, own, bufs, sems):
        self.n_dp, self.chunks, self.own = n_dp, chunks, own
        (self.pair_in, self.dp_in, self.prefix, self.suffix, self.go_r, self.go_l, self.final, self.other) = bufs
        (self.pair_send, self.pair_recv, self.dp_send, self.dp_recv,
         self.send_r, self.send_l, self.recv_r, self.recv_l, self.last_send, self.last_recv) = sems
        self.me, self.mine = lax.axis_index("dp"), lax.axis_index("expert")
        self.core = lax.rem(self.mine, 2)
        self.z = lax.div(self.mine, 2)
        self.depth = n_exp // 2
        self.pair = self.mine + 1 - 2 * self.core
        self.has_left, self.has_right = self.z > 0, self.z < self.depth - 1
        self.orders = bit_orders(n_dp)

    @staticmethod
    def scratch(n_dp, chunks, half, columns):
        sem = pltpu.SemaphoreType.DMA
        stages = max(1, n_dp.bit_length() - 1)
        one = pltpu.VMEM((chunks, half, columns), LOW)
        many = pltpu.VMEM((chunks, n_dp, half, columns), LOW)
        bufs = [many, many, one, one, one, one, one, one]
        sems = [sem((chunks, n_dp)), sem((chunks, n_dp)), sem((chunks, n_dp)), sem((chunks, n_dp))]
        return bufs, sems + [sem((chunks,))] * 6

    def partners(self):
        return [(None, {"dp": self.me ^ bit}) for bit in self.orders[0]] + [
            (self.has_left, {"expert": self.mine - 2}), (self.has_right, {"expert": self.mine + 2})]

    def total(self, i, r):
        return self.own.at[i, self.me ^ r, self.core]

    def across(self, i, d):
        return remote(self.own.at[i, d, 1 - self.core], self.pair_in.at[i, d], self.pair_send.at[i, d],
                      self.pair_recv.at[i, d], expert=self.pair)

    def moved(self, i, j):
        order = self.orders[i % len(self.orders)]
        blocks = [0]
        for bit in order[j + 1 :]:
            blocks = blocks + [r | bit for r in blocks]
        return order[j], [r | order[j] for r in blocks]

    def dp_copy(self, i, r, bit):
        return remote(self.total(i, r), self.dp_in.at[i, r], self.dp_send.at[i, r], self.dp_recv.at[i, r], dp=self.me ^ bit)

    def start(self, i):
        for d in range(self.n_dp):
            self.across(i, d).start()

    def paired(self, i):
        for r in range(self.n_dp - 1, -1, -1):
            d = self.me ^ r
            self.across(i, d).wait_recv()
            add_rows(self.total(i, r), self.total(i, r), self.pair_in.at[i, d])
        self.leave(i, 0)

    def leave(self, i, j):
        if j < len(self.orders[0]):
            bit, blocks = self.moved(i, j)
            for r in blocks:
                self.dp_copy(i, r, bit).start()

    def met(self, i, j):
        bit, blocks = self.moved(i, j)
        for r in blocks:
            self.dp_copy(i, r, bit).wait_recv()
            add_rows(self.total(i, r ^ bit), self.total(i, r ^ bit), self.dp_in.at[i, r])
        self.leave(i, j + 1)

    def right(self, i):
        return remote(self.go_r.at[i], self.prefix.at[i], self.send_r.at[i], self.recv_r.at[i], expert=self.mine + 2)

    def left(self, i):
        return remote(self.go_l.at[i], self.suffix.at[i], self.send_l.at[i], self.recv_l.at[i], expert=self.mine - 2)

    def line(self, t):
        i = t - 2 * self.z
        has_left, has_right = self.has_left, self.has_right

        @pl.when(jnp.logical_and(i >= 0, i < self.chunks))
        def _():
            @pl.when(has_left)
            def _():
                remote(self.go_r.at[i], self.prefix.at[i], self.send_r.at[i], self.recv_r.at[i], expert=self.mine).wait_recv()

            @pl.when(jnp.logical_and(has_left, has_right))
            def _():
                add_rows(self.go_r.at[i], self.total(i, 0), self.prefix.at[i])

            @pl.when(jnp.logical_not(has_left))
            def _():
                add_rows(self.go_r.at[i], self.total(i, 0))

            pl.when(has_right)(lambda: self.right(i).start())

        k = t - 2 * (self.depth - 1 - self.z)

        @pl.when(jnp.logical_and(k >= 0, k < self.chunks))
        def _():
            @pl.when(has_right)
            def _():
                remote(self.go_l.at[k], self.suffix.at[k], self.send_l.at[k], self.recv_l.at[k], expert=self.mine).wait_recv()

            @pl.when(jnp.logical_and(has_left, has_right))
            def _():
                add_rows(self.go_l.at[k], self.total(k, 0), self.suffix.at[k])

            @pl.when(jnp.logical_not(has_right))
            def _():
                add_rows(self.go_l.at[k], self.total(k, 0))

            pl.when(has_left)(lambda: self.left(k).start())

    def last(self, i):
        return remote(self.final.at[i], self.other.at[i], self.last_send.at[i], self.last_recv.at[i], expert=self.pair)

    def close(self, i):
        has_left, has_right = self.has_left, self.has_right

        @pl.when(jnp.logical_and(has_left, has_right))
        def _():
            add_rows(self.final.at[i], self.total(i, 0), self.prefix.at[i], self.suffix.at[i])

        @pl.when(jnp.logical_not(has_left))
        def _():
            add_rows(self.final.at[i], self.total(i, 0), self.suffix.at[i])

        @pl.when(jnp.logical_not(has_right))
        def _():
            add_rows(self.final.at[i], self.total(i, 0), self.prefix.at[i])

        self.last(i).start()

    def finish(self, i):
        self.last(i).wait_send()
        pl.when(self.has_right)(lambda: self.right(i).wait_send())
        pl.when(self.has_left)(lambda: self.left(i).wait_send())
        for d in range(self.n_dp):
            self.across(i, d).wait_send()
        for j in range(len(self.orders[0])):
            bit, blocks = self.moved(i, j)
            for r in blocks:
                self.dp_copy(i, r, bit).wait_send()


def two_parts(field):
    high = field.astype(LOW)
    return high, (field - high.astype(F32)).astype(LOW)


def norm_back(field, gain, grad):
    r = inverse_rms(field)
    scaled = grad * gain
    back = r * scaled - field * (r * r * r) * jnp.mean(field * scaled, axis=-1, keepdims=True)
    return back, jnp.sum(field * r * grad, axis=0, keepdims=True)


def back_body(n_dp, n_exp, local, with_late, x_ref, cot, hid_sum, gates_in, routes_t, parents, cosine, sine,
              hidden, queries, keys, values, attended, middle, hidden2, log_total,
              query_hbm, keyval_hbm, output_hbm, router_t, gains, *refs):
    if with_late:
        late_hbm, refs = refs[0], refs[1:]
    outs, refs = refs[: 5 + 2 * with_late], refs[5 + 2 * with_late :]
    input_hbm, grad_q, grad_kv, grad_o, grad_s = outs[:5]
    (bias, branch, grad_att, grad_q_pre, grad_kv_pre, rhs, own, own_s, grad_hid, query_full, keyval_full, output_full,
     load_sem, input_grad, *rest) = refs
    big = GradSum(n_dp, n_exp, own.shape[0], own, rest[:8], rest[8:18])
    little = GradSum(n_dp, n_exp, 1, own_s, rest[18:26], rest[26:36])
    tree, width = x_ref.shape
    ring = Ring(n_exp)
    greet(big.partners() + [(None, {"expert": ring.pair})])
    loads = [
        pltpu.make_async_copy(src, dst, load_sem.at[k])
        for k, (src, dst) in enumerate(((output_hbm, output_full), (query_hbm, query_full), (keyval_hbm, keyval_full)))
    ]
    if with_late:
        late_sem, late_send, late_recv, wide_sem, late_buf = rest[36:41]
        cut = late_hbm.shape[0] // (2 * n_dp)
        kept = {(0, 0): 0, (0, 1): 1, (2, 0): 2, (1, 1): 3}

        def late_rows(r, h):
            return late_hbm.at[pl.ds(pl.multiple_of((big.me ^ r) * 2 * cut + h * cut, 16), cut)]

        def late_half(r, h):
            return late_buf.at[pl.ds(kept[r, h] * cut, cut)]

        def late_land(k):
            return late_buf.at[pl.ds((4 + k) * cut, cut)]

        late = ExpertSum(big.me, late_rows, late_half, late_land, lambda k: late_send.at[k], lambda k: late_recv.at[k])
        late.start()
        late_loads = [pltpu.make_async_copy(late_rows(r, h), late_half(r, h), late_sem.at[k]) for (r, h), k in kept.items()]
        for copy in late_loads:
            copy.start()
        in_rows = outs[5].shape[0]

        def late_end():
            for h in range(2):
                late.end(h, grad_hid.at[pl.ds(0, cut)])
                if h == 0:
                    copies = [pltpu.make_async_copy(grad_hid.at[pl.ds(0, cut)], outs[5].at[pl.ds(0, cut)], wide_sem.at[0])]
                else:
                    copies = [
                        pltpu.make_async_copy(grad_hid.at[pl.ds(0, in_rows - cut)], outs[5].at[pl.ds(cut, in_rows - cut)], wide_sem.at[0]),
                        pltpu.make_async_copy(grad_hid.at[pl.ds(in_rows - cut, 2 * cut - in_rows)], outs[6], wide_sem.at[1])]
                for copy in copies:
                    copy.start()
                for copy in copies:
                    copy.wait()
            late.finish()

    for copy in loads:
        copy.start()
    shard = width // n_dp
    side = shard // 2
    tile = 512
    lane = lanes_of((tree, 128))
    left = lane < HD

    def gain_row(i):
        return gains[...].astype(F32)[i : i + 1]

    bias[...] = mask_bias(parents, tree)

    names = routes_t[...].astype(F32)
    pick = jnp.where(lax.broadcasted_iota(jnp.int32, (16, 128), 0) == lanes_of((16, 128)), 1.0, 0.0).astype(LOW)
    names = dot(jnp.concatenate([names, jnp.zeros_like(names)], axis=0).astype(LOW), pick, 0, 0)
    chosen = jnp.zeros((tree, 128), F32)
    for k in range(routes_t.shape[0]):
        chosen = jnp.maximum(chosen, jnp.where(names[:, k : k + 1] == lane.astype(F32), 1.0, 0.0))
    logits = jnp.where(chosen > 0.5, dot(hidden2[...], router_t[...], 1, 1), -1e30)
    powers = jnp.exp(logits - jnp.max(logits, axis=1, keepdims=True))
    gate = powers / jnp.sum(powers, axis=1, keepdims=True)
    count = gates_in.shape[0]
    where_row = lax.broadcasted_iota(jnp.int32, (count, 128), 0)
    where_lane = lanes_of((count, 128))
    group_row = lax.rem(where_row, 8)
    target = lax.div(where_row, 8) * local + group_row
    pick = jnp.where(group_row < local, jnp.where(target == where_lane, 1.0, 0.0), 0.0).astype(LOW)
    high, low = two_parts(gates_in[...])
    gate_back = dot(high, pick, 0, 0) + dot(low, pick, 0, 0)
    grad_logits = (gate * (gate_back - jnp.sum(gate * gate_back, axis=1, keepdims=True))).astype(LOW)
    grad_router = dot(grad_logits, hidden2[...], 0, 0)[:EXPERTS]
    grad_hidden2 = hid_sum[...] + dot(grad_logits, router_t[...])
    back, gain2_sum = norm_back(middle[...], gain_row(1), grad_hidden2)
    grad_middle = cot[...].astype(F32) + back
    input_grad[...] = grad_middle
    branch[...] = grad_middle.astype(LOW)

    def chunk_grads(i, lhs, rhs_ref):
        def part(n, carry):
            made = dot(lhs[:, pl.ds(pl.multiple_of(n * tile, tile), tile)], rhs_ref[...], 0, 0).astype(LOW)
            for k in range(tile // side):
                own[i, n * (tile // shard) + k // 2, k % 2] = made[k * side : (k + 1) * side]
            return carry

        if tile % shard == 0:
            lax.fori_loop(0, width // tile, part, 0)

    for i in range(2):
        rhs[...] = branch[:, pl.ds(i * tile, tile)]
        chunk_grads(i, attended, rhs)
        big.start(i)

    loads[0].wait()

    def att_tile(n, carry):
        rows = pl.ds(pl.multiple_of(n * tile, tile), tile)
        grad_att[:, rows] = dot(branch[...], output_full[rows, :], 1, 1).astype(LOW)
        return carry

    lax.fori_loop(0, width // tile, att_tile, 0)

    def unrotate(field):
        return field * cosine[...] - turned(field * sine[...])

    scale = HD**-0.5

    def group(c):
        cols = pl.ds(pl.multiple_of(c * 128, 128), 128)
        pair, grad_pair = queries[:, cols], grad_att[:, cols]
        zero = jnp.zeros_like(pair)
        key, value = keys[c], values[c]
        grad_query, grad_key, grad_value = [], 0.0, 0.0
        for h in range(2):
            here = left if h == 0 else jnp.logical_not(left)
            query, grad_out = jnp.where(here, pair, zero), jnp.where(here, grad_pair, zero)
            logs = jnp.sum(jnp.where(lane == 2 * c + h, log_total[...], 0.0), axis=1, keepdims=True)
            probs = jnp.exp(dot(query, key, 1, 1) * scale + bias[...] - logs)
            grad_probs = dot(grad_out, value, 1, 1)
            grad_scores = (probs * (grad_probs - jnp.sum(probs * grad_probs, axis=1, keepdims=True))).astype(LOW)
            grad_value = grad_value + dot(probs.astype(LOW), grad_out, 0, 0)
            grad_query.append(dot(grad_scores, key))
            grad_key = grad_key + dot(grad_scores, query, 0, 0)
        grad_q_pre[:, cols] = unrotate(jnp.where(left, grad_query[0], grad_query[1]) * scale).astype(LOW)
        grad_key = (grad_key + pltpu.roll(grad_key, HD, 1)) * scale
        return unrotate(grad_key), grad_value + pltpu.roll(grad_value, HD, 1)

    def two_groups(i):
        key_a, value_a = group(2 * i)
        key_b, value_b = group(2 * i + 1)
        at = pl.multiple_of(i * 128, 128)
        grad_kv_pre[:, pl.ds(at, 128)] = jnp.where(left, key_a, key_b).astype(LOW)
        at = pl.multiple_of(KV * HD + i * 128, 128)
        grad_kv_pre[:, pl.ds(at, 128)] = jnp.where(left, value_a, value_b).astype(LOW)

    def gather_rhs(i):
        rhs[:, pl.ds(0, 256)] = grad_q_pre[:, pl.ds(i * 256, 256)]
        rhs[:, pl.ds(256, 128)] = grad_kv_pre[:, pl.ds(i * 128, 128)]
        rhs[:, pl.ds(384, 128)] = grad_kv_pre[:, pl.ds(KV * HD + i * 128, 128)]

    for i in range(KV // 2):
        two_groups(i)
        gather_rhs(i)
        chunk_grads(2 + i, hidden, rhs)
        big.start(2 + i)
        if i == 0:
            big.paired(0)
            big.paired(1)
        if i == 1:
            big.paired(2)
        if i == 2:
            big.paired(3)
        if i == 3:
            big.met(0, 0)
            big.met(1, 0)
            big.paired(4)
            big.met(2, 0)

    for copy in loads[1:]:
        copy.wait()

    def hidden_tile(n, carry):
        cols = pl.ds(pl.multiple_of(n * tile, tile), tile)
        grad_hid[:, cols] = dot(grad_q_pre[...], query_full[cols, :], 1, 1) + dot(grad_kv_pre[...], keyval_full[cols, :], 1, 1)
        return carry

    lax.fori_loop(0, width // tile, hidden_tile, 0)
    big.paired(5)
    big.met(3, 0)
    big.met(0, 1)
    big.line(0)
    big.met(1, 1)
    big.line(1)
    back, gain1_sum = norm_back(x_ref[...].astype(F32), gain_row(0), grad_hid[...])
    input_grad[...] = input_grad[...] + back
    input_copy = pltpu.make_async_copy(input_grad, input_hbm, load_sem.at[3])
    input_copy.start()

    sub = lax.broadcasted_iota(jnp.int32, (16, width), 0)
    sums = jnp.where(sub == 0, gain1_sum, jnp.where(sub == 1, gain2_sum, 0.0))
    little_all = jnp.concatenate([grad_router, sums], axis=0).astype(LOW)
    for d in range(n_dp):
        for k in range(2):
            at = d * shard + k * side
            own_s[0, d, k] = little_all[:, at : at + side]
    little.start(0)
    big.met(2, 1)
    big.line(2)
    big.met(4, 0)
    little.paired(0)
    big.met(3, 1)
    big.line(3)
    big.met(5, 0)
    if with_late:
        for copy in late_loads:
            copy.wait()
        late.turn()
    little.met(0, 0)
    big.met(4, 1)
    big.line(4)
    little.met(0, 1)
    big.met(5, 1)
    big.line(5)
    def place(i, which, field):
        rows = pl.ds(pl.multiple_of(which * side, 16), side)
        if i < 2:
            add_rows(grad_o.at[rows, pl.ds(i * tile, tile)], field)
            return
        i = i - 2
        add_rows(grad_q.at[rows, pl.ds(i * 256, 256)], field.at[:, pl.ds(0, 256)])
        add_rows(grad_kv.at[rows, pl.ds(i * 128, 128)], field.at[:, pl.ds(256, 128)])
        add_rows(grad_kv.at[rows, pl.ds(KV * HD + i * 128, 128)], field.at[:, pl.ds(384, 128)])

    def settle(i):
        big.last(i).wait_recv()
        place(i, 1 - big.core, big.other.at[i])

    chunks = own.shape[0]
    hop = 2 * (big.depth - 1)
    for t in range(chunks, chunks + hop):
        big.line(t)
        little.line(t - chunks)
        if t >= hop:
            big.close(t - hop)
            place(t - hop, big.core, big.final.at[t - hop])
        if t > hop:
            settle(t - hop - 1)
        if with_late and t == chunks + hop // 2:
            late_end()
    little.line(hop)
    little.close(0)
    add_rows(grad_s.at[big.core], little.final.at[0])
    settle(chunks - 1)
    for i in range(chunks):
        big.finish(i)
    little.last(0).wait_recv()
    add_rows(grad_s.at[1 - big.core], little.other.at[0])
    little.finish(0)
    input_copy.wait()


def back(n_dp, n_exp, local, tokens, cotangent, hid_sum, gates_in, routes_t, parents, tables, saved, late, collective_id):
    tree, width = tokens.shape
    shard = width // n_dp
    shape, vm, sem = jax.ShapeDtypeStruct, pltpu.VMEM, pltpu.SemaphoreType.DMA
    side, chunks, tile, rows = shard // 2, 6, 512, EXPERTS + 16
    big_bufs, big_sems = GradSum.scratch(n_dp, chunks, side, tile)
    little_bufs, little_sems = GradSum.scratch(n_dp, 1, rows, side)
    args = (tokens, cotangent, hid_sum, gates_in, routes_t, parents, *tables, *saved)
    spaces = [VMEM] * len(args)
    spaces[16:19] = [ANY] * 3
    out_shape = [
        shape((tree, width), F32), shape((shard, width), F32), shape((shard, width), F32), shape((shard, width), F32),
        shape((2, rows, side), F32),
    ]
    extra = []
    if late is not None:
        args, spaces = (*args, late), spaces + [ANY]
        out_rows = late.shape[0] // n_dp - shard
        out_shape += [shape((shard, width), F32), shape((out_rows, width), F32)]
        extra = [sem((4,)), sem((6,)), sem((6,)), sem((2,)), vm((10 * late.shape[0] // (2 * n_dp), width), LOW)]
    return pl.pallas_call(
        functools.partial(back_body, n_dp, n_exp, local, late is not None),
        out_shape=out_shape,
        in_specs=[pl.BlockSpec(memory_space=s) for s in spaces],
        out_specs=[pl.BlockSpec(memory_space=s) for s in ([ANY] + [VMEM] * 4 + [ANY] * 2)[: len(out_shape)]],
        scratch_shapes=[
            vm((tree, tree), F32), vm((tree, width), LOW), vm((tree, width), LOW), vm((tree, width), LOW), vm((tree, width), LOW),
            vm((tree, tile), LOW), vm((chunks, n_dp, 2, side, tile), LOW), vm((1, n_dp, 2, rows, side), LOW),
            vm((tree, width), F32), vm((width, width), LOW), vm((width, width), LOW), vm((width, width), LOW), sem((4,)), vm((tree, width), F32),
            *big_bufs, *big_sems, *little_bufs, *little_sems, *extra,
        ],
        compiler_params=pltpu.CompilerParams(
            collective_id=collective_id, has_side_effects=True, vmem_limit_bytes=63 * MIB),
        name="back",
    )(*args)


def rope_pairs(tree_rows):
    unit = tree_rows // 20
    row = np.arange(tree_rows)
    position = np.where(row < 8 * unit, row, np.where(row < 12 * unit, 8 * unit + row % unit, 9 * unit + row % unit))
    frequency = 10000.0 ** (-np.arange(0, HD, 2) / HD)
    angles = position[:, None] * frequency[None, :]
    return tuple(jnp.asarray(np.concatenate([table] * 4, axis=1), jnp.float32) for table in (np.cos(angles), np.sin(angles)))


def gated_unit(gate_up):
    width_ff = gate_up.shape[-1] // 2
    gate_part = gate_up[..., :width_ff]
    return gate_part / (1.0 + jnp.exp(-gate_part)) * gate_up[..., width_ff:]


def experts_plain(
    n_dp, n_exp, hidden2, grad_y, routes_all, router_full, expert_in, expert_out, middle
):
    tree_rows, width = hidden2.shape
    capacity = CAP
    routes_all = routes_all.transpose(0, 2, 1)
    expert_ids = jnp.arange(EXPERTS, dtype=jnp.int32)
    here = lax.axis_index("expert")
    local = expert_in.shape[0]
    first = here * local
    hidden_all = lax.all_gather(hidden2, "expert", axis=0, tiled=False)
    own_ids = first + jnp.arange(local, dtype=jnp.int32)
    hot_all = routes_all[:, :, :, None] == expert_ids[None, None, None, :]
    chosen_all = jnp.any(hot_all, axis=2)
    chosen = jnp.any(routes_all[:, :, :, None] == own_ids[None, None, None, :], axis=2)
    lower = jnp.tril(jnp.ones((tree_rows, tree_rows), jnp.bfloat16), -1)
    rank = jnp.einsum(
        "tu,jue->jet", lower, chosen.astype(jnp.bfloat16), preferred_element_type=jnp.float32
    ).astype(jnp.int32)
    slots = jnp.arange(capacity, dtype=jnp.int32)
    chosen_t = chosen.transpose(0, 2, 1)
    place = (rank[:, :, None, :] == slots[None, None, :, None]) & chosen_t[:, :, None, :]
    place = place.astype(jnp.bfloat16)
    logits_all = jnp.einsum(
        "jtd,de->jte", hidden_all, router_full, preferred_element_type=jnp.float32
    )
    masked = jnp.where(chosen_all, logits_all, -1e30)
    weight = jnp.exp(masked - jnp.max(masked, axis=-1, keepdims=True))
    weight = weight / jnp.sum(weight, axis=-1, keepdims=True)
    gates_own = lax.dynamic_slice_in_dim(weight, first, local, axis=2)
    gate_slot = jnp.einsum(
        "jest,jte->ejs", place.astype(jnp.float32), gates_own, precision=lax.Precision.HIGHEST
    )[..., None]
    sent = jnp.einsum("jest,jtd->ejsd", place, hidden_all, preferred_element_type=jnp.float32)
    sent = sent.astype(jnp.bfloat16)
    grad_rows = jnp.einsum("jest,jtd->ejsd", place, grad_y, preferred_element_type=jnp.float32)
    grad_rows = grad_rows.astype(jnp.bfloat16)
    gate_up = jnp.einsum("ejsd,edf->ejsf", sent, expert_in, preferred_element_type=jnp.float32)
    activated, glu_back = jax.vjp(gated_unit, gate_up)
    act_low = activated.astype(jnp.bfloat16).astype(jnp.float32)
    act_scaled = (act_low * gate_slot).astype(jnp.bfloat16)
    made = jnp.einsum(
        "ejsf,efd->ejsd", act_scaled, expert_out, preferred_element_type=jnp.float32
    ).astype(jnp.bfloat16)
    out_part = jnp.einsum("jest,ejsd->jtd", place, made, preferred_element_type=jnp.float32)
    out_sum = lax.psum_scatter(
        out_part.astype(jnp.bfloat16), "expert", scatter_dimension=0, tiled=False
    ).astype(jnp.float32)
    result = middle + out_sum
    block_out = result.astype(jnp.bfloat16)
    grad_act = jnp.einsum(
        "ejsd,efd->ejsf", grad_rows, expert_out, preferred_element_type=jnp.float32
    )
    gate_dot = jnp.sum(act_low * grad_act, axis=-1)
    gates_back = jnp.einsum(
        "jest,ejs->jte", place.astype(jnp.float32), gate_dot, precision=lax.Precision.HIGHEST
    )
    grad_out_w = jnp.einsum(
        "ejsf,ejsd->efd", act_scaled, grad_rows, preferred_element_type=jnp.float32
    )
    grad_gate_up = glu_back(grad_act * gate_slot)[0].astype(jnp.bfloat16)
    grad_sent = jnp.einsum(
        "ejsf,edf->ejsd", grad_gate_up, expert_in, preferred_element_type=jnp.float32
    ).astype(jnp.bfloat16)
    grad_in_w = jnp.einsum(
        "ejsd,ejsf->edf", sent, grad_gate_up, preferred_element_type=jnp.float32
    )
    hid_part = jnp.einsum("jest,ejsd->jtd", place, grad_sent, preferred_element_type=jnp.float32)
    gates_mine = lax.all_to_all(gates_back, "expert", split_axis=0, concat_axis=2, tiled=True)[0]
    hid_sum = lax.psum_scatter(
        hid_part.astype(jnp.bfloat16), "expert", scatter_dimension=0, tiled=False
    ).astype(jnp.float32)
    local, units = expert_in.shape[0], expert_out.shape[1]
    low = jnp.bfloat16
    grads = jnp.concatenate(
        [
            grad_in_w.astype(low).reshape(local, n_dp, width // n_dp, width),
            grad_out_w.astype(low).reshape(local, n_dp, units // n_dp, width),
        ],
        axis=2,
    ).reshape(local, width + units, width)
    share = lax.psum_scatter(grads, "dp", scatter_dimension=1, tiled=True).astype(jnp.float32)
    gates_mine = jnp.pad(gates_mine.T.reshape(n_exp, local, tree_rows), ((0, 0), (0, 8 - local), (0, 0)))
    return block_out, hid_sum, gates_mine, share[:, : width // n_dp], share[:, width // n_dp :]


def shards(
    tokens,
    attn_gain,
    w_query,
    w_keyval,
    w_output,
    moe_gain,
    w_router,
    expert_in,
    expert_out,
    cotangent,
    routes,
    parents,
):
    n_dp, n_exp = lax.axis_size("dp"), lax.axis_size("expert")
    local = expert_in.shape[0]
    tree_rows = tokens.shape[0]
    tables = rope_pairs(tree_rows)
    routes_t = routes.T
    (hidden, queries, keys, values, attended, middle, hidden2, log_total, *full, gains, routes_all, grad_y) = front(
        n_dp, n_exp, tokens, jnp.stack([attn_gain, moe_gain]), w_router.T, w_query, w_keyval, w_output, routes_t, parents, tables, cotangent, 1
    )
    router_t = full[3]
    if (n_dp, n_exp) == (4, 8):
        block_out, hid_sum, gate_grads, expert_in_share, expert_out_share, late = experts(
            n_dp, n_exp, hidden2, grad_y, routes_all, router_t, expert_in, expert_out, middle, 2
        )
    else:
        late = None
        block_out, hid_sum, gate_grads, expert_in_share, expert_out_share = experts_plain(
            n_dp, n_exp, hidden2, grad_y, routes_all, router_t[:EXPERTS].T, expert_in, expert_out, middle
        )
    saved = (hidden, queries, keys, values, attended, middle, hidden2, log_total, *full, gains)
    input_grad, grad_q, grad_kv, grad_o, grad_small, *made = back(
        n_dp, n_exp, local, tokens, cotangent, hid_sum, gate_grads.reshape(n_exp * 8, tree_rows), routes_t, parents, tables, saved, late, 3
    )
    if late is not None:
        expert_in_share = jnp.concatenate([expert_in_share, made[0][None]], axis=0)
        expert_out_share = jnp.concatenate([expert_out_share, made[1][None]], axis=0)
    return (
        block_out,
        input_grad,
        grad_small[:, EXPERTS].reshape(-1),
        grad_q,
        grad_kv,
        grad_o,
        grad_small[:, EXPERTS + 1].reshape(-1),
        jnp.concatenate([grad_small[0, :EXPERTS], grad_small[1, :EXPERTS]], axis=1).T,
        expert_in_share,
        expert_out_share,
    )


def solution(mesh):
    in_specs = (
        P(("dp", "expert"), None),
        P("dp"),
        P("dp", None),
        P("dp", None),
        P("dp", None),
        P("dp"),
        P("dp", None),
        P("expert", None, None),
        P("expert", None, None),
        P(("dp", "expert"), None),
        P(("dp", "expert"), None),
        P(("dp", "expert"), None),
    )
    out_specs = (
        P(("dp", "expert"), None),
        P(("dp", "expert"), None),
        P("dp"),
        P("dp", None),
        P("dp", None),
        P("dp", None),
        P("dp"),
        P("dp", None),
        P("expert", "dp", None),
        P("expert", "dp", None),
    )
    return jax.shard_map(shards, mesh=mesh, in_specs=in_specs, out_specs=out_specs, check_vma=False)
```

```python
import functools

import jax
import jax.numpy as jnp
import numpy as np
from jax import lax
from jax.experimental import pallas as pl
from jax.experimental.pallas import tpu as pltpu
from jax.sharding import PartitionSpec as P

H = 16
KV = 8
HD = 64
EXPERTS = 32
TOPK = 8
CAP = 120


EPSILON = 1e-06


MESH = pl.DeviceIdType.MESH
MIB = 1024 * 1024
VMEM = pltpu.VMEM
ANY = pl.ANY


def remote(src, dst, send_sem, recv_sem, **where):
    return pltpu.make_async_remote_copy(
        src_ref=src, dst_ref=dst, send_sem=send_sem, recv_sem=recv_sem,
        device_id=where, device_id_type=MESH,
    )


def greet(partners):
    barrier = pltpu.get_barrier_semaphore()
    for condition, where in partners:
        def signal(where=where):
            pl.semaphore_signal(barrier, inc=1, device_id=where, device_id_type=MESH)
        if condition is None:
            signal()
        else:
            pl.when(condition)(signal)
    count = sum(1 if c is None else c.astype(jnp.int32) for c, _ in partners)
    pl.semaphore_wait(barrier, count)


def add_rows(out, *terms):
    rows = out.shape[0]
    step = 32 if rows % 32 == 0 else 16

    def body(i, carry):
        at = pl.ds(pl.multiple_of(i * step, step), step)
        total = terms[0][at, :].astype(jnp.float32)
        for term in terms[1:]:
            total = total + term[at, :].astype(jnp.float32)
        out[at, :] = total.astype(out.dtype)
        return carry

    lax.fori_loop(0, rows // step, body, 0)


def bit_orders(n):
    bits = [1 << j for j in range(n.bit_length() - 1)]
    return [bits[p:] + bits[:p] for p in range(len(bits))] or [[]]


class Ring:
    def __init__(self, n_exp):
        self.mine = lax.axis_index("expert")
        self.core = lax.rem(self.mine, 2)
        self.z = lax.div(self.mine, 2)
        self.depth = n_exp // 2
        self.far = self.depth // 2
        self.pair = self.mine + 1 - 2 * self.core
        self.right, self.left = self.dev(1), self.dev(-1)

    def dev(self, d):
        return lax.rem(self.z + d + self.depth, self.depth) * 2 + self.core

    def partners(self):
        return [(None, {"expert": e}) for e in (self.pair, self.right, self.left)]


class RingGather:
    def __init__(self, ring, own, out, sems):
        self.ring, self.own, self.out = ring, own, out
        self.send, self.recv, self.pair_send, self.pair_recv = sems
        self.half = own.shape[0] // 2

    @staticmethod
    def scratch(n_exp):
        far, depth = n_exp // 4, n_exp // 2
        sem = pltpu.SemaphoreType.DMA
        return [sem((2, far + 1, 2)), sem((2, far + 1, 2)), sem((depth, 2)), sem((depth, 2))]

    def rows(self, h):
        return pl.ds(h * self.half, self.half)

    def goes(self, side, s, h):
        far = self.ring.far
        return s < far or (s == far and h == side)

    def block(self, d, h):
        return self.out.at[self.ring.dev(d), self.rows(h)]

    def hop(self, side, s, h):
        d = -s if side == 0 else s
        src = self.own.at[self.rows(h)] if s == 0 else self.block(d, h)
        to = self.ring.right if side == 0 else self.ring.left
        return remote(src, self.block(d, h), self.send.at[side, s, h], self.recv.at[side, s + 1, h], expert=to)

    def across(self, d, h):
        src = self.own.at[self.rows(h)] if d == 0 else self.block(d, h)
        slot = d % self.ring.depth
        return remote(src, self.block(d, h), self.pair_send.at[slot, h], self.pair_recv.at[slot, h], expert=self.ring.pair)

    ORDER = ((0, 0), (1, 1), (0, 1), (1, 0))

    def start(self):
        for side, h in self.ORDER:
            if self.goes(side, 1, h):
                self.hop(side, 0, h).start()
        self.across(0, 0).start()
        self.across(0, 1).start()

    def events(self):
        return [(side, s, h) for s in range(1, self.ring.far + 1) for side, h in self.ORDER if self.goes(side, s, h)]

    def handle(self, event):
        side, s, h = event
        d = -s if side == 0 else s
        here = self.block(d, h)
        remote(here, here, self.send.at[side, s, h], self.recv.at[side, s, h], expert=self.ring.mine).wait_recv()
        if self.goes(side, s + 1, h):
            self.hop(side, s, h).start()
        self.across(d, h).start()

    def wait_pair(self, d, h):
        slot = d % self.ring.depth
        here = self.out.at[self.ring.pair - self.ring.mine + self.ring.dev(d), self.rows(h)]
        remote(here, here, self.pair_send.at[slot, h], self.pair_recv.at[slot, h], expert=self.ring.mine).wait_recv()

    def finish_own(self):
        for side, h in self.ORDER:
            if self.goes(side, 1, h):
                self.hop(side, 0, h).wait_send()
        self.across(0, 0).wait_send()
        self.across(0, 1).wait_send()

    def finish_event(self, event):
        side, s, h = event
        if self.goes(side, s + 1, h):
            self.hop(side, s, h).wait_send()
        self.across(-s if side == 0 else s, h).wait_send()


class RingScatter:
    def __init__(self, ring, part, bufs, sems):
        self.ring, self.part = ring, part
        self.pair_buf, self.held, self.got = bufs
        self.pair_send, self.pair_recv, self.send, self.recv = sems
        self.half = self.held(0).shape[0] // 2

    @staticmethod
    def scratch(n_exp, block, dtype):
        far, depth = n_exp // 4, n_exp // 2
        sem = pltpu.SemaphoreType.DMA
        bufs = [pltpu.VMEM((depth,) + block, dtype), pltpu.VMEM((depth,) + block, dtype),
                pltpu.VMEM((2, far) + block, dtype)]
        return bufs, [sem((depth,)), sem((depth,)), sem((2, far + 1, 2)), sem((2, far + 1, 2))]

    def rows(self, h):
        return pl.ds(h * self.half, self.half)

    def order(self):
        far, depth = self.ring.far, self.ring.depth
        order = [far]
        for s in range(far - 1, 0, -1):
            order += [s, depth - s]
        return order + [0]

    def comes(self, side, d, h):
        far = self.ring.far
        return d + 1 < far or (d + 1 == far and h == side)

    def across(self, d):
        ring = self.ring
        return remote(self.part(d, 1), self.pair_buf(d),
                      self.pair_send.at[d], self.pair_recv.at[d], expert=ring.pair)

    def start_pair(self, d):
        self.across(d).start()

    def wait_pair(self, d):
        self.across(d).wait_recv()

    def wait_got(self, side, d, h):
        here = self.got(side, d).at[self.rows(h)]
        remote(here, here, self.send.at[side, d, h], self.recv.at[side, d, h], expert=self.ring.mine).wait_recv()

    def hop(self, side, d, h):
        slot = d if side == 0 else self.ring.depth - d
        rows = self.rows(h)
        return remote(self.held(slot).at[rows], self.got(side, d - 1).at[rows], self.send.at[side, d, h],
                      self.recv.at[side, d - 1, h], expert=self.ring.right if side == 0 else self.ring.left)

    def push(self, side, d, h):
        ring = self.ring
        slot = d if side == 0 else ring.depth - d
        rows = self.rows(h)
        terms = [self.part(slot, 0).at[rows], self.pair_buf(slot).at[rows]]
        if self.comes(side, d, h):
            self.wait_got(side, d, h)
            terms.append(self.got(side, d).at[rows])
        add_rows(self.held(slot).at[rows], *terms)
        self.hop(side, d, h).start()

    def first(self):
        far = self.ring.far
        self.wait_pair(far)
        self.push(0, far, 0)
        self.push(1, far, 1)

    def early(self):
        for d in range(self.ring.far - 1, 0, -1):
            self.wait_pair(d)
            self.push(0, d, 1)
            self.wait_pair(self.ring.depth - d)
            self.push(1, d, 0)

    def late(self):
        for d in range(self.ring.far - 1, 0, -1):
            self.push(0, d, 0)
            self.push(1, d, 1)

    def last(self, out, *more):
        self.wait_pair(0)
        for h in range(2):
            rows = self.rows(h)
            terms = [self.part(0, 0).at[rows], self.pair_buf(0).at[rows]] + [m.at[rows] for m in more]
            for side in range(2):
                if self.comes(side, 0, h):
                    self.wait_got(side, 0, h)
                    terms.append(self.got(side, 0).at[rows])
            add_rows(out.at[rows], *terms)

    def finish_sends(self):
        far = self.ring.far
        for side in range(2):
            for d in range(1, far + 1):
                for h in range(2):
                    if d < far or h == side:
                        self.hop(side, d, h).wait_send()
        for d in range(self.ring.depth):
            self.across(d).wait_send()


def views(bufs):
    pair_buf, held, got = bufs
    return (lambda d: pair_buf.at[d], lambda d: held.at[d], lambda side, d: got.at[side, d])


SLOTS = 128
F32, LOW = jnp.float32, jnp.bfloat16


def dot(a, b, over_a=1, over_b=0):
    return lax.dot_general(a, b, (((over_a,), (over_b,)), ((), ())), preferred_element_type=F32)


class ExpertSum:
    def __init__(self, me, first, half, land, send, recv):
        self.me, self.first, self.half, self.land, self.send, self.recv = me, first, half, land, send, recv

    def hop(self, step, h, which):
        bit = (1, 2)[h] if step == 0 else (2, 1)[h]
        r = bit if which == 0 else 3
        k = 2 * h + which if step == 0 else 4 + h
        src = self.first(r, h) if step == 0 else self.half(r, h)
        return remote(src, self.land(k), self.send(k), self.recv(k), dp=self.me ^ bit)

    def start(self, blocks=(1, 0)):
        for which in blocks:
            for h in range(2):
                self.hop(0, h, which).start()

    def turn(self, blocks=(1, 0)):
        for which in blocks:
            for h in range(2):
                self.hop(0, h, which).wait_recv()
                kept = 0 if which == 0 else (2, 1)[h]
                add_rows(self.half(kept, h), self.half(kept, h), self.land(2 * h + which))
                if which == 1:
                    self.hop(1, h, 0).start()

    def end(self, h, out):
        self.hop(1, h, 0).wait_recv()
        add_rows(out, self.half(0, h), self.land(4 + h))

    def finish(self):
        for step, h, which in ((0, 0, 0), (0, 0, 1), (0, 1, 0), (0, 1, 1), (1, 0, 0), (1, 1, 0)):
            self.hop(step, h, which).wait_send()


def experts_body(n_dp, n_exp, hid_ref, gy_hbm, routes_t, wr_t, w_in_hbm, w_out_hbm, middle,
                 block_out, hid_sum, gates_out, in_share, out_share, late,
                 x_all, w_in, w_out, sent, grows, gu, tmp, acts, stage, slots, gates, dots, wide,
                 pair_buf, held, got, *sems):
    w_sem, gy_sem, wide_sem, own_sem, ready, late_sem, gate_send, gate_recv, dp_ready, dp_send, dp_recv = sems[:11]
    gather_sems, out_sems, hid_sems = sems[11:15], sems[15:19], sems[19:23]
    me = lax.axis_index("dp")
    local, _, width = sent.shape
    tree, hidden_units = hid_ref.shape[0], w_out.shape[1]
    rows_e = local * SLOTS
    ring = Ring(n_exp)
    mine, core, depth = ring.mine, ring.core, ring.depth
    first = mine * local
    peers = [lax.rem(mine + k, n_exp) for k in range(1, n_exp)]
    greet([(None, {"expert": e}) for e in peers] + [(None, {"dp": me ^ bit}) for bit in (1, 2)])

    weights = [pltpu.make_async_copy(w_in_hbm, w_in, w_sem.at[0]), pltpu.make_async_copy(w_out_hbm, w_out, w_sem.at[1])]
    gather = RingGather(ring, hid_ref, x_all, gather_sems)
    gather.start()
    for copy in weights:
        copy.start()
    own = pltpu.make_async_copy(hid_ref, x_all.at[mine], own_sem)
    own.start()

    def gy_buf(j):
        return stage.at[lax.rem(j, 2), pl.ds(0, tree)]

    def gy_copy(j):
        return pltpu.make_async_copy(gy_hbm.at[j], gy_buf(j), gy_sem.at[lax.rem(j, 2)])

    gy_copy(0).start()

    below = (lax.broadcasted_iota(jnp.int32, (tree, tree), 0) < lax.broadcasted_iota(jnp.int32, (tree, tree), 1)).astype(LOW)
    sub16 = lax.broadcasted_iota(jnp.int32, (16, tree), 0)

    def find_slots(j, carry):
        names = routes_t[j]
        chosen = jnp.zeros((16, tree), F32)
        for k in range(names.shape[0]):
            chosen = jnp.maximum(chosen, jnp.where(names[k : k + 1, :] == first + sub16, 1.0, 0.0))
        chosen = jnp.where(sub16 < local, chosen, 0.0)
        rank = dot(chosen.astype(LOW), below)
        slots[j] = jnp.where(chosen > 0.5, rank, -1.0)[:8]
        return carry

    lax.fori_loop(0, n_exp, find_slots, 0)

    slot_ids = lax.broadcasted_iota(jnp.int32, (SLOTS, tree), 0).astype(F32)

    def places(j):
        return jnp.concatenate(
            [jnp.where(slot_ids == slots[j, i : i + 1, :], 1.0, 0.0).astype(LOW) for i in range(local)], axis=0)

    def places_t(j):
        lane = lax.broadcasted_iota(jnp.int32, (tree, 128), 1)
        pick = jnp.where(lax.broadcasted_iota(jnp.int32, (16, 128), 0) == lax.broadcasted_iota(jnp.int32, (16, 128), 1), 1.0, 0.0)
        slot = dot(jnp.concatenate([slots[j], jnp.zeros((8, tree), F32)], axis=0).astype(LOW), pick.astype(LOW), 0, 0)
        lanes = lane.astype(F32)
        return jnp.concatenate(
            [jnp.where(lanes == slot[:, i : i + 1], 1.0, 0.0).astype(LOW) for i in range(local)], axis=1)

    def find_gates(j):
        names = routes_t[j]
        experts = lax.broadcasted_iota(jnp.int32, (EXPERTS, tree), 0)
        chosen = jnp.zeros((EXPERTS, tree), F32)
        for k in range(names.shape[0]):
            chosen = jnp.maximum(chosen, jnp.where(names[k : k + 1, :] == experts, 1.0, 0.0))
        logits = jnp.where(chosen > 0.5, dot(wr_t[pl.ds(0, EXPERTS), :], x_all[j], 1, 1), -1e30)
        powers = jnp.exp(logits - jnp.max(logits, axis=0, keepdims=True))
        share = powers / jnp.sum(powers, axis=0, keepdims=True)
        sub = lax.broadcasted_iota(jnp.int32, (8, tree), 0)
        own_gates = jnp.zeros((8, tree), F32)
        for i in range(local):
            row = jnp.sum(jnp.where(experts == first + i, share, 0.0), axis=0, keepdims=True)
            own_gates = jnp.where(sub == i, row, own_gates)
        gates[j] = own_gates

    halves = width // 512

    def dispatch(j, src, dest):
        place = places(j)

        def body(n, carry):
            cols = pl.ds(pl.multiple_of(n * 512, 512), 512)
            picked = dot(place, src[:, cols]).astype(LOW)
            for i in range(local):
                dest[i, pl.ds(pl.multiple_of(j * SLOTS, SLOTS), SLOTS), cols] = picked[i * SLOTS : (i + 1) * SLOTS]
            return carry

        lax.fori_loop(0, halves, body, 0)

    def slot_gate(j, e):
        return jnp.sum(jnp.where(slot_ids == slots[j, pl.ds(e, 1), :], gates[j, pl.ds(e, 1), :], 0.0), axis=1, keepdims=True)

    def forward(chip):
        pair_rows = pl.ds(pl.multiple_of(chip * 2 * SLOTS, 2 * SLOTS), 2 * SLOTS)

        def one_tree(q, carry):
            j = 2 * chip + q
            find_gates(j)
            dispatch(j, x_all.at[j], sent)
            return carry

        lax.fori_loop(0, 2, one_tree, 0)

        def one_expert(e, carry):
            both = dot(sent[e, pair_rows, :], w_in[e])
            gu[e, pair_rows, :] = both.astype(LOW)
            a, b = both[:, :hidden_units], both[:, hidden_units:]
            act = (a / (1.0 + jnp.exp(-a)) * b).astype(LOW).astype(F32)
            gate = jnp.concatenate([slot_gate(2 * chip, e), slot_gate(2 * chip + 1, e)], axis=0)
            made = dot((act * gate).astype(LOW), w_out[e]).astype(LOW)
            for q in range(2):
                tmp[pl.ds(pl.multiple_of(q * rows_e + e * SLOTS, SLOTS), SLOTS), :] = made[q * SLOTS : (q + 1) * SLOTS]
            return carry

        lax.fori_loop(0, local, one_expert, 0)

    def combine_out(chip, q):
        rows = pl.ds(pl.multiple_of(q * rows_e, rows_e), rows_e)
        x_all[2 * chip + q] = dot(places_t(2 * chip + q), tmp[rows, :]).astype(LOW)

    def grad_rows(j, carry):
        pl.when(j + 1 < n_exp)(lambda: gy_copy(j + 1).start())
        gy_copy(j).wait()
        dispatch(j, gy_buf(j), grows)
        return carry

    events = gather.events()

    def out_part(d, other):
        return x_all.at[ring.dev(d) + other * (1 - 2 * core)]

    out = RingScatter(ring, out_part, views((pair_buf, held, got)), out_sems)

    def chip_at(d):
        return lax.rem(ring.z + d, depth)

    def group(g, carry):
        d = jnp.where(g == 0, 0, jnp.where(g == 1, depth - 1, jnp.where(g == 2, 1, 2)))
        chip = chip_at(d)

        @pl.when(g == 0)
        def _():
            own.wait()
            gather.wait_pair(0, 0)
            gather.wait_pair(0, 1)
            for copy in weights:
                copy.wait()

        @pl.when(g == 1)
        def _():
            for event in events[:4]:
                gather.handle(event)
            gather.wait_pair(-1, 0)
            gather.wait_pair(-1, 1)

        @pl.when(g == 2)
        def _():
            gather.wait_pair(1, 0)
            gather.wait_pair(1, 1)

        @pl.when(g == 3)
        def _():
            for event in events[4:]:
                gather.handle(event)
            out.early()
            gather.wait_pair(2, 0)
            gather.wait_pair(2, 1)

        forward(chip)

        @pl.when(g == 0)
        def _():
            gather.finish_own()
            lax.fori_loop(0, n_exp, grad_rows, 0)

        for at, d in ((1, -1), (2, 1), (3, 2)):
            @pl.when(g == at)
            def _():
                for event in events:
                    if event[1] == abs(d) and (abs(d) == 2 or (event[0] == 0) == (d < 0)):
                        gather.finish_event(event)

        combine_out(chip, 1 - core)
        pl.when(g == 0)(lambda: out.start_pair(0))
        pl.when(g == 1)(lambda: out.start_pair(depth - 1))
        pl.when(g == 2)(lambda: out.start_pair(1))
        pl.when(g == 3)(lambda: out.start_pair(2))
        combine_out(chip, core)
        return carry

    lax.fori_loop(0, depth, group, 0)
    out.first()
    middle_copy = pltpu.make_async_copy(middle, wide.at[pl.ds(0, tree)], wide_sem.at[0])
    middle_copy.start()

    in_rows, out_rows = width // n_dp, hidden_units // n_dp
    cut = (in_rows + out_rows) // 2

    def grad_half(e, r, h):
        at = 2 * r + h
        return gu.at[e, pl.ds(at * cut, cut)] if at < 5 else stage.at[e, pl.ds((at - 5) * cut, cut)]

    def grad_land(e, k):
        return w_in.at[e, pl.ds(k * cut, cut)] if k < 5 else w_out.at[e, pl.ds(0, cut)]

    def grad_sum(e):
        half = lambda r, h: grad_half(e, r, h)
        return ExpertSum(me, half, half, lambda k: grad_land(e, k), lambda k: dp_send.at[e, k], lambda k: dp_recv.at[e, k])

    def grads_start(e):
        pl.semaphore_wait(dp_ready.at[e], 2)
        grad_sum(e).start()

    def grads_turn(e):
        grad_sum(e).turn()

    def wide_copies(e):
        return (
            pltpu.make_async_copy(wide.at[pl.ds(0, in_rows)], in_share.at[e], wide_sem.at[0]),
            pltpu.make_async_copy(wide.at[pl.ds(in_rows, out_rows)], out_share.at[e], wide_sem.at[1]),
        )

    def grads_end(e):
        for h in range(2):
            grad_sum(e).end(h, wide.at[pl.ds(h * cut, cut)])
        for copy in wide_copies(e):
            copy.start()
        grad_sum(e).finish()
        for copy in wide_copies(e):
            copy.wait()

    block = 4 * SLOTS
    sub8 = lax.broadcasted_iota(jnp.int32, (8, tree), 0)

    def back_units(e):
        def one_block(m, inner):
            rows = pl.ds(pl.multiple_of(m * block, block), block)
            grad_act = dot(grows[e, rows, :], w_out[e], 1, 1)
            a = gu[e, rows, pl.ds(0, hidden_units)].astype(F32)
            b = gu[e, rows, pl.ds(hidden_units, hidden_units)].astype(F32)
            sg = 1.0 / (1.0 + jnp.exp(-a))
            sw = a * sg
            act = (sw * b).astype(LOW).astype(F32)
            gate = jnp.concatenate([slot_gate(4 * m + q, e) for q in range(4)], axis=0)
            told = jnp.sum(act * grad_act, axis=1, keepdims=True)
            acts[rows, :] = (act * gate).astype(LOW)
            grad_act = grad_act * gate
            tmp[rows, pl.ds(0, hidden_units)] = (grad_act * b * sg * (1.0 + a * (1.0 - sg))).astype(LOW)
            tmp[rows, pl.ds(hidden_units, hidden_units)] = (grad_act * sw).astype(LOW)
            for q in range(4):
                j = 4 * m + q
                row = jnp.sum(
                    jnp.where(slot_ids == slots[j, pl.ds(e, 1), :], told[q * SLOTS : (q + 1) * SLOTS], 0.0),
                    axis=0, keepdims=True)
                dots[j] = jnp.where(sub8 == e, row, dots[j])
            return inner

        lax.fori_loop(0, n_exp // 4, one_block, 0)

    def back_weights(e):
        for r in range(n_dp):
            d = me ^ r
            grad_in = dot(sent[e, :, pl.ds(pl.multiple_of(d * in_rows, in_rows), in_rows)], tmp[...], 0, 0).astype(LOW)
            grad_out = dot(acts[:, pl.ds(pl.multiple_of(d * out_rows, out_rows), out_rows)], grows[e], 0, 0).astype(LOW)
            grad_half(e, r, 0)[...] = grad_in[:cut]
            half = grad_half(e, r, 1)
            half[pl.ds(0, in_rows - cut), :] = grad_in[cut:]
            half[pl.ds(in_rows - cut, out_rows), :] = grad_out

    def back_rows(e, dest):
        def back_half(m, inner):
            rows = pl.ds(pl.multiple_of(m * 512, 512), 512)
            dest[rows, :] = dot(tmp[rows, :], w_in[e], 1, 1).astype(LOW)
            return inner

        lax.fori_loop(0, n_exp * SLOTS // 512, back_half, 0)

    end = local - 1

    def backward(e, carry):
        back_units(e)
        pl.when(e > 0)(lambda: grads_start(e - 1))
        back_weights(e)
        back_rows(e, sent.at[e])
        for bit in (1, 2):
            pl.semaphore_signal(dp_ready.at[e], inc=1, device_id={"dp": me ^ bit}, device_id_type=MESH)
        pl.when(e == 1)(out.late)
        return carry

    dots[...] = jnp.zeros(dots.shape, F32)
    lax.fori_loop(0, end, backward, 0)
    back_units(end)
    grads_start(end - 1)
    back_rows(end, grows.at[end - 1])


    def hid_part(d, other):
        if d == 0:
            return x_all.at[mine + other * (1 - 2 * core)]
        k = 2 * (d - 1) + other
        return grows.at[k // 3, pl.ds((k % 3) * tree, tree)]

    hid = RingScatter(ring, hid_part, views((pair_buf, held, got)), hid_sems)

    def combine_hid(d):
        for other in range(2):
            j = ring.dev(d) + other * (1 - 2 * core)
            rows = pl.ds(pl.multiple_of(j * SLOTS, SLOTS), SLOTS)
            made = jnp.concatenate([sent[i, rows, :] for i in range(end)] + [grows[end - 1, rows, :]], axis=0)
            hid_part(d, other)[...] = dot(places_t(j), made).astype(LOW)


    gate_copies = []
    for k, e in enumerate(peers):
        copy = remote(dots.at[e], gates_out.at[mine], gate_send.at[k], gate_recv.at[k], expert=e)
        copy.start()
        gate_copies.append(copy)
    gates_out[mine] = dots[mine]
    middle_copy.wait()
    out.last(block_out, wide.at[pl.ds(0, tree)])
    out.finish_sends()
    for partner in (ring.pair, ring.right, ring.left):
        pl.semaphore_signal(ready, inc=1, device_id={"expert": partner}, device_id_type=MESH)
    combine_hid(2)
    pl.semaphore_wait(ready, 3)
    hid.start_pair(2)
    combine_hid(1)
    hid.start_pair(1)
    hid.first()
    combine_hid(depth - 1)
    hid.start_pair(depth - 1)
    combine_hid(0)
    hid.start_pair(0)
    hid.early()
    back_weights(end)

    def late_copy(r, h):
        at = pl.multiple_of((me ^ r) * 2 * cut + h * cut, 16)
        return pltpu.make_async_copy(grad_half(end, r, h), late.at[pl.ds(at, cut)], late_sem.at[2 * r + h])

    for r in range(n_dp):
        for h in range(2):
            late_copy(r, h).start()
    hid.late()
    grads_turn(0)
    grads_turn(end - 2)
    grads_end(0)
    grads_turn(end - 1)
    grads_end(1)
    hid.last(wide.at[pl.ds(0, tree)])
    hid_copy = pltpu.make_async_copy(wide.at[pl.ds(0, tree)], hid_sum, wide_sem.at[0])
    hid_copy.start()
    hid_copy.wait()
    for e in range(2, end):
        grads_end(e)
    for r in range(n_dp):
        for h in range(2):
            late_copy(r, h).wait()
    for k, copy in enumerate(gate_copies):
        copy.wait_send()
        source = lax.rem(mine + n_exp - 1 - k, n_exp)
        remote(dots.at[mine], gates_out.at[source], gate_send.at[k], gate_recv.at[k], expert=mine).wait_recv()
    hid.finish_sends()


def experts(n_dp, n_exp, hidden2, grad_y, routes_all, router_t, expert_in, expert_out, middle, collective_id):
    local, width, both = expert_in.shape
    units = expert_out.shape[1]
    tree = hidden2.shape[0]
    rows = n_exp * SLOTS
    sem = pltpu.SemaphoreType.DMA
    bufs, out_sems = RingScatter.scratch(n_exp, (tree, width), LOW)
    _, hid_sems = RingScatter.scratch(n_exp, (tree, width), LOW)
    shape = jax.ShapeDtypeStruct
    return pl.pallas_call(
        functools.partial(experts_body, n_dp, n_exp),
        out_shape=[
            shape((tree, width), LOW),
            shape((tree, width), F32),
            shape((n_exp, 8, tree), F32),
            shape((local - 1, width // n_dp, width), F32),
            shape((local - 1, units // n_dp, width), F32),
            shape((width + units, width), LOW),
        ],
        in_specs=[pl.BlockSpec(memory_space=s) for s in (VMEM, ANY, VMEM, VMEM, ANY, ANY, ANY)],
        out_specs=[pl.BlockSpec(memory_space=s) for s in (VMEM, ANY, VMEM, ANY, ANY, ANY)],
        scratch_shapes=[
            pltpu.VMEM((n_exp, tree, width), LOW),
            pltpu.VMEM((local, width, both), LOW),
            pltpu.VMEM((local, units, width), LOW),
            pltpu.VMEM((local, rows, width), LOW),
            pltpu.VMEM((local, rows, width), LOW),
            pltpu.VMEM((local, rows, both), LOW),
            pltpu.VMEM((max(rows, 2 * local * SLOTS), width), LOW),
            pltpu.VMEM((rows, units), LOW),
            pltpu.VMEM((local, 3 * (width + units) // (2 * n_dp), width), LOW),
            pltpu.VMEM((n_exp, 8, tree), F32),
            pltpu.VMEM((n_exp, 8, tree), F32),
            pltpu.VMEM((n_exp, 8, tree), F32),
            pltpu.VMEM(((width + units) // n_dp, width), F32),
            *bufs,
            sem((2,)), sem((2,)), sem((2,)), sem, pltpu.SemaphoreType.REGULAR, sem((2 * n_dp,)), sem((n_exp - 1,)), sem((n_exp - 1,)),
            pltpu.SemaphoreType.REGULAR((local,)), sem((local, 6)), sem((local, 6)),
            *RingGather.scratch(n_exp), *out_sems, *hid_sems,
        ],
        compiler_params=pltpu.CompilerParams(
            collective_id=collective_id, has_side_effects=True, vmem_limit_bytes=63 * MIB),
        name="experts",
    )(hidden2, grad_y, routes_all, router_t, expert_in, expert_out, middle)


def lanes_of(shape):
    return lax.broadcasted_iota(jnp.int32, shape, 1)


def turned(field):
    low_half = lax.rem(lanes_of(field.shape), HD) < HD // 2
    return jnp.where(low_half, -pltpu.roll(field, 128 - HD // 2, 1), pltpu.roll(field, HD // 2, 1))


def mask_bias(parents, tree):
    unit = tree // 20

    def segment(row):
        return jnp.where(row < 8 * unit, 0, jnp.where(row < 12 * unit, 1 + lax.div(row - 8 * unit, unit), 5 + lax.div(row - 12 * unit, unit)))

    count = parents.shape[1]
    names = parents[...].astype(F32)
    wide = (tree, count)
    seg = segment(lax.broadcasted_iota(jnp.int32, wide, 0)).astype(F32)
    lane = lanes_of(wide).astype(F32)
    own = seg[:, :1]
    parent = jnp.sum(jnp.where(lane == seg, names, 0.0), axis=1, keepdims=True)
    grand = jnp.sum(jnp.where(lane == parent, names, 0.0), axis=1, keepdims=True)
    square = (tree, tree)
    row, col = lax.broadcasted_iota(jnp.int32, square, 0), lanes_of(square)
    there = segment(col).astype(F32)
    hit = jnp.maximum(
        jnp.maximum(jnp.where(there == own, 1.0, 0.0), jnp.where(there == parent, 1.0, 0.0)), jnp.where(there == grand, 1.0, 0.0))
    hit = jnp.where(col <= row, hit, 0.0)
    return jnp.where(hit > 0.5, 0.0, -1e30)


def inverse_rms(field):
    return lax.rsqrt(jnp.mean(field * field, axis=-1, keepdims=True) + EPSILON)


class DpGather:
    def __init__(self, n_dp, mine, me, ins, outs, sems):
        self.n_dp, self.me, self.ins, self.outs = n_dp, me, ins, outs
        self.send, self.recv, self.pair_send, self.pair_recv, self.own_sem = sems
        self.core = lax.rem(mine, 2)
        self.pair = mine + 1 - 2 * self.core
        self.shard = ins[0].shape[0]
        half = self.shard // 2
        self.orders = bit_orders(n_dp)
        self.cuts = min(2, len(self.orders), half // 16)
        self.size = half // self.cuts

    @staticmethod
    def scratch(count, n_dp):
        sem = pltpu.SemaphoreType.DMA
        bits = max(1, n_dp.bit_length() - 1)
        return [sem((count, 2, n_dp, bits)), sem((count, 2, n_dp)), sem((count, 2, n_dp)), sem((count, 2, n_dp)), sem((count,))]

    def rows(self, start, side, p):
        return pl.ds(pl.multiple_of(start + side * (self.shard // 2) + p * self.size, 16), self.size)

    def hop(self, a, p, r, bit):
        there = self.outs[a].at[self.rows((self.me ^ r) * self.shard, self.core, p)]
        src = self.ins[a].at[self.rows(0, self.core, p)] if r == 0 else there
        return remote(src, there, self.send.at[a, p, r, bit.bit_length() - 1], self.recv.at[a, p, r ^ bit], dp=self.me ^ bit)

    def own(self, a):
        at = pl.ds(pl.multiple_of(self.me * self.shard, 16), self.shard)
        return pltpu.make_async_copy(self.ins[a], self.outs[a].at[at], self.own_sem.at[a])

    def across(self, a, p, r, side):
        here = self.outs[a].at[self.rows((self.me ^ r) * self.shard, side, p)]
        return remote(here, here, self.pair_send.at[a, p, r], self.pair_recv.at[a, p, r], expert=self.pair)

    def start(self, a):
        for p in range(self.cuts):
            for bit in self.orders[p]:
                self.hop(a, p, 0, bit).start()
        self.own(a).start()

    def stage(self, p, j):
        order = self.orders[p]
        blocks = [0]
        for bit in order[:j]:
            blocks = blocks + [r | bit for r in blocks]
        return [r | order[j] for r in blocks], order[j + 1 :]

    def turn(self, a, j):
        for p in range(self.cuts):
            blocks, onward = self.stage(p, j)
            for r in blocks:
                here = self.outs[a].at[self.rows((self.me ^ r) * self.shard, self.core, p)]
                remote(here, here, self.send.at[a, p, r, 0], self.recv.at[a, p, r], dp=self.me).wait_recv()
                for bit in onward:
                    self.hop(a, p, r, bit).start()
                self.across(a, p, r, self.core).start()

    def ready(self, a):
        self.own(a).wait()
        for p in range(self.cuts):
            for r in range(1, self.n_dp):
                self.across(a, p, r, 1 - self.core).wait_recv()

    def finish(self, a):
        for p in range(self.cuts):
            for bit in self.orders[p]:
                self.hop(a, p, 0, bit).wait_send()
            for j in range(len(self.orders[p])):
                blocks, onward = self.stage(p, j)
                for r in blocks:
                    for bit in onward:
                        self.hop(a, p, r, bit).wait_send()
                    self.across(a, p, r, self.core).wait_send()


def front_body(n_dp, n_exp, x_ref, gain_pair, router_in, w_query, w_keyval, w_output, routes_t, parents, cosine, sine, cot,
               hidden_hbm, queries_hbm, keys_hbm, values_hbm, attended_hbm, middle_hbm, hidden2_hbm, log_hbm,
               query_hbm, keyval_hbm, output_hbm, router_t, gains, routes_all, grad_y,
               hidden, queries, keys, values, query_full, keyval_full, output_full, small, small_all, bias,
               attended, middle, hidden2, log_total, *sems):
    gather_sems, (small_send, small_recv, route_send, route_recv, out_sem), ring_sems = sems[:5], sems[5:10], sems[10:14]
    me, mine = lax.axis_index("dp"), lax.axis_index("expert")
    peers = [lax.rem(mine + k, n_exp) for k in range(1, n_exp)]
    greet([(None, {"expert": e}) for e in peers] + [(None, {"dp": me ^ k}) for k in range(1, n_dp)])
    tree, width = x_ref.shape
    shard = w_query.shape[0]

    small[...] = jnp.zeros(small.shape, LOW)
    small[pl.ds(0, EXPERTS), :] = router_in[...]
    sub = lax.broadcasted_iota(jnp.int32, (16, shard), 0)
    gain_rows = gain_pair[...].astype(F32)
    small[pl.ds(EXPERTS, 16), :] = jnp.where(sub == 0, gain_rows[:1], jnp.where(sub == 1, gain_rows[1:], 0.0)).astype(LOW)

    gather = DpGather(n_dp, mine, me, (w_query, w_keyval, w_output), (query_full, keyval_full, output_full), gather_sems)

    def small_copy(k):
        return remote(small, small_all.at[me], small_send.at[k], small_recv.at[k], dp=me ^ k)

    def route_copy(k, e):
        return remote(routes_t, routes_all.at[mine], route_send.at[k], route_recv.at[k], expert=e)

    saves = [
        pltpu.make_async_copy(src, dst, out_sem.at[k])
        for k, (src, dst) in enumerate((
            (query_full, query_hbm), (keyval_full, keyval_hbm), (output_full, output_hbm), (hidden, hidden_hbm),
            (queries, queries_hbm), (keys, keys_hbm), (values, values_hbm), (cot, grad_y.at[mine]),
            (attended, attended_hbm), (log_total, log_hbm), (middle, middle_hbm), (hidden2, hidden2_hbm)))
    ]
    ring = RingGather(Ring(n_exp), cot, grad_y, ring_sems)
    events = ring.events()
    for k in range(1, n_dp):
        small_copy(k).start()
    ring.start()
    gather.start(0)
    gather.start(1)
    saves[7].start()
    for k, e in enumerate(peers):
        route_copy(k, e).start()
    small_all[me] = small[...]
    routes_all[mine] = routes_t[...]
    bias[...] = mask_bias(parents, tree)
    log_total[...] = jnp.zeros(log_total.shape, F32)
    x = x_ref[...].astype(F32)
    scaled = x * inverse_rms(x)
    for k in range(1, n_dp):
        remote(small, small_all.at[me ^ k], small_send.at[k], small_recv.at[k], dp=me).wait_recv()
    joined = jnp.concatenate([small_all[d] for d in range(n_dp)], axis=1)
    router_t[...] = jnp.zeros(router_t.shape, LOW)
    router_t[pl.ds(0, EXPERTS), :] = joined[:EXPERTS]
    gains[...] = joined[EXPERTS:]
    gain_rows = joined[EXPERTS:].astype(F32)
    hidden[...] = (scaled * gain_rows[:1]).astype(LOW)
    saves[3].start()
    stages = len(gather.orders[0])
    for j in range(stages - 1):
        gather.turn(0, j)
        gather.turn(1, j)
    gather.start(2)
    for event in events[:2]:
        ring.handle(event)
    gather.turn(0, stages - 1)
    gather.turn(1, stages - 1)
    gather.ready(0)
    saves[0].start()

    def rotate(field):
        return field * cosine[...] + turned(field) * sine[...]

    left = lanes_of((tree, 128)) < HD
    tile = 512

    def query_tile(n, carry):
        cols = pl.ds(pl.multiple_of(n * tile, tile), tile)
        pre = dot(hidden[...], query_full[:, cols])
        for i in range(tile // 128):
            at = pl.multiple_of(n * tile + i * 128, 128)
            queries[:, pl.ds(at, 128)] = rotate(pre[:, i * 128 : (i + 1) * 128]).astype(LOW)
        return carry

    lax.fori_loop(0, width // tile, query_tile, 0)
    saves[4].start()
    gather.ready(1)
    saves[1].start()

    def spread(field, out, i):
        other = pltpu.roll(field, HD, 1)
        out[2 * i] = jnp.where(left, field, other).astype(LOW)
        out[2 * i + 1] = jnp.where(left, other, field).astype(LOW)

    half = KV * HD
    pre = dot(hidden[...], keyval_full[:, pl.ds(0, half)])
    for i in range(half // 128):
        spread(rotate(pre[:, i * 128 : (i + 1) * 128]), keys, i)
    saves[5].start()
    pre = dot(hidden[...], keyval_full[:, pl.ds(half, half)])
    for i in range(half // 128):
        spread(pre[:, i * 128 : (i + 1) * 128], values, i)
    saves[6].start()
    for j in range(stages):
        gather.turn(2, j)

    def heads(c, carry):
        cols = pl.ds(pl.multiple_of(c * 128, 128), 128)
        pair = queries[:, cols]
        made = []
        for h in range(2):
            mine_lanes = left if h == 0 else jnp.logical_not(left)
            query = jnp.where(mine_lanes, pair, jnp.zeros_like(pair))
            scores = dot(query, keys[c], 1, 1) * HD**-0.5 + bias[...]
            top = jnp.max(scores, axis=1, keepdims=True)
            powers = jnp.exp(scores - top)
            total = jnp.sum(powers, axis=1, keepdims=True)
            made.append(dot((powers / total).astype(LOW), values[c]))
            log_total[...] = jnp.where(lanes_of((tree, 128)) == 2 * c + h, top + jnp.log(total), log_total[...])
        attended[:, cols] = jnp.where(left, made[0], made[1]).astype(LOW)
        return carry

    lax.fori_loop(0, KV, heads, 0)
    saves[8].start()
    saves[9].start()
    for event in events[2:4]:
        ring.handle(event)
    gather.ready(2)
    saves[2].start()

    def middle_tile(n, carry):
        cols = pl.ds(pl.multiple_of(n * tile, tile), tile)
        middle[:, cols] = x_ref[:, cols].astype(F32) + dot(attended[...], output_full[:, cols])
        return carry

    lax.fori_loop(0, width // tile, middle_tile, 0)
    saves[10].start()
    field = middle[...]
    hidden2[...] = (field * inverse_rms(field) * gain_rows[1:2]).astype(LOW)
    saves[11].start()
    for a in range(3):
        gather.finish(a)
    for k in range(1, n_dp):
        small_copy(k).wait_send()
    for k, e in enumerate(peers):
        route_copy(k, e).wait_send()
        source = lax.rem(mine + n_exp - 1 - k, n_exp)
        remote(routes_t, routes_all.at[source], route_send.at[k], route_recv.at[k], expert=mine).wait_recv()
    for event in events[4:]:
        ring.handle(event)
    ring.finish_own()
    for h in range(2):
        ring.wait_pair(0, h)
    for event in events:
        ring.finish_event(event)
        ring.wait_pair(-event[1] if event[0] == 0 else event[1], event[2])
    for copy in saves:
        copy.wait()


def front(n_dp, n_exp, tokens, gain_pair, router_in, w_query, w_keyval, w_output, routes_t, parents, tables, cot, collective_id):
    tree, width = tokens.shape
    shard = w_query.shape[0]
    shape, sem, vm = jax.ShapeDtypeStruct, pltpu.SemaphoreType.DMA, pltpu.VMEM
    low = shape((tree, width), LOW)
    spread = shape((KV, tree, 128), LOW)
    full = shape((n_dp * shard, width), LOW)
    small = (EXPERTS + 16, shard)
    return pl.pallas_call(
        functools.partial(front_body, n_dp, n_exp),
        out_shape=[
            low, low, spread, spread, low, shape((tree, width), F32), low, shape((tree, 128), F32),
            full, full, full, shape((128, width), LOW), shape((16, width), LOW),
            shape((n_exp,) + routes_t.shape, jnp.int32), shape((n_exp, tree, width), LOW),
        ],
        in_specs=[pl.BlockSpec(memory_space=VMEM)] * 11,
        out_specs=[pl.BlockSpec(memory_space=s) for s in [ANY] * 11 + [VMEM] * 3 + [ANY]],
        scratch_shapes=[
            vm((tree, width), LOW), vm((tree, width), LOW), vm(spread.shape, LOW), vm(spread.shape, LOW),
            vm(full.shape, LOW), vm(full.shape, LOW), vm(full.shape, LOW),
            vm(small, LOW), vm((n_dp,) + small, LOW), vm((tree, tree), F32),
            vm((tree, width), LOW), vm((tree, width), F32), vm((tree, width), LOW), vm((tree, 128), F32),
            *DpGather.scratch(3, n_dp), sem((n_dp,)), sem((n_dp,)), sem((n_exp - 1,)), sem((n_exp - 1,)), sem((12,)),
            *RingGather.scratch(n_exp),
        ],
        compiler_params=pltpu.CompilerParams(
            collective_id=collective_id, has_side_effects=True, vmem_limit_bytes=56 * MIB),
        name="front",
    )(tokens, gain_pair, router_in, w_query, w_keyval, w_output, routes_t, parents, *tables, cot)


class GradSum:
    def __init__(self, n_dp, n_exp, chunks, own, bufs, sems):
        self.n_dp, self.chunks, self.own = n_dp, chunks, own
        (self.pair_in, self.dp_in, self.prefix, self.suffix, self.go_r, self.go_l, self.final, self.other) = bufs
        (self.pair_send, self.pair_recv, self.dp_send, self.dp_recv,
         self.send_r, self.send_l, self.recv_r, self.recv_l, self.last_send, self.last_recv) = sems
        self.me, self.mine = lax.axis_index("dp"), lax.axis_index("expert")
        self.core = lax.rem(self.mine, 2)
        self.z = lax.div(self.mine, 2)
        self.depth = n_exp // 2
        self.pair = self.mine + 1 - 2 * self.core
        self.has_left, self.has_right = self.z > 0, self.z < self.depth - 1
        self.orders = bit_orders(n_dp)

    @staticmethod
    def scratch(n_dp, chunks, half, columns):
        sem = pltpu.SemaphoreType.DMA
        stages = max(1, n_dp.bit_length() - 1)
        one = pltpu.VMEM((chunks, half, columns), LOW)
        many = pltpu.VMEM((chunks, n_dp, half, columns), LOW)
        bufs = [many, many, one, one, one, one, one, one]
        sems = [sem((chunks, n_dp)), sem((chunks, n_dp)), sem((chunks, n_dp)), sem((chunks, n_dp))]
        return bufs, sems + [sem((chunks,))] * 6

    def partners(self):
        return [(None, {"dp": self.me ^ bit}) for bit in self.orders[0]] + [
            (self.has_left, {"expert": self.mine - 2}), (self.has_right, {"expert": self.mine + 2})]

    def total(self, i, r):
        return self.own.at[i, self.me ^ r, self.core]

    def across(self, i, d):
        return remote(self.own.at[i, d, 1 - self.core], self.pair_in.at[i, d], self.pair_send.at[i, d],
                      self.pair_recv.at[i, d], expert=self.pair)

    def moved(self, i, j):
        order = self.orders[i % len(self.orders)]
        blocks = [0]
        for bit in order[j + 1 :]:
            blocks = blocks + [r | bit for r in blocks]
        return order[j], [r | order[j] for r in blocks]

    def dp_copy(self, i, r, bit):
        return remote(self.total(i, r), self.dp_in.at[i, r], self.dp_send.at[i, r], self.dp_recv.at[i, r], dp=self.me ^ bit)

    def start(self, i):
        for d in range(self.n_dp):
            self.across(i, d).start()

    def paired(self, i):
        for r in range(self.n_dp - 1, -1, -1):
            d = self.me ^ r
            self.across(i, d).wait_recv()
            add_rows(self.total(i, r), self.total(i, r), self.pair_in.at[i, d])
        self.leave(i, 0)

    def leave(self, i, j):
        if j < len(self.orders[0]):
            bit, blocks = self.moved(i, j)
            for r in blocks:
                self.dp_copy(i, r, bit).start()

    def met(self, i, j):
        bit, blocks = self.moved(i, j)
        for r in blocks:
            self.dp_copy(i, r, bit).wait_recv()
            add_rows(self.total(i, r ^ bit), self.total(i, r ^ bit), self.dp_in.at[i, r])
        self.leave(i, j + 1)

    def right(self, i):
        return remote(self.go_r.at[i], self.prefix.at[i], self.send_r.at[i], self.recv_r.at[i], expert=self.mine + 2)

    def left(self, i):
        return remote(self.go_l.at[i], self.suffix.at[i], self.send_l.at[i], self.recv_l.at[i], expert=self.mine - 2)

    def line(self, t):
        i = t - 2 * self.z
        has_left, has_right = self.has_left, self.has_right

        @pl.when(jnp.logical_and(i >= 0, i < self.chunks))
        def _():
            @pl.when(has_left)
            def _():
                remote(self.go_r.at[i], self.prefix.at[i], self.send_r.at[i], self.recv_r.at[i], expert=self.mine).wait_recv()

            @pl.when(jnp.logical_and(has_left, has_right))
            def _():
                add_rows(self.go_r.at[i], self.total(i, 0), self.prefix.at[i])

            @pl.when(jnp.logical_not(has_left))
            def _():
                add_rows(self.go_r.at[i], self.total(i, 0))

            pl.when(has_right)(lambda: self.right(i).start())

        k = t - 2 * (self.depth - 1 - self.z)

        @pl.when(jnp.logical_and(k >= 0, k < self.chunks))
        def _():
            @pl.when(has_right)
            def _():
                remote(self.go_l.at[k], self.suffix.at[k], self.send_l.at[k], self.recv_l.at[k], expert=self.mine).wait_recv()

            @pl.when(jnp.logical_and(has_left, has_right))
            def _():
                add_rows(self.go_l.at[k], self.total(k, 0), self.suffix.at[k])

            @pl.when(jnp.logical_not(has_right))
            def _():
                add_rows(self.go_l.at[k], self.total(k, 0))

            pl.when(has_left)(lambda: self.left(k).start())

    def last(self, i):
        return remote(self.final.at[i], self.other.at[i], self.last_send.at[i], self.last_recv.at[i], expert=self.pair)

    def close(self, i):
        has_left, has_right = self.has_left, self.has_right

        @pl.when(jnp.logical_and(has_left, has_right))
        def _():
            add_rows(self.final.at[i], self.total(i, 0), self.prefix.at[i], self.suffix.at[i])

        @pl.when(jnp.logical_not(has_left))
        def _():
            add_rows(self.final.at[i], self.total(i, 0), self.suffix.at[i])

        @pl.when(jnp.logical_not(has_right))
        def _():
            add_rows(self.final.at[i], self.total(i, 0), self.prefix.at[i])

        self.last(i).start()

    def finish(self, i):
        self.last(i).wait_send()
        pl.when(self.has_right)(lambda: self.right(i).wait_send())
        pl.when(self.has_left)(lambda: self.left(i).wait_send())
        for d in range(self.n_dp):
            self.across(i, d).wait_send()
        for j in range(len(self.orders[0])):
            bit, blocks = self.moved(i, j)
            for r in blocks:
                self.dp_copy(i, r, bit).wait_send()


def two_parts(field):
    high = field.astype(LOW)
    return high, (field - high.astype(F32)).astype(LOW)


def norm_back(field, gain, grad):
    r = inverse_rms(field)
    scaled = grad * gain
    back = r * scaled - field * (r * r * r) * jnp.mean(field * scaled, axis=-1, keepdims=True)
    return back, jnp.sum(field * r * grad, axis=0, keepdims=True)


def back_body(n_dp, n_exp, local, with_late, x_ref, cot, hid_sum, gates_in, routes_t, parents, cosine, sine,
              hidden, queries, keys, values, attended, middle, hidden2, log_total,
              query_hbm, keyval_hbm, output_hbm, router_t, gains, *refs):
    if with_late:
        late_hbm, refs = refs[0], refs[1:]
    outs, refs = refs[: 5 + 2 * with_late], refs[5 + 2 * with_late :]
    input_hbm, grad_q, grad_kv, grad_o, grad_s = outs[:5]
    (bias, branch, grad_att, grad_q_pre, grad_kv_pre, rhs, own, own_s, grad_hid, query_full, keyval_full, output_full,
     load_sem, input_grad, *rest) = refs
    big = GradSum(n_dp, n_exp, own.shape[0], own, rest[:8], rest[8:18])
    little = GradSum(n_dp, n_exp, 1, own_s, rest[18:26], rest[26:36])
    tree, width = x_ref.shape
    ring = Ring(n_exp)
    greet(big.partners() + [(None, {"expert": ring.pair})])
    loads = [
        pltpu.make_async_copy(src, dst, load_sem.at[k])
        for k, (src, dst) in enumerate(((output_hbm, output_full), (query_hbm, query_full), (keyval_hbm, keyval_full)))
    ]
    if with_late:
        late_sem, late_send, late_recv, wide_sem, late_buf = rest[36:41]
        cut = late_hbm.shape[0] // (2 * n_dp)
        kept = {(0, 0): 0, (0, 1): 1, (2, 0): 2, (1, 1): 3}

        def late_rows(r, h):
            return late_hbm.at[pl.ds(pl.multiple_of((big.me ^ r) * 2 * cut + h * cut, 16), cut)]

        def late_half(r, h):
            return late_buf.at[pl.ds(kept[r, h] * cut, cut)]

        def late_land(k):
            return late_buf.at[pl.ds((4 + k) * cut, cut)]

        late = ExpertSum(big.me, late_rows, late_half, late_land, lambda k: late_send.at[k], lambda k: late_recv.at[k])
        late.start()
        late_loads = [pltpu.make_async_copy(late_rows(r, h), late_half(r, h), late_sem.at[k]) for (r, h), k in kept.items()]
        for copy in late_loads:
            copy.start()
        in_rows = outs[5].shape[0]

        def late_end():
            for h in range(2):
                late.end(h, grad_hid.at[pl.ds(0, cut)])
                if h == 0:
                    copies = [pltpu.make_async_copy(grad_hid.at[pl.ds(0, cut)], outs[5].at[pl.ds(0, cut)], wide_sem.at[0])]
                else:
                    copies = [
                        pltpu.make_async_copy(grad_hid.at[pl.ds(0, in_rows - cut)], outs[5].at[pl.ds(cut, in_rows - cut)], wide_sem.at[0]),
                        pltpu.make_async_copy(grad_hid.at[pl.ds(in_rows - cut, 2 * cut - in_rows)], outs[6], wide_sem.at[1])]
                for copy in copies:
                    copy.start()
                for copy in copies:
                    copy.wait()
            late.finish()

    for copy in loads:
        copy.start()
    shard = width // n_dp
    side = shard // 2
    tile = 512
    lane = lanes_of((tree, 128))
    left = lane < HD

    def gain_row(i):
        return gains[...].astype(F32)[i : i + 1]

    bias[...] = mask_bias(parents, tree)

    names = routes_t[...].astype(F32)
    pick = jnp.where(lax.broadcasted_iota(jnp.int32, (16, 128), 0) == lanes_of((16, 128)), 1.0, 0.0).astype(LOW)
    names = dot(jnp.concatenate([names, jnp.zeros_like(names)], axis=0).astype(LOW), pick, 0, 0)
    chosen = jnp.zeros((tree, 128), F32)
    for k in range(routes_t.shape[0]):
        chosen = jnp.maximum(chosen, jnp.where(names[:, k : k + 1] == lane.astype(F32), 1.0, 0.0))
    logits = jnp.where(chosen > 0.5, dot(hidden2[...], router_t[...], 1, 1), -1e30)
    powers = jnp.exp(logits - jnp.max(logits, axis=1, keepdims=True))
    gate = powers / jnp.sum(powers, axis=1, keepdims=True)
    count = gates_in.shape[0]
    where_row = lax.broadcasted_iota(jnp.int32, (count, 128), 0)
    where_lane = lanes_of((count, 128))
    group_row = lax.rem(where_row, 8)
    target = lax.div(where_row, 8) * local + group_row
    pick = jnp.where(group_row < local, jnp.where(target == where_lane, 1.0, 0.0), 0.0).astype(LOW)
    high, low = two_parts(gates_in[...])
    gate_back = dot(high, pick, 0, 0) + dot(low, pick, 0, 0)
    grad_logits = (gate * (gate_back - jnp.sum(gate * gate_back, axis=1, keepdims=True))).astype(LOW)
    grad_router = dot(grad_logits, hidden2[...], 0, 0)[:EXPERTS]
    grad_hidden2 = hid_sum[...] + dot(grad_logits, router_t[...])
    back, gain2_sum = norm_back(middle[...], gain_row(1), grad_hidden2)
    grad_middle = cot[...].astype(F32) + back
    input_grad[...] = grad_middle
    branch[...] = grad_middle.astype(LOW)

    def chunk_grads(i, lhs, rhs_ref):
        def part(n, carry):
            made = dot(lhs[:, pl.ds(pl.multiple_of(n * tile, tile), tile)], rhs_ref[...], 0, 0).astype(LOW)
            for k in range(tile // side):
                own[i, n * (tile // shard) + k // 2, k % 2] = made[k * side : (k + 1) * side]
            return carry

        if tile % shard == 0:
            lax.fori_loop(0, width // tile, part, 0)

    for i in range(2):
        rhs[...] = branch[:, pl.ds(i * tile, tile)]
        chunk_grads(i, attended, rhs)
        big.start(i)

    loads[0].wait()

    def att_tile(n, carry):
        rows = pl.ds(pl.multiple_of(n * tile, tile), tile)
        grad_att[:, rows] = dot(branch[...], output_full[rows, :], 1, 1).astype(LOW)
        return carry

    lax.fori_loop(0, width // tile, att_tile, 0)

    def unrotate(field):
        return field * cosine[...] - turned(field * sine[...])

    scale = HD**-0.5

    def group(c):
        cols = pl.ds(pl.multiple_of(c * 128, 128), 128)
        pair, grad_pair = queries[:, cols], grad_att[:, cols]
        zero = jnp.zeros_like(pair)
        key, value = keys[c], values[c]
        grad_query, grad_key, grad_value = [], 0.0, 0.0
        for h in range(2):
            here = left if h == 0 else jnp.logical_not(left)
            query, grad_out = jnp.where(here, pair, zero), jnp.where(here, grad_pair, zero)
            logs = jnp.sum(jnp.where(lane == 2 * c + h, log_total[...], 0.0), axis=1, keepdims=True)
            probs = jnp.exp(dot(query, key, 1, 1) * scale + bias[...] - logs)
            grad_probs = dot(grad_out, value, 1, 1)
            grad_scores = (probs * (grad_probs - jnp.sum(probs * grad_probs, axis=1, keepdims=True))).astype(LOW)
            grad_value = grad_value + dot(probs.astype(LOW), grad_out, 0, 0)
            grad_query.append(dot(grad_scores, key))
            grad_key = grad_key + dot(grad_scores, query, 0, 0)
        grad_q_pre[:, cols] = unrotate(jnp.where(left, grad_query[0], grad_query[1]) * scale).astype(LOW)
        grad_key = (grad_key + pltpu.roll(grad_key, HD, 1)) * scale
        return unrotate(grad_key), grad_value + pltpu.roll(grad_value, HD, 1)

    def two_groups(i):
        key_a, value_a = group(2 * i)
        key_b, value_b = group(2 * i + 1)
        at = pl.multiple_of(i * 128, 128)
        grad_kv_pre[:, pl.ds(at, 128)] = jnp.where(left, key_a, key_b).astype(LOW)
        at = pl.multiple_of(KV * HD + i * 128, 128)
        grad_kv_pre[:, pl.ds(at, 128)] = jnp.where(left, value_a, value_b).astype(LOW)

    def gather_rhs(i):
        rhs[:, pl.ds(0, 256)] = grad_q_pre[:, pl.ds(i * 256, 256)]
        rhs[:, pl.ds(256, 128)] = grad_kv_pre[:, pl.ds(i * 128, 128)]
        rhs[:, pl.ds(384, 128)] = grad_kv_pre[:, pl.ds(KV * HD + i * 128, 128)]

    for i in range(KV // 2):
        two_groups(i)
        gather_rhs(i)
        chunk_grads(2 + i, hidden, rhs)
        big.start(2 + i)
        if i == 0:
            big.paired(0)
            big.paired(1)
        if i == 1:
            big.paired(2)
        if i == 2:
            big.paired(3)
        if i == 3:
            big.met(0, 0)
            big.met(1, 0)
            big.paired(4)
            big.met(2, 0)

    for copy in loads[1:]:
        copy.wait()

    def hidden_tile(n, carry):
        cols = pl.ds(pl.multiple_of(n * tile, tile), tile)
        grad_hid[:, cols] = dot(grad_q_pre[...], query_full[cols, :], 1, 1) + dot(grad_kv_pre[...], keyval_full[cols, :], 1, 1)
        return carry

    lax.fori_loop(0, width // tile, hidden_tile, 0)
    big.paired(5)
    big.met(3, 0)
    big.met(0, 1)
    big.line(0)
    big.met(1, 1)
    big.line(1)
    back, gain1_sum = norm_back(x_ref[...].astype(F32), gain_row(0), grad_hid[...])
    input_grad[...] = input_grad[...] + back
    input_copy = pltpu.make_async_copy(input_grad, input_hbm, load_sem.at[3])
    input_copy.start()

    sub = lax.broadcasted_iota(jnp.int32, (16, width), 0)
    sums = jnp.where(sub == 0, gain1_sum, jnp.where(sub == 1, gain2_sum, 0.0))
    little_all = jnp.concatenate([grad_router, sums], axis=0).astype(LOW)
    for d in range(n_dp):
        for k in range(2):
            at = d * shard + k * side
            own_s[0, d, k] = little_all[:, at : at + side]
    little.start(0)
    big.met(2, 1)
    big.line(2)
    big.met(4, 0)
    little.paired(0)
    big.met(3, 1)
    big.line(3)
    big.met(5, 0)
    if with_late:
        for copy in late_loads:
            copy.wait()
        late.turn()
    little.met(0, 0)
    big.met(4, 1)
    big.line(4)
    little.met(0, 1)
    big.met(5, 1)
    big.line(5)
    def place(i, which, field):
        rows = pl.ds(pl.multiple_of(which * side, 16), side)
        if i < 2:
            add_rows(grad_o.at[rows, pl.ds(i * tile, tile)], field)
            return
        i = i - 2
        add_rows(grad_q.at[rows, pl.ds(i * 256, 256)], field.at[:, pl.ds(0, 256)])
        add_rows(grad_kv.at[rows, pl.ds(i * 128, 128)], field.at[:, pl.ds(256, 128)])
        add_rows(grad_kv.at[rows, pl.ds(KV * HD + i * 128, 128)], field.at[:, pl.ds(384, 128)])

    def settle(i):
        big.last(i).wait_recv()
        place(i, 1 - big.core, big.other.at[i])

    chunks = own.shape[0]
    hop = 2 * (big.depth - 1)
    for t in range(chunks, chunks + hop):
        big.line(t)
        little.line(t - chunks)
        if t >= hop:
            big.close(t - hop)
            place(t - hop, big.core, big.final.at[t - hop])
        if t > hop:
            settle(t - hop - 1)
        if with_late and t == chunks + hop // 2:
            late_end()
    little.line(hop)
    little.close(0)
    add_rows(grad_s.at[big.core], little.final.at[0])
    settle(chunks - 1)
    for i in range(chunks):
        big.finish(i)
    little.last(0).wait_recv()
    add_rows(grad_s.at[1 - big.core], little.other.at[0])
    little.finish(0)
    input_copy.wait()


def back(n_dp, n_exp, local, tokens, cotangent, hid_sum, gates_in, routes_t, parents, tables, saved, late, collective_id):
    tree, width = tokens.shape
    shard = width // n_dp
    shape, vm, sem = jax.ShapeDtypeStruct, pltpu.VMEM, pltpu.SemaphoreType.DMA
    side, chunks, tile, rows = shard // 2, 6, 512, EXPERTS + 16
    big_bufs, big_sems = GradSum.scratch(n_dp, chunks, side, tile)
    little_bufs, little_sems = GradSum.scratch(n_dp, 1, rows, side)
    args = (tokens, cotangent, hid_sum, gates_in, routes_t, parents, *tables, *saved)
    spaces = [VMEM] * len(args)
    spaces[16:19] = [ANY] * 3
    out_shape = [
        shape((tree, width), F32), shape((shard, width), F32), shape((shard, width), F32), shape((shard, width), F32),
        shape((2, rows, side), F32),
    ]
    extra = []
    if late is not None:
        args, spaces = (*args, late), spaces + [ANY]
        out_rows = late.shape[0] // n_dp - shard
        out_shape += [shape((shard, width), F32), shape((out_rows, width), F32)]
        extra = [sem((4,)), sem((6,)), sem((6,)), sem((2,)), vm((10 * late.shape[0] // (2 * n_dp), width), LOW)]
    return pl.pallas_call(
        functools.partial(back_body, n_dp, n_exp, local, late is not None),
        out_shape=out_shape,
        in_specs=[pl.BlockSpec(memory_space=s) for s in spaces],
        out_specs=[pl.BlockSpec(memory_space=s) for s in ([ANY] + [VMEM] * 4 + [ANY] * 2)[: len(out_shape)]],
        scratch_shapes=[
            vm((tree, tree), F32), vm((tree, width), LOW), vm((tree, width), LOW), vm((tree, width), LOW), vm((tree, width), LOW),
            vm((tree, tile), LOW), vm((chunks, n_dp, 2, side, tile), LOW), vm((1, n_dp, 2, rows, side), LOW),
            vm((tree, width), F32), vm((width, width), LOW), vm((width, width), LOW), vm((width, width), LOW), sem((4,)), vm((tree, width), F32),
            *big_bufs, *big_sems, *little_bufs, *little_sems, *extra,
        ],
        compiler_params=pltpu.CompilerParams(
            collective_id=collective_id, has_side_effects=True, vmem_limit_bytes=63 * MIB),
        name="back",
    )(*args)


def rope_pairs(tree_rows):
    unit = tree_rows // 20
    row = np.arange(tree_rows)
    position = np.where(row < 8 * unit, row, np.where(row < 12 * unit, 8 * unit + row % unit, 9 * unit + row % unit))
    frequency = 10000.0 ** (-np.arange(0, HD, 2) / HD)
    angles = position[:, None] * frequency[None, :]
    return tuple(jnp.asarray(np.concatenate([table] * 4, axis=1), jnp.float32) for table in (np.cos(angles), np.sin(angles)))


def gated_unit(gate_up):
    width_ff = gate_up.shape[-1] // 2
    gate_part = gate_up[..., :width_ff]
    return gate_part / (1.0 + jnp.exp(-gate_part)) * gate_up[..., width_ff:]


def experts_plain(
    n_dp, n_exp, hidden2, grad_y, routes_all, router_full, expert_in, expert_out, middle
):
    tree_rows, width = hidden2.shape
    capacity = CAP
    routes_all = routes_all.transpose(0, 2, 1)
    expert_ids = jnp.arange(EXPERTS, dtype=jnp.int32)
    here = lax.axis_index("expert")
    local = expert_in.shape[0]
    first = here * local
    hidden_all = lax.all_gather(hidden2, "expert", axis=0, tiled=False)
    own_ids = first + jnp.arange(local, dtype=jnp.int32)
    hot_all = routes_all[:, :, :, None] == expert_ids[None, None, None, :]
    chosen_all = jnp.any(hot_all, axis=2)
    chosen = jnp.any(routes_all[:, :, :, None] == own_ids[None, None, None, :], axis=2)
    lower = jnp.tril(jnp.ones((tree_rows, tree_rows), jnp.bfloat16), -1)
    rank = jnp.einsum(
        "tu,jue->jet", lower, chosen.astype(jnp.bfloat16), preferred_element_type=jnp.float32
    ).astype(jnp.int32)
    slots = jnp.arange(capacity, dtype=jnp.int32)
    chosen_t = chosen.transpose(0, 2, 1)
    place = (rank[:, :, None, :] == slots[None, None, :, None]) & chosen_t[:, :, None, :]
    place = place.astype(jnp.bfloat16)
    logits_all = jnp.einsum(
        "jtd,de->jte", hidden_all, router_full, preferred_element_type=jnp.float32
    )
    masked = jnp.where(chosen_all, logits_all, -1e30)
    weight = jnp.exp(masked - jnp.max(masked, axis=-1, keepdims=True))
    weight = weight / jnp.sum(weight, axis=-1, keepdims=True)
    gates_own = lax.dynamic_slice_in_dim(weight, first, local, axis=2)
    gate_slot = jnp.einsum(
        "jest,jte->ejs", place.astype(jnp.float32), gates_own, precision=lax.Precision.HIGHEST
    )[..., None]
    sent = jnp.einsum("jest,jtd->ejsd", place, hidden_all, preferred_element_type=jnp.float32)
    sent = sent.astype(jnp.bfloat16)
    grad_rows = jnp.einsum("jest,jtd->ejsd", place, grad_y, preferred_element_type=jnp.float32)
    grad_rows = grad_rows.astype(jnp.bfloat16)
    gate_up = jnp.einsum("ejsd,edf->ejsf", sent, expert_in, preferred_element_type=jnp.float32)
    activated, glu_back = jax.vjp(gated_unit, gate_up)
    act_low = activated.astype(jnp.bfloat16).astype(jnp.float32)
    act_scaled = (act_low * gate_slot).astype(jnp.bfloat16)
    made = jnp.einsum(
        "ejsf,efd->ejsd", act_scaled, expert_out, preferred_element_type=jnp.float32
    ).astype(jnp.bfloat16)
    out_part = jnp.einsum("jest,ejsd->jtd", place, made, preferred_element_type=jnp.float32)
    out_sum = lax.psum_scatter(
        out_part.astype(jnp.bfloat16), "expert", scatter_dimension=0, tiled=False
    ).astype(jnp.float32)
    result = middle + out_sum
    block_out = result.astype(jnp.bfloat16)
    grad_act = jnp.einsum(
        "ejsd,efd->ejsf", grad_rows, expert_out, preferred_element_type=jnp.float32
    )
    gate_dot = jnp.sum(act_low * grad_act, axis=-1)
    gates_back = jnp.einsum(
        "jest,ejs->jte", place.astype(jnp.float32), gate_dot, precision=lax.Precision.HIGHEST
    )
    grad_out_w = jnp.einsum(
        "ejsf,ejsd->efd", act_scaled, grad_rows, preferred_element_type=jnp.float32
    )
    grad_gate_up = glu_back(grad_act * gate_slot)[0].astype(jnp.bfloat16)
    grad_sent = jnp.einsum(
        "ejsf,edf->ejsd", grad_gate_up, expert_in, preferred_element_type=jnp.float32
    ).astype(jnp.bfloat16)
    grad_in_w = jnp.einsum(
        "ejsd,ejsf->edf", sent, grad_gate_up, preferred_element_type=jnp.float32
    )
    hid_part = jnp.einsum("jest,ejsd->jtd", place, grad_sent, preferred_element_type=jnp.float32)
    gates_mine = lax.all_to_all(gates_back, "expert", split_axis=0, concat_axis=2, tiled=True)[0]
    hid_sum = lax.psum_scatter(
        hid_part.astype(jnp.bfloat16), "expert", scatter_dimension=0, tiled=False
    ).astype(jnp.float32)
    local, units = expert_in.shape[0], expert_out.shape[1]
    low = jnp.bfloat16
    grads = jnp.concatenate(
        [
            grad_in_w.astype(low).reshape(local, n_dp, width // n_dp, width),
            grad_out_w.astype(low).reshape(local, n_dp, units // n_dp, width),
        ],
        axis=2,
    ).reshape(local, width + units, width)
    share = lax.psum_scatter(grads, "dp", scatter_dimension=1, tiled=True).astype(jnp.float32)
    gates_mine = jnp.pad(gates_mine.T.reshape(n_exp, local, tree_rows), ((0, 0), (0, 8 - local), (0, 0)))
    return block_out, hid_sum, gates_mine, share[:, : width // n_dp], share[:, width // n_dp :]


def shards(
    tokens,
    attn_gain,
    w_query,
    w_keyval,
    w_output,
    moe_gain,
    w_router,
    expert_in,
    expert_out,
    cotangent,
    routes,
    parents,
):
    n_dp, n_exp = lax.axis_size("dp"), lax.axis_size("expert")
    local = expert_in.shape[0]
    tree_rows = tokens.shape[0]
    tables = rope_pairs(tree_rows)
    routes_t = routes.T
    (hidden, queries, keys, values, attended, middle, hidden2, log_total, *full, gains, routes_all, grad_y) = front(
        n_dp, n_exp, tokens, jnp.stack([attn_gain, moe_gain]), w_router.T, w_query, w_keyval, w_output, routes_t, parents, tables, cotangent, 1
    )
    router_t = full[3]
    if (n_dp, n_exp) == (4, 8):
        block_out, hid_sum, gate_grads, expert_in_share, expert_out_share, late = experts(
            n_dp, n_exp, hidden2, grad_y, routes_all, router_t, expert_in, expert_out, middle, 2
        )
    else:
        late = None
        block_out, hid_sum, gate_grads, expert_in_share, expert_out_share = experts_plain(
            n_dp, n_exp, hidden2, grad_y, routes_all, router_t[:EXPERTS].T, expert_in, expert_out, middle
        )
    saved = (hidden, queries, keys, values, attended, middle, hidden2, log_total, *full, gains)
    input_grad, grad_q, grad_kv, grad_o, grad_small, *made = back(
        n_dp, n_exp, local, tokens, cotangent, hid_sum, gate_grads.reshape(n_exp * 8, tree_rows), routes_t, parents, tables, saved, late, 3
    )
    if late is not None:
        expert_in_share = jnp.concatenate([expert_in_share, made[0][None]], axis=0)
        expert_out_share = jnp.concatenate([expert_out_share, made[1][None]], axis=0)
    return (
        block_out,
        input_grad,
        grad_small[:, EXPERTS].reshape(-1),
        grad_q,
        grad_kv,
        grad_o,
        grad_small[:, EXPERTS + 1].reshape(-1),
        jnp.concatenate([grad_small[0, :EXPERTS], grad_small[1, :EXPERTS]], axis=1).T,
        expert_in_share,
        expert_out_share,
    )


def solution(mesh):
    in_specs = (
        P(("dp", "expert"), None),
        P("dp"),
        P("dp", None),
        P("dp", None),
        P("dp", None),
        P("dp"),
        P("dp", None),
        P("expert", None, None),
        P("expert", None, None),
        P(("dp", "expert"), None),
        P(("dp", "expert"), None),
        P(("dp", "expert"), None),
    )
    out_specs = (
        P(("dp", "expert"), None),
        P(("dp", "expert"), None),
        P("dp"),
        P("dp", None),
        P("dp", None),
        P("dp", None),
        P("dp"),
        P("dp", None),
        P("expert", "dp", None),
        P("expert", "dp", None),
    )
    return jax.shard_map(shards, mesh=mesh, in_specs=in_specs, out_specs=out_specs, check_vma=False)
```
